128 devices in a mesh: fsdp: 16 (over z, y), tp: 8 (over x, core).
Axes of the slice: x: 4, y: 4, z: 4, core: 2. Of those that a mesh axis runs over, the one named last changes fastest.
Arguments:
- gradient: bfloat16 [28672, 8192], P('fsdp', 'tp'), may hold values from -6 to 6
- momentum: float32 [28672, 8192], P('fsdp', 'tp'), may hold values from -36 to 36
- basis: float32 [8192, 256], P('tp'), may hold values from -0.0625 to 0.0625
Outputs:
- new_momentum: float32 [28672, 8192], P('fsdp', 'tp')
- new_basis: float32 [8192, 256], P('tp')
- update: bfloat16 [28672, 8192], P('fsdp', 'tp')
The draws below stay inside these ranges and needn't reach their ends.
All inputs are finite; a program needn't handle non-finite values.
Results may differ from the reference program's by a relative error of at most 0.0015.
Values sent between devices are 32-bit elements; how exact they have to be, the bound alone decides.
A program may use at most 128 MiB of HBM per device.

```python
import math
import jax
import jax.numpy as jnp
from jax import lax

ROWS = 28672
COLS = 8192
RANK = 256


def draw_momentum(key, part):
    key = jax.random.fold_in(key, 7)
    key_rows, key_cols, key_vals = jax.random.split(key, 3)
    spread = math.log(3.0)
    values = jnp.clip(jax.random.normal(key_vals, (ROWS, COLS), jnp.float32), -4.0, 4.0)
    row_scale = jnp.exp(jax.random.uniform(key_rows, (ROWS, 1), jnp.float32, -spread, spread))
    col_scale = jnp.exp(jax.random.uniform(key_cols, (1, COLS), jnp.float32, -spread, spread))
    return values * row_scale * col_scale


def block_scale(stream_key, shape, cuts, low, largest):
    def one(axis_at, shards_of):
        steps = jax.random.uniform(jax.random.fold_in(jax.random.fold_in(stream_key, 6), axis_at), (shards_of,), jnp.float32, low / len(cuts), largest / len(cuts))
        return jnp.repeat(jnp.exp(steps), shape[axis_at] // shards_of).reshape((-1,) + (1,) * (len(shape) - axis_at - 1))

    gain = one(*cuts[0])
    for cut in cuts[1:]:
        gain = gain * one(*cut)
    return gain


def noise(key, shape, width, most, cuts=(), dtype=jnp.bfloat16):
    drawn = width * jax.random.normal(key, shape, jnp.float32)
    if cuts:
        drawn = drawn * block_scale(key, shape, cuts, -0.22, 0.18)
    return jnp.clip(drawn, -most, most).astype(dtype)


def setup_inputs(seed: int = 0) -> dict:
    keys = jax.random.split(jax.random.key(seed), 4)
    return {
        "gradient": noise(keys[0], (ROWS, COLS), 1.0, 6.0, ((0, 16), (1, 8))),
        "momentum": draw_momentum(jax.random.fold_in(keys[3], 71), 0),
        "basis": noise(keys[2], (COLS, RANK), COLS ** -0.5, 0.0625, ((0, 8),), jnp.float32),
    }


HIGH = lax.Precision.HIGHEST

def reference(gradient, momentum, basis):
    blend = momentum + gradient.astype(jnp.float32)
    projected = jnp.dot(blend.astype(jnp.float32), basis.astype(jnp.float32), precision=HIGH, preferred_element_type=jnp.float32)
    gram = lax.dot_general(projected.astype(jnp.float32), projected.astype(jnp.float32), (((0,), (0,)), ((), ())), precision=HIGH, preferred_element_type=jnp.float32)
    factor = jnp.linalg.cholesky(gram)
    ortho = lax.linalg.triangular_solve(factor, projected, left_side=False, lower=True, transpose_a=True)
    back = lax.dot_general(blend.astype(jnp.float32), ortho.astype(jnp.float32), (((0,), (0,)), ((), ())), precision=HIGH, preferred_element_type=jnp.float32)
    new_momentum = blend - 0.05 * jnp.dot(ortho.astype(jnp.float32), back.T.astype(jnp.float32), precision=HIGH, preferred_element_type=jnp.float32)
    squares = lax.optimization_barrier(jnp.sum(back * back, axis=0))
    new_basis = back * lax.rsqrt(squares + 1e-06)
    scale = math_scale(ROWS, COLS, RANK)
    update = (scale * jnp.dot(ortho.astype(jnp.float32), new_basis.T.astype(jnp.float32), precision=HIGH, preferred_element_type=jnp.float32)).astype(jnp.bfloat16)
    return (new_momentum, new_basis, update)

def math_scale(rows_all, cols_all, rank_all):
    return (rows_all * cols_all / rank_all) ** 0.5
```

```python
import functools

import jax
import jax.numpy as jnp
from jax import lax
from jax.experimental import pallas as pl
from jax.experimental.pallas import tpu as pltpu
from jax.sharding import PartitionSpec as P

ROWS = 28672
COLS = 8192
RANK = 256

F32 = jnp.float32
BF16 = jnp.bfloat16
HIGH = lax.Precision.HIGHEST
MESH = pl.DeviceIdType.MESH

LOCAL_ROWS = 1792
LOCAL_COLS = 1024
HALF = 896
PIECE = 224
PART = 112
WIDE = 512


class Names:
    def __init__(self):
        self.count = 0

    def take(self, many=1):
        first = self.count
        self.count += many
        return first


NAMES = Names()
N_HOP_A, N_HOP_B = NAMES.take(), NAMES.take()
N_LEFT_A, N_LEFT_B = NAMES.take(), NAMES.take()
N_RIGHT_A, N_RIGHT_B = NAMES.take(), NAMES.take()
G_LEFT_A, G_LEFT_B = NAMES.take(), NAMES.take()
G_RIGHT_A, G_RIGHT_B = NAMES.take(), NAMES.take()
G_OPP_A, G_OPP_B = NAMES.take(), NAMES.take()
N_CORE = NAMES.take(4)
G_CORE = NAMES.take(4)
GRAM_SUM = NAMES.take(15)
GRAM_X = NAMES.take(3)
GRAM_ALL = NAMES.take(15)
SQ = NAMES.take(7)
GRAM_CORE = NAMES.take()
W_HOP = NAMES.take(4)
W_NEXT = NAMES.take(8)
W_RING = NAMES.take(8)
W_FAR = NAMES.take(4)
W_SUB = NAMES.take(6)
W_ALL = NAMES.take(6)


def nn(a, b, precision=None):
    return lax.dot_general(
        a, b, (((1,), (0,)), ((), ())), precision=precision, preferred_element_type=F32
    )


def tn(a, b, precision=None):
    return lax.dot_general(
        a, b, (((0,), (0,)), ((), ())), precision=precision, preferred_element_type=F32
    )


def nt(a, b, precision=None):
    return lax.dot_general(
        a, b, (((1,), (1,)), ((), ())), precision=precision, preferred_element_type=F32
    )


def pick(index, values):
    out = values[0]
    for at in range(1, len(values)):
        out = out + (values[at] - values[at - 1]) * ((index + len(values) - at) // len(values))
    return out


def split(x):
    hi = x.astype(BF16)
    return hi, (x - hi.astype(F32)).astype(BF16)


def row_copy(x, j):
    return jnp.broadcast_to(x[j : j + 1, :], (8, 128))


def inverse_factor(x):
    n = len(x)
    sub = lax.broadcasted_iota(jnp.int32, (8, 128), 0)
    lane = lax.broadcasted_iota(jnp.int32, (8, 128), 1)
    col = [
        [None if i < k // 8 else jnp.broadcast_to(x[i][:, k : k + 1], (8, 128)) for i in range(n)]
        for k in range(8 * n)
    ]
    inverse = [jnp.where(lane == sub + 8 * i, 1.0, 0.0) for i in range(n)]
    for j in range(8 * n):
        g, r = j // 8, j % 8
        pivot = row_copy(col[j][g], r)
        inv = 1.0 / pivot
        row = row_copy(inverse[g], r)
        entry = {k: row_copy(col[j][k // 8], k % 8) for k in range(j + 1, 8 * n)}
        mult = [None if i < g else col[j][i] * inv for i in range(n)]
        if r < 7:
            mult[g] = jnp.where(sub > r, mult[g], 0.0)
        for k in range(j + 1, 8 * n):
            for i in range(k // 8, n):
                col[k][i] = col[k][i] - mult[i] * entry[k]
        for i in range(g + (r == 7), n):
            inverse[i] = inverse[i] - mult[i] * row
        inverse[g] = jnp.where(sub == r, row * lax.rsqrt(pivot), inverse[g])
    return jnp.concatenate(inverse, axis=0)


def eliminate(k, m_ref):
    rows = pl.ds(pl.multiple_of(32 * k, 32), 32)
    tile = pl.ds(pl.multiple_of(128 * (k // 4), 128), 128)
    d = pltpu.roll(m_ref[rows, tile], (128 - 32 * (k % 4)) % 128, 1)
    inverse = inverse_factor([d[8 * i : 8 * i + 8] for i in range(4)])
    scaled = nn(inverse[:, :32], m_ref[rows, :], HIGH)
    m_ref[rows, :] = scaled

    @pl.when(k < 7)
    def _():
        subl = lax.broadcasted_iota(jnp.int32, (RANK, 32), 0)
        lower = jnp.where(subl >= 32 * k + 32, scaled[:, :RANK].T, 0.0)
        m_ref[...] -= nn(lower, scaled, HIGH)


def main_kernel(
    grad,
    mom,
    basis,
    blend_out,
    ortho_out,
    back_out,
    norm_out,
    grad_v,
    basis_v,
    bases,
    hi_v,
    lo_v,
    part_v,
    from_core,
    hop_v,
    side_v,
    proj,
    gram_part,
    gram_in,
    gram_x,
    gram,
    elim,
    turned,
    w,
    w_hop,
    w_side,
    w_sub,
    w_full,
    sq_v,
    load_sem,
    send_sem,
    recv_sem,
):
    f = lax.axis_index("fsdp")
    t = lax.axis_index("tp")
    x, c = t // 2, t % 2
    z, y = f // 4, f % 4

    def tp_dev(xx, cc):
        return {"fsdp": f, "tp": xx * 2 + cc}

    def f_dev(ff):
        return {"fsdp": ff, "tp": t}

    right = tp_dev((x + 1) % 4, c)
    left = tp_dev((x + 3) % 4, c)
    twin = tp_dev(x, 1 - c)

    def remote(src, dst, number, device):
        return pltpu.make_async_remote_copy(
            src_ref=src,
            dst_ref=dst,
            send_sem=send_sem.at[number],
            recv_sem=recv_sem.at[number],
            device_id=device,
            device_id_type=MESH,
        )

    def send(src, dst, number, device):
        remote(src, dst, number, device).start()

    def arrive(dst, number):
        remote(dst, dst, number, twin).wait_recv()

    def all_sent(first, many, ref):
        @pl.loop(first, first + many)
        def _(number):
            remote(ref, ref, number, twin).wait_send()

    def piece_row(core, chip):
        return pl.multiple_of(core * HALF + chip * PIECE, 32)

    def chunk_row(i):
        g = 3 - i // 2
        d = g + (g // 2) * (1 - 2 * (g % 2))
        core = (1 - c) * (1 - i % 2) + c * (i % 2)
        return piece_row(core, (x + d) % 4)

    def load(i):
        rows = pl.ds(chunk_row(i), PIECE)
        return (
            pltpu.make_async_copy(mom.at[rows], blend_out.at[rows], load_sem.at[2 * i]),
            pltpu.make_async_copy(grad.at[rows], grad_v.at[i % 4], load_sem.at[2 * i + 1]),
        )

    basis_copy = pltpu.make_async_copy(basis, basis_v, load_sem.at[16])
    basis_copy.start()

    @pl.loop(0, 3)
    def _(i):
        for copy in load(i):
            copy.start()

    barrier = pltpu.get_barrier_semaphore()

    @pl.loop(1, 16)
    def _(d):
        pl.semaphore_signal(barrier, inc=1, device_id=f_dev((f + d) % 16), device_id_type=MESH)

    @pl.loop(1, 8)
    def _(d):
        pl.semaphore_signal(
            barrier, inc=1, device_id={"fsdp": f, "tp": (t + d) % 8}, device_id_type=MESH
        )

    basis_copy.wait()
    basis_hi, basis_lo = split(basis_v[...])
    bases[:LOCAL_COLS] = basis_hi
    bases[LOCAL_COLS : 2 * LOCAL_COLS] = basis_lo
    bases[2 * LOCAL_COLS :] = basis_hi
    turned[...] = jnp.zeros_like(turned)
    hi_v[LOCAL_ROWS:, :] = jnp.zeros((32, LOCAL_COLS), BF16)
    lo_v[LOCAL_ROWS:, :] = jnp.zeros((32, LOCAL_COLS), BF16)

    def partial(i):
        for copy in load(i):
            copy.wait()
        rows = pl.ds(chunk_row(i), PIECE)

        @pl.when(i < 5)
        def _():
            for copy in load(i + 3):
                copy.start()

        blend = blend_out[rows, :] + grad_v[i % 4].astype(F32)
        blend_out[rows, :] = blend
        hi, lo = split(blend)
        hi_v[rows, :] = hi
        lo_v[rows, :] = lo
        return nn(jnp.concatenate([hi, hi, lo], axis=1), bases[...])

    a_rows, b_rows = pl.ds(0, PART), pl.ds(PART, PART)

    def add_core(j):
        arrive(from_core.at[j], N_CORE + j)
        part_v[2 * j + 1] += from_core[j]

    @pl.loop(0, 8)
    def _(i):
        part_v[i] = partial(i)
        j = i // 2
        core = remote(part_v.at[i], from_core.at[j], N_CORE + j, twin)

        @pl.when(i == 0)
        def _():
            pl.semaphore_wait(barrier, 22)

        @pl.when(i % 2 == 0)
        def _():
            core.start()

        @pl.when(i == 2)
        def _():
            add_core(0)
            send(part_v.at[1, a_rows], hop_v.at[0], N_HOP_A, right)
            send(part_v.at[1, b_rows], hop_v.at[1], N_HOP_B, left)

        @pl.when(i == 4)
        def _():
            add_core(1)
            send(part_v.at[3, a_rows], side_v.at[2], N_RIGHT_A, left)

        @pl.when(i == 6)
        def _():
            add_core(2)
            send(part_v.at[5, b_rows], side_v.at[1], N_LEFT_B, right)

    add_core(3)
    arrive(hop_v.at[0], N_HOP_A)
    part_v[5, a_rows] += hop_v[0]
    send(part_v.at[5, a_rows], side_v.at[0], N_LEFT_A, right)
    arrive(hop_v.at[1], N_HOP_B)
    part_v[3, b_rows] += hop_v[1]
    send(part_v.at[3, b_rows], side_v.at[3], N_RIGHT_B, left)

    my_row = piece_row(c, x)
    arrive(side_v.at[2], N_RIGHT_A)
    arrive(side_v.at[0], N_LEFT_A)
    proj[pl.ds(my_row, PART), :] = part_v[7, a_rows] + (side_v[0] + side_v[2])
    arrive(side_v.at[1], N_LEFT_B)
    arrive(side_v.at[3], N_RIGHT_B)
    proj[pl.ds(my_row + PART, PART), :] = part_v[7, b_rows] + (side_v[1] + side_v[3])

    def part_of(core, chip, b):
        return proj.at[pl.ds(pl.multiple_of(piece_row(core, chip) + b * PART, 16), PART)]

    def whole_of(core, chip):
        return proj.at[pl.ds(piece_row(core, chip), PIECE)]

    def send_part(chip, b, number, device):
        send(part_of(c, chip, b), part_of(c, chip, b), number, device)

    def send_whole(chip, number):
        send(whole_of(c, chip), whole_of(c, chip), number, twin)

    xl, xr, xo = (x + 3) % 4, (x + 1) % 4, (x + 2) % 4
    send_part(x, 0, G_LEFT_A, right)
    send_part(x, 1, G_RIGHT_B, left)
    send_whole(x, G_CORE)
    send_part(x, 1, G_LEFT_B, right)
    send_part(x, 0, G_RIGHT_A, left)

    half_cols = pl.ds(pl.multiple_of(c * 128, 128), 128)

    def eight(row):
        return pl.ds(pl.multiple_of(row * 8, 8), 8)

    def gram_start():
        gram_part[...] = jnp.zeros((128, RANK), F32)

        @pl.loop(0, 2)
        def _(core):
            rows = pl.ds(piece_row(core, x), PIECE)
            gram_part[...] += tn(proj[rows, half_cols], proj[rows, :], HIGH)

        @pl.loop(1, 16)
        def _(d):
            to = (f + d) % 16
            send(gram_part.at[eight(to)], gram_in.at[d], GRAM_SUM + d - 1, f_dev(to))

    def gram_across():
        gram_in[0] = gram_part[eight(f), :]

        @pl.loop(1, 16)
        def _(d):
            arrive(gram_in.at[d], GRAM_SUM + d - 1)

        gram_x[x] = jnp.sum(gram_in[...], axis=0)

        @pl.loop(1, 4)
        def _(d):
            send(gram_x.at[x], gram_x.at[x], GRAM_X + d - 1, tp_dev((x + d) % 4, c))

    def gram_row(ff):
        return pl.ds(pl.multiple_of(c * 128 + ff * 8, 8), 8)

    def gram_round():
        @pl.loop(1, 4)
        def _(d):
            arrive(gram_x.at[(x + 4 - d) % 4], GRAM_X + d - 1)

        gram[gram_row(f), :] = (gram_x[0] + gram_x[1]) + (gram_x[2] + gram_x[3])

        @pl.loop(1, 16)
        def _(d):
            mine = gram.at[gram_row(f)]
            send(mine, mine, GRAM_ALL + d - 1, f_dev((f + d) % 16))

    def gram_half(core):
        return gram.at[pl.ds(pl.multiple_of(core * 128, 128), 128)]

    def gram_pair():
        @pl.loop(1, 16)
        def _(d):
            arrive(gram.at[gram_row((f + 16 - d) % 16)], GRAM_ALL + d - 1)

        send(gram_half(c), gram_half(c), GRAM_CORE, twin)

    w[...] = jnp.zeros_like(w)

    @pl.loop(0, 8)
    def _(g):
        core = (c + pick(g, (0, 1, 0, 0, 0, 1, 1, 1))) % 2
        chip = (x + pick(g, (0, 0, 1, 3, 2, 1, 3, 2))) % 4

        @pl.when(g == 1)
        def _():
            arrive(whole_of(1 - c, x), G_CORE)
            gram_start()

        @pl.when(g == 2)
        def _():
            arrive(part_of(c, xl, 0), G_LEFT_A)
            send_part(xl, 0, G_OPP_A, right)
            arrive(part_of(c, xr, 1), G_RIGHT_B)
            send_part(xr, 1, G_OPP_B, left)
            gram_across()
            arrive(part_of(c, xr, 0), G_RIGHT_A)
            send_whole(xr, G_CORE + 1)
            arrive(part_of(c, xl, 1), G_LEFT_B)
            send_whole(xl, G_CORE + 2)

        @pl.when(g == 4)
        def _():
            arrive(part_of(c, xo, 0), G_OPP_A)
            arrive(part_of(c, xo, 1), G_OPP_B)
            send_whole(xo, G_CORE + 3)
            gram_round()

        @pl.when(g == 5)
        def _():
            arrive(whole_of(1 - c, xr), G_CORE + 1)

        @pl.when(g == 6)
        def _():
            arrive(whole_of(1 - c, xl), G_CORE + 2)

        @pl.when(g == 7)
        def _():
            arrive(whole_of(1 - c, xo), G_CORE + 3)

        rows = pl.ds(piece_row(core, chip), PIECE)
        p_hi, p_lo = split(proj[rows, :].T)
        turned[:, :PIECE] = p_hi
        turned[:, 256 : 256 + PIECE] = p_hi
        turned[:, 512 : 512 + PIECE] = p_lo
        more = pl.ds(piece_row(core, chip), 256)
        for n in range(4):
            cols = slice(256 * n, 256 * n + 256)
            hi = hi_v[more, cols]
            w[:, cols] += nn(turned[...], jnp.concatenate([hi, lo_v[more, cols], hi], axis=0))

    def places(h):
        k, q = y + h * (z - y), z + h * (y - z)

        def first(kk):
            return f_dev(z * 4 + kk + h * (kk * 4 + y - z * 4 - kk))

        def second(qq):
            return f_dev(qq * 4 + y + h * (z * 4 + qq - qq * 4 - y))

        return k, q, first, second

    ca, cb = pl.ds(0, WIDE), pl.ds(WIDE, WIDE)

    def rows32(h, k):
        return pl.ds(pl.multiple_of(128 * h + 32 * k, 32), 32)

    def rows8(h, k, q):
        return pl.ds(pl.multiple_of(128 * h + 32 * k + 8 * q, 8), 8)

    def w_step_1(h):
        k, q, first, _ = places(h)
        kr, kl, ko = (k + 1) % 4, (k + 3) % 4, (k + 2) % 4
        send(w.at[rows32(h, ko), ca], w_hop.at[2 * h], W_HOP + 2 * h, first(kr))
        send(w.at[rows32(h, ko), cb], w_hop.at[2 * h + 1], W_HOP + 2 * h + 1, first(kl))
        send(w.at[rows32(h, kr), cb], w_side.at[4 * h + 1], W_NEXT + 4 * h + 1, first(kr))
        send(w.at[rows32(h, kl), ca], w_side.at[4 * h + 2], W_NEXT + 4 * h + 2, first(kl))

    def w_step_2(h):
        k, q, first, _ = places(h)
        kr, kl = (k + 1) % 4, (k + 3) % 4
        arrive(w_hop.at[2 * h], W_HOP + 2 * h)
        w[rows32(h, kr), ca] += w_hop[2 * h]
        send(w.at[rows32(h, kr), ca], w_side.at[4 * h], W_NEXT + 4 * h, first(kr))
        arrive(w_hop.at[2 * h + 1], W_HOP + 2 * h + 1)
        w[rows32(h, kl), cb] += w_hop[2 * h + 1]
        send(w.at[rows32(h, kl), cb], w_side.at[4 * h + 3], W_NEXT + 4 * h + 3, first(kl))

    def w_step_3(h):
        k, q, _, second = places(h)
        for s in range(4):
            arrive(w_side.at[4 * h + s], W_NEXT + 4 * h + s)
        w[rows32(h, k), ca] += w_side[4 * h] + w_side[4 * h + 2]
        w[rows32(h, k), cb] += w_side[4 * h + 1] + w_side[4 * h + 3]

        @pl.loop(1, 4)
        def _(d):
            to, slot = (q + d) % 4, 3 * h + d - 1
            send(w.at[rows8(h, k, to)], w_sub.at[slot], W_SUB + slot, second(to))

    def w_step_4(h):
        k, q, _, second = places(h)

        @pl.loop(0, 3)
        def _(d):
            arrive(w_sub.at[3 * h + d], W_SUB + 3 * h + d)

        w_full[rows8(h, k, q), :] = (w[rows8(h, k, q), :] + w_sub[3 * h]) + (
            w_sub[3 * h + 1] + w_sub[3 * h + 2]
        )

        @pl.loop(1, 4)
        def _(d):
            mine = w_full.at[rows8(h, k, q)]
            send(mine, mine, W_ALL + 3 * h + d - 1, second((q + d) % 4))

    def w_step_5(h):
        k, q, first, _ = places(h)
        dr, dl = first((k + 1) % 4), first((k + 3) % 4)

        @pl.loop(1, 4)
        def _(d):
            arrive(w_full.at[rows8(h, k, (q + 4 - d) % 4)], W_ALL + 3 * h + d - 1)

        mine_a, mine_b = w_full.at[rows32(h, k), ca], w_full.at[rows32(h, k), cb]
        send(mine_a, mine_a, W_RING + 4 * h, dr)
        send(mine_b, mine_b, W_RING + 4 * h + 3, dl)
        send(mine_b, mine_b, W_RING + 4 * h + 1, dr)
        send(mine_a, mine_a, W_RING + 4 * h + 2, dl)

    def w_step_6(h):
        k, q, first, _ = places(h)
        kr, kl = (k + 1) % 4, (k + 3) % 4
        from_left = w_full.at[rows32(h, kl), ca]
        arrive(from_left, W_RING + 4 * h)
        send(from_left, from_left, W_FAR + 2 * h, first(kr))
        from_right = w_full.at[rows32(h, kr), cb]
        arrive(from_right, W_RING + 4 * h + 3)
        send(from_right, from_right, W_FAR + 2 * h + 1, first(kl))

    def w_step_7(h):
        k = places(h)[0]
        kr, kl, ko = (k + 1) % 4, (k + 3) % 4, (k + 2) % 4
        arrive(w_full.at[rows32(h, kl), cb], W_RING + 4 * h + 1)
        arrive(w_full.at[rows32(h, kr), ca], W_RING + 4 * h + 2)
        arrive(w_full.at[rows32(h, ko), ca], W_FAR + 2 * h)
        arrive(w_full.at[rows32(h, ko), cb], W_FAR + 2 * h + 1)

    def both_halves(step):
        @pl.loop(0, 2)
        def _(h):
            step(h)

    both_halves(w_step_1)
    gram_pair()
    w_steps_at = (w_step_2, None, w_step_3, w_step_4, None, w_step_5, w_step_6, w_step_7)

    arrive(gram_half(1 - c), GRAM_CORE)
    elim[:, :RANK] = gram[...]
    rr = lax.broadcasted_iota(jnp.int32, (RANK, RANK), 0)
    cc = lax.broadcasted_iota(jnp.int32, (RANK, RANK), 1)
    elim[:, RANK:] = jnp.where(rr == cc, 1.0, 0.0).astype(F32)

    @pl.loop(0, 8)
    def _(k):
        eliminate(k, elim)
        for at, step in enumerate(w_steps_at):
            if step is not None:

                @pl.when(k == at)
                def _():
                    both_halves(step)

    f_hi, f_lo = split(elim[:, RANK:])
    factor = jnp.concatenate([f_hi, f_hi, f_lo], axis=1)
    squares = jnp.zeros((RANK, 128), F32)
    for n in range(4):
        cols = slice(256 * n, 256 * n + 256)
        w_hi, w_lo = split(w_full[:, cols])
        back = nn(factor, jnp.concatenate([w_hi, w_lo, w_hi], axis=0))
        back_out[:, cols] = back
        squares = squares + (back[:, :128] * back[:, :128] + back[:, 128:] * back[:, 128:])
    sq_v[t] = nt(jnp.ones((8, 128), F32), squares, HIGH)

    @pl.loop(1, 8)
    def _(d):
        send(sq_v.at[t], sq_v.at[t], SQ + d - 1, {"fsdp": f, "tp": (t + d) % 8})


    t_hi, t_lo = split(elim[:, RANK:].T)
    turned[:, :256] = t_hi
    turned[:, 256:512] = t_lo

    @pl.loop(0, 8)
    def _(i):
        rows = pl.ds(pl.multiple_of(i * PIECE, 32), PIECE)
        hi, lo = split(proj[rows, :])
        first = turned[:, :256]
        ortho_out[rows, :] = nn(
            jnp.concatenate([hi, hi, lo], axis=1),
            jnp.concatenate([first, turned[:, 256:512], first], axis=0),
        )

    all_sent(N_HOP_A, 12, side_v.at[0])
    all_sent(N_CORE, 8, part_v.at[0])
    all_sent(GRAM_SUM, 33, sq_v.at[0])
    all_sent(GRAM_CORE, 1, gram_part)
    all_sent(W_HOP, 24, w_hop.at[0])
    all_sent(W_SUB, 12, w_sub.at[0])

    @pl.loop(1, 8)
    def _(d):
        arrive(sq_v.at[(t + 8 - d) % 8], SQ + d - 1)

    norm_out[...] = lax.rsqrt(jnp.sum(sq_v[...], axis=0) + 1e-06)
    all_sent(SQ, 7, sq_v.at[0])


def write_kernel(
    blend, ortho, back, norm, mom_out, basis_out, update_out, backs, mom_v, basis_v, update_v, sems
):
    hi, lo = split(back[...])
    backs[:RANK] = hi
    backs[RANK : 2 * RANK] = lo
    backs[2 * RANK :] = hi
    scale = (ROWS * COLS / RANK) ** 0.5
    norms = norm[0:1, :]

    def copies(i):
        rows = pl.ds(pl.multiple_of(i * PIECE, 32), PIECE)
        rank_rows = pl.ds(pl.multiple_of(i * 128, 128), 128)
        slot = i % 2
        return (
            pltpu.make_async_copy(mom_v.at[slot], mom_out.at[rows], sems.at[slot, 0]),
            pltpu.make_async_copy(update_v.at[slot], update_out.at[rows], sems.at[slot, 1]),
            pltpu.make_async_copy(basis_v.at[slot], basis_out.at[rank_rows], sems.at[slot, 2]),
        )

    @pl.loop(0, 8)
    def _(i):
        slot = i % 2

        @pl.when(i >= 2)
        def _():
            for copy in copies(i - 2):
                copy.wait()

        rows = pl.ds(pl.multiple_of(i * PIECE, 32), PIECE)
        cols = pl.ds(pl.multiple_of(i * 128, 128), 128)
        basis_v[slot] = back[:, cols].T * norms
        plain = ortho[rows, :]
        mom_v[slot] = blend[rows, :] - nn((0.05 * plain).astype(BF16), backs[:RANK])
        hi, lo = split(plain * (scale * norms))
        update_v[slot] = nn(jnp.concatenate([hi, hi, lo], axis=1), backs[...]).astype(BF16)
        for copy in copies(i):
            copy.start()

    for i in (6, 7):
        for copy in copies(i):
            copy.wait()


def body(gradient, momentum, basis):
    anywhere = pl.BlockSpec(memory_space=pl.ANY)
    inside = pl.BlockSpec(memory_space=pltpu.VMEM)
    vmem = pltpu.VMEM
    fixed = [pltpu.with_memory_space_constraint(a, pltpu.HBM) for a in (gradient, momentum, basis)]
    results = pl.pallas_call(
        main_kernel,
        out_shape=(
            vmem((LOCAL_ROWS, LOCAL_COLS), F32),
            vmem((LOCAL_ROWS, RANK), F32),
            vmem((RANK, LOCAL_COLS), F32),
            vmem((8, RANK), F32),
        ),
        in_specs=[anywhere] * 3,
        out_specs=(inside,) * 4,
        scratch_shapes=[
            vmem((4, PIECE, LOCAL_COLS), BF16),
            vmem((LOCAL_COLS, RANK), F32),
            vmem((3 * LOCAL_COLS, RANK), BF16),
            vmem((LOCAL_ROWS + 32, LOCAL_COLS), BF16),
            vmem((LOCAL_ROWS + 32, LOCAL_COLS), BF16),
            vmem((8, PIECE, RANK), F32),
            vmem((4, PIECE, RANK), F32),
            vmem((2, PART, RANK), F32),
            vmem((4, PART, RANK), F32),
            vmem((LOCAL_ROWS, RANK), F32),
            vmem((128, RANK), F32),
            vmem((16, 8, RANK), F32),
            vmem((4, 8, RANK), F32),
            vmem((RANK, RANK), F32),
            vmem((RANK, 2 * RANK), F32),
            vmem((RANK, 3 * 256), BF16),
            vmem((RANK, LOCAL_COLS), F32),
            vmem((4, 32, WIDE), F32),
            vmem((8, 32, WIDE), F32),
            vmem((6, 8, LOCAL_COLS), F32),
            vmem((RANK, LOCAL_COLS), F32),
            vmem((8, 8, RANK), F32),
            pltpu.SemaphoreType.DMA((17,)),
            pltpu.SemaphoreType.DMA((NAMES.count,)),
            pltpu.SemaphoreType.DMA((NAMES.count,)),
        ],
        compiler_params=pltpu.CompilerParams(
            collective_id=0, has_side_effects=True, vmem_limit_bytes=44 * 2**20
        ),
        name="transfers",
    )(*fixed)
    results = [pltpu.with_memory_space_constraint(a, pltpu.VMEM) for a in results]

    return pl.pallas_call(
        write_kernel,
        out_shape=(
            jax.ShapeDtypeStruct((LOCAL_ROWS, LOCAL_COLS), F32),
            jax.ShapeDtypeStruct((LOCAL_COLS, RANK), F32),
            jax.ShapeDtypeStruct((LOCAL_ROWS, LOCAL_COLS), BF16),
        ),
        in_specs=[inside] * 4,
        out_specs=(anywhere,) * 3,
        scratch_shapes=[
            vmem((3 * RANK, LOCAL_COLS), BF16),
            vmem((2, PIECE, LOCAL_COLS), F32),
            vmem((2, 128, RANK), F32),
            vmem((2, PIECE, LOCAL_COLS), BF16),
            pltpu.SemaphoreType.DMA((2, 3)),
        ],
        compiler_params=pltpu.CompilerParams(vmem_limit_bytes=32 * 2**20),
        name="outputs",
    )(*results)


def solution(mesh):
    placed = (P("fsdp", "tp"), P("fsdp", "tp"), P("tp", None))
    return jax.shard_map(
        body,
        mesh=mesh,
        in_specs=placed,
        out_specs=(P("fsdp", "tp"), P("tp", None), P("fsdp", "tp")),
        check_vma=False,
    )
```

```python
import functools

import jax
import jax.numpy as jnp
from jax import lax
from jax.experimental import pallas as pl
from jax.experimental.pallas import tpu as pltpu
from jax.sharding import PartitionSpec as P

ROWS = 28672
COLS = 8192
RANK = 256

F32 = jnp.float32
BF16 = jnp.bfloat16
HIGH = lax.Precision.HIGHEST
MESH = pl.DeviceIdType.MESH

LOCAL_ROWS = 1792
LOCAL_COLS = 1024
HALF = 896
PIECE = 224
PART = 112
STEP = 448
WIDE = 512


class Names:
    def __init__(self):
        self.count = 0

    def take(self, many=1):
        first = self.count
        self.count += many
        return first


NAMES = Names()
N_HOP_A, N_HOP_B = NAMES.take(), NAMES.take()
N_LEFT_A, N_LEFT_B = NAMES.take(), NAMES.take()
N_RIGHT_A, N_RIGHT_B = NAMES.take(), NAMES.take()
G_LEFT_A, G_LEFT_B = NAMES.take(), NAMES.take()
G_RIGHT_A, G_RIGHT_B = NAMES.take(), NAMES.take()
G_OPP_A, G_OPP_B = NAMES.take(), NAMES.take()
N_CORE = NAMES.take(4)
G_CORE = NAMES.take(4)
GRAM_SUM = NAMES.take(15)
GRAM_X = NAMES.take(3)
GRAM_ALL = NAMES.take(15)
SQ = NAMES.take(7)
GRAM_CORE = NAMES.take()
W_HOP = NAMES.take(4)
W_NEXT = NAMES.take(8)
W_RING = NAMES.take(8)
W_FAR = NAMES.take(4)
W_SUB = NAMES.take(6)
W_ALL = NAMES.take(6)


def nn(a, b, precision=None):
    return lax.dot_general(
        a, b, (((1,), (0,)), ((), ())), precision=precision, preferred_element_type=F32
    )


def tn(a, b, precision=None):
    return lax.dot_general(
        a, b, (((0,), (0,)), ((), ())), precision=precision, preferred_element_type=F32
    )


def nt(a, b, precision=None):
    return lax.dot_general(
        a, b, (((1,), (1,)), ((), ())), precision=precision, preferred_element_type=F32
    )


def pick(index, values):
    out = values[0]
    for at in range(1, len(values)):
        out = out + (values[at] - values[at - 1]) * ((index + len(values) - at) // len(values))
    return out


def split(x):
    hi = x.astype(BF16)
    return hi, (x - hi.astype(F32)).astype(BF16)


def row_copy(x, j):
    return jnp.broadcast_to(x[j : j + 1, :], (8, 128))


def inverse_factor(x):
    n = len(x)
    sub = lax.broadcasted_iota(jnp.int32, (8, 128), 0)
    lane = lax.broadcasted_iota(jnp.int32, (8, 128), 1)
    col = [
        [None if i < k // 8 else jnp.broadcast_to(x[i][:, k : k + 1], (8, 128)) for i in range(n)]
        for k in range(8 * n)
    ]
    inverse = [jnp.where(lane == sub + 8 * i, 1.0, 0.0) for i in range(n)]
    for j in range(8 * n):
        g, r = j // 8, j % 8
        pivot = row_copy(col[j][g], r)
        inv = 1.0 / pivot
        row = row_copy(inverse[g], r)
        entry = {k: row_copy(col[j][k // 8], k % 8) for k in range(j + 1, 8 * n)}
        mult = [None if i < g else col[j][i] * inv for i in range(n)]
        if r < 7:
            mult[g] = jnp.where(sub > r, mult[g], 0.0)
        for k in range(j + 1, 8 * n):
            for i in range(k // 8, n):
                col[k][i] = col[k][i] - mult[i] * entry[k]
        for i in range(g + (r == 7), n):
            inverse[i] = inverse[i] - mult[i] * row
        inverse[g] = jnp.where(sub == r, row * lax.rsqrt(pivot), inverse[g])
    return jnp.concatenate(inverse, axis=0)


def eliminate(k, half, m_ref):
    left = 128 * half
    cols = slice(left, left + 384)
    rows = pl.ds(pl.multiple_of(32 * k, 32), 32)
    d = pltpu.roll(m_ref[rows, left : left + 128], (128 - 32 * (k % 4)) % 128, 1)
    inverse = inverse_factor([d[8 * i : 8 * i + 8] for i in range(4)])
    scaled = nn(inverse[:, :32], m_ref[rows, cols], HIGH)
    m_ref[rows, cols] = scaled

    @pl.when(k < 7)
    def _():
        subl = lax.broadcasted_iota(jnp.int32, (RANK - left, 32), 0)
        lower = jnp.where(subl >= 32 * k + 32 - left, scaled[:, : RANK - left].T, 0.0)
        m_ref[left:, cols] -= nn(lower, scaled, HIGH)


def main_kernel(
    grad,
    mom,
    basis,
    blend_out,
    ortho_out,
    back_out,
    norm_out,
    grad_v,
    basis_v,
    bases,
    hi_v,
    lo_v,
    part_v,
    from_core,
    hop_v,
    side_v,
    proj,
    gram_part,
    gram_in,
    gram_x,
    gram,
    elim,
    turned,
    w,
    w_hop,
    w_side,
    w_sub,
    w_full,
    sq_v,
    load_sem,
    send_sem,
    recv_sem,
):
    f = lax.axis_index("fsdp")
    t = lax.axis_index("tp")
    x, c = t // 2, t % 2
    z, y = f // 4, f % 4

    def tp_dev(xx, cc):
        return {"fsdp": f, "tp": xx * 2 + cc}

    def f_dev(ff):
        return {"fsdp": ff, "tp": t}

    right = tp_dev((x + 1) % 4, c)
    left = tp_dev((x + 3) % 4, c)
    twin = tp_dev(x, 1 - c)

    def remote(src, dst, number, device):
        return pltpu.make_async_remote_copy(
            src_ref=src,
            dst_ref=dst,
            send_sem=send_sem.at[number],
            recv_sem=recv_sem.at[number],
            device_id=device,
            device_id_type=MESH,
        )

    def send(src, dst, number, device):
        remote(src, dst, number, device).start()

    def arrive(dst, number):
        remote(dst, dst, number, twin).wait_recv()

    def all_sent(first, many, ref):
        @pl.loop(first, first + many)
        def _(number):
            remote(ref, ref, number, twin).wait_send()

    def piece_row(core, chip):
        return pl.multiple_of(core * HALF + chip * PIECE, 32)

    def chunk_row(i):
        g = 3 - i // 2
        d = g + (g // 2) * (1 - 2 * (g % 2))
        core = (1 - c) * (1 - i % 2) + c * (i % 2)
        return piece_row(core, (x + d) % 4)

    def load(i):
        rows = pl.ds(chunk_row(i), PIECE)
        return (
            pltpu.make_async_copy(mom.at[rows], blend_out.at[rows], load_sem.at[2 * i]),
            pltpu.make_async_copy(grad.at[rows], grad_v.at[i % 4], load_sem.at[2 * i + 1]),
        )

    basis_copy = pltpu.make_async_copy(basis, basis_v, load_sem.at[16])
    basis_copy.start()

    @pl.loop(0, 3)
    def _(i):
        for copy in load(i):
            copy.start()

    barrier = pltpu.get_barrier_semaphore()

    @pl.loop(1, 16)
    def _(d):
        pl.semaphore_signal(barrier, inc=1, device_id=f_dev((f + d) % 16), device_id_type=MESH)

    @pl.loop(1, 8)
    def _(d):
        pl.semaphore_signal(
            barrier, inc=1, device_id={"fsdp": f, "tp": (t + d) % 8}, device_id_type=MESH
        )

    basis_copy.wait()
    basis_hi, basis_lo = split(basis_v[...])
    bases[:LOCAL_COLS] = basis_hi
    bases[LOCAL_COLS : 2 * LOCAL_COLS] = basis_lo
    bases[2 * LOCAL_COLS :] = basis_hi
    turned[...] = jnp.zeros_like(turned)
    hi_v[LOCAL_ROWS:, :] = jnp.zeros((32, LOCAL_COLS), BF16)
    lo_v[LOCAL_ROWS:, :] = jnp.zeros((32, LOCAL_COLS), BF16)

    def partial(i):
        for copy in load(i):
            copy.wait()
        rows = pl.ds(chunk_row(i), PIECE)

        @pl.when(i < 5)
        def _():
            for copy in load(i + 3):
                copy.start()

        blend = blend_out[rows, :] + grad_v[i % 4].astype(F32)
        blend_out[rows, :] = blend
        hi, lo = split(blend)
        hi_v[rows, :] = hi
        lo_v[rows, :] = lo
        return nn(jnp.concatenate([hi, hi, lo], axis=1), bases[...])

    a_rows, b_rows = pl.ds(0, PART), pl.ds(PART, PART)

    def add_core(j):
        arrive(from_core.at[j], N_CORE + j)
        part_v[2 * j + 1] += from_core[j]

    @pl.loop(0, 8)
    def _(i):
        part_v[i] = partial(i)
        j = i // 2
        core = remote(part_v.at[i], from_core.at[j], N_CORE + j, twin)

        @pl.when(i == 0)
        def _():
            pl.semaphore_wait(barrier, 22)

        @pl.when(i % 2 == 0)
        def _():
            core.start()

        @pl.when(i == 2)
        def _():
            add_core(0)
            send(part_v.at[1, a_rows], hop_v.at[0], N_HOP_A, right)
            send(part_v.at[1, b_rows], hop_v.at[1], N_HOP_B, left)

        @pl.when(i == 4)
        def _():
            add_core(1)
            send(part_v.at[3, a_rows], side_v.at[2], N_RIGHT_A, left)

        @pl.when(i == 6)
        def _():
            add_core(2)
            send(part_v.at[5, b_rows], side_v.at[1], N_LEFT_B, right)

    add_core(3)
    arrive(hop_v.at[0], N_HOP_A)
    part_v[5, a_rows] += hop_v[0]
    send(part_v.at[5, a_rows], side_v.at[0], N_LEFT_A, right)
    arrive(hop_v.at[1], N_HOP_B)
    part_v[3, b_rows] += hop_v[1]
    send(part_v.at[3, b_rows], side_v.at[3], N_RIGHT_B, left)

    my_row = piece_row(c, x)
    arrive(side_v.at[2], N_RIGHT_A)
    arrive(side_v.at[0], N_LEFT_A)
    proj[pl.ds(my_row, PART), :] = part_v[7, a_rows] + (side_v[0] + side_v[2])
    arrive(side_v.at[1], N_LEFT_B)
    arrive(side_v.at[3], N_RIGHT_B)
    proj[pl.ds(my_row + PART, PART), :] = part_v[7, b_rows] + (side_v[1] + side_v[3])

    def part_of(core, chip, b):
        return proj.at[pl.ds(pl.multiple_of(piece_row(core, chip) + b * PART, 16), PART)]

    def whole_of(core, chip):
        return proj.at[pl.ds(piece_row(core, chip), PIECE)]

    def send_part(chip, b, number, device):
        send(part_of(c, chip, b), part_of(c, chip, b), number, device)

    def send_whole(chip, number):
        send(whole_of(c, chip), whole_of(c, chip), number, twin)

    xl, xr, xo = (x + 3) % 4, (x + 1) % 4, (x + 2) % 4
    send_part(x, 0, G_LEFT_A, right)
    send_part(x, 1, G_RIGHT_B, left)
    send_whole(x, G_CORE)
    send_part(x, 1, G_LEFT_B, right)
    send_part(x, 0, G_RIGHT_A, left)

    half_cols = pl.ds(pl.multiple_of(c * 128, 128), 128)

    def eight(row):
        return pl.ds(pl.multiple_of(row * 8, 8), 8)

    def gram_start():
        gram_part[...] = jnp.zeros((128, RANK), F32)

        @pl.loop(0, 2)
        def _(core):
            rows = pl.ds(piece_row(core, x), PIECE)
            gram_part[...] += tn(proj[rows, half_cols], proj[rows, :], HIGH)

        @pl.loop(1, 16)
        def _(d):
            to = (f + d) % 16
            send(gram_part.at[eight(to)], gram_in.at[d], GRAM_SUM + d - 1, f_dev(to))

    def gram_across():
        gram_in[0] = gram_part[eight(f), :]

        @pl.loop(1, 16)
        def _(d):
            arrive(gram_in.at[d], GRAM_SUM + d - 1)

        gram_x[x] = jnp.sum(gram_in[...], axis=0)

        @pl.loop(1, 4)
        def _(d):
            send(gram_x.at[x], gram_x.at[x], GRAM_X + d - 1, tp_dev((x + d) % 4, c))

    def gram_row(ff):
        return pl.ds(pl.multiple_of(c * 128 + ff * 8, 8), 8)

    def gram_round():
        @pl.loop(1, 4)
        def _(d):
            arrive(gram_x.at[(x + 4 - d) % 4], GRAM_X + d - 1)

        gram[gram_row(f), :] = (gram_x[0] + gram_x[1]) + (gram_x[2] + gram_x[3])

        @pl.loop(1, 16)
        def _(d):
            mine = gram.at[gram_row(f)]
            send(mine, mine, GRAM_ALL + d - 1, f_dev((f + d) % 16))

    def gram_half(core):
        return gram.at[pl.ds(pl.multiple_of(core * 128, 128), 128)]

    def gram_pair():
        @pl.loop(1, 16)
        def _(d):
            arrive(gram.at[gram_row((f + 16 - d) % 16)], GRAM_ALL + d - 1)

        send(gram_half(c), gram_half(c), GRAM_CORE, twin)

    w[...] = jnp.zeros_like(w)

    @pl.loop(0, 8)
    def _(g):
        core = (c + pick(g, (0, 1, 0, 0, 0, 1, 1, 1))) % 2
        chip = (x + pick(g, (0, 0, 1, 3, 2, 1, 3, 2))) % 4

        @pl.when(g == 1)
        def _():
            arrive(whole_of(1 - c, x), G_CORE)
            gram_start()

        @pl.when(g == 2)
        def _():
            arrive(part_of(c, xl, 0), G_LEFT_A)
            send_part(xl, 0, G_OPP_A, right)
            arrive(part_of(c, xr, 1), G_RIGHT_B)
            send_part(xr, 1, G_OPP_B, left)
            gram_across()
            arrive(part_of(c, xr, 0), G_RIGHT_A)
            send_whole(xr, G_CORE + 1)
            arrive(part_of(c, xl, 1), G_LEFT_B)
            send_whole(xl, G_CORE + 2)

        @pl.when(g == 4)
        def _():
            arrive(part_of(c, xo, 0), G_OPP_A)
            arrive(part_of(c, xo, 1), G_OPP_B)
            send_whole(xo, G_CORE + 3)
            gram_round()

        @pl.when(g == 5)
        def _():
            arrive(whole_of(1 - c, xr), G_CORE + 1)

        @pl.when(g == 6)
        def _():
            arrive(whole_of(1 - c, xl), G_CORE + 2)

        @pl.when(g == 7)
        def _():
            arrive(whole_of(1 - c, xo), G_CORE + 3)

        rows = pl.ds(piece_row(core, chip), PIECE)
        p_hi, p_lo = split(proj[rows, :].T)
        turned[:, :PIECE] = p_hi
        turned[:, 256 : 256 + PIECE] = p_hi
        turned[:, 512 : 512 + PIECE] = p_lo
        more = pl.ds(piece_row(core, chip), 256)
        for n in range(4):
            cols = slice(256 * n, 256 * n + 256)
            hi = hi_v[more, cols]
            w[:, cols] += nn(turned[...], jnp.concatenate([hi, lo_v[more, cols], hi], axis=0))

    def places(h):
        k, q = y + h * (z - y), z + h * (y - z)

        def first(kk):
            return f_dev(z * 4 + kk + h * (kk * 4 + y - z * 4 - kk))

        def second(qq):
            return f_dev(qq * 4 + y + h * (z * 4 + qq - qq * 4 - y))

        return k, q, first, second

    ca, cb = pl.ds(0, WIDE), pl.ds(WIDE, WIDE)

    def rows32(h, k):
        return pl.ds(pl.multiple_of(128 * h + 32 * k, 32), 32)

    def rows8(h, k, q):
        return pl.ds(pl.multiple_of(128 * h + 32 * k + 8 * q, 8), 8)

    def w_step_1(h):
        k, q, first, _ = places(h)
        kr, kl, ko = (k + 1) % 4, (k + 3) % 4, (k + 2) % 4
        send(w.at[rows32(h, ko), ca], w_hop.at[2 * h], W_HOP + 2 * h, first(kr))
        send(w.at[rows32(h, ko), cb], w_hop.at[2 * h + 1], W_HOP + 2 * h + 1, first(kl))
        send(w.at[rows32(h, kr), cb], w_side.at[4 * h + 1], W_NEXT + 4 * h + 1, first(kr))
        send(w.at[rows32(h, kl), ca], w_side.at[4 * h + 2], W_NEXT + 4 * h + 2, first(kl))

    def w_step_2(h):
        k, q, first, _ = places(h)
        kr, kl = (k + 1) % 4, (k + 3) % 4
        arrive(w_hop.at[2 * h], W_HOP + 2 * h)
        w[rows32(h, kr), ca] += w_hop[2 * h]
        send(w.at[rows32(h, kr), ca], w_side.at[4 * h], W_NEXT + 4 * h, first(kr))
        arrive(w_hop.at[2 * h + 1], W_HOP + 2 * h + 1)
        w[rows32(h, kl), cb] += w_hop[2 * h + 1]
        send(w.at[rows32(h, kl), cb], w_side.at[4 * h + 3], W_NEXT + 4 * h + 3, first(kl))

    def w_step_3(h):
        k, q, _, second = places(h)
        for s in range(4):
            arrive(w_side.at[4 * h + s], W_NEXT + 4 * h + s)
        w[rows32(h, k), ca] += w_side[4 * h] + w_side[4 * h + 2]
        w[rows32(h, k), cb] += w_side[4 * h + 1] + w_side[4 * h + 3]

        @pl.loop(1, 4)
        def _(d):
            to, slot = (q + d) % 4, 3 * h + d - 1
            send(w.at[rows8(h, k, to)], w_sub.at[slot], W_SUB + slot, second(to))

    def w_step_4(h):
        k, q, _, second = places(h)

        @pl.loop(0, 3)
        def _(d):
            arrive(w_sub.at[3 * h + d], W_SUB + 3 * h + d)

        w_full[rows8(h, k, q), :] = (w[rows8(h, k, q), :] + w_sub[3 * h]) + (
            w_sub[3 * h + 1] + w_sub[3 * h + 2]
        )

        @pl.loop(1, 4)
        def _(d):
            mine = w_full.at[rows8(h, k, q)]
            send(mine, mine, W_ALL + 3 * h + d - 1, second((q + d) % 4))

    def w_step_5(h):
        k, q, first, _ = places(h)
        dr, dl = first((k + 1) % 4), first((k + 3) % 4)

        @pl.loop(1, 4)
        def _(d):
            arrive(w_full.at[rows8(h, k, (q + 4 - d) % 4)], W_ALL + 3 * h + d - 1)

        mine_a, mine_b = w_full.at[rows32(h, k), ca], w_full.at[rows32(h, k), cb]
        send(mine_a, mine_a, W_RING + 4 * h, dr)
        send(mine_b, mine_b, W_RING + 4 * h + 3, dl)
        send(mine_b, mine_b, W_RING + 4 * h + 1, dr)
        send(mine_a, mine_a, W_RING + 4 * h + 2, dl)

    def w_step_6(h):
        k, q, first, _ = places(h)
        kr, kl = (k + 1) % 4, (k + 3) % 4
        from_left = w_full.at[rows32(h, kl), ca]
        arrive(from_left, W_RING + 4 * h)
        send(from_left, from_left, W_FAR + 2 * h, first(kr))
        from_right = w_full.at[rows32(h, kr), cb]
        arrive(from_right, W_RING + 4 * h + 3)
        send(from_right, from_right, W_FAR + 2 * h + 1, first(kl))

    def w_step_7(h):
        k = places(h)[0]
        kr, kl, ko = (k + 1) % 4, (k + 3) % 4, (k + 2) % 4
        arrive(w_full.at[rows32(h, kl), cb], W_RING + 4 * h + 1)
        arrive(w_full.at[rows32(h, kr), ca], W_RING + 4 * h + 2)
        arrive(w_full.at[rows32(h, ko), ca], W_FAR + 2 * h)
        arrive(w_full.at[rows32(h, ko), cb], W_FAR + 2 * h + 1)

    def both_halves(step):
        @pl.loop(0, 2)
        def _(h):
            step(h)

    both_halves(w_step_1)
    gram_pair()
    w_steps_at = (w_step_2, None, w_step_3, w_step_4, None, w_step_5, w_step_6, w_step_7)

    all_sent(N_HOP_A, 12, side_v.at[0])
    all_sent(N_CORE, 8, part_v.at[0])
    all_sent(GRAM_SUM, 33, sq_v.at[0])
    all_sent(GRAM_CORE, 1, gram_part)
    arrive(gram_half(1 - c), GRAM_CORE)
    elim[:, :RANK] = gram[...]
    rr = lax.broadcasted_iota(jnp.int32, (RANK, RANK), 0)
    cc = lax.broadcasted_iota(jnp.int32, (RANK, RANK), 1)
    elim[:, RANK:] = jnp.where(rr == cc, 1.0, 0.0).astype(F32)

    for half in range(2):

        @pl.loop(4 * half, 4 * half + 4)
        def _(k):
            eliminate(k, half, elim)
            for at in range(4 * half, 4 * half + 4):
                if w_steps_at[at] is not None:

                    @pl.when(k == at)
                    def _():
                        both_halves(w_steps_at[at])

    f_hi, f_lo = split(elim[:, RANK:])
    factor = jnp.concatenate([f_hi, f_hi, f_lo], axis=1)
    squares = jnp.zeros((RANK, 128), F32)
    for n in range(4):
        cols = slice(256 * n, 256 * n + 256)
        w_hi, w_lo = split(w_full[:, cols])
        back = nn(factor, jnp.concatenate([w_hi, w_lo, w_hi], axis=0))
        back_out[:, cols] = back
        squares = squares + (back[:, :128] * back[:, :128] + back[:, 128:] * back[:, 128:])
    sq_v[t] = nt(jnp.ones((8, 128), F32), squares, HIGH)

    @pl.loop(1, 8)
    def _(d):
        send(sq_v.at[t], sq_v.at[t], SQ + d - 1, {"fsdp": f, "tp": (t + d) % 8})


    t_hi, t_lo = split(elim[:, RANK:].T)
    turned[:, :256] = t_hi
    turned[:, 256:512] = t_lo

    @pl.loop(0, 8)
    def _(i):
        rows = pl.ds(pl.multiple_of(i * PIECE, 32), PIECE)
        hi, lo = split(proj[rows, :])
        first = turned[:, :256]
        ortho_out[rows, :] = nn(
            jnp.concatenate([hi, hi, lo], axis=1),
            jnp.concatenate([first, turned[:, 256:512], first], axis=0),
        )

    all_sent(W_HOP, 24, w_hop.at[0])
    all_sent(W_SUB, 12, w_sub.at[0])

    @pl.loop(1, 8)
    def _(d):
        arrive(sq_v.at[(t + 8 - d) % 8], SQ + d - 1)

    norm_out[...] = lax.rsqrt(jnp.sum(sq_v[...], axis=0) + 1e-06)
    all_sent(SQ, 7, sq_v.at[0])


def write_kernel(
    blend, ortho, back, norm, mom_out, basis_out, update_out, backs, mom_v, basis_v, update_v, sems
):
    hi, lo = split(back[...])
    backs[:RANK] = hi
    backs[RANK : 2 * RANK] = lo
    backs[2 * RANK :] = hi
    scale = (ROWS * COLS / RANK) ** 0.5
    norms = norm[0:1, :]

    def copies(i):
        rows = pl.ds(pl.multiple_of(i * STEP, 64), STEP)
        rank_rows = pl.ds(pl.multiple_of(i * 256, 256), 256)
        slot = i % 2
        return (
            pltpu.make_async_copy(mom_v.at[slot], mom_out.at[rows], sems.at[slot, 0]),
            pltpu.make_async_copy(update_v.at[slot], update_out.at[rows], sems.at[slot, 1]),
            pltpu.make_async_copy(basis_v.at[slot], basis_out.at[rank_rows], sems.at[slot, 2]),
        )

    @pl.loop(0, LOCAL_ROWS // STEP)
    def _(i):
        slot = i % 2

        @pl.when(i >= 2)
        def _():
            for copy in copies(i - 2):
                copy.wait()

        rows = pl.ds(pl.multiple_of(i * STEP, 64), STEP)
        cols = pl.ds(pl.multiple_of(i * 256, 256), 256)
        basis_v[slot] = back[:, cols].T * norms
        plain = ortho[rows, :]
        mom_v[slot] = blend[rows, :] - nn((0.05 * plain).astype(BF16), backs[:RANK])
        hi, lo = split(plain * (scale * norms))
        update_v[slot] = nn(jnp.concatenate([hi, hi, lo], axis=1), backs[...]).astype(BF16)
        for copy in copies(i):
            copy.start()

    for i in (2, 3):
        for copy in copies(i):
            copy.wait()


def body(gradient, momentum, basis):
    anywhere = pl.BlockSpec(memory_space=pl.ANY)
    inside = pl.BlockSpec(memory_space=pltpu.VMEM)
    vmem = pltpu.VMEM
    fixed = [pltpu.with_memory_space_constraint(a, pltpu.HBM) for a in (gradient, momentum, basis)]
    results = pl.pallas_call(
        main_kernel,
        out_shape=(
            vmem((LOCAL_ROWS, LOCAL_COLS), F32),
            vmem((LOCAL_ROWS, RANK), F32),
            vmem((RANK, LOCAL_COLS), F32),
            vmem((8, RANK), F32),
        ),
        in_specs=[anywhere] * 3,
        out_specs=(inside,) * 4,
        scratch_shapes=[
            vmem((4, PIECE, LOCAL_COLS), BF16),
            vmem((LOCAL_COLS, RANK), F32),
            vmem((3 * LOCAL_COLS, RANK), BF16),
            vmem((LOCAL_ROWS + 32, LOCAL_COLS), BF16),
            vmem((LOCAL_ROWS + 32, LOCAL_COLS), BF16),
            vmem((8, PIECE, RANK), F32),
            vmem((4, PIECE, RANK), F32),
            vmem((2, PART, RANK), F32),
            vmem((4, PART, RANK), F32),
            vmem((LOCAL_ROWS, RANK), F32),
            vmem((128, RANK), F32),
            vmem((16, 8, RANK), F32),
            vmem((4, 8, RANK), F32),
            vmem((RANK, RANK), F32),
            vmem((RANK, 2 * RANK), F32),
            vmem((RANK, 3 * 256), BF16),
            vmem((RANK, LOCAL_COLS), F32),
            vmem((4, 32, WIDE), F32),
            vmem((8, 32, WIDE), F32),
            vmem((6, 8, LOCAL_COLS), F32),
            vmem((RANK, LOCAL_COLS), F32),
            vmem((8, 8, RANK), F32),
            pltpu.SemaphoreType.DMA((17,)),
            pltpu.SemaphoreType.DMA((NAMES.count,)),
            pltpu.SemaphoreType.DMA((NAMES.count,)),
        ],
        compiler_params=pltpu.CompilerParams(
            collective_id=0, has_side_effects=True, vmem_limit_bytes=44 * 2**20
        ),
        name="transfers",
    )(*fixed)
    results = [pltpu.with_memory_space_constraint(a, pltpu.VMEM) for a in results]

    return pl.pallas_call(
        write_kernel,
        out_shape=(
            jax.ShapeDtypeStruct((LOCAL_ROWS, LOCAL_COLS), F32),
            jax.ShapeDtypeStruct((LOCAL_COLS, RANK), F32),
            jax.ShapeDtypeStruct((LOCAL_ROWS, LOCAL_COLS), BF16),
        ),
        in_specs=[inside] * 4,
        out_specs=(anywhere,) * 3,
        scratch_shapes=[
            vmem((3 * RANK, LOCAL_COLS), BF16),
            vmem((2, STEP, LOCAL_COLS), F32),
            vmem((2, 256, RANK), F32),
            vmem((2, STEP, LOCAL_COLS), BF16),
            pltpu.SemaphoreType.DMA((2, 3)),
        ],
        compiler_params=pltpu.CompilerParams(vmem_limit_bytes=32 * 2**20),
        name="outputs",
    )(*results)


def solution(mesh):
    placed = (P("fsdp", "tp"), P("fsdp", "tp"), P("tp", None))
    return jax.shard_map(
        body,
        mesh=mesh,
        in_specs=placed,
        out_specs=(P("fsdp", "tp"), P("tp", None), P("fsdp", "tp")),
        check_vma=False,
    )
```

```python
import functools

import jax
import jax.numpy as jnp
from jax import lax
from jax.experimental import pallas as pl
from jax.experimental.pallas import tpu as pltpu
from jax.sharding import PartitionSpec as P

ROWS = 28672
COLS = 8192
RANK = 256

F32 = jnp.float32
BF16 = jnp.bfloat16
HIGH = lax.Precision.HIGHEST
MESH = pl.DeviceIdType.MESH

LOCAL_ROWS = 1792
LOCAL_COLS = 1024
HALF = 896
PIECE = 224
PART = 112
STEP = 448
WIDE = 512


class Names:
    def __init__(self):
        self.count = 0

    def take(self, many=1):
        first = self.count
        self.count += many
        return first


NAMES = Names()
N_HOP_A, N_HOP_B = NAMES.take(), NAMES.take()
N_LEFT_A, N_LEFT_B = NAMES.take(), NAMES.take()
N_RIGHT_A, N_RIGHT_B = NAMES.take(), NAMES.take()
G_LEFT_A, G_LEFT_B = NAMES.take(), NAMES.take()
G_RIGHT_A, G_RIGHT_B = NAMES.take(), NAMES.take()
G_OPP_A, G_OPP_B = NAMES.take(), NAMES.take()
N_CORE = NAMES.take(4)
G_CORE = NAMES.take(4)
GRAM_SUM = NAMES.take(15)
GRAM_X = NAMES.take(3)
GRAM_ALL = NAMES.take(15)
SQ = NAMES.take(7)
GRAM_CORE = NAMES.take()
W_HOP = NAMES.take(4)
W_NEXT = NAMES.take(8)
W_RING = NAMES.take(8)
W_FAR = NAMES.take(4)
W_SUB = NAMES.take(6)
W_ALL = NAMES.take(6)


def nn(a, b, precision=None):
    return lax.dot_general(
        a, b, (((1,), (0,)), ((), ())), precision=precision, preferred_element_type=F32
    )


def tn(a, b, precision=None):
    return lax.dot_general(
        a, b, (((0,), (0,)), ((), ())), precision=precision, preferred_element_type=F32
    )


def nt(a, b, precision=None):
    return lax.dot_general(
        a, b, (((1,), (1,)), ((), ())), precision=precision, preferred_element_type=F32
    )


def pick(index, values):
    out = values[0]
    for at in range(1, len(values)):
        out = out + (values[at] - values[at - 1]) * ((index + len(values) - at) // len(values))
    return out


def split(x):
    hi = x.astype(BF16)
    return hi, (x - hi.astype(F32)).astype(BF16)


def row_copy(x, j):
    return jnp.broadcast_to(x[j : j + 1, :], (8, 128))


def inverse_factor(x):
    n = len(x)
    sub = lax.broadcasted_iota(jnp.int32, (8, 128), 0)
    lane = lax.broadcasted_iota(jnp.int32, (8, 128), 1)
    col = [
        [None if i < k // 8 else jnp.broadcast_to(x[i][:, k : k + 1], (8, 128)) for i in range(n)]
        for k in range(8 * n)
    ]
    inverse = [jnp.where(lane == sub + 8 * i, 1.0, 0.0) for i in range(n)]
    for j in range(8 * n):
        g, r = j // 8, j % 8
        pivot = row_copy(col[j][g], r)
        inv = 1.0 / pivot
        row = row_copy(inverse[g], r)
        entry = {k: row_copy(col[j][k // 8], k % 8) for k in range(j + 1, 8 * n)}
        mult = [None if i < g else col[j][i] * inv for i in range(n)]
        if r < 7:
            mult[g] = jnp.where(sub > r, mult[g], 0.0)
        for k in range(j + 1, 8 * n):
            for i in range(k // 8, n):
                col[k][i] = col[k][i] - mult[i] * entry[k]
        for i in range(g + (r == 7), n):
            inverse[i] = inverse[i] - mult[i] * row
        inverse[g] = jnp.where(sub == r, row * lax.rsqrt(pivot), inverse[g])
    return jnp.concatenate(inverse, axis=0)


def eliminate(k, half, m_ref):
    left = 128 * half
    cols = slice(left, left + 384)
    rows = pl.ds(pl.multiple_of(32 * k, 32), 32)
    d = pltpu.roll(m_ref[rows, left : left + 128], (128 - 32 * (k % 4)) % 128, 1)
    inverse = inverse_factor([d[8 * i : 8 * i + 8] for i in range(4)])
    scaled = nn(inverse[:, :32], m_ref[rows, cols], HIGH)
    m_ref[rows, cols] = scaled

    @pl.when(k < 7)
    def _():
        subl = lax.broadcasted_iota(jnp.int32, (RANK - left, 32), 0)
        lower = jnp.where(subl >= 32 * k + 32 - left, scaled[:, : RANK - left].T, 0.0)
        m_ref[left:, cols] -= nn(lower, scaled, HIGH)


def main_kernel(
    grad,
    mom,
    basis,
    blend_out,
    ortho_out,
    back_out,
    norm_out,
    grad_v,
    basis_v,
    bases,
    hi_v,
    lo_v,
    part_v,
    from_core,
    hop_v,
    side_v,
    proj,
    gram_part,
    gram_in,
    gram_x,
    gram,
    elim,
    turned,
    w,
    w_hop,
    w_side,
    w_sub,
    w_full,
    back_hi,
    sq_v,
    load_sem,
    send_sem,
    recv_sem,
):
    f = lax.axis_index("fsdp")
    t = lax.axis_index("tp")
    x, c = t // 2, t % 2
    z, y = f // 4, f % 4

    def tp_dev(xx, cc):
        return {"fsdp": f, "tp": xx * 2 + cc}

    def f_dev(ff):
        return {"fsdp": ff, "tp": t}

    right = tp_dev((x + 1) % 4, c)
    left = tp_dev((x + 3) % 4, c)
    twin = tp_dev(x, 1 - c)

    def remote(src, dst, number, device):
        return pltpu.make_async_remote_copy(
            src_ref=src,
            dst_ref=dst,
            send_sem=send_sem.at[number],
            recv_sem=recv_sem.at[number],
            device_id=device,
            device_id_type=MESH,
        )

    def send(src, dst, number, device):
        remote(src, dst, number, device).start()

    def arrive(dst, number):
        remote(dst, dst, number, twin).wait_recv()

    def all_sent(first, many, ref):
        @pl.loop(first, first + many)
        def _(number):
            remote(ref, ref, number, twin).wait_send()

    def piece_row(core, chip):
        return pl.multiple_of(core * HALF + chip * PIECE, 32)

    def chunk_row(i):
        g = 3 - i // 2
        d = g + (g // 2) * (1 - 2 * (g % 2))
        core = (1 - c) * (1 - i % 2) + c * (i % 2)
        return piece_row(core, (x + d) % 4)

    def load(i):
        rows = pl.ds(chunk_row(i), PIECE)
        return (
            pltpu.make_async_copy(mom.at[rows], blend_out.at[rows], load_sem.at[2 * i]),
            pltpu.make_async_copy(grad.at[rows], grad_v.at[i % 4], load_sem.at[2 * i + 1]),
        )

    basis_copy = pltpu.make_async_copy(basis, basis_v, load_sem.at[16])
    basis_copy.start()

    @pl.loop(0, 3)
    def _(i):
        for copy in load(i):
            copy.start()

    barrier = pltpu.get_barrier_semaphore()

    @pl.loop(1, 16)
    def _(d):
        pl.semaphore_signal(barrier, inc=1, device_id=f_dev((f + d) % 16), device_id_type=MESH)

    @pl.loop(1, 8)
    def _(d):
        pl.semaphore_signal(
            barrier, inc=1, device_id={"fsdp": f, "tp": (t + d) % 8}, device_id_type=MESH
        )

    basis_copy.wait()
    basis_hi, basis_lo = split(basis_v[...])
    bases[:LOCAL_COLS] = basis_hi
    bases[LOCAL_COLS : 2 * LOCAL_COLS] = basis_lo
    bases[2 * LOCAL_COLS :] = basis_hi
    turned[...] = jnp.zeros_like(turned)
    hi_v[LOCAL_ROWS:, :] = jnp.zeros((32, LOCAL_COLS), BF16)
    lo_v[LOCAL_ROWS:, :] = jnp.zeros((32, LOCAL_COLS), BF16)

    def partial(i):
        for copy in load(i):
            copy.wait()
        rows = pl.ds(chunk_row(i), PIECE)

        @pl.when(i < 5)
        def _():
            for copy in load(i + 3):
                copy.start()

        blend = blend_out[rows, :] + grad_v[i % 4].astype(F32)
        blend_out[rows, :] = blend
        hi, lo = split(blend)
        hi_v[rows, :] = hi
        lo_v[rows, :] = lo
        return nn(jnp.concatenate([hi, hi, lo], axis=1), bases[...])

    a_rows, b_rows = pl.ds(0, PART), pl.ds(PART, PART)

    def add_core(j):
        arrive(from_core.at[j], N_CORE + j)
        part_v[2 * j + 1] += from_core[j]

    @pl.loop(0, 8)
    def _(i):
        part_v[i] = partial(i)
        j = i // 2
        core = remote(part_v.at[i], from_core.at[j], N_CORE + j, twin)

        @pl.when(i == 0)
        def _():
            pl.semaphore_wait(barrier, 22)

        @pl.when(i % 2 == 0)
        def _():
            core.start()

        @pl.when(i == 2)
        def _():
            add_core(0)
            send(part_v.at[1, a_rows], hop_v.at[0], N_HOP_A, right)
            send(part_v.at[1, b_rows], hop_v.at[1], N_HOP_B, left)

        @pl.when(i == 4)
        def _():
            add_core(1)
            send(part_v.at[3, a_rows], side_v.at[2], N_RIGHT_A, left)

        @pl.when(i == 6)
        def _():
            add_core(2)
            send(part_v.at[5, b_rows], side_v.at[1], N_LEFT_B, right)
            arrive(hop_v.at[0], N_HOP_A)
            part_v[5, a_rows] += hop_v[0]
            send(part_v.at[5, a_rows], side_v.at[0], N_LEFT_A, right)
            arrive(hop_v.at[1], N_HOP_B)
            part_v[3, b_rows] += hop_v[1]
            send(part_v.at[3, b_rows], side_v.at[3], N_RIGHT_B, left)

    add_core(3)
    my_row = piece_row(c, x)
    arrive(side_v.at[2], N_RIGHT_A)
    arrive(side_v.at[0], N_LEFT_A)
    proj[pl.ds(my_row, PART), :] = part_v[7, a_rows] + (side_v[0] + side_v[2])
    arrive(side_v.at[1], N_LEFT_B)
    arrive(side_v.at[3], N_RIGHT_B)
    proj[pl.ds(my_row + PART, PART), :] = part_v[7, b_rows] + (side_v[1] + side_v[3])

    def part_of(core, chip, b):
        return proj.at[pl.ds(pl.multiple_of(piece_row(core, chip) + b * PART, 16), PART)]

    def whole_of(core, chip):
        return proj.at[pl.ds(piece_row(core, chip), PIECE)]

    def send_part(chip, b, number, device):
        send(part_of(c, chip, b), part_of(c, chip, b), number, device)

    def send_whole(chip, number):
        send(whole_of(c, chip), whole_of(c, chip), number, twin)

    xl, xr, xo = (x + 3) % 4, (x + 1) % 4, (x + 2) % 4
    send_part(x, 0, G_LEFT_A, right)
    send_part(x, 1, G_RIGHT_B, left)
    send_whole(x, G_CORE)
    send_part(x, 1, G_LEFT_B, right)
    send_part(x, 0, G_RIGHT_A, left)

    half_cols = pl.ds(pl.multiple_of(c * 128, 128), 128)

    def eight(row):
        return pl.ds(pl.multiple_of(row * 8, 8), 8)

    def gram_start():
        gram_part[...] = jnp.zeros((128, RANK), F32)

        @pl.loop(0, 2)
        def _(core):
            rows = pl.ds(piece_row(core, x), PIECE)
            gram_part[...] += tn(proj[rows, half_cols], proj[rows, :], HIGH)

        @pl.loop(1, 16)
        def _(d):
            to = (f + d) % 16
            send(gram_part.at[eight(to)], gram_in.at[d], GRAM_SUM + d - 1, f_dev(to))

    def gram_across():
        gram_in[0] = gram_part[eight(f), :]

        @pl.loop(1, 16)
        def _(d):
            arrive(gram_in.at[d], GRAM_SUM + d - 1)

        gram_x[x] = jnp.sum(gram_in[...], axis=0)

        @pl.loop(1, 4)
        def _(d):
            send(gram_x.at[x], gram_x.at[x], GRAM_X + d - 1, tp_dev((x + d) % 4, c))

    def gram_row(ff):
        return pl.ds(pl.multiple_of(c * 128 + ff * 8, 8), 8)

    def gram_round():
        @pl.loop(1, 4)
        def _(d):
            arrive(gram_x.at[(x + 4 - d) % 4], GRAM_X + d - 1)

        gram[gram_row(f), :] = (gram_x[0] + gram_x[1]) + (gram_x[2] + gram_x[3])

        @pl.loop(1, 16)
        def _(d):
            mine = gram.at[gram_row(f)]
            send(mine, mine, GRAM_ALL + d - 1, f_dev((f + d) % 16))

    def gram_half(core):
        return gram.at[pl.ds(pl.multiple_of(core * 128, 128), 128)]

    def gram_pair():
        @pl.loop(1, 16)
        def _(d):
            arrive(gram.at[gram_row((f + 16 - d) % 16)], GRAM_ALL + d - 1)

        send(gram_half(c), gram_half(c), GRAM_CORE, twin)

    w[...] = jnp.zeros_like(w)

    @pl.loop(0, 8)
    def _(g):
        core = (c + pick(g, (0, 1, 0, 0, 0, 1, 1, 1))) % 2
        chip = (x + pick(g, (0, 0, 1, 3, 2, 1, 3, 2))) % 4

        @pl.when(g == 1)
        def _():
            arrive(whole_of(1 - c, x), G_CORE)
            gram_start()

        @pl.when(g == 2)
        def _():
            arrive(part_of(c, xl, 0), G_LEFT_A)
            send_part(xl, 0, G_OPP_A, right)
            arrive(part_of(c, xr, 1), G_RIGHT_B)
            send_part(xr, 1, G_OPP_B, left)
            gram_across()
            arrive(part_of(c, xr, 0), G_RIGHT_A)
            send_whole(xr, G_CORE + 1)
            arrive(part_of(c, xl, 1), G_LEFT_B)
            send_whole(xl, G_CORE + 2)

        @pl.when(g == 4)
        def _():
            arrive(part_of(c, xo, 0), G_OPP_A)
            arrive(part_of(c, xo, 1), G_OPP_B)
            send_whole(xo, G_CORE + 3)
            gram_round()

        @pl.when(g == 5)
        def _():
            arrive(whole_of(1 - c, xr), G_CORE + 1)

        @pl.when(g == 6)
        def _():
            arrive(whole_of(1 - c, xl), G_CORE + 2)

        @pl.when(g == 7)
        def _():
            arrive(whole_of(1 - c, xo), G_CORE + 3)

        rows = pl.ds(piece_row(core, chip), PIECE)
        p_hi, p_lo = split(proj[rows, :].T)
        turned[:, :PIECE] = p_hi
        turned[:, 256 : 256 + PIECE] = p_hi
        turned[:, 512 : 512 + PIECE] = p_lo
        more = pl.ds(piece_row(core, chip), 256)
        for n in range(4):
            cols = slice(256 * n, 256 * n + 256)
            hi = hi_v[more, cols]
            w[:, cols] += nn(turned[...], jnp.concatenate([hi, lo_v[more, cols], hi], axis=0))

    def places(h):
        k, q = y + h * (z - y), z + h * (y - z)

        def first(kk):
            return f_dev(z * 4 + kk + h * (kk * 4 + y - z * 4 - kk))

        def second(qq):
            return f_dev(qq * 4 + y + h * (z * 4 + qq - qq * 4 - y))

        return k, q, first, second

    ca, cb = pl.ds(0, WIDE), pl.ds(WIDE, WIDE)

    def rows32(h, k):
        return pl.ds(pl.multiple_of(128 * h + 32 * k, 32), 32)

    def rows8(h, k, q):
        return pl.ds(pl.multiple_of(128 * h + 32 * k + 8 * q, 8), 8)

    def w_step_1(h):
        k, q, first, _ = places(h)
        kr, kl, ko = (k + 1) % 4, (k + 3) % 4, (k + 2) % 4
        send(w.at[rows32(h, ko), ca], w_hop.at[2 * h], W_HOP + 2 * h, first(kr))
        send(w.at[rows32(h, ko), cb], w_hop.at[2 * h + 1], W_HOP + 2 * h + 1, first(kl))
        send(w.at[rows32(h, kr), cb], w_side.at[4 * h + 1], W_NEXT + 4 * h + 1, first(kr))
        send(w.at[rows32(h, kl), ca], w_side.at[4 * h + 2], W_NEXT + 4 * h + 2, first(kl))

    def w_step_2(h):
        k, q, first, _ = places(h)
        kr, kl = (k + 1) % 4, (k + 3) % 4
        arrive(w_hop.at[2 * h], W_HOP + 2 * h)
        w[rows32(h, kr), ca] += w_hop[2 * h]
        send(w.at[rows32(h, kr), ca], w_side.at[4 * h], W_NEXT + 4 * h, first(kr))
        arrive(w_hop.at[2 * h + 1], W_HOP + 2 * h + 1)
        w[rows32(h, kl), cb] += w_hop[2 * h + 1]
        send(w.at[rows32(h, kl), cb], w_side.at[4 * h + 3], W_NEXT + 4 * h + 3, first(kl))

    def w_step_3(h):
        k, q, _, second = places(h)
        for s in range(4):
            arrive(w_side.at[4 * h + s], W_NEXT + 4 * h + s)
        w[rows32(h, k), ca] += w_side[4 * h] + w_side[4 * h + 2]
        w[rows32(h, k), cb] += w_side[4 * h + 1] + w_side[4 * h + 3]

        @pl.loop(1, 4)
        def _(d):
            to, slot = (q + d) % 4, 3 * h + d - 1
            send(w.at[rows8(h, k, to)], w_sub.at[slot], W_SUB + slot, second(to))

    def w_step_4(h):
        k, q, _, second = places(h)

        @pl.loop(0, 3)
        def _(d):
            arrive(w_sub.at[3 * h + d], W_SUB + 3 * h + d)

        w_full[rows8(h, k, q), :] = (w[rows8(h, k, q), :] + w_sub[3 * h]) + (
            w_sub[3 * h + 1] + w_sub[3 * h + 2]
        )

        @pl.loop(1, 4)
        def _(d):
            mine = w_full.at[rows8(h, k, q)]
            send(mine, mine, W_ALL + 3 * h + d - 1, second((q + d) % 4))

    def w_step_5(h):
        k, q, first, _ = places(h)
        dr, dl = first((k + 1) % 4), first((k + 3) % 4)

        @pl.loop(1, 4)
        def _(d):
            arrive(w_full.at[rows8(h, k, (q + 4 - d) % 4)], W_ALL + 3 * h + d - 1)

        mine_a, mine_b = w_full.at[rows32(h, k), ca], w_full.at[rows32(h, k), cb]
        send(mine_a, mine_a, W_RING + 4 * h, dr)
        send(mine_b, mine_b, W_RING + 4 * h + 3, dl)
        send(mine_b, mine_b, W_RING + 4 * h + 1, dr)
        send(mine_a, mine_a, W_RING + 4 * h + 2, dl)

    def w_step_6(h):
        k, q, first, _ = places(h)
        kr, kl = (k + 1) % 4, (k + 3) % 4
        from_left = w_full.at[rows32(h, kl), ca]
        arrive(from_left, W_RING + 4 * h)
        send(from_left, from_left, W_FAR + 2 * h, first(kr))
        from_right = w_full.at[rows32(h, kr), cb]
        arrive(from_right, W_RING + 4 * h + 3)
        send(from_right, from_right, W_FAR + 2 * h + 1, first(kl))

    def w_step_7(h):
        k = places(h)[0]
        kr, kl, ko = (k + 1) % 4, (k + 3) % 4, (k + 2) % 4
        arrive(w_full.at[rows32(h, kl), cb], W_RING + 4 * h + 1)
        arrive(w_full.at[rows32(h, kr), ca], W_RING + 4 * h + 2)
        arrive(w_full.at[rows32(h, ko), ca], W_FAR + 2 * h)
        arrive(w_full.at[rows32(h, ko), cb], W_FAR + 2 * h + 1)

    def both_halves(step):
        @pl.loop(0, 2)
        def _(h):
            step(h)

    both_halves(w_step_1)
    gram_pair()
    both_halves(w_step_2)
    w_steps_at = (None, w_step_3, None, w_step_4, None, w_step_5, None, w_step_6)

    arrive(gram_half(1 - c), GRAM_CORE)
    elim[:, :RANK] = gram[...]
    rr = lax.broadcasted_iota(jnp.int32, (RANK, RANK), 0)
    cc = lax.broadcasted_iota(jnp.int32, (RANK, RANK), 1)
    elim[:, RANK:] = jnp.where(rr == cc, 1.0, 0.0).astype(F32)

    for half in range(2):

        @pl.loop(4 * half, 4 * half + 4)
        def _(k):
            eliminate(k, half, elim)
            for at in range(4 * half, 4 * half + 4):
                if w_steps_at[at] is not None:

                    @pl.when(k == at)
                    def _():
                        both_halves(w_steps_at[at])

    t_hi, t_lo = split(elim[:, RANK:].T)
    turned[:, :256] = t_hi
    turned[:, 256:512] = t_lo

    @pl.loop(0, 8)
    def _(i):
        rows = pl.ds(pl.multiple_of(i * PIECE, 32), PIECE)
        hi, lo = split(proj[rows, :])
        first = turned[:, :256]
        ortho_out[rows, :] = nn(
            jnp.concatenate([hi, hi, lo], axis=1),
            jnp.concatenate([first, turned[:, 256:512], first], axis=0),
        )

    all_sent(N_HOP_A, 12, side_v.at[0])
    all_sent(N_CORE, 8, part_v.at[0])
    all_sent(GRAM_SUM, 33, sq_v.at[0])
    all_sent(GRAM_CORE, 1, gram_part)
    both_halves(w_step_7)
    f_hi, f_lo = split(elim[:, RANK:])
    factor = jnp.concatenate([f_hi, f_hi, f_lo], axis=1)
    squares = jnp.zeros((RANK, 128), F32)
    for n in range(4):
        cols = slice(256 * n, 256 * n + 256)
        w_hi, w_lo = split(w_full[:, cols])
        back = nn(factor, jnp.concatenate([w_hi, w_lo, w_hi], axis=0))
        back_out[:, cols] = back
        back_hi[:, cols] = back.astype(BF16)
        squares = squares + (back[:, :128] * back[:, :128] + back[:, 128:] * back[:, 128:])
    sq_v[t] = nt(jnp.ones((8, 128), F32), squares, HIGH)

    @pl.loop(1, 8)
    def _(d):
        send(sq_v.at[t], sq_v.at[t], SQ + d - 1, {"fsdp": f, "tp": (t + d) % 8})


    @pl.loop(0, LOCAL_ROWS // STEP)
    def _(i):
        rows = pl.ds(pl.multiple_of(i * STEP, 64), STEP)
        blend_out[rows, :] -= nn((0.05 * ortho_out[rows, :]).astype(BF16), back_hi[...])

    all_sent(W_HOP, 24, w_hop.at[0])
    all_sent(W_SUB, 12, w_sub.at[0])

    @pl.loop(1, 8)
    def _(d):
        arrive(sq_v.at[(t + 8 - d) % 8], SQ + d - 1)

    norm_out[...] = lax.rsqrt(jnp.sum(sq_v[...], axis=0) + 1e-06)
    all_sent(SQ, 7, sq_v.at[0])


def write_kernel(
    new_mom, ortho, back, norm, mom_out, basis_out, update_out, backs, basis_v, update_v, sems, mom_sem
):
    mom_copy = pltpu.make_async_copy(new_mom, mom_out, mom_sem.at[0])
    mom_copy.start()
    hi, lo = split(back[...])
    backs[:RANK] = hi
    backs[RANK : 2 * RANK] = lo
    backs[2 * RANK :] = hi
    scale = (ROWS * COLS / RANK) ** 0.5
    norms = norm[0:1, :]

    def copies(i):
        rows = pl.ds(pl.multiple_of(i * STEP, 64), STEP)
        rank_rows = pl.ds(pl.multiple_of(i * 256, 256), 256)
        slot = i % 2
        return (
            pltpu.make_async_copy(update_v.at[slot], update_out.at[rows], sems.at[slot, 0]),
            pltpu.make_async_copy(basis_v.at[slot], basis_out.at[rank_rows], sems.at[slot, 1]),
        )

    @pl.loop(0, LOCAL_ROWS // STEP)
    def _(i):
        slot = i % 2

        @pl.when(i >= 2)
        def _():
            for copy in copies(i - 2):
                copy.wait()

        rows = pl.ds(pl.multiple_of(i * STEP, 64), STEP)
        cols = pl.ds(pl.multiple_of(i * 256, 256), 256)
        basis_v[slot] = back[:, cols].T * norms
        hi, lo = split(ortho[rows, :] * (scale * norms))
        update_v[slot] = nn(jnp.concatenate([hi, hi, lo], axis=1), backs[...]).astype(BF16)
        for copy in copies(i):
            copy.start()

    for i in (2, 3):
        for copy in copies(i):
            copy.wait()
    mom_copy.wait()


def body(gradient, momentum, basis):
    anywhere = pl.BlockSpec(memory_space=pl.ANY)
    inside = pl.BlockSpec(memory_space=pltpu.VMEM)
    vmem = pltpu.VMEM
    fixed = [pltpu.with_memory_space_constraint(a, pltpu.HBM) for a in (gradient, momentum, basis)]
    results = pl.pallas_call(
        main_kernel,
        out_shape=(
            vmem((LOCAL_ROWS, LOCAL_COLS), F32),
            vmem((LOCAL_ROWS, RANK), F32),
            vmem((RANK, LOCAL_COLS), F32),
            vmem((8, RANK), F32),
        ),
        in_specs=[anywhere] * 3,
        out_specs=(inside,) * 4,
        scratch_shapes=[
            vmem((4, PIECE, LOCAL_COLS), BF16),
            vmem((LOCAL_COLS, RANK), F32),
            vmem((3 * LOCAL_COLS, RANK), BF16),
            vmem((LOCAL_ROWS + 32, LOCAL_COLS), BF16),
            vmem((LOCAL_ROWS + 32, LOCAL_COLS), BF16),
            vmem((8, PIECE, RANK), F32),
            vmem((4, PIECE, RANK), F32),
            vmem((2, PART, RANK), F32),
            vmem((4, PART, RANK), F32),
            vmem((LOCAL_ROWS, RANK), F32),
            vmem((128, RANK), F32),
            vmem((16, 8, RANK), F32),
            vmem((4, 8, RANK), F32),
            vmem((RANK, RANK), F32),
            vmem((RANK, 2 * RANK), F32),
            vmem((RANK, 3 * 256), BF16),
            vmem((RANK, LOCAL_COLS), F32),
            vmem((4, 32, WIDE), F32),
            vmem((8, 32, WIDE), F32),
            vmem((6, 8, LOCAL_COLS), F32),
            vmem((RANK, LOCAL_COLS), F32),
            vmem((RANK, LOCAL_COLS), BF16),
            vmem((8, 8, RANK), F32),
            pltpu.SemaphoreType.DMA((17,)),
            pltpu.SemaphoreType.DMA((NAMES.count,)),
            pltpu.SemaphoreType.DMA((NAMES.count,)),
        ],
        compiler_params=pltpu.CompilerParams(
            collective_id=0, has_side_effects=True, vmem_limit_bytes=44 * 2**20
        ),
        name="transfers",
    )(*fixed)
    results = [pltpu.with_memory_space_constraint(a, pltpu.VMEM) for a in results]

    return pl.pallas_call(
        write_kernel,
        out_shape=(
            jax.ShapeDtypeStruct((LOCAL_ROWS, LOCAL_COLS), F32),
            jax.ShapeDtypeStruct((LOCAL_COLS, RANK), F32),
            jax.ShapeDtypeStruct((LOCAL_ROWS, LOCAL_COLS), BF16),
        ),
        in_specs=[inside] * 4,
        out_specs=(anywhere,) * 3,
        scratch_shapes=[
            vmem((3 * RANK, LOCAL_COLS), BF16),
            vmem((2, 256, RANK), F32),
            vmem((2, STEP, LOCAL_COLS), BF16),
            pltpu.SemaphoreType.DMA((2, 2)),
            pltpu.SemaphoreType.DMA((1,)),
        ],
        compiler_params=pltpu.CompilerParams(vmem_limit_bytes=32 * 2**20),
        name="outputs",
    )(*results)


def solution(mesh):
    placed = (P("fsdp", "tp"), P("fsdp", "tp"), P("tp", None))
    return jax.shard_map(
        body,
        mesh=mesh,
        in_specs=placed,
        out_specs=(P("fsdp", "tp"), P("tp", None), P("fsdp", "tp")),
        check_vma=False,
    )
```

```python
import functools

import jax
import jax.numpy as jnp
from jax import lax
from jax.experimental import pallas as pl
from jax.experimental.pallas import tpu as pltpu
from jax.sharding import PartitionSpec as P

ROWS = 28672
COLS = 8192
RANK = 256

F32 = jnp.float32
BF16 = jnp.bfloat16
HIGH = lax.Precision.HIGHEST
MESH = pl.DeviceIdType.MESH

LOCAL_ROWS = 1792
LOCAL_COLS = 1024
HALF = 896
PIECE = 224
PART = 112
STEP = 448
WIDE = 512


class Names:
    def __init__(self):
        self.count = 0

    def take(self, many=1):
        first = self.count
        self.count += many
        return first


NAMES = Names()
N_HOP_A, N_HOP_B = NAMES.take(), NAMES.take()
N_LEFT_A, N_LEFT_B = NAMES.take(), NAMES.take()
N_RIGHT_A, N_RIGHT_B = NAMES.take(), NAMES.take()
G_LEFT_A, G_LEFT_B = NAMES.take(), NAMES.take()
G_RIGHT_A, G_RIGHT_B = NAMES.take(), NAMES.take()
G_OPP_A, G_OPP_B = NAMES.take(), NAMES.take()
N_CORE = NAMES.take(4)
G_CORE = NAMES.take(4)
GRAM_SUM = NAMES.take(15)
GRAM_X = NAMES.take(3)
GRAM_ALL = NAMES.take(15)
SQ = NAMES.take(7)
GRAM_CORE = NAMES.take()
W_HOP = NAMES.take(8)
W_NEXT = NAMES.take(16)
W_RING = NAMES.take(16)
W_FAR = NAMES.take(8)
W_SUB = NAMES.take(12)
W_ALL = NAMES.take(12)


def nn(a, b, precision=None):
    return lax.dot_general(
        a, b, (((1,), (0,)), ((), ())), precision=precision, preferred_element_type=F32
    )


def tn(a, b, precision=None):
    return lax.dot_general(
        a, b, (((0,), (0,)), ((), ())), precision=precision, preferred_element_type=F32
    )


def nt(a, b, precision=None):
    return lax.dot_general(
        a, b, (((1,), (1,)), ((), ())), precision=precision, preferred_element_type=F32
    )


def pick(index, values):
    out = values[0]
    for at in range(1, len(values)):
        out = out + (values[at] - values[at - 1]) * ((index + len(values) - at) // len(values))
    return out


def split(x):
    hi = x.astype(BF16)
    return hi, (x - hi.astype(F32)).astype(BF16)


def row_copy(x, j):
    return jnp.broadcast_to(x[j : j + 1, :], (8, 128))


def inverse_factor(x):
    n = len(x)
    sub = lax.broadcasted_iota(jnp.int32, (8, 128), 0)
    lane = lax.broadcasted_iota(jnp.int32, (8, 128), 1)
    col = [
        [None if i < k // 8 else jnp.broadcast_to(x[i][:, k : k + 1], (8, 128)) for i in range(n)]
        for k in range(8 * n)
    ]
    inverse = [jnp.where(lane == sub + 8 * i, 1.0, 0.0) for i in range(n)]
    for j in range(8 * n):
        g, r = j // 8, j % 8
        pivot = row_copy(col[j][g], r)
        inv = 1.0 / pivot
        row = row_copy(inverse[g], r)
        entry = {k: row_copy(col[j][k // 8], k % 8) for k in range(j + 1, 8 * n)}
        mult = [None if i < g else col[j][i] * inv for i in range(n)]
        if r < 7:
            mult[g] = jnp.where(sub > r, mult[g], 0.0)
        for k in range(j + 1, 8 * n):
            for i in range(k // 8, n):
                col[k][i] = col[k][i] - mult[i] * entry[k]
        for i in range(g + (r == 7), n):
            inverse[i] = inverse[i] - mult[i] * row
        inverse[g] = jnp.where(sub == r, row * lax.rsqrt(pivot), inverse[g])
    return jnp.concatenate(inverse, axis=0)


def eliminate(k, half, m_ref):
    left = 128 * half
    cols = slice(left, left + 384)
    rows = pl.ds(pl.multiple_of(32 * k, 32), 32)
    d = pltpu.roll(m_ref[rows, left : left + 128], (128 - 32 * (k % 4)) % 128, 1)
    inverse = inverse_factor([d[8 * i : 8 * i + 8] for i in range(4)])
    scaled = nn(inverse[:, :32], m_ref[rows, cols], HIGH)
    m_ref[rows, cols] = scaled

    @pl.when(k < 7)
    def _():
        subl = lax.broadcasted_iota(jnp.int32, (RANK - left, 32), 0)
        lower = jnp.where(subl >= 32 * k + 32 - left, scaled[:, : RANK - left].T, 0.0)
        m_ref[left:, cols] -= nn(lower, scaled, HIGH)


def main_kernel(
    grad,
    mom,
    basis,
    blend_out,
    ortho_out,
    back_out,
    norm_out,
    grad_v,
    basis_v,
    bases,
    hi_v,
    lo_v,
    part_v,
    from_core,
    hop_v,
    side_v,
    proj,
    gram_part,
    gram_in,
    gram_x,
    gram,
    elim,
    turned,
    w,
    w_hop,
    w_side,
    w_sub,
    w_full,
    back_hi,
    sq_v,
    load_sem,
    send_sem,
    recv_sem,
):
    f = lax.axis_index("fsdp")
    t = lax.axis_index("tp")
    x, c = t // 2, t % 2
    z, y = f // 4, f % 4

    def tp_dev(xx, cc):
        return {"fsdp": f, "tp": xx * 2 + cc}

    def f_dev(ff):
        return {"fsdp": ff, "tp": t}

    right = tp_dev((x + 1) % 4, c)
    left = tp_dev((x + 3) % 4, c)
    twin = tp_dev(x, 1 - c)

    def remote(src, dst, number, device):
        return pltpu.make_async_remote_copy(
            src_ref=src,
            dst_ref=dst,
            send_sem=send_sem.at[number],
            recv_sem=recv_sem.at[number],
            device_id=device,
            device_id_type=MESH,
        )

    def send(src, dst, number, device):
        remote(src, dst, number, device).start()

    def arrive(dst, number):
        remote(dst, dst, number, twin).wait_recv()

    def all_sent(first, many, ref):
        @pl.loop(first, first + many)
        def _(number):
            remote(ref, ref, number, twin).wait_send()

    def piece_row(core, chip):
        return pl.multiple_of(core * HALF + chip * PIECE, 32)

    def chunk_row(i):
        g = 3 - i // 2
        d = g + (g // 2) * (1 - 2 * (g % 2))
        core = (1 - c) * (1 - i % 2) + c * (i % 2)
        return piece_row(core, (x + d) % 4)

    def load(i):
        rows = pl.ds(chunk_row(i), PIECE)
        return (
            pltpu.make_async_copy(mom.at[rows], blend_out.at[rows], load_sem.at[2 * i]),
            pltpu.make_async_copy(grad.at[rows], grad_v.at[i % 4], load_sem.at[2 * i + 1]),
        )

    basis_copy = pltpu.make_async_copy(basis, basis_v, load_sem.at[16])
    basis_copy.start()

    @pl.loop(0, 3)
    def _(i):
        for copy in load(i):
            copy.start()

    barrier = pltpu.get_barrier_semaphore()

    @pl.loop(1, 16)
    def _(d):
        pl.semaphore_signal(barrier, inc=1, device_id=f_dev((f + d) % 16), device_id_type=MESH)

    @pl.loop(1, 8)
    def _(d):
        pl.semaphore_signal(
            barrier, inc=1, device_id={"fsdp": f, "tp": (t + d) % 8}, device_id_type=MESH
        )

    basis_copy.wait()
    basis_hi, basis_lo = split(basis_v[...])
    bases[:LOCAL_COLS] = basis_hi
    bases[LOCAL_COLS : 2 * LOCAL_COLS] = basis_lo
    bases[2 * LOCAL_COLS :] = basis_hi
    turned[...] = jnp.zeros_like(turned)
    hi_v[LOCAL_ROWS:, :] = jnp.zeros((32, LOCAL_COLS), BF16)
    lo_v[LOCAL_ROWS:, :] = jnp.zeros((32, LOCAL_COLS), BF16)

    def partial(i):
        for copy in load(i):
            copy.wait()
        rows = pl.ds(chunk_row(i), PIECE)

        @pl.when(i < 5)
        def _():
            for copy in load(i + 3):
                copy.start()

        blend = blend_out[rows, :] + grad_v[i % 4].astype(F32)
        blend_out[rows, :] = blend
        hi, lo = split(blend)
        hi_v[rows, :] = hi
        lo_v[rows, :] = lo
        return nn(jnp.concatenate([hi, hi, lo], axis=1), bases[...])

    a_rows, b_rows = pl.ds(0, PART), pl.ds(PART, PART)

    def add_core(j):
        arrive(from_core.at[j], N_CORE + j)
        part_v[2 * j + 1] += from_core[j]

    @pl.loop(0, 8)
    def _(i):
        part_v[i] = partial(i)
        j = i // 2
        core = remote(part_v.at[i], from_core.at[j], N_CORE + j, twin)

        @pl.when(i == 0)
        def _():
            pl.semaphore_wait(barrier, 22)

        @pl.when(i % 2 == 0)
        def _():
            core.start()

        @pl.when(i == 2)
        def _():
            add_core(0)
            send(part_v.at[1, a_rows], hop_v.at[0], N_HOP_A, right)
            send(part_v.at[1, b_rows], hop_v.at[1], N_HOP_B, left)

        @pl.when(i == 4)
        def _():
            add_core(1)
            send(part_v.at[3, a_rows], side_v.at[2], N_RIGHT_A, left)

        @pl.when(i == 6)
        def _():
            add_core(2)
            send(part_v.at[5, b_rows], side_v.at[1], N_LEFT_B, right)
            arrive(hop_v.at[0], N_HOP_A)
            part_v[5, a_rows] += hop_v[0]
            send(part_v.at[5, a_rows], side_v.at[0], N_LEFT_A, right)
            arrive(hop_v.at[1], N_HOP_B)
            part_v[3, b_rows] += hop_v[1]
            send(part_v.at[3, b_rows], side_v.at[3], N_RIGHT_B, left)

    add_core(3)
    my_row = piece_row(c, x)
    arrive(side_v.at[2], N_RIGHT_A)
    arrive(side_v.at[0], N_LEFT_A)
    proj[pl.ds(my_row, PART), :] = part_v[7, a_rows] + (side_v[0] + side_v[2])
    arrive(side_v.at[1], N_LEFT_B)
    arrive(side_v.at[3], N_RIGHT_B)
    proj[pl.ds(my_row + PART, PART), :] = part_v[7, b_rows] + (side_v[1] + side_v[3])

    def part_of(core, chip, b):
        return proj.at[pl.ds(pl.multiple_of(piece_row(core, chip) + b * PART, 16), PART)]

    def whole_of(core, chip):
        return proj.at[pl.ds(piece_row(core, chip), PIECE)]

    def send_part(chip, b, number, device):
        send(part_of(c, chip, b), part_of(c, chip, b), number, device)

    def send_whole(chip, number):
        send(whole_of(c, chip), whole_of(c, chip), number, twin)

    xl, xr, xo = (x + 3) % 4, (x + 1) % 4, (x + 2) % 4
    send_part(x, 0, G_LEFT_A, right)
    send_part(x, 1, G_RIGHT_B, left)
    send_whole(x, G_CORE)
    send_part(x, 1, G_LEFT_B, right)
    send_part(x, 0, G_RIGHT_A, left)

    half_cols = pl.ds(pl.multiple_of(c * 128, 128), 128)

    def eight(row):
        return pl.ds(pl.multiple_of(row * 8, 8), 8)

    def gram_start():
        gram_part[...] = jnp.zeros((128, RANK), F32)

        @pl.loop(0, 2)
        def _(core):
            rows = pl.ds(piece_row(core, x), PIECE)
            gram_part[...] += tn(proj[rows, half_cols], proj[rows, :], HIGH)

        @pl.loop(1, 16)
        def _(d):
            to = (f + d) % 16
            send(gram_part.at[eight(to)], gram_in.at[d], GRAM_SUM + d - 1, f_dev(to))

    def gram_across():
        gram_in[0] = gram_part[eight(f), :]

        @pl.loop(1, 16)
        def _(d):
            arrive(gram_in.at[d], GRAM_SUM + d - 1)

        gram_x[x] = jnp.sum(gram_in[...], axis=0)

        @pl.loop(1, 4)
        def _(d):
            send(gram_x.at[x], gram_x.at[x], GRAM_X + d - 1, tp_dev((x + d) % 4, c))

    def gram_row(ff):
        return pl.ds(pl.multiple_of(c * 128 + ff * 8, 8), 8)

    def gram_round():
        @pl.loop(1, 4)
        def _(d):
            arrive(gram_x.at[(x + 4 - d) % 4], GRAM_X + d - 1)

        gram[gram_row(f), :] = (gram_x[0] + gram_x[1]) + (gram_x[2] + gram_x[3])

        @pl.loop(1, 16)
        def _(d):
            mine = gram.at[gram_row(f)]
            send(mine, mine, GRAM_ALL + d - 1, f_dev((f + d) % 16))

    def gram_half(core):
        return gram.at[pl.ds(pl.multiple_of(core * 128, 128), 128)]

    def gram_pair():
        @pl.loop(1, 16)
        def _(d):
            arrive(gram.at[gram_row((f + 16 - d) % 16)], GRAM_ALL + d - 1)

        send(gram_half(c), gram_half(c), GRAM_CORE, twin)

    w[...] = jnp.zeros_like(w)

    @pl.loop(0, 8)
    def _(g):
        core = (c + pick(g, (0, 1, 0, 0, 0, 1, 1, 1))) % 2
        chip = (x + pick(g, (0, 0, 1, 3, 2, 1, 3, 2))) % 4

        @pl.when(g == 1)
        def _():
            arrive(whole_of(1 - c, x), G_CORE)
            gram_start()

        @pl.when(g == 2)
        def _():
            arrive(part_of(c, xl, 0), G_LEFT_A)
            send_part(xl, 0, G_OPP_A, right)
            arrive(part_of(c, xr, 1), G_RIGHT_B)
            send_part(xr, 1, G_OPP_B, left)
            gram_across()
            arrive(part_of(c, xr, 0), G_RIGHT_A)
            send_whole(xr, G_CORE + 1)
            arrive(part_of(c, xl, 1), G_LEFT_B)
            send_whole(xl, G_CORE + 2)

        @pl.when(g == 4)
        def _():
            arrive(part_of(c, xo, 0), G_OPP_A)
            arrive(part_of(c, xo, 1), G_OPP_B)
            send_whole(xo, G_CORE + 3)
            gram_round()

        @pl.when(g == 5)
        def _():
            arrive(whole_of(1 - c, xr), G_CORE + 1)

        @pl.when(g == 6)
        def _():
            arrive(whole_of(1 - c, xl), G_CORE + 2)

        @pl.when(g == 7)
        def _():
            arrive(whole_of(1 - c, xo), G_CORE + 3)

        rows = pl.ds(piece_row(core, chip), PIECE)
        p_hi, p_lo = split(proj[rows, :].T)
        turned[:, :PIECE] = p_hi
        turned[:, 256 : 256 + PIECE] = p_hi
        turned[:, 512 : 512 + PIECE] = p_lo
        more = pl.ds(piece_row(core, chip), 256)
        for n in range(4):
            cols = slice(256 * n, 256 * n + 256)
            hi = hi_v[more, cols]
            w[:, cols] += nn(turned[...], jnp.concatenate([hi, lo_v[more, cols], hi], axis=0))

    def places(u):
        k, q = y + u * (z - y), z + u * (y - z)

        def first(kk):
            return f_dev(z * 4 + kk + u * (kk * 4 + y - z * 4 - kk))

        def second(qq):
            return f_dev(qq * 4 + y + u * (z * 4 + qq - qq * 4 - y))

        return k, q, first, second

    def cols_ab(u):
        start = pl.multiple_of(WIDE * u, WIDE)
        return pl.ds(start, 256), pl.ds(pl.multiple_of(start + 256, 256), 256)

    def cols_u(u):
        return pl.ds(pl.multiple_of(WIDE * u, WIDE), WIDE)

    def rows32(h, k):
        return pl.ds(pl.multiple_of(128 * h + 32 * k, 32), 32)

    def rows8(h, k, q):
        return pl.ds(pl.multiple_of(128 * h + 32 * k + 8 * q, 8), 8)

    def w_step_1(h, u):
        k, q, first, _ = places(u)
        ca, cb = cols_ab(u)
        i = 2 * h + u
        kr, kl, ko = (k + 1) % 4, (k + 3) % 4, (k + 2) % 4
        send(w.at[rows32(h, ko), ca], w_hop.at[2 * i], W_HOP + 2 * i, first(kr))
        send(w.at[rows32(h, ko), cb], w_hop.at[2 * i + 1], W_HOP + 2 * i + 1, first(kl))
        send(w.at[rows32(h, kr), cb], w_side.at[4 * i + 1], W_NEXT + 4 * i + 1, first(kr))
        send(w.at[rows32(h, kl), ca], w_side.at[4 * i + 2], W_NEXT + 4 * i + 2, first(kl))

    def w_step_2(h, u):
        k, q, first, _ = places(u)
        ca, cb = cols_ab(u)
        i = 2 * h + u
        kr, kl = (k + 1) % 4, (k + 3) % 4
        arrive(w_hop.at[2 * i], W_HOP + 2 * i)
        w[rows32(h, kr), ca] += w_hop[2 * i]
        send(w.at[rows32(h, kr), ca], w_side.at[4 * i], W_NEXT + 4 * i, first(kr))
        arrive(w_hop.at[2 * i + 1], W_HOP + 2 * i + 1)
        w[rows32(h, kl), cb] += w_hop[2 * i + 1]
        send(w.at[rows32(h, kl), cb], w_side.at[4 * i + 3], W_NEXT + 4 * i + 3, first(kl))

    def w_step_3(h, u):
        k, q, _, second = places(u)
        ca, cb = cols_ab(u)
        i = 2 * h + u
        for s in range(4):
            arrive(w_side.at[4 * i + s], W_NEXT + 4 * i + s)
        w[rows32(h, k), ca] += w_side[4 * i] + w_side[4 * i + 2]
        w[rows32(h, k), cb] += w_side[4 * i + 1] + w_side[4 * i + 3]

        @pl.loop(1, 4)
        def _(d):
            to, slot = (q + d) % 4, 3 * i + d - 1
            send(w.at[rows8(h, k, to), cols_u(u)], w_sub.at[slot], W_SUB + slot, second(to))

    def w_step_4(h, u):
        k, q, _, second = places(u)
        i = 2 * h + u

        @pl.loop(0, 3)
        def _(d):
            arrive(w_sub.at[3 * i + d], W_SUB + 3 * i + d)

        w_full[rows8(h, k, q), cols_u(u)] = (w[rows8(h, k, q), cols_u(u)] + w_sub[3 * i]) + (
            w_sub[3 * i + 1] + w_sub[3 * i + 2]
        )

        @pl.loop(1, 4)
        def _(d):
            mine = w_full.at[rows8(h, k, q), cols_u(u)]
            send(mine, mine, W_ALL + 3 * i + d - 1, second((q + d) % 4))

    def w_step_5(h, u):
        k, q, first, _ = places(u)
        ca, cb = cols_ab(u)
        i = 2 * h + u
        dr, dl = first((k + 1) % 4), first((k + 3) % 4)

        @pl.loop(1, 4)
        def _(d):
            arrive(w_full.at[rows8(h, k, (q + 4 - d) % 4), cols_u(u)], W_ALL + 3 * i + d - 1)

        mine_a, mine_b = w_full.at[rows32(h, k), ca], w_full.at[rows32(h, k), cb]
        send(mine_a, mine_a, W_RING + 4 * i, dr)
        send(mine_b, mine_b, W_RING + 4 * i + 3, dl)
        send(mine_b, mine_b, W_RING + 4 * i + 1, dr)
        send(mine_a, mine_a, W_RING + 4 * i + 2, dl)

    def w_step_6(h, u):
        k, q, first, _ = places(u)
        ca, cb = cols_ab(u)
        i = 2 * h + u
        kr, kl = (k + 1) % 4, (k + 3) % 4
        from_left = w_full.at[rows32(h, kl), ca]
        arrive(from_left, W_RING + 4 * i)
        send(from_left, from_left, W_FAR + 2 * i, first(kr))
        from_right = w_full.at[rows32(h, kr), cb]
        arrive(from_right, W_RING + 4 * i + 3)
        send(from_right, from_right, W_FAR + 2 * i + 1, first(kl))

    def w_step_7(h, u):
        k = places(u)[0]
        ca, cb = cols_ab(u)
        i = 2 * h + u
        kr, kl, ko = (k + 1) % 4, (k + 3) % 4, (k + 2) % 4
        arrive(w_full.at[rows32(h, kl), cb], W_RING + 4 * i + 1)
        arrive(w_full.at[rows32(h, kr), ca], W_RING + 4 * i + 2)
        arrive(w_full.at[rows32(h, ko), ca], W_FAR + 2 * i)
        arrive(w_full.at[rows32(h, ko), cb], W_FAR + 2 * i + 1)

    def all_parts(step):
        @pl.loop(0, 4)
        def _(i):
            step(i // 2, i % 2)

    all_parts(w_step_1)
    gram_pair()
    all_parts(w_step_2)
    w_steps_at = (None, w_step_3, None, w_step_4, None, w_step_5, None, w_step_6)

    arrive(gram_half(1 - c), GRAM_CORE)
    elim[:, :RANK] = gram[...]
    rr = lax.broadcasted_iota(jnp.int32, (RANK, RANK), 0)
    cc = lax.broadcasted_iota(jnp.int32, (RANK, RANK), 1)
    elim[:, RANK:] = jnp.where(rr == cc, 1.0, 0.0).astype(F32)

    for half in range(2):

        @pl.loop(4 * half, 4 * half + 4)
        def _(k):
            eliminate(k, half, elim)
            for at in range(4 * half, 4 * half + 4):
                if w_steps_at[at] is not None:

                    @pl.when(k == at)
                    def _():
                        all_parts(w_steps_at[at])

    t_hi, t_lo = split(elim[:, RANK:].T)
    turned[:, :256] = t_hi
    turned[:, 256:512] = t_lo

    @pl.loop(0, 8)
    def _(i):
        rows = pl.ds(pl.multiple_of(i * PIECE, 32), PIECE)
        hi, lo = split(proj[rows, :])
        first = turned[:, :256]
        ortho_out[rows, :] = nn(
            jnp.concatenate([hi, hi, lo], axis=1),
            jnp.concatenate([first, turned[:, 256:512], first], axis=0),
        )

    all_sent(N_HOP_A, 12, side_v.at[0])
    all_sent(N_CORE, 8, part_v.at[0])
    all_sent(GRAM_SUM, 33, sq_v.at[0])
    all_sent(GRAM_CORE, 1, gram_part)
    all_parts(w_step_7)
    f_hi, f_lo = split(elim[:, RANK:])
    factor = jnp.concatenate([f_hi, f_hi, f_lo], axis=1)
    squares = jnp.zeros((RANK, 128), F32)
    for n in range(4):
        cols = slice(256 * n, 256 * n + 256)
        w_hi, w_lo = split(w_full[:, cols])
        back = nn(factor, jnp.concatenate([w_hi, w_lo, w_hi], axis=0))
        back_out[:, cols] = back
        back_hi[:, cols] = back.astype(BF16)
        squares = squares + (back[:, :128] * back[:, :128] + back[:, 128:] * back[:, 128:])
    sq_v[t] = nt(jnp.ones((8, 128), F32), squares, HIGH)

    @pl.loop(1, 8)
    def _(d):
        send(sq_v.at[t], sq_v.at[t], SQ + d - 1, {"fsdp": f, "tp": (t + d) % 8})


    @pl.loop(0, LOCAL_ROWS // STEP)
    def _(i):
        rows = pl.ds(pl.multiple_of(i * STEP, 64), STEP)
        blend_out[rows, :] -= nn((0.05 * ortho_out[rows, :]).astype(BF16), back_hi[...])

    all_sent(W_HOP, 48, w_hop.at[0])
    all_sent(W_SUB, 24, w_sub.at[0])

    @pl.loop(1, 8)
    def _(d):
        arrive(sq_v.at[(t + 8 - d) % 8], SQ + d - 1)

    norm_out[...] = lax.rsqrt(jnp.sum(sq_v[...], axis=0) + 1e-06)
    all_sent(SQ, 7, sq_v.at[0])


def write_kernel(
    new_mom, ortho, back, norm, mom_out, basis_out, update_out, backs, basis_v, update_v, sems, mom_sem
):
    def mom_copy(i):
        rows = pl.ds(PIECE * i, PIECE)
        return pltpu.make_async_copy(new_mom.at[rows], mom_out.at[rows], mom_sem.at[i])

    for i in range(8):
        mom_copy(i).start(priority=i % 2)
    hi, lo = split(back[...])
    backs[:RANK] = hi
    backs[RANK : 2 * RANK] = lo
    backs[2 * RANK :] = hi
    scale = (ROWS * COLS / RANK) ** 0.5
    norms = norm[0:1, :]

    def copies(i):
        rows = pl.ds(pl.multiple_of(i * STEP, 64), STEP)
        rank_rows = pl.ds(pl.multiple_of(i * 256, 256), 256)
        slot = i % 2
        return (
            pltpu.make_async_copy(update_v.at[slot], update_out.at[rows], sems.at[slot, 0]),
            pltpu.make_async_copy(basis_v.at[slot], basis_out.at[rank_rows], sems.at[slot, 1]),
        )

    @pl.loop(0, LOCAL_ROWS // STEP)
    def _(i):
        slot = i % 2

        @pl.when(i >= 2)
        def _():
            for copy in copies(i - 2):
                copy.wait()

        rows = pl.ds(pl.multiple_of(i * STEP, 64), STEP)
        cols = pl.ds(pl.multiple_of(i * 256, 256), 256)
        basis_v[slot] = back[:, cols].T * norms
        hi, lo = split(ortho[rows, :] * (scale * norms))
        update_v[slot] = nn(jnp.concatenate([hi, hi, lo], axis=1), backs[...]).astype(BF16)
        for copy in copies(i):
            copy.start()

    for i in (2, 3):
        for copy in copies(i):
            copy.wait()
    for i in range(8):
        mom_copy(i).wait()


def body(gradient, momentum, basis):
    anywhere = pl.BlockSpec(memory_space=pl.ANY)
    inside = pl.BlockSpec(memory_space=pltpu.VMEM)
    vmem = pltpu.VMEM
    fixed = [pltpu.with_memory_space_constraint(a, pltpu.HBM) for a in (gradient, momentum, basis)]
    results = pl.pallas_call(
        main_kernel,
        out_shape=(
            vmem((LOCAL_ROWS, LOCAL_COLS), F32),
            vmem((LOCAL_ROWS, RANK), F32),
            vmem((RANK, LOCAL_COLS), F32),
            vmem((8, RANK), F32),
        ),
        in_specs=[anywhere] * 3,
        out_specs=(inside,) * 4,
        scratch_shapes=[
            vmem((4, PIECE, LOCAL_COLS), BF16),
            vmem((LOCAL_COLS, RANK), F32),
            vmem((3 * LOCAL_COLS, RANK), BF16),
            vmem((LOCAL_ROWS + 32, LOCAL_COLS), BF16),
            vmem((LOCAL_ROWS + 32, LOCAL_COLS), BF16),
            vmem((8, PIECE, RANK), F32),
            vmem((4, PIECE, RANK), F32),
            vmem((2, PART, RANK), F32),
            vmem((4, PART, RANK), F32),
            vmem((LOCAL_ROWS, RANK), F32),
            vmem((128, RANK), F32),
            vmem((16, 8, RANK), F32),
            vmem((4, 8, RANK), F32),
            vmem((RANK, RANK), F32),
            vmem((RANK, 2 * RANK), F32),
            vmem((RANK, 3 * 256), BF16),
            vmem((RANK, LOCAL_COLS), F32),
            vmem((8, 32, 256), F32),
            vmem((16, 32, 256), F32),
            vmem((12, 8, WIDE), F32),
            vmem((RANK, LOCAL_COLS), F32),
            vmem((RANK, LOCAL_COLS), BF16),
            vmem((8, 8, RANK), F32),
            pltpu.SemaphoreType.DMA((17,)),
            pltpu.SemaphoreType.DMA((NAMES.count,)),
            pltpu.SemaphoreType.DMA((NAMES.count,)),
        ],
        compiler_params=pltpu.CompilerParams(
            collective_id=0, has_side_effects=True, vmem_limit_bytes=44 * 2**20
        ),
        name="transfers",
    )(*fixed)
    results = [pltpu.with_memory_space_constraint(a, pltpu.VMEM) for a in results]

    return pl.pallas_call(
        write_kernel,
        out_shape=(
            jax.ShapeDtypeStruct((LOCAL_ROWS, LOCAL_COLS), F32),
            jax.ShapeDtypeStruct((LOCAL_COLS, RANK), F32),
            jax.ShapeDtypeStruct((LOCAL_ROWS, LOCAL_COLS), BF16),
        ),
        in_specs=[inside] * 4,
        out_specs=(anywhere,) * 3,
        scratch_shapes=[
            vmem((3 * RANK, LOCAL_COLS), BF16),
            vmem((2, 256, RANK), F32),
            vmem((2, STEP, LOCAL_COLS), BF16),
            pltpu.SemaphoreType.DMA((2, 2)),
            pltpu.SemaphoreType.DMA((8,)),
        ],
        compiler_params=pltpu.CompilerParams(vmem_limit_bytes=32 * 2**20),
        name="outputs",
    )(*results)


def solution(mesh):
    placed = (P("fsdp", "tp"), P("fsdp", "tp"), P("tp", None))
    return jax.shard_map(
        body,
        mesh=mesh,
        in_specs=placed,
        out_specs=(P("fsdp", "tp"), P("tp", None), P("fsdp", "tp")),
        check_vma=False,
    )
```

```python
import functools

import jax
import jax.numpy as jnp
from jax import lax
from jax.experimental import pallas as pl
from jax.experimental.pallas import tpu as pltpu
from jax.sharding import PartitionSpec as P

ROWS = 28672
COLS = 8192
RANK = 256

F32 = jnp.float32
BF16 = jnp.bfloat16
HIGH = lax.Precision.HIGHEST
MESH = pl.DeviceIdType.MESH

LOCAL_ROWS = 1792
LOCAL_COLS = 1024
HALF = 896
PIECE = 224
PART = 112
STEP = 448
WIDE = 512


class Names:
    def __init__(self):
        self.count = 0

    def take(self, many=1):
        first = self.count
        self.count += many
        return first


NAMES = Names()
N_HOP_A, N_HOP_B = NAMES.take(), NAMES.take()
N_LEFT_A, N_LEFT_B = NAMES.take(), NAMES.take()
N_RIGHT_A, N_RIGHT_B = NAMES.take(), NAMES.take()
G_LEFT_A, G_LEFT_B = NAMES.take(), NAMES.take()
G_RIGHT_A, G_RIGHT_B = NAMES.take(), NAMES.take()
G_OPP_A, G_OPP_B = NAMES.take(), NAMES.take()
N_CORE = NAMES.take(4)
G_CORE = NAMES.take(4)
GRAM_SUM = NAMES.take(15)
GRAM_X = NAMES.take(3)
GRAM_ALL = NAMES.take(15)
SQ = NAMES.take(7)
GRAM_CORE = NAMES.take()
W_HOP = NAMES.take(8)
W_NEXT = NAMES.take(16)
W_RING = NAMES.take(16)
W_FAR = NAMES.take(8)
W_SUB = NAMES.take(12)
W_ALL = NAMES.take(12)


def nn(a, b, precision=None):
    return lax.dot_general(
        a, b, (((1,), (0,)), ((), ())), precision=precision, preferred_element_type=F32
    )


def tn(a, b, precision=None):
    return lax.dot_general(
        a, b, (((0,), (0,)), ((), ())), precision=precision, preferred_element_type=F32
    )


def nt(a, b, precision=None):
    return lax.dot_general(
        a, b, (((1,), (1,)), ((), ())), precision=precision, preferred_element_type=F32
    )


def pick(index, values):
    out = values[0]
    for at in range(1, len(values)):
        out = out + (values[at] - values[at - 1]) * ((index + len(values) - at) // len(values))
    return out


def split(x):
    hi = x.astype(BF16)
    return hi, (x - hi.astype(F32)).astype(BF16)


def row_copy(x, j):
    return jnp.broadcast_to(x[j : j + 1, :], (8, 128))


def inverse_factor(x):
    n = len(x)
    sub = lax.broadcasted_iota(jnp.int32, (8, 128), 0)
    lane = lax.broadcasted_iota(jnp.int32, (8, 128), 1)
    col = [
        [None if i < k // 8 else jnp.broadcast_to(x[i][:, k : k + 1], (8, 128)) for i in range(n)]
        for k in range(8 * n)
    ]
    inverse = [jnp.where(lane == sub + 8 * i, 1.0, 0.0) for i in range(n)]
    for j in range(8 * n):
        g, r = j // 8, j % 8
        pivot = row_copy(col[j][g], r)
        inv = 1.0 / pivot
        row = row_copy(inverse[g], r)
        entry = {k: row_copy(col[j][k // 8], k % 8) for k in range(j + 1, 8 * n)}
        mult = [None if i < g else col[j][i] * inv for i in range(n)]
        if r < 7:
            mult[g] = jnp.where(sub > r, mult[g], 0.0)
        for k in range(j + 1, 8 * n):
            for i in range(k // 8, n):
                col[k][i] = col[k][i] - mult[i] * entry[k]
        for i in range(g + (r == 7), n):
            inverse[i] = inverse[i] - mult[i] * row
        inverse[g] = jnp.where(sub == r, row * lax.rsqrt(pivot), inverse[g])
    return jnp.concatenate(inverse, axis=0)


def eliminate(k, half, m_ref):
    left = 128 * half
    cols = slice(left, left + 384)
    rows = pl.ds(pl.multiple_of(32 * k, 32), 32)
    d = pltpu.roll(m_ref[rows, left : left + 128], (128 - 32 * (k % 4)) % 128, 1)
    inverse = inverse_factor([d[8 * i : 8 * i + 8] for i in range(4)])
    scaled = nn(inverse[:, :32], m_ref[rows, cols], HIGH)
    m_ref[rows, cols] = scaled

    @pl.when(k < 7)
    def _():
        subl = lax.broadcasted_iota(jnp.int32, (RANK - left, 32), 0)
        lower = jnp.where(subl >= 32 * k + 32 - left, scaled[:, : RANK - left].T, 0.0)
        m_ref[left:, cols] -= nn(lower, scaled, HIGH)


def main_kernel(
    grad,
    mom,
    basis,
    blend_out,
    ortho_out,
    back_out,
    norm_out,
    grad_v,
    basis_v,
    bases,
    hi_v,
    lo_v,
    part_v,
    from_core,
    hop_v,
    side_v,
    proj,
    gram_part,
    gram_in,
    gram_x,
    gram,
    elim,
    turned,
    w,
    w_hop,
    w_side,
    w_sub,
    w_full,
    sq_v,
    load_sem,
    send_sem,
    recv_sem,
):
    f = lax.axis_index("fsdp")
    t = lax.axis_index("tp")
    x, c = t // 2, t % 2
    z, y = f // 4, f % 4

    def tp_dev(xx, cc):
        return {"fsdp": f, "tp": xx * 2 + cc}

    def f_dev(ff):
        return {"fsdp": ff, "tp": t}

    right = tp_dev((x + 1) % 4, c)
    left = tp_dev((x + 3) % 4, c)
    twin = tp_dev(x, 1 - c)

    def remote(src, dst, number, device):
        return pltpu.make_async_remote_copy(
            src_ref=src,
            dst_ref=dst,
            send_sem=send_sem.at[number],
            recv_sem=recv_sem.at[number],
            device_id=device,
            device_id_type=MESH,
        )

    def send(src, dst, number, device):
        remote(src, dst, number, device).start()

    def arrive(dst, number):
        remote(dst, dst, number, twin).wait_recv()

    def all_sent(first, many, ref):
        @pl.loop(first, first + many)
        def _(number):
            remote(ref, ref, number, twin).wait_send()

    def piece_row(core, chip):
        return pl.multiple_of(core * HALF + chip * PIECE, 32)

    def chunk_row(i):
        g = 3 - i // 2
        d = g + (g // 2) * (1 - 2 * (g % 2))
        core = (1 - c) * (1 - i % 2) + c * (i % 2)
        return piece_row(core, (x + d) % 4)

    def load(i):
        rows = pl.ds(chunk_row(i), PIECE)
        return (
            pltpu.make_async_copy(mom.at[rows], blend_out.at[rows], load_sem.at[2 * i]),
            pltpu.make_async_copy(grad.at[rows], grad_v.at[i % 4], load_sem.at[2 * i + 1]),
        )

    basis_copy = pltpu.make_async_copy(basis, basis_v, load_sem.at[16])
    basis_copy.start()

    @pl.loop(0, 3)
    def _(i):
        for copy in load(i):
            copy.start()

    barrier = pltpu.get_barrier_semaphore()

    @pl.loop(1, 16)
    def _(d):
        pl.semaphore_signal(barrier, inc=1, device_id=f_dev((f + d) % 16), device_id_type=MESH)

    @pl.loop(1, 8)
    def _(d):
        pl.semaphore_signal(
            barrier, inc=1, device_id={"fsdp": f, "tp": (t + d) % 8}, device_id_type=MESH
        )

    basis_copy.wait()
    basis_hi, basis_lo = split(basis_v[...])
    bases[:LOCAL_COLS] = basis_hi
    bases[LOCAL_COLS : 2 * LOCAL_COLS] = basis_lo
    bases[2 * LOCAL_COLS :] = basis_hi
    turned[...] = jnp.zeros_like(turned)
    hi_v[LOCAL_ROWS:, :] = jnp.zeros((32, LOCAL_COLS), BF16)
    lo_v[LOCAL_ROWS:, :] = jnp.zeros((32, LOCAL_COLS), BF16)

    def partial(i):
        for copy in load(i):
            copy.wait()
        rows = pl.ds(chunk_row(i), PIECE)

        @pl.when(i < 5)
        def _():
            for copy in load(i + 3):
                copy.start()

        blend = blend_out[rows, :] + grad_v[i % 4].astype(F32)
        blend_out[rows, :] = blend
        hi, lo = split(blend)
        hi_v[rows, :] = hi
        lo_v[rows, :] = lo
        return nn(jnp.concatenate([hi, hi, lo], axis=1), bases[...])

    a_rows, b_rows = pl.ds(0, PART), pl.ds(PART, PART)

    def add_core(j):
        arrive(from_core.at[j], N_CORE + j)
        part_v[2 * j + 1] += from_core[j]

    @pl.loop(0, 8)
    def _(i):
        part_v[i] = partial(i)
        j = i // 2
        core = remote(part_v.at[i], from_core.at[j], N_CORE + j, twin)

        @pl.when(i == 0)
        def _():
            pl.semaphore_wait(barrier, 22)

        @pl.when(i % 2 == 0)
        def _():
            core.start()

        @pl.when(i == 2)
        def _():
            add_core(0)
            send(part_v.at[1, a_rows], hop_v.at[0], N_HOP_A, right)
            send(part_v.at[1, b_rows], hop_v.at[1], N_HOP_B, left)

        @pl.when(i == 4)
        def _():
            add_core(1)
            send(part_v.at[3, a_rows], side_v.at[2], N_RIGHT_A, left)

        @pl.when(i == 6)
        def _():
            add_core(2)
            send(part_v.at[5, b_rows], side_v.at[1], N_LEFT_B, right)
            arrive(hop_v.at[0], N_HOP_A)
            part_v[5, a_rows] += hop_v[0]
            send(part_v.at[5, a_rows], side_v.at[0], N_LEFT_A, right)
            arrive(hop_v.at[1], N_HOP_B)
            part_v[3, b_rows] += hop_v[1]
            send(part_v.at[3, b_rows], side_v.at[3], N_RIGHT_B, left)

    add_core(3)
    my_row = piece_row(c, x)
    arrive(side_v.at[2], N_RIGHT_A)
    arrive(side_v.at[0], N_LEFT_A)
    proj[pl.ds(my_row, PART), :] = part_v[7, a_rows] + (side_v[0] + side_v[2])
    arrive(side_v.at[1], N_LEFT_B)
    arrive(side_v.at[3], N_RIGHT_B)
    proj[pl.ds(my_row + PART, PART), :] = part_v[7, b_rows] + (side_v[1] + side_v[3])

    def part_of(core, chip, b):
        return proj.at[pl.ds(pl.multiple_of(piece_row(core, chip) + b * PART, 16), PART)]

    def whole_of(core, chip):
        return proj.at[pl.ds(piece_row(core, chip), PIECE)]

    def send_part(chip, b, number, device):
        send(part_of(c, chip, b), part_of(c, chip, b), number, device)

    def send_whole(chip, number):
        send(whole_of(c, chip), whole_of(c, chip), number, twin)

    xl, xr, xo = (x + 3) % 4, (x + 1) % 4, (x + 2) % 4
    send_part(x, 0, G_LEFT_A, right)
    send_part(x, 1, G_RIGHT_B, left)
    send_whole(x, G_CORE)
    send_part(x, 1, G_LEFT_B, right)
    send_part(x, 0, G_RIGHT_A, left)

    half_cols = pl.ds(pl.multiple_of(c * 128, 128), 128)

    def eight(row):
        return pl.ds(pl.multiple_of(row * 8, 8), 8)

    def gram_start():
        gram_part[...] = jnp.zeros((128, RANK), F32)

        @pl.loop(0, 2)
        def _(core):
            rows = pl.ds(piece_row(core, x), PIECE)
            gram_part[...] += tn(proj[rows, half_cols], proj[rows, :], HIGH)

        @pl.loop(1, 16)
        def _(d):
            to = (f + d) % 16
            send(gram_part.at[eight(to)], gram_in.at[d], GRAM_SUM + d - 1, f_dev(to))

    def gram_across():
        gram_in[0] = gram_part[eight(f), :]

        @pl.loop(1, 16)
        def _(d):
            arrive(gram_in.at[d], GRAM_SUM + d - 1)

        gram_x[x] = jnp.sum(gram_in[...], axis=0)

        @pl.loop(1, 4)
        def _(d):
            send(gram_x.at[x], gram_x.at[x], GRAM_X + d - 1, tp_dev((x + d) % 4, c))

    def gram_row(ff):
        return pl.ds(pl.multiple_of(c * 128 + ff * 8, 8), 8)

    def gram_round():
        @pl.loop(1, 4)
        def _(d):
            arrive(gram_x.at[(x + 4 - d) % 4], GRAM_X + d - 1)

        gram[gram_row(f), :] = (gram_x[0] + gram_x[1]) + (gram_x[2] + gram_x[3])

        @pl.loop(1, 16)
        def _(d):
            mine = gram.at[gram_row(f)]
            send(mine, mine, GRAM_ALL + d - 1, f_dev((f + d) % 16))

    def gram_half(core):
        return gram.at[pl.ds(pl.multiple_of(core * 128, 128), 128)]

    def gram_pair():
        @pl.loop(1, 16)
        def _(d):
            arrive(gram.at[gram_row((f + 16 - d) % 16)], GRAM_ALL + d - 1)

        send(gram_half(c), gram_half(c), GRAM_CORE, twin)

    w[...] = jnp.zeros_like(w)

    @pl.loop(0, 8)
    def _(g):
        core = (c + pick(g, (0, 1, 0, 0, 0, 1, 1, 1))) % 2
        chip = (x + pick(g, (0, 0, 1, 3, 2, 1, 3, 2))) % 4

        @pl.when(g == 1)
        def _():
            arrive(whole_of(1 - c, x), G_CORE)
            gram_start()

        @pl.when(g == 2)
        def _():
            arrive(part_of(c, xl, 0), G_LEFT_A)
            send_part(xl, 0, G_OPP_A, right)
            arrive(part_of(c, xr, 1), G_RIGHT_B)
            send_part(xr, 1, G_OPP_B, left)
            gram_across()
            arrive(part_of(c, xr, 0), G_RIGHT_A)
            send_whole(xr, G_CORE + 1)
            arrive(part_of(c, xl, 1), G_LEFT_B)
            send_whole(xl, G_CORE + 2)

        @pl.when(g == 4)
        def _():
            arrive(part_of(c, xo, 0), G_OPP_A)
            arrive(part_of(c, xo, 1), G_OPP_B)
            send_whole(xo, G_CORE + 3)
            gram_round()

        @pl.when(g == 5)
        def _():
            arrive(whole_of(1 - c, xr), G_CORE + 1)

        @pl.when(g == 6)
        def _():
            arrive(whole_of(1 - c, xl), G_CORE + 2)

        @pl.when(g == 7)
        def _():
            arrive(whole_of(1 - c, xo), G_CORE + 3)

        rows = pl.ds(piece_row(core, chip), PIECE)
        p_hi, p_lo = split(proj[rows, :].T)
        turned[:, :PIECE] = p_hi
        turned[:, 256 : 256 + PIECE] = p_hi
        turned[:, 512 : 512 + PIECE] = p_lo
        more = pl.ds(piece_row(core, chip), 256)
        for n in range(4):
            cols = slice(256 * n, 256 * n + 256)
            hi = hi_v[more, cols]
            w[:, cols] += nn(turned[...], jnp.concatenate([hi, lo_v[more, cols], hi], axis=0))

    def places(u):
        k, q = y + u * (z - y), z + u * (y - z)

        def first(kk):
            return f_dev(z * 4 + kk + u * (kk * 4 + y - z * 4 - kk))

        def second(qq):
            return f_dev(qq * 4 + y + u * (z * 4 + qq - qq * 4 - y))

        return k, q, first, second

    def cols_ab(u):
        start = pl.multiple_of(WIDE * u, WIDE)
        return pl.ds(start, 256), pl.ds(pl.multiple_of(start + 256, 256), 256)

    def cols_u(u):
        return pl.ds(pl.multiple_of(WIDE * u, WIDE), WIDE)

    def rows32(h, k):
        return pl.ds(pl.multiple_of(128 * h + 32 * k, 32), 32)

    def rows8(h, k, q):
        return pl.ds(pl.multiple_of(128 * h + 32 * k + 8 * q, 8), 8)

    def w_step_1(h, u):
        k, q, first, _ = places(u)
        ca, cb = cols_ab(u)
        i = 2 * h + u
        kr, kl, ko = (k + 1) % 4, (k + 3) % 4, (k + 2) % 4
        send(w.at[rows32(h, ko), ca], w_hop.at[2 * i], W_HOP + 2 * i, first(kr))
        send(w.at[rows32(h, ko), cb], w_hop.at[2 * i + 1], W_HOP + 2 * i + 1, first(kl))
        send(w.at[rows32(h, kr), cb], w_side.at[4 * i + 1], W_NEXT + 4 * i + 1, first(kr))
        send(w.at[rows32(h, kl), ca], w_side.at[4 * i + 2], W_NEXT + 4 * i + 2, first(kl))

    def w_step_2(h, u):
        k, q, first, _ = places(u)
        ca, cb = cols_ab(u)
        i = 2 * h + u
        kr, kl = (k + 1) % 4, (k + 3) % 4
        arrive(w_hop.at[2 * i], W_HOP + 2 * i)
        w[rows32(h, kr), ca] += w_hop[2 * i]
        send(w.at[rows32(h, kr), ca], w_side.at[4 * i], W_NEXT + 4 * i, first(kr))
        arrive(w_hop.at[2 * i + 1], W_HOP + 2 * i + 1)
        w[rows32(h, kl), cb] += w_hop[2 * i + 1]
        send(w.at[rows32(h, kl), cb], w_side.at[4 * i + 3], W_NEXT + 4 * i + 3, first(kl))

    def w_step_3(h, u):
        k, q, _, second = places(u)
        ca, cb = cols_ab(u)
        i = 2 * h + u
        for s in range(4):
            arrive(w_side.at[4 * i + s], W_NEXT + 4 * i + s)
        w[rows32(h, k), ca] += w_side[4 * i] + w_side[4 * i + 2]
        w[rows32(h, k), cb] += w_side[4 * i + 1] + w_side[4 * i + 3]

        @pl.loop(1, 4)
        def _(d):
            to, slot = (q + d) % 4, 3 * i + d - 1
            send(w.at[rows8(h, k, to), cols_u(u)], w_sub.at[slot], W_SUB + slot, second(to))

    def w_step_4(h, u):
        k, q, _, second = places(u)
        i = 2 * h + u

        @pl.loop(0, 3)
        def _(d):
            arrive(w_sub.at[3 * i + d], W_SUB + 3 * i + d)

        w_full[rows8(h, k, q), cols_u(u)] = (w[rows8(h, k, q), cols_u(u)] + w_sub[3 * i]) + (
            w_sub[3 * i + 1] + w_sub[3 * i + 2]
        )

        @pl.loop(1, 4)
        def _(d):
            mine = w_full.at[rows8(h, k, q), cols_u(u)]
            send(mine, mine, W_ALL + 3 * i + d - 1, second((q + d) % 4))

    def w_step_5(h, u):
        k, q, first, _ = places(u)
        ca, cb = cols_ab(u)
        i = 2 * h + u
        dr, dl = first((k + 1) % 4), first((k + 3) % 4)

        @pl.loop(1, 4)
        def _(d):
            arrive(w_full.at[rows8(h, k, (q + 4 - d) % 4), cols_u(u)], W_ALL + 3 * i + d - 1)

        mine_a, mine_b = w_full.at[rows32(h, k), ca], w_full.at[rows32(h, k), cb]
        send(mine_a, mine_a, W_RING + 4 * i, dr)
        send(mine_b, mine_b, W_RING + 4 * i + 3, dl)
        send(mine_b, mine_b, W_RING + 4 * i + 1, dr)
        send(mine_a, mine_a, W_RING + 4 * i + 2, dl)

    def w_step_6(h, u):
        k, q, first, _ = places(u)
        ca, cb = cols_ab(u)
        i = 2 * h + u
        kr, kl = (k + 1) % 4, (k + 3) % 4
        from_left = w_full.at[rows32(h, kl), ca]
        arrive(from_left, W_RING + 4 * i)
        send(from_left, from_left, W_FAR + 2 * i, first(kr))
        from_right = w_full.at[rows32(h, kr), cb]
        arrive(from_right, W_RING + 4 * i + 3)
        send(from_right, from_right, W_FAR + 2 * i + 1, first(kl))

    def w_step_7(h, u):
        k = places(u)[0]
        ca, cb = cols_ab(u)
        i = 2 * h + u
        kr, kl, ko = (k + 1) % 4, (k + 3) % 4, (k + 2) % 4
        arrive(w_full.at[rows32(h, kl), cb], W_RING + 4 * i + 1)
        arrive(w_full.at[rows32(h, kr), ca], W_RING + 4 * i + 2)
        arrive(w_full.at[rows32(h, ko), ca], W_FAR + 2 * i)
        arrive(w_full.at[rows32(h, ko), cb], W_FAR + 2 * i + 1)

    def all_parts(step):
        @pl.loop(0, 4)
        def _(i):
            step(i // 2, i % 2)

    all_parts(w_step_1)
    gram_pair()
    all_parts(w_step_2)
    w_steps_at = (w_step_3, None, w_step_4, None, w_step_5, None, w_step_6, w_step_7)

    arrive(gram_half(1 - c), GRAM_CORE)
    elim[:, :RANK] = gram[...]
    rr = lax.broadcasted_iota(jnp.int32, (RANK, RANK), 0)
    cc = lax.broadcasted_iota(jnp.int32, (RANK, RANK), 1)
    elim[:, RANK:] = jnp.where(rr == cc, 1.0, 0.0).astype(F32)

    for half in range(2):

        @pl.loop(4 * half, 4 * half + 4)
        def _(k):
            eliminate(k, half, elim)
            for at in range(4 * half, 4 * half + 4):
                if w_steps_at[at] is not None:

                    @pl.when(k == at)
                    def _():
                        all_parts(w_steps_at[at])

    f_hi, f_lo = split(elim[:, RANK:])
    factor = jnp.concatenate([f_hi, f_hi, f_lo], axis=1)
    squares = jnp.zeros((RANK, 128), F32)
    for n in range(4):
        cols = slice(256 * n, 256 * n + 256)
        w_hi, w_lo = split(w_full[:, cols])
        back = nn(factor, jnp.concatenate([w_hi, w_lo, w_hi], axis=0))
        back_out[:, cols] = back
        squares = squares + (back[:, :128] * back[:, :128] + back[:, 128:] * back[:, 128:])
    sq_v[t] = nt(jnp.ones((8, 128), F32), squares, HIGH)

    @pl.loop(1, 8)
    def _(d):
        send(sq_v.at[t], sq_v.at[t], SQ + d - 1, {"fsdp": f, "tp": (t + d) % 8})


    t_hi, t_lo = split(elim[:, RANK:].T)
    turned[:, :256] = t_hi
    turned[:, 256:512] = t_lo

    @pl.loop(0, 8)
    def _(i):
        rows = pl.ds(pl.multiple_of(i * PIECE, 32), PIECE)
        hi, lo = split(proj[rows, :])
        first = turned[:, :256]
        ortho_out[rows, :] = nn(
            jnp.concatenate([hi, hi, lo], axis=1),
            jnp.concatenate([first, turned[:, 256:512], first], axis=0),
        )

    all_sent(N_HOP_A, 12, side_v.at[0])
    all_sent(N_CORE, 8, part_v.at[0])
    all_sent(GRAM_SUM, 33, sq_v.at[0])
    all_sent(GRAM_CORE, 1, gram_part)
    all_sent(W_HOP, 48, w_hop.at[0])
    all_sent(W_SUB, 24, w_sub.at[0])

    @pl.loop(1, 8)
    def _(d):
        arrive(sq_v.at[(t + 8 - d) % 8], SQ + d - 1)

    norm_out[...] = lax.rsqrt(jnp.sum(sq_v[...], axis=0) + 1e-06)
    all_sent(SQ, 7, sq_v.at[0])


def write_kernel(
    blend, ortho, back, norm, mom_out, basis_out, update_out, backs, mom_v, basis_v, update_v, sems
):
    hi, lo = split(back[...])
    backs[:RANK] = hi
    backs[RANK : 2 * RANK] = lo
    backs[2 * RANK :] = hi
    scale = (ROWS * COLS / RANK) ** 0.5
    norms = norm[0:1, :]

    def copies(i):
        slot = i % 2
        found = []
        for p in range(2):
            rows = pl.ds(pl.multiple_of(i * STEP + p * PIECE, 32), PIECE)
            here = pl.ds(p * PIECE, PIECE)
            found.append(pltpu.make_async_copy(mom_v.at[slot, here], mom_out.at[rows], sems.at[slot, p]))
            found.append(
                pltpu.make_async_copy(update_v.at[slot, here], update_out.at[rows], sems.at[slot, 2 + p])
            )
        rank_rows = pl.ds(pl.multiple_of(i * 256, 256), 256)
        found.append(pltpu.make_async_copy(basis_v.at[slot], basis_out.at[rank_rows], sems.at[slot, 4]))
        return found

    @pl.loop(0, LOCAL_ROWS // STEP)
    def _(i):
        slot = i % 2

        @pl.when(i >= 2)
        def _():
            for copy in copies(i - 2):
                copy.wait()

        rows = pl.ds(pl.multiple_of(i * STEP, 64), STEP)
        cols = pl.ds(pl.multiple_of(i * 256, 256), 256)
        basis_v[slot] = back[:, cols].T * norms
        plain = ortho[rows, :]
        mom_v[slot] = blend[rows, :] - nn((0.05 * plain).astype(BF16), backs[:RANK])
        mom_a, update_a, mom_b, update_b, basis_copy = copies(i)
        mom_a.start()
        mom_b.start(priority=1)
        basis_copy.start()
        hi, lo = split(plain * (scale * norms))
        update_v[slot] = nn(jnp.concatenate([hi, hi, lo], axis=1), backs[...]).astype(BF16)
        update_a.start()
        update_b.start(priority=1)

    for i in (2, 3):
        for copy in copies(i):
            copy.wait()


def body(gradient, momentum, basis):
    anywhere = pl.BlockSpec(memory_space=pl.ANY)
    inside = pl.BlockSpec(memory_space=pltpu.VMEM)
    vmem = pltpu.VMEM
    fixed = [pltpu.with_memory_space_constraint(a, pltpu.HBM) for a in (gradient, momentum, basis)]
    results = pl.pallas_call(
        main_kernel,
        out_shape=(
            vmem((LOCAL_ROWS, LOCAL_COLS), F32),
            vmem((LOCAL_ROWS, RANK), F32),
            vmem((RANK, LOCAL_COLS), F32),
            vmem((8, RANK), F32),
        ),
        in_specs=[anywhere] * 3,
        out_specs=(inside,) * 4,
        scratch_shapes=[
            vmem((4, PIECE, LOCAL_COLS), BF16),
            vmem((LOCAL_COLS, RANK), F32),
            vmem((3 * LOCAL_COLS, RANK), BF16),
            vmem((LOCAL_ROWS + 32, LOCAL_COLS), BF16),
            vmem((LOCAL_ROWS + 32, LOCAL_COLS), BF16),
            vmem((8, PIECE, RANK), F32),
            vmem((4, PIECE, RANK), F32),
            vmem((2, PART, RANK), F32),
            vmem((4, PART, RANK), F32),
            vmem((LOCAL_ROWS, RANK), F32),
            vmem((128, RANK), F32),
            vmem((16, 8, RANK), F32),
            vmem((4, 8, RANK), F32),
            vmem((RANK, RANK), F32),
            vmem((RANK, 2 * RANK), F32),
            vmem((RANK, 3 * 256), BF16),
            vmem((RANK, LOCAL_COLS), F32),
            vmem((8, 32, 256), F32),
            vmem((16, 32, 256), F32),
            vmem((12, 8, WIDE), F32),
            vmem((RANK, LOCAL_COLS), F32),
            vmem((8, 8, RANK), F32),
            pltpu.SemaphoreType.DMA((17,)),
            pltpu.SemaphoreType.DMA((NAMES.count,)),
            pltpu.SemaphoreType.DMA((NAMES.count,)),
        ],
        compiler_params=pltpu.CompilerParams(
            collective_id=0, has_side_effects=True, vmem_limit_bytes=44 * 2**20
        ),
        name="transfers",
    )(*fixed)
    results = [pltpu.with_memory_space_constraint(a, pltpu.VMEM) for a in results]

    return pl.pallas_call(
        write_kernel,
        out_shape=(
            jax.ShapeDtypeStruct((LOCAL_ROWS, LOCAL_COLS), F32),
            jax.ShapeDtypeStruct((LOCAL_COLS, RANK), F32),
            jax.ShapeDtypeStruct((LOCAL_ROWS, LOCAL_COLS), BF16),
        ),
        in_specs=[inside] * 4,
        out_specs=(anywhere,) * 3,
        scratch_shapes=[
            vmem((3 * RANK, LOCAL_COLS), BF16),
            vmem((2, STEP, LOCAL_COLS), F32),
            vmem((2, 256, RANK), F32),
            vmem((2, STEP, LOCAL_COLS), BF16),
            pltpu.SemaphoreType.DMA((2, 5)),
        ],
        compiler_params=pltpu.CompilerParams(vmem_limit_bytes=32 * 2**20),
        name="outputs",
    )(*results)


def solution(mesh):
    placed = (P("fsdp", "tp"), P("fsdp", "tp"), P("tp", None))
    return jax.shard_map(
        body,
        mesh=mesh,
        in_specs=placed,
        out_specs=(P("fsdp", "tp"), P("tp", None), P("fsdp", "tp")),
        check_vma=False,
    )
```

```python
import functools

import jax
import jax.numpy as jnp
from jax import lax
from jax.experimental import pallas as pl
from jax.experimental.pallas import tpu as pltpu
from jax.sharding import PartitionSpec as P

ROWS = 28672
COLS = 8192
RANK = 256

F32 = jnp.float32
BF16 = jnp.bfloat16
HIGH = lax.Precision.HIGHEST
MESH = pl.DeviceIdType.MESH

LOCAL_ROWS = 1792
LOCAL_COLS = 1024
HALF = 896
PIECE = 224
PART = 112
STEP = 448
WIDE = 512


class Names:
    def __init__(self):
        self.count = 0

    def take(self, many=1):
        first = self.count
        self.count += many
        return first


NAMES = Names()
N_HOP_A, N_HOP_B = NAMES.take(), NAMES.take()
N_LEFT_A, N_LEFT_B = NAMES.take(), NAMES.take()
N_RIGHT_A, N_RIGHT_B = NAMES.take(), NAMES.take()
G_LEFT_A, G_LEFT_B = NAMES.take(), NAMES.take()
G_RIGHT_A, G_RIGHT_B = NAMES.take(), NAMES.take()
G_OPP_A, G_OPP_B = NAMES.take(), NAMES.take()
N_CORE = NAMES.take(4)
G_CORE = NAMES.take(4)
GRAM_SUM = NAMES.take(15)
GRAM_X = NAMES.take(3)
GRAM_ALL = NAMES.take(15)
SQ = NAMES.take(7)
GRAM_CORE = NAMES.take()
W_HOP = NAMES.take(8)
W_NEXT = NAMES.take(16)
W_RING = NAMES.take(16)
W_FAR = NAMES.take(8)
W_SUB = NAMES.take(12)
W_ALL = NAMES.take(12)


def nn(a, b, precision=None):
    return lax.dot_general(
        a, b, (((1,), (0,)), ((), ())), precision=precision, preferred_element_type=F32
    )


def tn(a, b, precision=None):
    return lax.dot_general(
        a, b, (((0,), (0,)), ((), ())), precision=precision, preferred_element_type=F32
    )


def nt(a, b, precision=None):
    return lax.dot_general(
        a, b, (((1,), (1,)), ((), ())), precision=precision, preferred_element_type=F32
    )


def pick(index, values):
    out = values[0]
    for at in range(1, len(values)):
        out = out + (values[at] - values[at - 1]) * ((index + len(values) - at) // len(values))
    return out


def split(x):
    hi = x.astype(BF16)
    return hi, (x - hi.astype(F32)).astype(BF16)


def row_copy(x, j):
    return jnp.broadcast_to(x[j : j + 1, :], (8, 128))


def inverse_factor(x):
    n = len(x)
    sub = lax.broadcasted_iota(jnp.int32, (8, 128), 0)
    lane = lax.broadcasted_iota(jnp.int32, (8, 128), 1)
    col = [
        [None if i < k // 8 else jnp.broadcast_to(x[i][:, k : k + 1], (8, 128)) for i in range(n)]
        for k in range(8 * n)
    ]
    inverse = [jnp.where(lane == sub + 8 * i, 1.0, 0.0) for i in range(n)]
    for j in range(8 * n):
        g, r = j // 8, j % 8
        pivot = row_copy(col[j][g], r)
        inv = 1.0 / pivot
        row = row_copy(inverse[g], r)
        entry = {k: row_copy(col[j][k // 8], k % 8) for k in range(j + 1, 8 * n)}
        mult = [None if i < g else col[j][i] * inv for i in range(n)]
        if r < 7:
            mult[g] = jnp.where(sub > r, mult[g], 0.0)
        for k in range(j + 1, 8 * n):
            for i in range(k // 8, n):
                col[k][i] = col[k][i] - mult[i] * entry[k]
        for i in range(g + (r == 7), n):
            inverse[i] = inverse[i] - mult[i] * row
        inverse[g] = jnp.where(sub == r, row * lax.rsqrt(pivot), inverse[g])
    return jnp.concatenate(inverse, axis=0)


def eliminate(k, half, m_ref):
    left = 128 * half
    cols = slice(left, left + 384)
    rows = pl.ds(pl.multiple_of(32 * k, 32), 32)
    d = pltpu.roll(m_ref[rows, left : left + 128], (128 - 32 * (k % 4)) % 128, 1)
    inverse = inverse_factor([d[8 * i : 8 * i + 8] for i in range(4)])
    scaled = nn(inverse[:, :32], m_ref[rows, cols], HIGH)
    m_ref[rows, cols] = scaled

    @pl.when(k < 7)
    def _():
        subl = lax.broadcasted_iota(jnp.int32, (RANK - left, 32), 0)
        lower = jnp.where(subl >= 32 * k + 32 - left, scaled[:, : RANK - left].T, 0.0)
        m_ref[left:, cols] -= nn(lower, scaled, HIGH)


def main_kernel(
    grad,
    mom,
    basis,
    blend_out,
    ortho_out,
    back_out,
    norm_out,
    grad_v,
    basis_v,
    bases,
    hi_v,
    lo_v,
    part_v,
    from_core,
    hop_v,
    side_v,
    proj,
    gram_part,
    gram_in,
    gram_x,
    gram,
    elim,
    turned,
    w,
    w_hop,
    w_side,
    w_sub,
    w_full,
    sq_v,
    load_sem,
    send_sem,
    recv_sem,
):
    f = lax.axis_index("fsdp")
    t = lax.axis_index("tp")
    x, c = t // 2, t % 2
    z, y = f // 4, f % 4

    def tp_dev(xx, cc):
        return {"fsdp": f, "tp": xx * 2 + cc}

    def f_dev(ff):
        return {"fsdp": ff, "tp": t}

    right = tp_dev((x + 1) % 4, c)
    left = tp_dev((x + 3) % 4, c)
    twin = tp_dev(x, 1 - c)

    def remote(src, dst, number, device):
        return pltpu.make_async_remote_copy(
            src_ref=src,
            dst_ref=dst,
            send_sem=send_sem.at[number],
            recv_sem=recv_sem.at[number],
            device_id=device,
            device_id_type=MESH,
        )

    def send(src, dst, number, device):
        remote(src, dst, number, device).start()

    def arrive(dst, number):
        remote(dst, dst, number, twin).wait_recv()

    def all_sent(first, many, ref):
        @pl.loop(first, first + many)
        def _(number):
            remote(ref, ref, number, twin).wait_send()

    def piece_row(core, chip):
        return pl.multiple_of(core * HALF + chip * PIECE, 32)

    def chunk_row(i):
        g = 3 - i // 2
        d = g + (g // 2) * (1 - 2 * (g % 2))
        core = (1 - c) * (1 - i % 2) + c * (i % 2)
        return piece_row(core, (x + d) % 4)

    def load(i):
        rows = pl.ds(chunk_row(i), PIECE)
        return (
            pltpu.make_async_copy(mom.at[rows], blend_out.at[rows], load_sem.at[2 * i]),
            pltpu.make_async_copy(grad.at[rows], grad_v.at[i % 4], load_sem.at[2 * i + 1]),
        )

    basis_copy = pltpu.make_async_copy(basis, basis_v, load_sem.at[16])
    basis_copy.start()

    @pl.loop(0, 3)
    def _(i):
        for copy in load(i):
            copy.start()

    barrier = pltpu.get_barrier_semaphore()

    @pl.loop(1, 16)
    def _(d):
        pl.semaphore_signal(barrier, inc=1, device_id=f_dev((f + d) % 16), device_id_type=MESH)

    @pl.loop(1, 8)
    def _(d):
        pl.semaphore_signal(
            barrier, inc=1, device_id={"fsdp": f, "tp": (t + d) % 8}, device_id_type=MESH
        )

    basis_copy.wait()
    basis_hi, basis_lo = split(basis_v[...])
    bases[:LOCAL_COLS] = basis_hi
    bases[LOCAL_COLS : 2 * LOCAL_COLS] = basis_lo
    bases[2 * LOCAL_COLS :] = basis_hi
    turned[...] = jnp.zeros_like(turned)
    hi_v[LOCAL_ROWS:, :] = jnp.zeros((32, LOCAL_COLS), BF16)
    lo_v[LOCAL_ROWS:, :] = jnp.zeros((32, LOCAL_COLS), BF16)

    def partial(i):
        for copy in load(i):
            copy.wait()
        rows = pl.ds(chunk_row(i), PIECE)

        @pl.when(i < 5)
        def _():
            for copy in load(i + 3):
                copy.start()

        blend = blend_out[rows, :] + grad_v[i % 4].astype(F32)
        blend_out[rows, :] = blend
        hi, lo = split(blend)
        hi_v[rows, :] = hi
        lo_v[rows, :] = lo
        return nn(jnp.concatenate([hi, hi, lo], axis=1), bases[...])

    a_rows, b_rows = pl.ds(0, PART), pl.ds(PART, PART)

    def add_core(j):
        arrive(from_core.at[j], N_CORE + j)
        part_v[2 * j + 1] += from_core[j]

    @pl.loop(0, 8)
    def _(i):
        part_v[i] = partial(i)
        j = i // 2
        core = remote(part_v.at[i], from_core.at[j], N_CORE + j, twin)

        @pl.when(i == 0)
        def _():
            pl.semaphore_wait(barrier, 22)

        @pl.when(i % 2 == 0)
        def _():
            core.start()

        @pl.when(i == 2)
        def _():
            add_core(0)
            send(part_v.at[1, a_rows], hop_v.at[0], N_HOP_A, right)
            send(part_v.at[1, b_rows], hop_v.at[1], N_HOP_B, left)

        @pl.when(i == 4)
        def _():
            add_core(1)
            send(part_v.at[3, a_rows], side_v.at[2], N_RIGHT_A, left)

        @pl.when(i == 6)
        def _():
            add_core(2)
            send(part_v.at[5, b_rows], side_v.at[1], N_LEFT_B, right)
            arrive(hop_v.at[0], N_HOP_A)
            part_v[5, a_rows] += hop_v[0]
            send(part_v.at[5, a_rows], side_v.at[0], N_LEFT_A, right)
            arrive(hop_v.at[1], N_HOP_B)
            part_v[3, b_rows] += hop_v[1]
            send(part_v.at[3, b_rows], side_v.at[3], N_RIGHT_B, left)

    add_core(3)
    my_row = piece_row(c, x)
    arrive(side_v.at[2], N_RIGHT_A)
    arrive(side_v.at[0], N_LEFT_A)
    proj[pl.ds(my_row, PART), :] = part_v[7, a_rows] + (side_v[0] + side_v[2])
    arrive(side_v.at[1], N_LEFT_B)
    arrive(side_v.at[3], N_RIGHT_B)
    proj[pl.ds(my_row + PART, PART), :] = part_v[7, b_rows] + (side_v[1] + side_v[3])

    def part_of(core, chip, b):
        return proj.at[pl.ds(pl.multiple_of(piece_row(core, chip) + b * PART, 16), PART)]

    def whole_of(core, chip):
        return proj.at[pl.ds(piece_row(core, chip), PIECE)]

    def send_part(chip, b, number, device):
        send(part_of(c, chip, b), part_of(c, chip, b), number, device)

    def send_whole(chip, number):
        send(whole_of(c, chip), whole_of(c, chip), number, twin)

    xl, xr, xo = (x + 3) % 4, (x + 1) % 4, (x + 2) % 4
    send_part(x, 0, G_LEFT_A, right)
    send_part(x, 1, G_RIGHT_B, left)
    send_whole(x, G_CORE)
    send_part(x, 1, G_LEFT_B, right)
    send_part(x, 0, G_RIGHT_A, left)

    half_cols = pl.ds(pl.multiple_of(c * 128, 128), 128)

    def eight(row):
        return pl.ds(pl.multiple_of(row * 8, 8), 8)

    def gram_start():
        gram_part[...] = jnp.zeros((128, RANK), F32)

        @pl.loop(0, 2)
        def _(core):
            rows = pl.ds(piece_row(core, x), PIECE)
            gram_part[...] += tn(proj[rows, half_cols], proj[rows, :], HIGH)

        @pl.loop(1, 16)
        def _(d):
            to = (f + d) % 16
            send(gram_part.at[eight(to)], gram_in.at[d], GRAM_SUM + d - 1, f_dev(to))

    def gram_across():
        gram_in[0] = gram_part[eight(f), :]

        @pl.loop(1, 16)
        def _(d):
            arrive(gram_in.at[d], GRAM_SUM + d - 1)

        gram_x[x] = jnp.sum(gram_in[...], axis=0)

        @pl.loop(1, 4)
        def _(d):
            send(gram_x.at[x], gram_x.at[x], GRAM_X + d - 1, tp_dev((x + d) % 4, c))

    def gram_row(ff):
        return pl.ds(pl.multiple_of(c * 128 + ff * 8, 8), 8)

    def gram_round():
        @pl.loop(1, 4)
        def _(d):
            arrive(gram_x.at[(x + 4 - d) % 4], GRAM_X + d - 1)

        gram[gram_row(f), :] = (gram_x[0] + gram_x[1]) + (gram_x[2] + gram_x[3])

        @pl.loop(1, 16)
        def _(d):
            mine = gram.at[gram_row(f)]
            send(mine, mine, GRAM_ALL + d - 1, f_dev((f + d) % 16))

    def gram_half(core):
        return gram.at[pl.ds(pl.multiple_of(core * 128, 128), 128)]

    def gram_pair():
        @pl.loop(1, 16)
        def _(d):
            arrive(gram.at[gram_row((f + 16 - d) % 16)], GRAM_ALL + d - 1)

        send(gram_half(c), gram_half(c), GRAM_CORE, twin)

    w[...] = jnp.zeros_like(w)

    @pl.loop(0, 8)
    def _(g):
        core = (c + pick(g, (0, 1, 0, 0, 0, 1, 1, 1))) % 2
        chip = (x + pick(g, (0, 0, 1, 3, 2, 1, 3, 2))) % 4

        @pl.when(g == 1)
        def _():
            arrive(whole_of(1 - c, x), G_CORE)
            arrive(part_of(c, xl, 0), G_LEFT_A)
            send_part(xl, 0, G_OPP_A, right)
            arrive(part_of(c, xr, 1), G_RIGHT_B)
            send_part(xr, 1, G_OPP_B, left)
            gram_start()

        @pl.when(g == 2)
        def _():
            arrive(part_of(c, xr, 0), G_RIGHT_A)
            send_whole(xr, G_CORE + 1)
            arrive(part_of(c, xl, 1), G_LEFT_B)
            send_whole(xl, G_CORE + 2)

        @pl.when(g == 4)
        def _():
            arrive(part_of(c, xo, 0), G_OPP_A)
            arrive(part_of(c, xo, 1), G_OPP_B)
            send_whole(xo, G_CORE + 3)

        @pl.when(g == 5)
        def _():
            gram_across()
            arrive(whole_of(1 - c, xr), G_CORE + 1)

        @pl.when(g == 6)
        def _():
            arrive(whole_of(1 - c, xl), G_CORE + 2)

        @pl.when(g == 7)
        def _():
            arrive(whole_of(1 - c, xo), G_CORE + 3)

        rows = pl.ds(piece_row(core, chip), PIECE)
        p_hi, p_lo = split(proj[rows, :].T)
        turned[:, :PIECE] = p_hi
        turned[:, 256 : 256 + PIECE] = p_hi
        turned[:, 512 : 512 + PIECE] = p_lo
        more = pl.ds(piece_row(core, chip), 256)
        for n in range(4):
            cols = slice(256 * n, 256 * n + 256)
            hi = hi_v[more, cols]
            w[:, cols] += nn(turned[...], jnp.concatenate([hi, lo_v[more, cols], hi], axis=0))

    def places(u):
        k, q = y + u * (z - y), z + u * (y - z)

        def first(kk):
            return f_dev(z * 4 + kk + u * (kk * 4 + y - z * 4 - kk))

        def second(qq):
            return f_dev(qq * 4 + y + u * (z * 4 + qq - qq * 4 - y))

        return k, q, first, second

    def cols_ab(u):
        start = pl.multiple_of(WIDE * u, WIDE)
        return pl.ds(start, 256), pl.ds(pl.multiple_of(start + 256, 256), 256)

    def cols_u(u):
        return pl.ds(pl.multiple_of(WIDE * u, WIDE), WIDE)

    def rows32(h, k):
        return pl.ds(pl.multiple_of(128 * h + 32 * k, 32), 32)

    def rows8(h, k, q):
        return pl.ds(pl.multiple_of(128 * h + 32 * k + 8 * q, 8), 8)

    def w_step_1(h, u):
        k, q, first, _ = places(u)
        ca, cb = cols_ab(u)
        i = 2 * h + u
        kr, kl, ko = (k + 1) % 4, (k + 3) % 4, (k + 2) % 4
        send(w.at[rows32(h, ko), ca], w_hop.at[2 * i], W_HOP + 2 * i, first(kr))
        send(w.at[rows32(h, ko), cb], w_hop.at[2 * i + 1], W_HOP + 2 * i + 1, first(kl))
        send(w.at[rows32(h, kr), cb], w_side.at[4 * i + 1], W_NEXT + 4 * i + 1, first(kr))
        send(w.at[rows32(h, kl), ca], w_side.at[4 * i + 2], W_NEXT + 4 * i + 2, first(kl))

    def w_step_2(h, u):
        k, q, first, _ = places(u)
        ca, cb = cols_ab(u)
        i = 2 * h + u
        kr, kl = (k + 1) % 4, (k + 3) % 4
        arrive(w_hop.at[2 * i], W_HOP + 2 * i)
        w[rows32(h, kr), ca] += w_hop[2 * i]
        send(w.at[rows32(h, kr), ca], w_side.at[4 * i], W_NEXT + 4 * i, first(kr))
        arrive(w_hop.at[2 * i + 1], W_HOP + 2 * i + 1)
        w[rows32(h, kl), cb] += w_hop[2 * i + 1]
        send(w.at[rows32(h, kl), cb], w_side.at[4 * i + 3], W_NEXT + 4 * i + 3, first(kl))

    def w_step_3(h, u):
        k, q, _, second = places(u)
        ca, cb = cols_ab(u)
        i = 2 * h + u
        for s in range(4):
            arrive(w_side.at[4 * i + s], W_NEXT + 4 * i + s)
        w[rows32(h, k), ca] += w_side[4 * i] + w_side[4 * i + 2]
        w[rows32(h, k), cb] += w_side[4 * i + 1] + w_side[4 * i + 3]

        @pl.loop(1, 4)
        def _(d):
            to, slot = (q + d) % 4, 3 * i + d - 1
            send(w.at[rows8(h, k, to), cols_u(u)], w_sub.at[slot], W_SUB + slot, second(to))

    def w_step_4(h, u):
        k, q, _, second = places(u)
        i = 2 * h + u

        @pl.loop(0, 3)
        def _(d):
            arrive(w_sub.at[3 * i + d], W_SUB + 3 * i + d)

        w_full[rows8(h, k, q), cols_u(u)] = (w[rows8(h, k, q), cols_u(u)] + w_sub[3 * i]) + (
            w_sub[3 * i + 1] + w_sub[3 * i + 2]
        )

        @pl.loop(1, 4)
        def _(d):
            mine = w_full.at[rows8(h, k, q), cols_u(u)]
            send(mine, mine, W_ALL + 3 * i + d - 1, second((q + d) % 4))

    def w_step_5(h, u):
        k, q, first, _ = places(u)
        ca, cb = cols_ab(u)
        i = 2 * h + u
        dr, dl = first((k + 1) % 4), first((k + 3) % 4)

        @pl.loop(1, 4)
        def _(d):
            arrive(w_full.at[rows8(h, k, (q + 4 - d) % 4), cols_u(u)], W_ALL + 3 * i + d - 1)

        mine_a, mine_b = w_full.at[rows32(h, k), ca], w_full.at[rows32(h, k), cb]
        send(mine_a, mine_a, W_RING + 4 * i, dr)
        send(mine_b, mine_b, W_RING + 4 * i + 3, dl)
        send(mine_b, mine_b, W_RING + 4 * i + 1, dr)
        send(mine_a, mine_a, W_RING + 4 * i + 2, dl)

    def w_step_6(h, u):
        k, q, first, _ = places(u)
        ca, cb = cols_ab(u)
        i = 2 * h + u
        kr, kl = (k + 1) % 4, (k + 3) % 4
        from_left = w_full.at[rows32(h, kl), ca]
        arrive(from_left, W_RING + 4 * i)
        send(from_left, from_left, W_FAR + 2 * i, first(kr))
        from_right = w_full.at[rows32(h, kr), cb]
        arrive(from_right, W_RING + 4 * i + 3)
        send(from_right, from_right, W_FAR + 2 * i + 1, first(kl))

    def w_step_7(h, u):
        k = places(u)[0]
        ca, cb = cols_ab(u)
        i = 2 * h + u
        kr, kl, ko = (k + 1) % 4, (k + 3) % 4, (k + 2) % 4
        arrive(w_full.at[rows32(h, kl), cb], W_RING + 4 * i + 1)
        arrive(w_full.at[rows32(h, kr), ca], W_RING + 4 * i + 2)
        arrive(w_full.at[rows32(h, ko), ca], W_FAR + 2 * i)
        arrive(w_full.at[rows32(h, ko), cb], W_FAR + 2 * i + 1)

    def all_parts(step):
        @pl.loop(0, 4)
        def _(i):
            step(i // 2, i % 2)

    all_parts(w_step_1)
    gram_round()
    all_parts(w_step_2)
    gram_pair()
    w_steps_at = (w_step_3, None, w_step_4, None, w_step_5, None, w_step_6, w_step_7)

    arrive(gram_half(1 - c), GRAM_CORE)
    elim[:, :RANK] = gram[...]
    rr = lax.broadcasted_iota(jnp.int32, (RANK, RANK), 0)
    cc = lax.broadcasted_iota(jnp.int32, (RANK, RANK), 1)
    elim[:, RANK:] = jnp.where(rr == cc, 1.0, 0.0).astype(F32)

    for half in range(2):

        @pl.loop(4 * half, 4 * half + 4)
        def _(k):
            eliminate(k, half, elim)
            for at in range(4 * half, 4 * half + 4):
                if w_steps_at[at] is not None:

                    @pl.when(k == at)
                    def _():
                        all_parts(w_steps_at[at])

    f_hi, f_lo = split(elim[:, RANK:])
    factor = jnp.concatenate([f_hi, f_hi, f_lo], axis=1)
    squares = jnp.zeros((RANK, 128), F32)
    for n in range(4):
        cols = slice(256 * n, 256 * n + 256)
        w_hi, w_lo = split(w_full[:, cols])
        back = nn(factor, jnp.concatenate([w_hi, w_lo, w_hi], axis=0))
        back_out[:, cols] = back
        squares = squares + (back[:, :128] * back[:, :128] + back[:, 128:] * back[:, 128:])
    sq_v[t] = nt(jnp.ones((8, 128), F32), squares, HIGH)

    @pl.loop(1, 8)
    def _(d):
        send(sq_v.at[t], sq_v.at[t], SQ + d - 1, {"fsdp": f, "tp": (t + d) % 8})


    t_hi, t_lo = split(elim[:, RANK:].T)
    turned[:, :256] = t_hi
    turned[:, 256:512] = t_lo

    @pl.loop(0, 8)
    def _(i):
        rows = pl.ds(pl.multiple_of(i * PIECE, 32), PIECE)
        hi, lo = split(proj[rows, :])
        first = turned[:, :256]
        ortho_out[rows, :] = nn(
            jnp.concatenate([hi, hi, lo], axis=1),
            jnp.concatenate([first, turned[:, 256:512], first], axis=0),
        )

    all_sent(N_HOP_A, 12, side_v.at[0])
    all_sent(N_CORE, 8, part_v.at[0])
    all_sent(GRAM_SUM, 33, sq_v.at[0])
    all_sent(GRAM_CORE, 1, gram_part)
    all_sent(W_HOP, 48, w_hop.at[0])
    all_sent(W_SUB, 24, w_sub.at[0])

    @pl.loop(1, 8)
    def _(d):
        arrive(sq_v.at[(t + 8 - d) % 8], SQ + d - 1)

    norm_out[...] = lax.rsqrt(jnp.sum(sq_v[...], axis=0) + 1e-06)
    all_sent(SQ, 7, sq_v.at[0])


def write_kernel(
    blend, ortho, back, norm, mom_out, basis_out, update_out, backs, mom_v, basis_v, update_v, sems
):
    hi, lo = split(back[...])
    backs[:RANK] = hi
    backs[RANK : 2 * RANK] = lo
    backs[2 * RANK :] = hi
    scale = (ROWS * COLS / RANK) ** 0.5
    norms = norm[0:1, :]

    def copies(i):
        slot = i % 2
        found = []
        for p in range(2):
            rows = pl.ds(pl.multiple_of(i * STEP + p * PIECE, 32), PIECE)
            here = pl.ds(p * PIECE, PIECE)
            found.append(pltpu.make_async_copy(mom_v.at[slot, here], mom_out.at[rows], sems.at[slot, p]))
            found.append(
                pltpu.make_async_copy(update_v.at[slot, here], update_out.at[rows], sems.at[slot, 2 + p])
            )
        rank_rows = pl.ds(pl.multiple_of(i * 256, 256), 256)
        found.append(pltpu.make_async_copy(basis_v.at[slot], basis_out.at[rank_rows], sems.at[slot, 4]))
        return found

    @pl.loop(0, LOCAL_ROWS // STEP)
    def _(i):
        slot = i % 2

        @pl.when(i >= 2)
        def _():
            for copy in copies(i - 2):
                copy.wait()

        rows = pl.ds(pl.multiple_of(i * STEP, 64), STEP)
        cols = pl.ds(pl.multiple_of(i * 256, 256), 256)
        basis_v[slot] = back[:, cols].T * norms
        plain = ortho[rows, :]
        mom_v[slot] = blend[rows, :] - nn((0.05 * plain).astype(BF16), backs[:RANK])
        mom_a, update_a, mom_b, update_b, basis_copy = copies(i)
        mom_a.start()
        mom_b.start(priority=1)
        basis_copy.start()
        hi, lo = split(plain * (scale * norms))
        update_v[slot] = nn(jnp.concatenate([hi, hi, lo], axis=1), backs[...]).astype(BF16)
        update_a.start()
        update_b.start(priority=1)

    for i in (2, 3):
        for copy in copies(i):
            copy.wait()


def body(gradient, momentum, basis):
    anywhere = pl.BlockSpec(memory_space=pl.ANY)
    inside = pl.BlockSpec(memory_space=pltpu.VMEM)
    vmem = pltpu.VMEM
    fixed = [pltpu.with_memory_space_constraint(a, pltpu.HBM) for a in (gradient, momentum, basis)]
    results = pl.pallas_call(
        main_kernel,
        out_shape=(
            vmem((LOCAL_ROWS, LOCAL_COLS), F32),
            vmem((LOCAL_ROWS, RANK), F32),
            vmem((RANK, LOCAL_COLS), F32),
            vmem((8, RANK), F32),
        ),
        in_specs=[anywhere] * 3,
        out_specs=(inside,) * 4,
        scratch_shapes=[
            vmem((4, PIECE, LOCAL_COLS), BF16),
            vmem((LOCAL_COLS, RANK), F32),
            vmem((3 * LOCAL_COLS, RANK), BF16),
            vmem((LOCAL_ROWS + 32, LOCAL_COLS), BF16),
            vmem((LOCAL_ROWS + 32, LOCAL_COLS), BF16),
            vmem((8, PIECE, RANK), F32),
            vmem((4, PIECE, RANK), F32),
            vmem((2, PART, RANK), F32),
            vmem((4, PART, RANK), F32),
            vmem((LOCAL_ROWS, RANK), F32),
            vmem((128, RANK), F32),
            vmem((16, 8, RANK), F32),
            vmem((4, 8, RANK), F32),
            vmem((RANK, RANK), F32),
            vmem((RANK, 2 * RANK), F32),
            vmem((RANK, 3 * 256), BF16),
            vmem((RANK, LOCAL_COLS), F32),
            vmem((8, 32, 256), F32),
            vmem((16, 32, 256), F32),
            vmem((12, 8, WIDE), F32),
            vmem((RANK, LOCAL_COLS), F32),
            vmem((8, 8, RANK), F32),
            pltpu.SemaphoreType.DMA((17,)),
            pltpu.SemaphoreType.DMA((NAMES.count,)),
            pltpu.SemaphoreType.DMA((NAMES.count,)),
        ],
        compiler_params=pltpu.CompilerParams(
            collective_id=0, has_side_effects=True, vmem_limit_bytes=44 * 2**20
        ),
        name="transfers",
    )(*fixed)
    results = [pltpu.with_memory_space_constraint(a, pltpu.VMEM) for a in results]

    return pl.pallas_call(
        write_kernel,
        out_shape=(
            jax.ShapeDtypeStruct((LOCAL_ROWS, LOCAL_COLS), F32),
            jax.ShapeDtypeStruct((LOCAL_COLS, RANK), F32),
            jax.ShapeDtypeStruct((LOCAL_ROWS, LOCAL_COLS), BF16),
        ),
        in_specs=[inside] * 4,
        out_specs=(anywhere,) * 3,
        scratch_shapes=[
            vmem((3 * RANK, LOCAL_COLS), BF16),
            vmem((2, STEP, LOCAL_COLS), F32),
            vmem((2, 256, RANK), F32),
            vmem((2, STEP, LOCAL_COLS), BF16),
            pltpu.SemaphoreType.DMA((2, 5)),
        ],
        compiler_params=pltpu.CompilerParams(vmem_limit_bytes=32 * 2**20),
        name="outputs",
    )(*results)


def solution(mesh):
    placed = (P("fsdp", "tp"), P("fsdp", "tp"), P("tp", None))
    return jax.shard_map(
        body,
        mesh=mesh,
        in_specs=placed,
        out_specs=(P("fsdp", "tp"), P("tp", None), P("fsdp", "tp")),
        check_vma=False,
    )
```

```python
import functools

import jax
import jax.numpy as jnp
from jax import lax
from jax.experimental import pallas as pl
from jax.experimental.pallas import tpu as pltpu
from jax.sharding import PartitionSpec as P

ROWS = 28672
COLS = 8192
RANK = 256

F32 = jnp.float32
BF16 = jnp.bfloat16
HIGH = lax.Precision.HIGHEST
MESH = pl.DeviceIdType.MESH

LOCAL_ROWS = 1792
LOCAL_COLS = 1024
HALF = 896
PIECE = 224
PART = 112
STEP = 448
WIDE = 512


class Names:
    def __init__(self):
        self.count = 0

    def take(self, many=1):
        first = self.count
        self.count += many
        return first


NAMES = Names()
N_HOP_A, N_HOP_B = NAMES.take(), NAMES.take()
N_LEFT_A, N_LEFT_B = NAMES.take(), NAMES.take()
N_RIGHT_A, N_RIGHT_B = NAMES.take(), NAMES.take()
G_LEFT_A, G_LEFT_B = NAMES.take(), NAMES.take()
G_RIGHT_A, G_RIGHT_B = NAMES.take(), NAMES.take()
G_OPP_A, G_OPP_B = NAMES.take(), NAMES.take()
N_CORE = NAMES.take(4)
G_CORE = NAMES.take(4)
GRAM_SUM = NAMES.take(15)
GRAM_X = NAMES.take(3)
GRAM_ALL = NAMES.take(15)
SQ = NAMES.take(7)
GRAM_CORE = NAMES.take()
W_HOP = NAMES.take(8)
W_NEXT = NAMES.take(16)
W_RING = NAMES.take(16)
W_FAR = NAMES.take(8)
W_SUB = NAMES.take(12)
W_ALL = NAMES.take(12)


def nn(a, b, precision=None):
    return lax.dot_general(
        a, b, (((1,), (0,)), ((), ())), precision=precision, preferred_element_type=F32
    )


def tn(a, b, precision=None):
    return lax.dot_general(
        a, b, (((0,), (0,)), ((), ())), precision=precision, preferred_element_type=F32
    )


def nt(a, b, precision=None):
    return lax.dot_general(
        a, b, (((1,), (1,)), ((), ())), precision=precision, preferred_element_type=F32
    )


def pick(index, values):
    out = values[0]
    for at in range(1, len(values)):
        out = out + (values[at] - values[at - 1]) * ((index + len(values) - at) // len(values))
    return out


def split(x):
    hi = x.astype(BF16)
    return hi, (x - hi.astype(F32)).astype(BF16)


def row_copy(x, j):
    return jnp.broadcast_to(x[j : j + 1, :], (8, 128))


def inverse_factor(x):
    n = len(x)
    sub = lax.broadcasted_iota(jnp.int32, (8, 128), 0)
    lane = lax.broadcasted_iota(jnp.int32, (8, 128), 1)
    col = [
        [None if i < k // 8 else jnp.broadcast_to(x[i][:, k : k + 1], (8, 128)) for i in range(n)]
        for k in range(8 * n)
    ]
    inverse = [jnp.where(lane == sub + 8 * i, 1.0, 0.0) for i in range(n)]
    for g in range(n):
        entry = [[row_copy(col[8 * g + j][g], i) for j in range(i + 1)] for i in range(8)]
        rows = [row_copy(inverse[g], j) for j in range(8)]
        inv, mult = [], [[None] * 8 for _ in range(8)]
        for j in range(8):
            inv.append(1.0 / entry[j][j])
            for k in range(j + 1, 8):
                mult[k][j] = entry[k][j] * inv[j]
                for i in range(k, 8):
                    entry[i][k] = entry[i][k] - entry[i][j] * mult[k][j]
                rows[k] = rows[k] - mult[k][j] * rows[j]
        final = jnp.zeros((8, 128), F32)
        for j in range(8):
            final = jnp.where(sub == j, rows[j] * lax.rsqrt(entry[j][j]), final)
        inverse[g] = final
        below = {}
        for i in range(g + 1, n):
            c = [col[8 * g + j][i] for j in range(8)]
            for j in range(8):
                for k in range(j + 1, 8):
                    c[k] = c[k] - c[j] * mult[k][j]
            below[i] = (c, [c[j] * inv[j] for j in range(8)])
        for k in range(8 * g + 8, 8 * n):
            across = [row_copy(below[k // 8][0][j], k % 8) for j in range(8)]
            for i in range(k // 8, n):
                for j in range(8):
                    col[k][i] = col[k][i] - below[i][1][j] * across[j]
        for i in range(g + 1, n):
            for j in range(8):
                inverse[i] = inverse[i] - below[i][1][j] * rows[j]
    return jnp.concatenate(inverse, axis=0)


def split3(x):
    first = x.astype(BF16)
    rest = x - first.astype(F32)
    second = rest.astype(BF16)
    return first, second, (rest - second.astype(F32)).astype(BF16)


def eliminate(k, half, m_ref):
    left = 128 * half
    cols = slice(left, left + 384)
    rows = pl.ds(pl.multiple_of(32 * k, 32), 32)
    d = pltpu.roll(m_ref[rows, left : left + 128], (128 - 32 * (k % 4)) % 128, 1)
    inverse = inverse_factor([d[8 * i : 8 * i + 8] for i in range(4)])
    scaled = nn(inverse[:, :32], m_ref[rows, cols], HIGH)
    m_ref[rows, cols] = scaled

    @pl.when(k < 7)
    def _():
        lane = lax.broadcasted_iota(jnp.int32, (32, RANK - left), 1)
        lower = jnp.where(lane >= 32 * k + 32 - left, scaled[:, : RANK - left], 0.0)
        a, b, c = split3(lower)
        d, e, f = split3(scaled)
        m_ref[left:, cols] -= tn(
            jnp.concatenate([a, a, b, a, b, c], axis=0), jnp.concatenate([d, e, d, f, e, d], axis=0)
        )


def main_kernel(
    grad,
    mom,
    basis,
    blend_out,
    ortho_out,
    back_out,
    norm_out,
    grad_v,
    basis_v,
    bases,
    hi_v,
    lo_v,
    part_v,
    from_core,
    hop_v,
    side_v,
    proj,
    gram_part,
    gram_in,
    gram_x,
    gram,
    elim,
    turned,
    w,
    w_hop,
    w_side,
    w_sub,
    w_full,
    sq_v,
    load_sem,
    send_sem,
    recv_sem,
):
    f = lax.axis_index("fsdp")
    t = lax.axis_index("tp")
    x, c = t // 2, t % 2
    z, y = f // 4, f % 4

    def tp_dev(xx, cc):
        return {"fsdp": f, "tp": xx * 2 + cc}

    def f_dev(ff):
        return {"fsdp": ff, "tp": t}

    right = tp_dev((x + 1) % 4, c)
    left = tp_dev((x + 3) % 4, c)
    twin = tp_dev(x, 1 - c)

    def remote(src, dst, number, device):
        return pltpu.make_async_remote_copy(
            src_ref=src,
            dst_ref=dst,
            send_sem=send_sem.at[number],
            recv_sem=recv_sem.at[number],
            device_id=device,
            device_id_type=MESH,
        )

    def send(src, dst, number, device):
        remote(src, dst, number, device).start()

    def arrive(dst, number):
        remote(dst, dst, number, twin).wait_recv()

    def all_sent(first, many, ref):
        @pl.loop(first, first + many)
        def _(number):
            remote(ref, ref, number, twin).wait_send()

    def piece_row(core, chip):
        return pl.multiple_of(core * HALF + chip * PIECE, 32)

    def chunk_row(i):
        g = 3 - i // 2
        d = g + (g // 2) * (1 - 2 * (g % 2))
        core = (1 - c) * (1 - i % 2) + c * (i % 2)
        return piece_row(core, (x + d) % 4)

    def load(i):
        rows = pl.ds(chunk_row(i), PIECE)
        return (
            pltpu.make_async_copy(mom.at[rows], blend_out.at[rows], load_sem.at[2 * i]),
            pltpu.make_async_copy(grad.at[rows], grad_v.at[i % 4], load_sem.at[2 * i + 1]),
        )

    basis_copy = pltpu.make_async_copy(basis, basis_v, load_sem.at[16])
    basis_copy.start()

    @pl.loop(0, 3)
    def _(i):
        for copy in load(i):
            copy.start()

    barrier = pltpu.get_barrier_semaphore()

    @pl.loop(1, 16)
    def _(d):
        pl.semaphore_signal(barrier, inc=1, device_id=f_dev((f + d) % 16), device_id_type=MESH)

    @pl.loop(1, 8)
    def _(d):
        pl.semaphore_signal(
            barrier, inc=1, device_id={"fsdp": f, "tp": (t + d) % 8}, device_id_type=MESH
        )

    basis_copy.wait()
    basis_hi, basis_lo = split(basis_v[...])
    bases[:LOCAL_COLS] = basis_hi
    bases[LOCAL_COLS : 2 * LOCAL_COLS] = basis_lo
    bases[2 * LOCAL_COLS :] = basis_hi
    turned[...] = jnp.zeros_like(turned)
    hi_v[LOCAL_ROWS:, :] = jnp.zeros((32, LOCAL_COLS), BF16)
    lo_v[LOCAL_ROWS:, :] = jnp.zeros((32, LOCAL_COLS), BF16)

    def partial(i):
        for copy in load(i):
            copy.wait()
        rows = pl.ds(chunk_row(i), PIECE)

        @pl.when(i < 5)
        def _():
            for copy in load(i + 3):
                copy.start()

        blend = blend_out[rows, :] + grad_v[i % 4].astype(F32)
        blend_out[rows, :] = blend
        hi, lo = split(blend)
        hi_v[rows, :] = hi
        lo_v[rows, :] = lo
        return nn(jnp.concatenate([hi, hi, lo], axis=1), bases[...])

    a_rows, b_rows = pl.ds(0, PART), pl.ds(PART, PART)

    def add_core(j):
        arrive(from_core.at[j], N_CORE + j)
        part_v[2 * j + 1] += from_core[j]

    @pl.loop(0, 8)
    def _(i):
        part_v[i] = partial(i)
        j = i // 2
        core = remote(part_v.at[i], from_core.at[j], N_CORE + j, twin)

        @pl.when(i == 0)
        def _():
            pl.semaphore_wait(barrier, 22)

        @pl.when(i % 2 == 0)
        def _():
            core.start()

        @pl.when(i == 2)
        def _():
            add_core(0)
            send(part_v.at[1, a_rows], hop_v.at[0], N_HOP_A, right)
            send(part_v.at[1, b_rows], hop_v.at[1], N_HOP_B, left)

        @pl.when(i == 4)
        def _():
            add_core(1)
            send(part_v.at[3, a_rows], side_v.at[2], N_RIGHT_A, left)

        @pl.when(i == 6)
        def _():
            add_core(2)
            send(part_v.at[5, b_rows], side_v.at[1], N_LEFT_B, right)
            arrive(hop_v.at[0], N_HOP_A)
            part_v[5, a_rows] += hop_v[0]
            send(part_v.at[5, a_rows], side_v.at[0], N_LEFT_A, right)
            arrive(hop_v.at[1], N_HOP_B)
            part_v[3, b_rows] += hop_v[1]
            send(part_v.at[3, b_rows], side_v.at[3], N_RIGHT_B, left)

    add_core(3)
    my_row = piece_row(c, x)
    arrive(side_v.at[2], N_RIGHT_A)
    arrive(side_v.at[0], N_LEFT_A)
    proj[pl.ds(my_row, PART), :] = part_v[7, a_rows] + (side_v[0] + side_v[2])
    arrive(side_v.at[1], N_LEFT_B)
    arrive(side_v.at[3], N_RIGHT_B)
    proj[pl.ds(my_row + PART, PART), :] = part_v[7, b_rows] + (side_v[1] + side_v[3])

    def part_of(core, chip, b):
        return proj.at[pl.ds(pl.multiple_of(piece_row(core, chip) + b * PART, 16), PART)]

    def whole_of(core, chip):
        return proj.at[pl.ds(piece_row(core, chip), PIECE)]

    def send_part(chip, b, number, device):
        send(part_of(c, chip, b), part_of(c, chip, b), number, device)

    def send_whole(chip, number):
        send(whole_of(c, chip), whole_of(c, chip), number, twin)

    xl, xr, xo = (x + 3) % 4, (x + 1) % 4, (x + 2) % 4
    send_part(x, 0, G_LEFT_A, right)
    send_part(x, 1, G_RIGHT_B, left)
    send_whole(x, G_CORE)
    send_part(x, 1, G_LEFT_B, right)
    send_part(x, 0, G_RIGHT_A, left)

    half_cols = pl.ds(pl.multiple_of(c * 128, 128), 128)

    def eight(row):
        return pl.ds(pl.multiple_of(row * 8, 8), 8)

    def gram_start():
        gram_part[...] = jnp.zeros((128, RANK), F32)

        @pl.loop(0, 2)
        def _(core):
            rows = pl.ds(piece_row(core, x), PIECE)
            gram_part[...] += tn(proj[rows, half_cols], proj[rows, :], HIGH)

        @pl.loop(1, 16)
        def _(d):
            to = (f + d) % 16
            send(gram_part.at[eight(to)], gram_in.at[d], GRAM_SUM + d - 1, f_dev(to))

    def gram_across():
        gram_in[0] = gram_part[eight(f), :]

        @pl.loop(1, 16)
        def _(d):
            arrive(gram_in.at[d], GRAM_SUM + d - 1)

        gram_x[x] = jnp.sum(gram_in[...], axis=0)

        @pl.loop(1, 4)
        def _(d):
            send(gram_x.at[x], gram_x.at[x], GRAM_X + d - 1, tp_dev((x + d) % 4, c))

    def gram_row(ff):
        return pl.ds(pl.multiple_of(c * 128 + ff * 8, 8), 8)

    def gram_round():
        @pl.loop(1, 4)
        def _(d):
            arrive(gram_x.at[(x + 4 - d) % 4], GRAM_X + d - 1)

        gram[gram_row(f), :] = (gram_x[0] + gram_x[1]) + (gram_x[2] + gram_x[3])

        @pl.loop(1, 16)
        def _(d):
            mine = gram.at[gram_row(f)]
            send(mine, mine, GRAM_ALL + d - 1, f_dev((f + d) % 16))

    def gram_half(core):
        return gram.at[pl.ds(pl.multiple_of(core * 128, 128), 128)]

    def gram_pair():
        @pl.loop(1, 16)
        def _(d):
            arrive(gram.at[gram_row((f + 16 - d) % 16)], GRAM_ALL + d - 1)

        send(gram_half(c), gram_half(c), GRAM_CORE, twin)

    w[...] = jnp.zeros_like(w)

    @pl.loop(0, 8)
    def _(g):
        core = (c + pick(g, (0, 1, 0, 0, 0, 1, 1, 1))) % 2
        chip = (x + pick(g, (0, 0, 1, 3, 2, 1, 3, 2))) % 4

        @pl.when(g == 1)
        def _():
            arrive(whole_of(1 - c, x), G_CORE)
            gram_start()

        @pl.when(g == 2)
        def _():
            arrive(part_of(c, xl, 0), G_LEFT_A)
            send_part(xl, 0, G_OPP_A, right)
            arrive(part_of(c, xr, 1), G_RIGHT_B)
            send_part(xr, 1, G_OPP_B, left)
            gram_across()
            arrive(part_of(c, xr, 0), G_RIGHT_A)
            send_whole(xr, G_CORE + 1)
            arrive(part_of(c, xl, 1), G_LEFT_B)
            send_whole(xl, G_CORE + 2)

        @pl.when(g == 4)
        def _():
            arrive(part_of(c, xo, 0), G_OPP_A)
            arrive(part_of(c, xo, 1), G_OPP_B)
            send_whole(xo, G_CORE + 3)
            gram_round()

        @pl.when(g == 5)
        def _():
            arrive(whole_of(1 - c, xr), G_CORE + 1)

        @pl.when(g == 6)
        def _():
            arrive(whole_of(1 - c, xl), G_CORE + 2)

        @pl.when(g == 7)
        def _():
            arrive(whole_of(1 - c, xo), G_CORE + 3)

        rows = pl.ds(piece_row(core, chip), PIECE)
        p_hi, p_lo = split(proj[rows, :].T)
        turned[:, :PIECE] = p_hi
        turned[:, 256 : 256 + PIECE] = p_hi
        turned[:, 512 : 512 + PIECE] = p_lo
        more = pl.ds(piece_row(core, chip), 256)
        for n in range(4):
            cols = slice(256 * n, 256 * n + 256)
            hi = hi_v[more, cols]
            w[:, cols] += nn(turned[...], jnp.concatenate([hi, lo_v[more, cols], hi], axis=0))

    def places(u):
        k, q = y + u * (z - y), z + u * (y - z)

        def first(kk):
            return f_dev(z * 4 + kk + u * (kk * 4 + y - z * 4 - kk))

        def second(qq):
            return f_dev(qq * 4 + y + u * (z * 4 + qq - qq * 4 - y))

        return k, q, first, second

    def cols_ab(u):
        start = pl.multiple_of(WIDE * u, WIDE)
        return pl.ds(start, 256), pl.ds(pl.multiple_of(start + 256, 256), 256)

    def cols_u(u):
        return pl.ds(pl.multiple_of(WIDE * u, WIDE), WIDE)

    def rows32(h, k):
        return pl.ds(pl.multiple_of(128 * h + 32 * k, 32), 32)

    def rows8(h, k, q):
        return pl.ds(pl.multiple_of(128 * h + 32 * k + 8 * q, 8), 8)

    def w_step_1(h, u):
        k, q, first, _ = places(u)
        ca, cb = cols_ab(u)
        i = 2 * h + u
        kr, kl, ko = (k + 1) % 4, (k + 3) % 4, (k + 2) % 4
        send(w.at[rows32(h, ko), ca], w_hop.at[2 * i], W_HOP + 2 * i, first(kr))
        send(w.at[rows32(h, ko), cb], w_hop.at[2 * i + 1], W_HOP + 2 * i + 1, first(kl))
        send(w.at[rows32(h, kr), cb], w_side.at[4 * i + 1], W_NEXT + 4 * i + 1, first(kr))
        send(w.at[rows32(h, kl), ca], w_side.at[4 * i + 2], W_NEXT + 4 * i + 2, first(kl))

    def w_step_2(h, u):
        k, q, first, _ = places(u)
        ca, cb = cols_ab(u)
        i = 2 * h + u
        kr, kl = (k + 1) % 4, (k + 3) % 4
        arrive(w_hop.at[2 * i], W_HOP + 2 * i)
        w[rows32(h, kr), ca] += w_hop[2 * i]
        send(w.at[rows32(h, kr), ca], w_side.at[4 * i], W_NEXT + 4 * i, first(kr))
        arrive(w_hop.at[2 * i + 1], W_HOP + 2 * i + 1)
        w[rows32(h, kl), cb] += w_hop[2 * i + 1]
        send(w.at[rows32(h, kl), cb], w_side.at[4 * i + 3], W_NEXT + 4 * i + 3, first(kl))

    def w_step_3(h, u):
        k, q, _, second = places(u)
        ca, cb = cols_ab(u)
        i = 2 * h + u
        for s in range(4):
            arrive(w_side.at[4 * i + s], W_NEXT + 4 * i + s)
        w[rows32(h, k), ca] += w_side[4 * i] + w_side[4 * i + 2]
        w[rows32(h, k), cb] += w_side[4 * i + 1] + w_side[4 * i + 3]

        @pl.loop(1, 4)
        def _(d):
            to, slot = (q + d) % 4, 3 * i + d - 1
            send(w.at[rows8(h, k, to), cols_u(u)], w_sub.at[slot], W_SUB + slot, second(to))

    def w_step_4(h, u):
        k, q, _, second = places(u)
        i = 2 * h + u

        @pl.loop(0, 3)
        def _(d):
            arrive(w_sub.at[3 * i + d], W_SUB + 3 * i + d)

        w_full[rows8(h, k, q), cols_u(u)] = (w[rows8(h, k, q), cols_u(u)] + w_sub[3 * i]) + (
            w_sub[3 * i + 1] + w_sub[3 * i + 2]
        )

        @pl.loop(1, 4)
        def _(d):
            mine = w_full.at[rows8(h, k, q), cols_u(u)]
            send(mine, mine, W_ALL + 3 * i + d - 1, second((q + d) % 4))

    def w_step_5(h, u):
        k, q, first, _ = places(u)
        ca, cb = cols_ab(u)
        i = 2 * h + u
        dr, dl = first((k + 1) % 4), first((k + 3) % 4)

        @pl.loop(1, 4)
        def _(d):
            arrive(w_full.at[rows8(h, k, (q + 4 - d) % 4), cols_u(u)], W_ALL + 3 * i + d - 1)

        mine_a, mine_b = w_full.at[rows32(h, k), ca], w_full.at[rows32(h, k), cb]
        send(mine_a, mine_a, W_RING + 4 * i, dr)
        send(mine_b, mine_b, W_RING + 4 * i + 3, dl)
        send(mine_b, mine_b, W_RING + 4 * i + 1, dr)
        send(mine_a, mine_a, W_RING + 4 * i + 2, dl)

    def w_step_6(h, u):
        k, q, first, _ = places(u)
        ca, cb = cols_ab(u)
        i = 2 * h + u
        kr, kl = (k + 1) % 4, (k + 3) % 4
        from_left = w_full.at[rows32(h, kl), ca]
        arrive(from_left, W_RING + 4 * i)
        send(from_left, from_left, W_FAR + 2 * i, first(kr))
        from_right = w_full.at[rows32(h, kr), cb]
        arrive(from_right, W_RING + 4 * i + 3)
        send(from_right, from_right, W_FAR + 2 * i + 1, first(kl))

    def w_step_7(h, u):
        k = places(u)[0]
        ca, cb = cols_ab(u)
        i = 2 * h + u
        kr, kl, ko = (k + 1) % 4, (k + 3) % 4, (k + 2) % 4
        arrive(w_full.at[rows32(h, kl), cb], W_RING + 4 * i + 1)
        arrive(w_full.at[rows32(h, kr), ca], W_RING + 4 * i + 2)
        arrive(w_full.at[rows32(h, ko), ca], W_FAR + 2 * i)
        arrive(w_full.at[rows32(h, ko), cb], W_FAR + 2 * i + 1)

    def all_parts(step):
        @pl.loop(0, 4)
        def _(i):
            step(i // 2, i % 2)

    all_parts(w_step_1)
    gram_pair()
    all_parts(w_step_2)
    w_steps_at = (w_step_3, None, w_step_4, None, w_step_5, None, w_step_6, w_step_7)

    arrive(gram_half(1 - c), GRAM_CORE)
    elim[:, :RANK] = gram[...]
    rr = lax.broadcasted_iota(jnp.int32, (RANK, RANK), 0)
    cc = lax.broadcasted_iota(jnp.int32, (RANK, RANK), 1)
    elim[:, RANK:] = jnp.where(rr == cc, 1.0, 0.0).astype(F32)

    for half in range(2):

        @pl.loop(4 * half, 4 * half + 4)
        def _(k):
            eliminate(k, half, elim)
            for at in range(4 * half, 4 * half + 4):
                if w_steps_at[at] is not None:

                    @pl.when(k == at)
                    def _():
                        all_parts(w_steps_at[at])

    f_hi, f_lo = split(elim[:, RANK:])
    factor = jnp.concatenate([f_hi, f_hi, f_lo], axis=1)
    squares = jnp.zeros((RANK, 128), F32)
    for n in range(4):
        cols = slice(256 * n, 256 * n + 256)
        w_hi, w_lo = split(w_full[:, cols])
        back = nn(factor, jnp.concatenate([w_hi, w_lo, w_hi], axis=0))
        back_out[:, cols] = back
        squares = squares + (back[:, :128] * back[:, :128] + back[:, 128:] * back[:, 128:])
    sq_v[t] = nt(jnp.ones((8, 128), F32), squares, HIGH)

    @pl.loop(1, 8)
    def _(d):
        send(sq_v.at[t], sq_v.at[t], SQ + d - 1, {"fsdp": f, "tp": (t + d) % 8})


    t_hi, t_lo = split(elim[:, RANK:].T)
    turned[:, :256] = t_hi
    turned[:, 256:512] = t_lo

    @pl.loop(0, 8)
    def _(i):
        rows = pl.ds(pl.multiple_of(i * PIECE, 32), PIECE)
        hi, lo = split(proj[rows, :])
        first = turned[:, :256]
        ortho_out[rows, :] = nn(
            jnp.concatenate([hi, hi, lo], axis=1),
            jnp.concatenate([first, turned[:, 256:512], first], axis=0),
        )

    all_sent(N_HOP_A, 12, side_v.at[0])
    all_sent(N_CORE, 8, part_v.at[0])
    all_sent(GRAM_SUM, 33, sq_v.at[0])
    all_sent(GRAM_CORE, 1, gram_part)
    all_sent(W_HOP, 48, w_hop.at[0])
    all_sent(W_SUB, 24, w_sub.at[0])

    @pl.loop(1, 8)
    def _(d):
        arrive(sq_v.at[(t + 8 - d) % 8], SQ + d - 1)

    norm_out[...] = lax.rsqrt(jnp.sum(sq_v[...], axis=0) + 1e-06)
    all_sent(SQ, 7, sq_v.at[0])


def write_kernel(
    blend, ortho, back, norm, mom_out, basis_out, update_out, backs, mom_v, basis_v, update_v, sems
):
    hi, lo = split(back[...])
    backs[:RANK] = hi
    backs[RANK : 2 * RANK] = lo
    backs[2 * RANK :] = hi
    scale = (ROWS * COLS / RANK) ** 0.5
    norms = norm[0:1, :]

    def copies(i):
        slot = i % 2
        found = []
        for p in range(2):
            rows = pl.ds(pl.multiple_of(i * STEP + p * PIECE, 32), PIECE)
            here = pl.ds(p * PIECE, PIECE)
            found.append(pltpu.make_async_copy(mom_v.at[slot, here], mom_out.at[rows], sems.at[slot, p]))
            found.append(
                pltpu.make_async_copy(update_v.at[slot, here], update_out.at[rows], sems.at[slot, 2 + p])
            )
        rank_rows = pl.ds(pl.multiple_of(i * 256, 256), 256)
        found.append(pltpu.make_async_copy(basis_v.at[slot], basis_out.at[rank_rows], sems.at[slot, 4]))
        return found

    @pl.loop(0, LOCAL_ROWS // STEP)
    def _(i):
        slot = i % 2

        @pl.when(i >= 2)
        def _():
            for copy in copies(i - 2):
                copy.wait()

        rows = pl.ds(pl.multiple_of(i * STEP, 64), STEP)
        cols = pl.ds(pl.multiple_of(i * 256, 256), 256)
        basis_v[slot] = back[:, cols].T * norms
        plain = ortho[rows, :]
        mom_v[slot] = blend[rows, :] - nn((0.05 * plain).astype(BF16), backs[:RANK])
        mom_a, update_a, mom_b, update_b, basis_copy = copies(i)
        mom_a.start()
        mom_b.start(priority=1)
        basis_copy.start()
        hi, lo = split(plain * (scale * norms))
        update_v[slot] = nn(jnp.concatenate([hi, hi, lo], axis=1), backs[...]).astype(BF16)
        update_a.start()
        update_b.start(priority=1)

    for i in (2, 3):
        for copy in copies(i):
            copy.wait()


def body(gradient, momentum, basis):
    anywhere = pl.BlockSpec(memory_space=pl.ANY)
    inside = pl.BlockSpec(memory_space=pltpu.VMEM)
    vmem = pltpu.VMEM
    fixed = [pltpu.with_memory_space_constraint(a, pltpu.HBM) for a in (gradient, momentum, basis)]
    results = pl.pallas_call(
        main_kernel,
        out_shape=(
            vmem((LOCAL_ROWS, LOCAL_COLS), F32),
            vmem((LOCAL_ROWS, RANK), F32),
            vmem((RANK, LOCAL_COLS), F32),
            vmem((8, RANK), F32),
        ),
        in_specs=[anywhere] * 3,
        out_specs=(inside,) * 4,
        scratch_shapes=[
            vmem((4, PIECE, LOCAL_COLS), BF16),
            vmem((LOCAL_COLS, RANK), F32),
            vmem((3 * LOCAL_COLS, RANK), BF16),
            vmem((LOCAL_ROWS + 32, LOCAL_COLS), BF16),
            vmem((LOCAL_ROWS + 32, LOCAL_COLS), BF16),
            vmem((8, PIECE, RANK), F32),
            vmem((4, PIECE, RANK), F32),
            vmem((2, PART, RANK), F32),
            vmem((4, PART, RANK), F32),
            vmem((LOCAL_ROWS, RANK), F32),
            vmem((128, RANK), F32),
            vmem((16, 8, RANK), F32),
            vmem((4, 8, RANK), F32),
            vmem((RANK, RANK), F32),
            vmem((RANK, 2 * RANK), F32),
            vmem((RANK, 3 * 256), BF16),
            vmem((RANK, LOCAL_COLS), F32),
            vmem((8, 32, 256), F32),
            vmem((16, 32, 256), F32),
            vmem((12, 8, WIDE), F32),
            vmem((RANK, LOCAL_COLS), F32),
            vmem((8, 8, RANK), F32),
            pltpu.SemaphoreType.DMA((17,)),
            pltpu.SemaphoreType.DMA((NAMES.count,)),
            pltpu.SemaphoreType.DMA((NAMES.count,)),
        ],
        compiler_params=pltpu.CompilerParams(
            collective_id=0, has_side_effects=True, vmem_limit_bytes=44 * 2**20
        ),
        name="transfers",
    )(*fixed)
    results = [pltpu.with_memory_space_constraint(a, pltpu.VMEM) for a in results]

    return pl.pallas_call(
        write_kernel,
        out_shape=(
            jax.ShapeDtypeStruct((LOCAL_ROWS, LOCAL_COLS), F32),
            jax.ShapeDtypeStruct((LOCAL_COLS, RANK), F32),
            jax.ShapeDtypeStruct((LOCAL_ROWS, LOCAL_COLS), BF16),
        ),
        in_specs=[inside] * 4,
        out_specs=(anywhere,) * 3,
        scratch_shapes=[
            vmem((3 * RANK, LOCAL_COLS), BF16),
            vmem((2, STEP, LOCAL_COLS), F32),
            vmem((2, 256, RANK), F32),
            vmem((2, STEP, LOCAL_COLS), BF16),
            pltpu.SemaphoreType.DMA((2, 5)),
        ],
        compiler_params=pltpu.CompilerParams(vmem_limit_bytes=32 * 2**20),
        name="outputs",
    )(*results)


def solution(mesh):
    placed = (P("fsdp", "tp"), P("fsdp", "tp"), P("tp", None))
    return jax.shard_map(
        body,
        mesh=mesh,
        in_specs=placed,
        out_specs=(P("fsdp", "tp"), P("tp", None), P("fsdp", "tp")),
        check_vma=False,
    )
```

```python
import functools

import jax
import jax.numpy as jnp
from jax import lax
from jax.experimental import pallas as pl
from jax.experimental.pallas import tpu as pltpu
from jax.sharding import PartitionSpec as P

ROWS = 28672
COLS = 8192
RANK = 256

F32 = jnp.float32
BF16 = jnp.bfloat16
HIGH = lax.Precision.HIGHEST
MESH = pl.DeviceIdType.MESH

LOCAL_ROWS = 1792
LOCAL_COLS = 1024
HALF = 896
PIECE = 224
PART = 112
STEP = 448
WIDE = 512


class Names:
    def __init__(self):
        self.count = 0

    def take(self, many=1):
        first = self.count
        self.count += many
        return first


NAMES = Names()
N_HOP_A, N_HOP_B = NAMES.take(), NAMES.take()
N_LEFT_A, N_LEFT_B = NAMES.take(), NAMES.take()
N_RIGHT_A, N_RIGHT_B = NAMES.take(), NAMES.take()
G_LEFT_A, G_LEFT_B = NAMES.take(), NAMES.take()
G_RIGHT_A, G_RIGHT_B = NAMES.take(), NAMES.take()
G_OPP_A, G_OPP_B = NAMES.take(), NAMES.take()
N_CORE = NAMES.take(4)
G_CORE = NAMES.take(4)
GRAM_SUM = NAMES.take(15)
GRAM_X = NAMES.take(3)
GRAM_ALL = NAMES.take(15)
SQ = NAMES.take(7)
GRAM_CORE = NAMES.take()
W_HOP = NAMES.take(4)
W_NEXT = NAMES.take(8)
W_RING = NAMES.take(8)
W_FAR = NAMES.take(4)
W_SUB = NAMES.take(6)
W_ALL = NAMES.take(6)


def nn(a, b, precision=None):
    return lax.dot_general(
        a, b, (((1,), (0,)), ((), ())), precision=precision, preferred_element_type=F32
    )


def tn(a, b, precision=None):
    return lax.dot_general(
        a, b, (((0,), (0,)), ((), ())), precision=precision, preferred_element_type=F32
    )


def nt(a, b, precision=None):
    return lax.dot_general(
        a, b, (((1,), (1,)), ((), ())), precision=precision, preferred_element_type=F32
    )


def pick(index, values):
    out = values[0]
    for at in range(1, len(values)):
        out = out + (values[at] - values[at - 1]) * ((index + len(values) - at) // len(values))
    return out


def split(x):
    hi = x.astype(BF16)
    return hi, (x - hi.astype(F32)).astype(BF16)


def row_copy(x, j):
    return jnp.broadcast_to(x[j : j + 1, :], (8, 128))


def inverse_factor(x):
    n = len(x)
    sub = lax.broadcasted_iota(jnp.int32, (8, 128), 0)
    lane = lax.broadcasted_iota(jnp.int32, (8, 128), 1)
    col = [
        [None if i < k // 8 else jnp.broadcast_to(x[i][:, k : k + 1], (8, 128)) for i in range(n)]
        for k in range(8 * n)
    ]
    inverse = [jnp.where(lane == sub + 8 * i, 1.0, 0.0) for i in range(n)]
    for g in range(n):
        entry = [[row_copy(col[8 * g + j][g], i) for j in range(i + 1)] for i in range(8)]
        rows = [row_copy(inverse[g], j) for j in range(8)]
        inv, mult = [], [[None] * 8 for _ in range(8)]
        for j in range(8):
            inv.append(1.0 / entry[j][j])
            for k in range(j + 1, 8):
                mult[k][j] = entry[k][j] * inv[j]
                for i in range(k, 8):
                    entry[i][k] = entry[i][k] - entry[i][j] * mult[k][j]
                rows[k] = rows[k] - mult[k][j] * rows[j]
        final = jnp.zeros((8, 128), F32)
        for j in range(8):
            final = jnp.where(sub == j, rows[j] * lax.rsqrt(entry[j][j]), final)
        inverse[g] = final
        below = {}
        for i in range(g + 1, n):
            c = [col[8 * g + j][i] for j in range(8)]
            for j in range(8):
                for k in range(j + 1, 8):
                    c[k] = c[k] - c[j] * mult[k][j]
            below[i] = (c, [c[j] * inv[j] for j in range(8)])
        for k in range(8 * g + 8, 8 * n):
            across = [row_copy(below[k // 8][0][j], k % 8) for j in range(8)]
            for i in range(k // 8, n):
                for j in range(8):
                    col[k][i] = col[k][i] - below[i][1][j] * across[j]
        for i in range(g + 1, n):
            for j in range(8):
                inverse[i] = inverse[i] - below[i][1][j] * rows[j]
    return jnp.concatenate(inverse, axis=0)


def split3(x):
    first = x.astype(BF16)
    rest = x - first.astype(F32)
    second = rest.astype(BF16)
    return first, second, (rest - second.astype(F32)).astype(BF16)


def eliminate(k, half, m_ref):
    left = 128 * half
    cols = slice(left, left + 384)
    rows = pl.ds(pl.multiple_of(32 * k, 32), 32)
    d = pltpu.roll(m_ref[rows, left : left + 128], (128 - 32 * (k % 4)) % 128, 1)
    inverse = inverse_factor([d[8 * i : 8 * i + 8] for i in range(4)])
    scaled = nn(inverse[:, :32], m_ref[rows, cols], HIGH)
    m_ref[rows, cols] = scaled

    @pl.when(k < 7)
    def _():
        lane = lax.broadcasted_iota(jnp.int32, (32, RANK - left), 1)
        lower = jnp.where(lane >= 32 * k + 32 - left, scaled[:, : RANK - left], 0.0)
        a, b, c = split3(lower)
        d, e, f = split3(scaled)
        m_ref[left:, cols] -= tn(
            jnp.concatenate([a, a, b, a, b, c], axis=0), jnp.concatenate([d, e, d, f, e, d], axis=0)
        )


def main_kernel(
    grad,
    mom,
    basis,
    blend_out,
    ortho_out,
    back_out,
    norm_out,
    grad_v,
    basis_v,
    bases,
    hi_v,
    lo_v,
    part_v,
    from_core,
    hop_v,
    side_v,
    proj,
    gram_part,
    gram_in,
    gram_x,
    gram,
    elim,
    turned,
    w,
    w_hop,
    w_side,
    w_sub,
    w_full,
    sq_v,
    load_sem,
    send_sem,
    recv_sem,
):
    f = lax.axis_index("fsdp")
    t = lax.axis_index("tp")
    x, c = t // 2, t % 2
    z, y = f // 4, f % 4

    def tp_dev(xx, cc):
        return {"fsdp": f, "tp": xx * 2 + cc}

    def f_dev(ff):
        return {"fsdp": ff, "tp": t}

    right = tp_dev((x + 1) % 4, c)
    left = tp_dev((x + 3) % 4, c)
    twin = tp_dev(x, 1 - c)

    def remote(src, dst, number, device):
        return pltpu.make_async_remote_copy(
            src_ref=src,
            dst_ref=dst,
            send_sem=send_sem.at[number],
            recv_sem=recv_sem.at[number],
            device_id=device,
            device_id_type=MESH,
        )

    def send(src, dst, number, device):
        remote(src, dst, number, device).start()

    def arrive(dst, number):
        remote(dst, dst, number, twin).wait_recv()

    def all_sent(first, many, ref):
        @pl.loop(first, first + many)
        def _(number):
            remote(ref, ref, number, twin).wait_send()

    def piece_row(core, chip):
        return pl.multiple_of(core * HALF + chip * PIECE, 32)

    def chunk_row(i):
        g = 3 - i // 2
        d = g + (g // 2) * (1 - 2 * (g % 2))
        core = (1 - c) * (1 - i % 2) + c * (i % 2)
        return piece_row(core, (x + d) % 4)

    def load(i):
        rows = pl.ds(chunk_row(i), PIECE)
        return (
            pltpu.make_async_copy(mom.at[rows], blend_out.at[rows], load_sem.at[2 * i]),
            pltpu.make_async_copy(grad.at[rows], grad_v.at[i % 4], load_sem.at[2 * i + 1]),
        )

    basis_copy = pltpu.make_async_copy(basis, basis_v, load_sem.at[16])
    basis_copy.start()

    @pl.loop(0, 3)
    def _(i):
        for copy in load(i):
            copy.start()

    barrier = pltpu.get_barrier_semaphore()

    @pl.loop(1, 16)
    def _(d):
        pl.semaphore_signal(barrier, inc=1, device_id=f_dev((f + d) % 16), device_id_type=MESH)

    @pl.loop(1, 8)
    def _(d):
        pl.semaphore_signal(
            barrier, inc=1, device_id={"fsdp": f, "tp": (t + d) % 8}, device_id_type=MESH
        )

    basis_copy.wait()
    basis_hi, basis_lo = split(basis_v[...])
    bases[:LOCAL_COLS] = basis_hi
    bases[LOCAL_COLS : 2 * LOCAL_COLS] = basis_lo
    bases[2 * LOCAL_COLS :] = basis_hi
    turned[...] = jnp.zeros_like(turned)
    hi_v[LOCAL_ROWS:, :] = jnp.zeros((32, LOCAL_COLS), BF16)
    lo_v[LOCAL_ROWS:, :] = jnp.zeros((32, LOCAL_COLS), BF16)

    def partial(i):
        for copy in load(i):
            copy.wait()
        rows = pl.ds(chunk_row(i), PIECE)

        @pl.when(i < 5)
        def _():
            for copy in load(i + 3):
                copy.start()

        blend = blend_out[rows, :] + grad_v[i % 4].astype(F32)
        blend_out[rows, :] = blend
        hi, lo = split(blend)
        hi_v[rows, :] = hi
        lo_v[rows, :] = lo
        return nn(jnp.concatenate([hi, hi, lo], axis=1), bases[...])

    a_rows, b_rows = pl.ds(0, PART), pl.ds(PART, PART)

    def add_core(j):
        arrive(from_core.at[j], N_CORE + j)
        part_v[2 * j + 1] += from_core[j]

    @pl.loop(0, 8)
    def _(i):
        part_v[i] = partial(i)
        j = i // 2
        core = remote(part_v.at[i], from_core.at[j], N_CORE + j, twin)

        @pl.when(i == 0)
        def _():
            pl.semaphore_wait(barrier, 22)

        @pl.when(i % 2 == 0)
        def _():
            core.start()

        @pl.when(i == 2)
        def _():
            add_core(0)
            send(part_v.at[1, a_rows], hop_v.at[0], N_HOP_A, right)
            send(part_v.at[1, b_rows], hop_v.at[1], N_HOP_B, left)

        @pl.when(i == 4)
        def _():
            add_core(1)
            send(part_v.at[3, a_rows], side_v.at[2], N_RIGHT_A, left)

        @pl.when(i == 6)
        def _():
            add_core(2)
            send(part_v.at[5, b_rows], side_v.at[1], N_LEFT_B, right)
            arrive(hop_v.at[0], N_HOP_A)
            part_v[5, a_rows] += hop_v[0]
            send(part_v.at[5, a_rows], side_v.at[0], N_LEFT_A, right)
            arrive(hop_v.at[1], N_HOP_B)
            part_v[3, b_rows] += hop_v[1]
            send(part_v.at[3, b_rows], side_v.at[3], N_RIGHT_B, left)

    add_core(3)
    my_row = piece_row(c, x)
    arrive(side_v.at[2], N_RIGHT_A)
    arrive(side_v.at[0], N_LEFT_A)
    proj[pl.ds(my_row, PART), :] = part_v[7, a_rows] + (side_v[0] + side_v[2])
    arrive(side_v.at[1], N_LEFT_B)
    arrive(side_v.at[3], N_RIGHT_B)
    proj[pl.ds(my_row + PART, PART), :] = part_v[7, b_rows] + (side_v[1] + side_v[3])

    def part_of(core, chip, b):
        return proj.at[pl.ds(pl.multiple_of(piece_row(core, chip) + b * PART, 16), PART)]

    def whole_of(core, chip):
        return proj.at[pl.ds(piece_row(core, chip), PIECE)]

    def send_part(chip, b, number, device):
        send(part_of(c, chip, b), part_of(c, chip, b), number, device)

    def send_whole(chip, number):
        send(whole_of(c, chip), whole_of(c, chip), number, twin)

    xl, xr, xo = (x + 3) % 4, (x + 1) % 4, (x + 2) % 4
    send_part(x, 0, G_LEFT_A, right)
    send_part(x, 1, G_RIGHT_B, left)
    send_whole(x, G_CORE)
    send_part(x, 1, G_LEFT_B, right)
    send_part(x, 0, G_RIGHT_A, left)

    half_cols = pl.ds(pl.multiple_of(c * 128, 128), 128)

    def eight(row):
        return pl.ds(pl.multiple_of(row * 8, 8), 8)

    def gram_start():
        left, right = [], []
        for core in range(2):
            rows = pl.ds(piece_row(core, x), PIECE)
            a, b, d = split3(proj[rows, half_cols])
            left += [a, a, b, a, b, d]
            a, b, d = split3(proj[rows, :])
            right += [a, b, a, d, b, a]
        gram_part[...] = tn(jnp.concatenate(left, axis=0), jnp.concatenate(right, axis=0))

        @pl.loop(1, 16)
        def _(d):
            to = (f + d) % 16
            send(gram_part.at[eight(to)], gram_in.at[d], GRAM_SUM + d - 1, f_dev(to))

    def gram_across():
        gram_in[0] = gram_part[eight(f), :]

        @pl.loop(1, 16)
        def _(d):
            arrive(gram_in.at[d], GRAM_SUM + d - 1)

        gram_x[x] = jnp.sum(gram_in[...], axis=0)

        @pl.loop(1, 4)
        def _(d):
            send(gram_x.at[x], gram_x.at[x], GRAM_X + d - 1, tp_dev((x + d) % 4, c))

    def gram_row(ff):
        return pl.ds(pl.multiple_of(c * 128 + ff * 8, 8), 8)

    def gram_round():
        @pl.loop(1, 4)
        def _(d):
            arrive(gram_x.at[(x + 4 - d) % 4], GRAM_X + d - 1)

        gram[gram_row(f), :] = (gram_x[0] + gram_x[1]) + (gram_x[2] + gram_x[3])

        @pl.loop(1, 16)
        def _(d):
            mine = gram.at[gram_row(f)]
            send(mine, mine, GRAM_ALL + d - 1, f_dev((f + d) % 16))

    def gram_half(core):
        return gram.at[pl.ds(pl.multiple_of(core * 128, 128), 128)]

    def gram_pair():
        @pl.loop(1, 16)
        def _(d):
            arrive(gram.at[gram_row((f + 16 - d) % 16)], GRAM_ALL + d - 1)

        send(gram_half(c), gram_half(c), GRAM_CORE, twin)

    w[...] = jnp.zeros_like(w)

    @pl.loop(0, 8)
    def _(g):
        core = (c + pick(g, (0, 1, 0, 0, 0, 1, 1, 1))) % 2
        chip = (x + pick(g, (0, 0, 1, 3, 2, 1, 3, 2))) % 4

        @pl.when(g == 1)
        def _():
            arrive(whole_of(1 - c, x), G_CORE)
            gram_start()

        @pl.when(g == 2)
        def _():
            arrive(part_of(c, xl, 0), G_LEFT_A)
            send_part(xl, 0, G_OPP_A, right)
            arrive(part_of(c, xr, 1), G_RIGHT_B)
            send_part(xr, 1, G_OPP_B, left)
            arrive(part_of(c, xr, 0), G_RIGHT_A)
            send_whole(xr, G_CORE + 1)
            arrive(part_of(c, xl, 1), G_LEFT_B)
            send_whole(xl, G_CORE + 2)

        @pl.when(g == 3)
        def _():
            gram_across()

        @pl.when(g == 4)
        def _():
            arrive(part_of(c, xo, 0), G_OPP_A)
            arrive(part_of(c, xo, 1), G_OPP_B)
            send_whole(xo, G_CORE + 3)

        @pl.when(g == 5)
        def _():
            gram_round()
            arrive(whole_of(1 - c, xr), G_CORE + 1)

        @pl.when(g == 6)
        def _():
            arrive(whole_of(1 - c, xl), G_CORE + 2)

        @pl.when(g == 7)
        def _():
            gram_pair()
            arrive(whole_of(1 - c, xo), G_CORE + 3)

        rows = pl.ds(piece_row(core, chip), PIECE)
        p_hi, p_lo = split(proj[rows, :].T)
        turned[:, :PIECE] = p_hi
        turned[:, 256 : 256 + PIECE] = p_hi
        turned[:, 512 : 512 + PIECE] = p_lo
        more = pl.ds(piece_row(core, chip), 256)
        for n in range(4):
            cols = slice(256 * n, 256 * n + 256)
            hi = hi_v[more, cols]
            w[:, cols] += nn(turned[...], jnp.concatenate([hi, lo_v[more, cols], hi], axis=0))

    def places(h):
        k, q = y + h * (z - y), z + h * (y - z)

        def first(kk):
            return f_dev(z * 4 + kk + h * (kk * 4 + y - z * 4 - kk))

        def second(qq):
            return f_dev(qq * 4 + y + h * (z * 4 + qq - qq * 4 - y))

        return k, q, first, second

    ca, cb = pl.ds(0, WIDE), pl.ds(WIDE, WIDE)

    def rows32(h, k):
        return pl.ds(pl.multiple_of(128 * h + 32 * k, 32), 32)

    def rows8(h, k, q):
        return pl.ds(pl.multiple_of(128 * h + 32 * k + 8 * q, 8), 8)

    def w_step_1(h):
        k, q, first, _ = places(h)
        kr, kl, ko = (k + 1) % 4, (k + 3) % 4, (k + 2) % 4
        send(w.at[rows32(h, ko), ca], w_hop.at[2 * h], W_HOP + 2 * h, first(kr))
        send(w.at[rows32(h, ko), cb], w_hop.at[2 * h + 1], W_HOP + 2 * h + 1, first(kl))

    def w_step_1b(h):
        k, q, first, _ = places(h)
        kr, kl = (k + 1) % 4, (k + 3) % 4
        send(w.at[rows32(h, kr), cb], w_side.at[4 * h + 1], W_NEXT + 4 * h + 1, first(kr))
        send(w.at[rows32(h, kl), ca], w_side.at[4 * h + 2], W_NEXT + 4 * h + 2, first(kl))

    def w_step_2(h):
        k, q, first, _ = places(h)
        kr, kl = (k + 1) % 4, (k + 3) % 4
        arrive(w_hop.at[2 * h], W_HOP + 2 * h)
        w[rows32(h, kr), ca] += w_hop[2 * h]
        send(w.at[rows32(h, kr), ca], w_side.at[4 * h], W_NEXT + 4 * h, first(kr))
        arrive(w_hop.at[2 * h + 1], W_HOP + 2 * h + 1)
        w[rows32(h, kl), cb] += w_hop[2 * h + 1]
        send(w.at[rows32(h, kl), cb], w_side.at[4 * h + 3], W_NEXT + 4 * h + 3, first(kl))

    def w_step_3(h):
        k, q, _, second = places(h)
        for s in range(4):
            arrive(w_side.at[4 * h + s], W_NEXT + 4 * h + s)
        w[rows32(h, k), ca] += w_side[4 * h] + w_side[4 * h + 2]
        w[rows32(h, k), cb] += w_side[4 * h + 1] + w_side[4 * h + 3]

        @pl.loop(1, 4)
        def _(d):
            to, slot = (q + d) % 4, 3 * h + d - 1
            send(w.at[rows8(h, k, to)], w_sub.at[slot], W_SUB + slot, second(to))

    def w_step_4(h):
        k, q, _, second = places(h)

        @pl.loop(0, 3)
        def _(d):
            arrive(w_sub.at[3 * h + d], W_SUB + 3 * h + d)

        w_full[rows8(h, k, q), :] = (w[rows8(h, k, q), :] + w_sub[3 * h]) + (
            w_sub[3 * h + 1] + w_sub[3 * h + 2]
        )

        @pl.loop(1, 4)
        def _(d):
            mine = w_full.at[rows8(h, k, q)]
            send(mine, mine, W_ALL + 3 * h + d - 1, second((q + d) % 4))

    def w_step_5(h):
        k, q, first, _ = places(h)
        dr, dl = first((k + 1) % 4), first((k + 3) % 4)

        @pl.loop(1, 4)
        def _(d):
            arrive(w_full.at[rows8(h, k, (q + 4 - d) % 4)], W_ALL + 3 * h + d - 1)

        mine_a, mine_b = w_full.at[rows32(h, k), ca], w_full.at[rows32(h, k), cb]
        send(mine_a, mine_a, W_RING + 4 * h, dr)
        send(mine_b, mine_b, W_RING + 4 * h + 3, dl)
        send(mine_b, mine_b, W_RING + 4 * h + 1, dr)
        send(mine_a, mine_a, W_RING + 4 * h + 2, dl)

    def w_step_6(h):
        k, q, first, _ = places(h)
        kr, kl = (k + 1) % 4, (k + 3) % 4
        from_left = w_full.at[rows32(h, kl), ca]
        arrive(from_left, W_RING + 4 * h)
        send(from_left, from_left, W_FAR + 2 * h, first(kr))
        from_right = w_full.at[rows32(h, kr), cb]
        arrive(from_right, W_RING + 4 * h + 3)
        send(from_right, from_right, W_FAR + 2 * h + 1, first(kl))

    def w_step_7(h):
        k = places(h)[0]
        kr, kl, ko = (k + 1) % 4, (k + 3) % 4, (k + 2) % 4
        arrive(w_full.at[rows32(h, kl), cb], W_RING + 4 * h + 1)
        arrive(w_full.at[rows32(h, kr), ca], W_RING + 4 * h + 2)
        arrive(w_full.at[rows32(h, ko), ca], W_FAR + 2 * h)
        arrive(w_full.at[rows32(h, ko), cb], W_FAR + 2 * h + 1)

    def both_halves(step):
        for h in range(2):
            step(h)

    both_halves(w_step_1)
    both_halves(w_step_1b)
    both_halves(w_step_2)
    w_steps_at = (w_step_3, None, w_step_4, None, w_step_5, None, w_step_6, w_step_7)

    arrive(gram_half(1 - c), GRAM_CORE)
    elim[:, :RANK] = gram[...]
    rr = lax.broadcasted_iota(jnp.int32, (RANK, RANK), 0)
    cc = lax.broadcasted_iota(jnp.int32, (RANK, RANK), 1)
    elim[:, RANK:] = jnp.where(rr == cc, 1.0, 0.0).astype(F32)

    for half in range(2):

        @pl.loop(4 * half, 4 * half + 4)
        def _(k):
            eliminate(k, half, elim)
            for at in range(4 * half, 4 * half + 4):
                if w_steps_at[at] is not None:

                    @pl.when(k == at)
                    def _():
                        both_halves(w_steps_at[at])

    f_hi, f_lo = split(elim[:, RANK:])
    factor = jnp.concatenate([f_hi, f_hi, f_lo], axis=1)
    squares = jnp.zeros((RANK, 128), F32)
    for n in range(4):
        cols = slice(256 * n, 256 * n + 256)
        w_hi, w_lo = split(w_full[:, cols])
        back = nn(factor, jnp.concatenate([w_hi, w_lo, w_hi], axis=0))
        back_out[:, cols] = back
        squares = squares + (back[:, :128] * back[:, :128] + back[:, 128:] * back[:, 128:])
    sq_v[t] = nt(jnp.ones((8, 128), F32), squares, HIGH)

    @pl.loop(1, 8)
    def _(d):
        send(sq_v.at[t], sq_v.at[t], SQ + d - 1, {"fsdp": f, "tp": (t + d) % 8})


    t_hi, t_lo = split(elim[:, RANK:].T)
    turned[:, :256] = t_hi
    turned[:, 256:512] = t_lo

    @pl.loop(0, 8)
    def _(i):
        rows = pl.ds(pl.multiple_of(i * PIECE, 32), PIECE)
        hi, lo = split(proj[rows, :])
        first = turned[:, :256]
        ortho_out[rows, :] = nn(
            jnp.concatenate([hi, hi, lo], axis=1),
            jnp.concatenate([first, turned[:, 256:512], first], axis=0),
        )

    all_sent(N_HOP_A, 12, side_v.at[0])
    all_sent(N_CORE, 8, part_v.at[0])
    all_sent(GRAM_SUM, 33, sq_v.at[0])
    all_sent(GRAM_CORE, 1, gram_part)
    all_sent(W_HOP, 24, w_hop.at[0])
    all_sent(W_SUB, 12, w_sub.at[0])

    @pl.loop(1, 8)
    def _(d):
        arrive(sq_v.at[(t + 8 - d) % 8], SQ + d - 1)

    norm_out[...] = lax.rsqrt(jnp.sum(sq_v[...], axis=0) + 1e-06)
    all_sent(SQ, 7, sq_v.at[0])


def write_kernel(
    blend, ortho, back, norm, mom_out, basis_out, update_out, backs, mom_v, basis_v, update_v, sems
):
    hi, lo = split(back[...])
    backs[:RANK] = hi
    backs[RANK : 2 * RANK] = lo
    backs[2 * RANK :] = hi
    scale = (ROWS * COLS / RANK) ** 0.5
    norms = norm[0:1, :]

    def copies(i):
        slot = i % 2
        found = []
        for p in range(2):
            rows = pl.ds(pl.multiple_of(i * STEP + p * PIECE, 32), PIECE)
            here = pl.ds(p * PIECE, PIECE)
            found.append(pltpu.make_async_copy(mom_v.at[slot, here], mom_out.at[rows], sems.at[slot, p]))
            found.append(
                pltpu.make_async_copy(update_v.at[slot, here], update_out.at[rows], sems.at[slot, 2 + p])
            )
        rank_rows = pl.ds(pl.multiple_of(i * 256, 256), 256)
        found.append(pltpu.make_async_copy(basis_v.at[slot], basis_out.at[rank_rows], sems.at[slot, 4]))
        return found

    @pl.loop(0, LOCAL_ROWS // STEP)
    def _(i):
        slot = i % 2

        @pl.when(i >= 2)
        def _():
            for copy in copies(i - 2):
                copy.wait()

        rows = pl.ds(pl.multiple_of(i * STEP, 64), STEP)
        cols = pl.ds(pl.multiple_of(i * 256, 256), 256)
        basis_v[slot] = back[:, cols].T * norms
        plain = ortho[rows, :]
        mom_v[slot] = blend[rows, :] - nn((0.05 * plain).astype(BF16), backs[:RANK])
        mom_a, update_a, mom_b, update_b, basis_copy = copies(i)
        mom_a.start()
        mom_b.start(priority=1)
        basis_copy.start()
        hi, lo = split(plain * (scale * norms))
        update_v[slot] = nn(jnp.concatenate([hi, hi, lo], axis=1), backs[...]).astype(BF16)
        update_a.start()
        update_b.start(priority=1)

    for i in (2, 3):
        for copy in copies(i):
            copy.wait()


def body(gradient, momentum, basis):
    anywhere = pl.BlockSpec(memory_space=pl.ANY)
    inside = pl.BlockSpec(memory_space=pltpu.VMEM)
    vmem = pltpu.VMEM
    fixed = [pltpu.with_memory_space_constraint(a, pltpu.HBM) for a in (gradient, momentum, basis)]
    results = pl.pallas_call(
        main_kernel,
        out_shape=(
            vmem((LOCAL_ROWS, LOCAL_COLS), F32),
            vmem((LOCAL_ROWS, RANK), F32),
            vmem((RANK, LOCAL_COLS), F32),
            vmem((8, RANK), F32),
        ),
        in_specs=[anywhere] * 3,
        out_specs=(inside,) * 4,
        scratch_shapes=[
            vmem((4, PIECE, LOCAL_COLS), BF16),
            vmem((LOCAL_COLS, RANK), F32),
            vmem((3 * LOCAL_COLS, RANK), BF16),
            vmem((LOCAL_ROWS + 32, LOCAL_COLS), BF16),
            vmem((LOCAL_ROWS + 32, LOCAL_COLS), BF16),
            vmem((8, PIECE, RANK), F32),
            vmem((4, PIECE, RANK), F32),
            vmem((2, PART, RANK), F32),
            vmem((4, PART, RANK), F32),
            vmem((LOCAL_ROWS, RANK), F32),
            vmem((128, RANK), F32),
            vmem((16, 8, RANK), F32),
            vmem((4, 8, RANK), F32),
            vmem((RANK, RANK), F32),
            vmem((RANK, 2 * RANK), F32),
            vmem((RANK, 3 * 256), BF16),
            vmem((RANK, LOCAL_COLS), F32),
            vmem((4, 32, WIDE), F32),
            vmem((8, 32, WIDE), F32),
            vmem((6, 8, LOCAL_COLS), F32),
            vmem((RANK, LOCAL_COLS), F32),
            vmem((8, 8, RANK), F32),
            pltpu.SemaphoreType.DMA((17,)),
            pltpu.SemaphoreType.DMA((NAMES.count,)),
            pltpu.SemaphoreType.DMA((NAMES.count,)),
        ],
        compiler_params=pltpu.CompilerParams(
            collective_id=0, has_side_effects=True, vmem_limit_bytes=44 * 2**20
        ),
        name="transfers",
    )(*fixed)
    results = [pltpu.with_memory_space_constraint(a, pltpu.VMEM) for a in results]

    return pl.pallas_call(
        write_kernel,
        out_shape=(
            jax.ShapeDtypeStruct((LOCAL_ROWS, LOCAL_COLS), F32),
            jax.ShapeDtypeStruct((LOCAL_COLS, RANK), F32),
            jax.ShapeDtypeStruct((LOCAL_ROWS, LOCAL_COLS), BF16),
        ),
        in_specs=[inside] * 4,
        out_specs=(anywhere,) * 3,
        scratch_shapes=[
            vmem((3 * RANK, LOCAL_COLS), BF16),
            vmem((2, STEP, LOCAL_COLS), F32),
            vmem((2, 256, RANK), F32),
            vmem((2, STEP, LOCAL_COLS), BF16),
            pltpu.SemaphoreType.DMA((2, 5)),
        ],
        compiler_params=pltpu.CompilerParams(vmem_limit_bytes=32 * 2**20),
        name="outputs",
    )(*results)


def solution(mesh):
    placed = (P("fsdp", "tp"), P("fsdp", "tp"), P("tp", None))
    return jax.shard_map(
        body,
        mesh=mesh,
        in_specs=placed,
        out_specs=(P("fsdp", "tp"), P("tp", None), P("fsdp", "tp")),
        check_vma=False,
    )
```

```python
import functools

import jax
import jax.numpy as jnp
from jax import lax
from jax.experimental import pallas as pl
from jax.experimental.pallas import tpu as pltpu
from jax.sharding import PartitionSpec as P

ROWS = 28672
COLS = 8192
RANK = 256

F32 = jnp.float32
BF16 = jnp.bfloat16
HIGH = lax.Precision.HIGHEST
MESH = pl.DeviceIdType.MESH

LOCAL_ROWS = 1792
LOCAL_COLS = 1024
HALF = 896
PIECE = 224
PART = 112
STEP = 448
WIDE = 512


class Names:
    def __init__(self):
        self.count = 0

    def take(self, many=1):
        first = self.count
        self.count += many
        return first


NAMES = Names()
N_HOP_A, N_HOP_B = NAMES.take(), NAMES.take()
N_LEFT_A, N_LEFT_B = NAMES.take(), NAMES.take()
N_RIGHT_A, N_RIGHT_B = NAMES.take(), NAMES.take()
G_LEFT_A, G_LEFT_B = NAMES.take(), NAMES.take()
G_RIGHT_A, G_RIGHT_B = NAMES.take(), NAMES.take()
G_OPP_A, G_OPP_B = NAMES.take(), NAMES.take()
N_CORE = NAMES.take(4)
G_CORE = NAMES.take(4)
GRAM_SUM = NAMES.take(15)
GRAM_X = NAMES.take(3)
GRAM_ALL = NAMES.take(15)
SQ = NAMES.take(7)
GRAM_CORE = NAMES.take()
W_HOP = NAMES.take(4)
W_NEXT = NAMES.take(8)
W_RING = NAMES.take(8)
W_FAR = NAMES.take(4)
W_SUB = NAMES.take(6)
W_ALL = NAMES.take(6)


def nn(a, b, precision=None):
    return lax.dot_general(
        a, b, (((1,), (0,)), ((), ())), precision=precision, preferred_element_type=F32
    )


def tn(a, b, precision=None):
    return lax.dot_general(
        a, b, (((0,), (0,)), ((), ())), precision=precision, preferred_element_type=F32
    )


def nt(a, b, precision=None):
    return lax.dot_general(
        a, b, (((1,), (1,)), ((), ())), precision=precision, preferred_element_type=F32
    )


def pick(index, values):
    out = values[0]
    for at in range(1, len(values)):
        out = out + (values[at] - values[at - 1]) * ((index + len(values) - at) // len(values))
    return out


def split(x):
    hi = x.astype(BF16)
    return hi, (x - hi.astype(F32)).astype(BF16)


def row_copy(x, j):
    return jnp.broadcast_to(x[j : j + 1, :], (8, 128))


def inverse_factor(x):
    n = len(x)
    sub = lax.broadcasted_iota(jnp.int32, (8, 128), 0)
    lane = lax.broadcasted_iota(jnp.int32, (8, 128), 1)
    col = [
        [None if i < k // 8 else jnp.broadcast_to(x[i][:, k : k + 1], (8, 128)) for i in range(n)]
        for k in range(8 * n)
    ]
    inverse = [jnp.where(lane == sub + 8 * i, 1.0, 0.0) for i in range(n)]
    for g in range(n):
        entry = [[row_copy(col[8 * g + j][g], i) for j in range(i + 1)] for i in range(8)]
        rows = [row_copy(inverse[g], j) for j in range(8)]
        inv, mult = [], [[None] * 8 for _ in range(8)]
        for j in range(8):
            inv.append(1.0 / entry[j][j])
            for k in range(j + 1, 8):
                mult[k][j] = entry[k][j] * inv[j]
                for i in range(k, 8):
                    entry[i][k] = entry[i][k] - entry[i][j] * mult[k][j]
                rows[k] = rows[k] - mult[k][j] * rows[j]
        final = jnp.zeros((8, 128), F32)
        for j in range(8):
            final = jnp.where(sub == j, rows[j] * lax.rsqrt(entry[j][j]), final)
        inverse[g] = final
        below = {}
        for i in range(g + 1, n):
            c = [col[8 * g + j][i] for j in range(8)]
            for j in range(8):
                for k in range(j + 1, 8):
                    c[k] = c[k] - c[j] * mult[k][j]
            below[i] = (c, [c[j] * inv[j] for j in range(8)])
        for k in range(8 * g + 8, 8 * n):
            across = [row_copy(below[k // 8][0][j], k % 8) for j in range(8)]
            for i in range(k // 8, n):
                for j in range(8):
                    col[k][i] = col[k][i] - below[i][1][j] * across[j]
        for i in range(g + 1, n):
            for j in range(8):
                inverse[i] = inverse[i] - below[i][1][j] * rows[j]
    return jnp.concatenate(inverse, axis=0)


def split3(x):
    first = x.astype(BF16)
    rest = x - first.astype(F32)
    second = rest.astype(BF16)
    return first, second, (rest - second.astype(F32)).astype(BF16)


def eliminate(k, half, m_ref):
    left = 128 * half
    cols = slice(left, left + 384)
    rows = pl.ds(pl.multiple_of(32 * k, 32), 32)
    d = pltpu.roll(m_ref[rows, left : left + 128], (128 - 32 * (k % 4)) % 128, 1)
    inverse = inverse_factor([d[8 * i : 8 * i + 8] for i in range(4)])
    scaled = nn(inverse[:, :32], m_ref[rows, cols], HIGH)
    m_ref[rows, cols] = scaled

    @pl.when(k < 7)
    def _():
        lane = lax.broadcasted_iota(jnp.int32, (32, RANK - left), 1)
        lower = jnp.where(lane >= 32 * k + 32 - left, scaled[:, : RANK - left], 0.0)
        a, b, c = split3(lower)
        d, e, f = split3(scaled)
        m_ref[left:, cols] -= tn(
            jnp.concatenate([a, a, b, a, b, c], axis=0), jnp.concatenate([d, e, d, f, e, d], axis=0)
        )


def main_kernel(
    grad,
    mom,
    basis,
    blend_out,
    ortho_out,
    back_out,
    norm_out,
    grad_v,
    basis_v,
    bases,
    hi_v,
    lo_v,
    part_v,
    from_core,
    hop_v,
    side_v,
    proj,
    gram_part,
    gram_in,
    gram_x,
    gram,
    elim,
    turned,
    w,
    w_hop,
    w_side,
    w_sub,
    w_full,
    sq_v,
    load_sem,
    send_sem,
    recv_sem,
):
    f = lax.axis_index("fsdp")
    t = lax.axis_index("tp")
    x, c = t // 2, t % 2
    z, y = f // 4, f % 4

    def tp_dev(xx, cc):
        return {"fsdp": f, "tp": xx * 2 + cc}

    def f_dev(ff):
        return {"fsdp": ff, "tp": t}

    right = tp_dev((x + 1) % 4, c)
    left = tp_dev((x + 3) % 4, c)
    twin = tp_dev(x, 1 - c)

    def remote(src, dst, number, device):
        return pltpu.make_async_remote_copy(
            src_ref=src,
            dst_ref=dst,
            send_sem=send_sem.at[number],
            recv_sem=recv_sem.at[number],
            device_id=device,
            device_id_type=MESH,
        )

    def send(src, dst, number, device):
        remote(src, dst, number, device).start()

    def arrive(dst, number):
        remote(dst, dst, number, twin).wait_recv()

    def all_sent(first, many, ref):
        @pl.loop(first, first + many)
        def _(number):
            remote(ref, ref, number, twin).wait_send()

    def piece_row(core, chip):
        return pl.multiple_of(core * HALF + chip * PIECE, 32)

    def chunk_row(i):
        g = 3 - i // 2
        d = g + (g // 2) * (1 - 2 * (g % 2))
        core = (1 - c) * (1 - i % 2) + c * (i % 2)
        return piece_row(core, (x + d) % 4)

    def load(i):
        rows = pl.ds(chunk_row(i), PIECE)
        return (
            pltpu.make_async_copy(mom.at[rows], blend_out.at[rows], load_sem.at[2 * i]),
            pltpu.make_async_copy(grad.at[rows], grad_v.at[i % 4], load_sem.at[2 * i + 1]),
        )

    basis_copy = pltpu.make_async_copy(basis, basis_v, load_sem.at[16])
    basis_copy.start()

    @pl.loop(0, 3)
    def _(i):
        for copy in load(i):
            copy.start()

    barrier = pltpu.get_barrier_semaphore()

    @pl.loop(1, 16)
    def _(d):
        pl.semaphore_signal(barrier, inc=1, device_id=f_dev((f + d) % 16), device_id_type=MESH)

    @pl.loop(1, 8)
    def _(d):
        pl.semaphore_signal(
            barrier, inc=1, device_id={"fsdp": f, "tp": (t + d) % 8}, device_id_type=MESH
        )

    basis_copy.wait()
    basis_hi, basis_lo = split(basis_v[...])
    bases[:LOCAL_COLS] = basis_hi
    bases[LOCAL_COLS : 2 * LOCAL_COLS] = basis_lo
    bases[2 * LOCAL_COLS :] = basis_hi
    turned[...] = jnp.zeros_like(turned)
    hi_v[LOCAL_ROWS:, :] = jnp.zeros((32, LOCAL_COLS), BF16)
    lo_v[LOCAL_ROWS:, :] = jnp.zeros((32, LOCAL_COLS), BF16)

    def partial(i):
        for copy in load(i):
            copy.wait()
        rows = pl.ds(chunk_row(i), PIECE)

        @pl.when(i < 5)
        def _():
            for copy in load(i + 3):
                copy.start()

        blend = blend_out[rows, :] + grad_v[i % 4].astype(F32)
        blend_out[rows, :] = blend
        hi, lo = split(blend)
        hi_v[rows, :] = hi
        lo_v[rows, :] = lo
        return nn(jnp.concatenate([hi, hi, lo], axis=1), bases[...])

    a_rows, b_rows = pl.ds(0, PART), pl.ds(PART, PART)

    def add_core(j):
        arrive(from_core.at[j], N_CORE + j)
        part_v[2 * j + 1] += from_core[j]

    @pl.loop(0, 8)
    def _(i):
        part_v[i] = partial(i)
        j = i // 2
        core = remote(part_v.at[i], from_core.at[j], N_CORE + j, twin)

        @pl.when(i == 0)
        def _():
            pl.semaphore_wait(barrier, 22)

        @pl.when(i % 2 == 0)
        def _():
            core.start()

        @pl.when(i == 2)
        def _():
            add_core(0)
            send(part_v.at[1, a_rows], hop_v.at[0], N_HOP_A, right)
            send(part_v.at[1, b_rows], hop_v.at[1], N_HOP_B, left)

        @pl.when(i == 4)
        def _():
            add_core(1)
            send(part_v.at[3, a_rows], side_v.at[2], N_RIGHT_A, left)

        @pl.when(i == 6)
        def _():
            add_core(2)
            send(part_v.at[5, b_rows], side_v.at[1], N_LEFT_B, right)
            arrive(hop_v.at[0], N_HOP_A)
            part_v[5, a_rows] += hop_v[0]
            send(part_v.at[5, a_rows], side_v.at[0], N_LEFT_A, right)
            arrive(hop_v.at[1], N_HOP_B)
            part_v[3, b_rows] += hop_v[1]
            send(part_v.at[3, b_rows], side_v.at[3], N_RIGHT_B, left)

    add_core(3)
    my_row = piece_row(c, x)
    arrive(side_v.at[2], N_RIGHT_A)
    arrive(side_v.at[0], N_LEFT_A)
    proj[pl.ds(my_row, PART), :] = part_v[7, a_rows] + (side_v[0] + side_v[2])
    arrive(side_v.at[1], N_LEFT_B)
    arrive(side_v.at[3], N_RIGHT_B)
    proj[pl.ds(my_row + PART, PART), :] = part_v[7, b_rows] + (side_v[1] + side_v[3])

    def part_of(core, chip, b):
        return proj.at[pl.ds(pl.multiple_of(piece_row(core, chip) + b * PART, 16), PART)]

    def whole_of(core, chip):
        return proj.at[pl.ds(piece_row(core, chip), PIECE)]

    def send_part(chip, b, number, device):
        send(part_of(c, chip, b), part_of(c, chip, b), number, device)

    def send_whole(chip, number):
        send(whole_of(c, chip), whole_of(c, chip), number, twin)

    xl, xr, xo = (x + 3) % 4, (x + 1) % 4, (x + 2) % 4
    send_part(x, 0, G_LEFT_A, right)
    send_part(x, 1, G_RIGHT_B, left)
    send_whole(x, G_CORE)
    send_part(x, 1, G_LEFT_B, right)
    send_part(x, 0, G_RIGHT_A, left)

    half_cols = pl.ds(pl.multiple_of(c * 128, 128), 128)

    def eight(row):
        return pl.ds(pl.multiple_of(row * 8, 8), 8)

    def gram_start():
        left, right = [], []
        for core in range(2):
            rows = pl.ds(piece_row(core, x), PIECE)
            a, b, d = split3(proj[rows, half_cols])
            left += [a, a, b, a, b, d]
            a, b, d = split3(proj[rows, :])
            right += [a, b, a, d, b, a]
        gram_part[...] = tn(jnp.concatenate(left, axis=0), jnp.concatenate(right, axis=0))

        @pl.loop(1, 16)
        def _(d):
            to = (f + d) % 16
            send(gram_part.at[eight(to)], gram_in.at[d], GRAM_SUM + d - 1, f_dev(to))

    def gram_across():
        gram_in[0] = gram_part[eight(f), :]

        @pl.loop(1, 16)
        def _(d):
            arrive(gram_in.at[d], GRAM_SUM + d - 1)

        gram_x[x] = jnp.sum(gram_in[...], axis=0)

        @pl.loop(1, 4)
        def _(d):
            send(gram_x.at[x], gram_x.at[x], GRAM_X + d - 1, tp_dev((x + d) % 4, c))

    def gram_row(ff):
        return pl.ds(pl.multiple_of(c * 128 + ff * 8, 8), 8)

    def gram_round():
        @pl.loop(1, 4)
        def _(d):
            arrive(gram_x.at[(x + 4 - d) % 4], GRAM_X + d - 1)

        gram[gram_row(f), :] = (gram_x[0] + gram_x[1]) + (gram_x[2] + gram_x[3])

        @pl.loop(1, 16)
        def _(d):
            mine = gram.at[gram_row(f)]
            send(mine, mine, GRAM_ALL + d - 1, f_dev((f + d) % 16))

    def gram_half(core):
        return gram.at[pl.ds(pl.multiple_of(core * 128, 128), 128)]

    def gram_pair():
        @pl.loop(1, 16)
        def _(d):
            arrive(gram.at[gram_row((f + 16 - d) % 16)], GRAM_ALL + d - 1)

        send(gram_half(c), gram_half(c), GRAM_CORE, twin)

    w[...] = jnp.zeros_like(w)

    @pl.loop(0, 8)
    def _(g):
        core = (c + pick(g, (0, 1, 0, 0, 0, 1, 1, 1))) % 2
        chip = (x + pick(g, (0, 0, 1, 3, 2, 1, 3, 2))) % 4

        @pl.when(g == 1)
        def _():
            arrive(whole_of(1 - c, x), G_CORE)
            gram_start()
            arrive(part_of(c, xl, 0), G_LEFT_A)
            send_part(xl, 0, G_OPP_A, right)
            arrive(part_of(c, xr, 1), G_RIGHT_B)
            send_part(xr, 1, G_OPP_B, left)

        @pl.when(g == 2)
        def _():
            arrive(part_of(c, xr, 0), G_RIGHT_A)
            send_whole(xr, G_CORE + 1)
            arrive(part_of(c, xl, 1), G_LEFT_B)
            send_whole(xl, G_CORE + 2)

        @pl.when(g == 4)
        def _():
            arrive(part_of(c, xo, 0), G_OPP_A)
            arrive(part_of(c, xo, 1), G_OPP_B)
            send_whole(xo, G_CORE + 3)
            gram_across()

        @pl.when(g == 5)
        def _():
            arrive(whole_of(1 - c, xr), G_CORE + 1)

        @pl.when(g == 6)
        def _():
            arrive(whole_of(1 - c, xl), G_CORE + 2)

        @pl.when(g == 7)
        def _():
            arrive(whole_of(1 - c, xo), G_CORE + 3)

        rows = pl.ds(piece_row(core, chip), PIECE)
        p_hi, p_lo = split(proj[rows, :].T)
        turned[:, :PIECE] = p_hi
        turned[:, 256 : 256 + PIECE] = p_hi
        turned[:, 512 : 512 + PIECE] = p_lo
        more = pl.ds(piece_row(core, chip), 256)
        for n in range(4):
            cols = slice(256 * n, 256 * n + 256)
            hi = hi_v[more, cols]
            w[:, cols] += nn(turned[...], jnp.concatenate([hi, lo_v[more, cols], hi], axis=0))

    def places(h):
        k, q = y + h * (z - y), z + h * (y - z)

        def first(kk):
            return f_dev(z * 4 + kk + h * (kk * 4 + y - z * 4 - kk))

        def second(qq):
            return f_dev(qq * 4 + y + h * (z * 4 + qq - qq * 4 - y))

        return k, q, first, second

    ca, cb = pl.ds(0, WIDE), pl.ds(WIDE, WIDE)

    def rows32(h, k):
        return pl.ds(pl.multiple_of(128 * h + 32 * k, 32), 32)

    def rows8(h, k, q):
        return pl.ds(pl.multiple_of(128 * h + 32 * k + 8 * q, 8), 8)

    def w_step_1(h):
        k, q, first, _ = places(h)
        kr, kl, ko = (k + 1) % 4, (k + 3) % 4, (k + 2) % 4
        send(w.at[rows32(h, ko), ca], w_hop.at[2 * h], W_HOP + 2 * h, first(kr))
        send(w.at[rows32(h, ko), cb], w_hop.at[2 * h + 1], W_HOP + 2 * h + 1, first(kl))

    def w_step_1b(h):
        k, q, first, _ = places(h)
        kr, kl = (k + 1) % 4, (k + 3) % 4
        send(w.at[rows32(h, kr), cb], w_side.at[4 * h + 1], W_NEXT + 4 * h + 1, first(kr))
        send(w.at[rows32(h, kl), ca], w_side.at[4 * h + 2], W_NEXT + 4 * h + 2, first(kl))

    def w_step_2(h):
        k, q, first, _ = places(h)
        kr, kl = (k + 1) % 4, (k + 3) % 4
        arrive(w_hop.at[2 * h], W_HOP + 2 * h)
        w[rows32(h, kr), ca] += w_hop[2 * h]
        send(w.at[rows32(h, kr), ca], w_side.at[4 * h], W_NEXT + 4 * h, first(kr))
        arrive(w_hop.at[2 * h + 1], W_HOP + 2 * h + 1)
        w[rows32(h, kl), cb] += w_hop[2 * h + 1]
        send(w.at[rows32(h, kl), cb], w_side.at[4 * h + 3], W_NEXT + 4 * h + 3, first(kl))

    def w_step_3(h):
        k, q, _, second = places(h)
        for s in range(4):
            arrive(w_side.at[4 * h + s], W_NEXT + 4 * h + s)
        w[rows32(h, k), ca] += w_side[4 * h] + w_side[4 * h + 2]
        w[rows32(h, k), cb] += w_side[4 * h + 1] + w_side[4 * h + 3]

        @pl.loop(1, 4)
        def _(d):
            to, slot = (q + d) % 4, 3 * h + d - 1
            send(w.at[rows8(h, k, to)], w_sub.at[slot], W_SUB + slot, second(to))

    def w_step_4(h):
        k, q, _, second = places(h)

        @pl.loop(0, 3)
        def _(d):
            arrive(w_sub.at[3 * h + d], W_SUB + 3 * h + d)

        w_full[rows8(h, k, q), :] = (w[rows8(h, k, q), :] + w_sub[3 * h]) + (
            w_sub[3 * h + 1] + w_sub[3 * h + 2]
        )

        @pl.loop(1, 4)
        def _(d):
            mine = w_full.at[rows8(h, k, q)]
            send(mine, mine, W_ALL + 3 * h + d - 1, second((q + d) % 4))

    def w_step_5(h):
        k, q, first, _ = places(h)
        dr, dl = first((k + 1) % 4), first((k + 3) % 4)

        @pl.loop(1, 4)
        def _(d):
            arrive(w_full.at[rows8(h, k, (q + 4 - d) % 4)], W_ALL + 3 * h + d - 1)

        mine_a, mine_b = w_full.at[rows32(h, k), ca], w_full.at[rows32(h, k), cb]
        send(mine_a, mine_a, W_RING + 4 * h, dr)
        send(mine_b, mine_b, W_RING + 4 * h + 3, dl)
        send(mine_b, mine_b, W_RING + 4 * h + 1, dr)
        send(mine_a, mine_a, W_RING + 4 * h + 2, dl)

    def w_step_6(h):
        k, q, first, _ = places(h)
        kr, kl = (k + 1) % 4, (k + 3) % 4
        from_left = w_full.at[rows32(h, kl), ca]
        arrive(from_left, W_RING + 4 * h)
        send(from_left, from_left, W_FAR + 2 * h, first(kr))
        from_right = w_full.at[rows32(h, kr), cb]
        arrive(from_right, W_RING + 4 * h + 3)
        send(from_right, from_right, W_FAR + 2 * h + 1, first(kl))

    def w_step_7(h):
        k = places(h)[0]
        kr, kl, ko = (k + 1) % 4, (k + 3) % 4, (k + 2) % 4
        arrive(w_full.at[rows32(h, kl), cb], W_RING + 4 * h + 1)
        arrive(w_full.at[rows32(h, kr), ca], W_RING + 4 * h + 2)
        arrive(w_full.at[rows32(h, ko), ca], W_FAR + 2 * h)
        arrive(w_full.at[rows32(h, ko), cb], W_FAR + 2 * h + 1)

    def both_halves(step):
        for h in range(2):
            step(h)

    both_halves(w_step_1)
    both_halves(w_step_1b)
    gram_round()
    both_halves(w_step_2)
    gram_pair()
    both_halves(w_step_3)
    w_steps_at = (w_step_4, None, w_step_5, None, w_step_6, None, w_step_7, None)

    arrive(gram_half(1 - c), GRAM_CORE)
    elim[:, :RANK] = gram[...]
    rr = lax.broadcasted_iota(jnp.int32, (RANK, RANK), 0)
    cc = lax.broadcasted_iota(jnp.int32, (RANK, RANK), 1)
    elim[:, RANK:] = jnp.where(rr == cc, 1.0, 0.0).astype(F32)

    for half in range(2):

        @pl.loop(4 * half, 4 * half + 4)
        def _(k):
            eliminate(k, half, elim)
            for at in range(4 * half, 4 * half + 4):
                if w_steps_at[at] is not None:

                    @pl.when(k == at)
                    def _():
                        both_halves(w_steps_at[at])

    f_hi, f_lo = split(elim[:, RANK:])
    factor = jnp.concatenate([f_hi, f_hi, f_lo], axis=1)
    squares = jnp.zeros((RANK, 128), F32)
    for n in range(4):
        cols = slice(256 * n, 256 * n + 256)
        w_hi, w_lo = split(w_full[:, cols])
        back = nn(factor, jnp.concatenate([w_hi, w_lo, w_hi], axis=0))
        back_out[:, cols] = back
        squares = squares + (back[:, :128] * back[:, :128] + back[:, 128:] * back[:, 128:])
    sq_v[t] = nt(jnp.ones((8, 128), F32), squares, HIGH)

    @pl.loop(1, 8)
    def _(d):
        send(sq_v.at[t], sq_v.at[t], SQ + d - 1, {"fsdp": f, "tp": (t + d) % 8})


    t_hi, t_lo = split(elim[:, RANK:].T)
    turned[:, :256] = t_hi
    turned[:, 256:512] = t_lo

    @pl.loop(0, 8)
    def _(i):
        rows = pl.ds(pl.multiple_of(i * PIECE, 32), PIECE)
        hi, lo = split(proj[rows, :])
        first = turned[:, :256]
        ortho_out[rows, :] = nn(
            jnp.concatenate([hi, hi, lo], axis=1),
            jnp.concatenate([first, turned[:, 256:512], first], axis=0),
        )

    all_sent(N_HOP_A, 12, side_v.at[0])
    all_sent(N_CORE, 8, part_v.at[0])
    all_sent(GRAM_SUM, 33, sq_v.at[0])
    all_sent(GRAM_CORE, 1, gram_part)
    all_sent(W_HOP, 24, w_hop.at[0])
    all_sent(W_SUB, 12, w_sub.at[0])

    @pl.loop(1, 8)
    def _(d):
        arrive(sq_v.at[(t + 8 - d) % 8], SQ + d - 1)

    norm_out[...] = lax.rsqrt(jnp.sum(sq_v[...], axis=0) + 1e-06)
    all_sent(SQ, 7, sq_v.at[0])


def write_kernel(
    blend, ortho, back, norm, mom_out, basis_out, update_out, backs, mom_v, basis_v, update_v, sems
):
    hi, lo = split(back[...])
    backs[:RANK] = hi
    backs[RANK : 2 * RANK] = lo
    backs[2 * RANK :] = hi
    scale = (ROWS * COLS / RANK) ** 0.5
    norms = norm[0:1, :]

    def copies(i):
        slot = i % 2
        found = []
        for p in range(2):
            rows = pl.ds(pl.multiple_of(i * STEP + p * PIECE, 32), PIECE)
            here = pl.ds(p * PIECE, PIECE)
            found.append(pltpu.make_async_copy(mom_v.at[slot, here], mom_out.at[rows], sems.at[slot, p]))
            found.append(
                pltpu.make_async_copy(update_v.at[slot, here], update_out.at[rows], sems.at[slot, 2 + p])
            )
        rank_rows = pl.ds(pl.multiple_of(i * 256, 256), 256)
        found.append(pltpu.make_async_copy(basis_v.at[slot], basis_out.at[rank_rows], sems.at[slot, 4]))
        return found

    @pl.loop(0, LOCAL_ROWS // STEP)
    def _(i):
        slot = i % 2

        @pl.when(i >= 2)
        def _():
            for copy in copies(i - 2):
                copy.wait()

        rows = pl.ds(pl.multiple_of(i * STEP, 64), STEP)
        cols = pl.ds(pl.multiple_of(i * 256, 256), 256)
        basis_v[slot] = back[:, cols].T * norms
        plain = ortho[rows, :]
        mom_v[slot] = blend[rows, :] - nn((0.05 * plain).astype(BF16), backs[:RANK])
        mom_a, update_a, mom_b, update_b, basis_copy = copies(i)
        mom_a.start()
        mom_b.start(priority=1)
        basis_copy.start()
        hi, lo = split(plain * (scale * norms))
        update_v[slot] = nn(jnp.concatenate([hi, hi, lo], axis=1), backs[...]).astype(BF16)
        update_a.start()
        update_b.start(priority=1)

    for i in (2, 3):
        for copy in copies(i):
            copy.wait()


def body(gradient, momentum, basis):
    anywhere = pl.BlockSpec(memory_space=pl.ANY)
    inside = pl.BlockSpec(memory_space=pltpu.VMEM)
    vmem = pltpu.VMEM
    fixed = [pltpu.with_memory_space_constraint(a, pltpu.HBM) for a in (gradient, momentum, basis)]
    results = pl.pallas_call(
        main_kernel,
        out_shape=(
            vmem((LOCAL_ROWS, LOCAL_COLS), F32),
            vmem((LOCAL_ROWS, RANK), F32),
            vmem((RANK, LOCAL_COLS), F32),
            vmem((8, RANK), F32),
        ),
        in_specs=[anywhere] * 3,
        out_specs=(inside,) * 4,
        scratch_shapes=[
            vmem((4, PIECE, LOCAL_COLS), BF16),
            vmem((LOCAL_COLS, RANK), F32),
            vmem((3 * LOCAL_COLS, RANK), BF16),
            vmem((LOCAL_ROWS + 32, LOCAL_COLS), BF16),
            vmem((LOCAL_ROWS + 32, LOCAL_COLS), BF16),
            vmem((8, PIECE, RANK), F32),
            vmem((4, PIECE, RANK), F32),
            vmem((2, PART, RANK), F32),
            vmem((4, PART, RANK), F32),
            vmem((LOCAL_ROWS, RANK), F32),
            vmem((128, RANK), F32),
            vmem((16, 8, RANK), F32),
            vmem((4, 8, RANK), F32),
            vmem((RANK, RANK), F32),
            vmem((RANK, 2 * RANK), F32),
            vmem((RANK, 3 * 256), BF16),
            vmem((RANK, LOCAL_COLS), F32),
            vmem((4, 32, WIDE), F32),
            vmem((8, 32, WIDE), F32),
            vmem((6, 8, LOCAL_COLS), F32),
            vmem((RANK, LOCAL_COLS), F32),
            vmem((8, 8, RANK), F32),
            pltpu.SemaphoreType.DMA((17,)),
            pltpu.SemaphoreType.DMA((NAMES.count,)),
            pltpu.SemaphoreType.DMA((NAMES.count,)),
        ],
        compiler_params=pltpu.CompilerParams(
            collective_id=0, has_side_effects=True, vmem_limit_bytes=44 * 2**20
        ),
        name="transfers",
    )(*fixed)
    results = [pltpu.with_memory_space_constraint(a, pltpu.VMEM) for a in results]

    return pl.pallas_call(
        write_kernel,
        out_shape=(
            jax.ShapeDtypeStruct((LOCAL_ROWS, LOCAL_COLS), F32),
            jax.ShapeDtypeStruct((LOCAL_COLS, RANK), F32),
            jax.ShapeDtypeStruct((LOCAL_ROWS, LOCAL_COLS), BF16),
        ),
        in_specs=[inside] * 4,
        out_specs=(anywhere,) * 3,
        scratch_shapes=[
            vmem((3 * RANK, LOCAL_COLS), BF16),
            vmem((2, STEP, LOCAL_COLS), F32),
            vmem((2, 256, RANK), F32),
            vmem((2, STEP, LOCAL_COLS), BF16),
            pltpu.SemaphoreType.DMA((2, 5)),
        ],
        compiler_params=pltpu.CompilerParams(vmem_limit_bytes=32 * 2**20),
        name="outputs",
    )(*results)


def solution(mesh):
    placed = (P("fsdp", "tp"), P("fsdp", "tp"), P("tp", None))
    return jax.shard_map(
        body,
        mesh=mesh,
        in_specs=placed,
        out_specs=(P("fsdp", "tp"), P("tp", None), P("fsdp", "tp")),
        check_vma=False,
    )
```

```python
import functools

import jax
import jax.numpy as jnp
from jax import lax
from jax.experimental import pallas as pl
from jax.experimental.pallas import tpu as pltpu
from jax.sharding import PartitionSpec as P

ROWS = 28672
COLS = 8192
RANK = 256

F32 = jnp.float32
BF16 = jnp.bfloat16
HIGH = lax.Precision.HIGHEST
MESH = pl.DeviceIdType.MESH

LOCAL_ROWS = 1792
LOCAL_COLS = 1024
HALF = 896
PIECE = 224
PART = 112
STEP = 448
WIDE = 512


class Names:
    def __init__(self):
        self.count = 0

    def take(self, many=1):
        first = self.count
        self.count += many
        return first


NAMES = Names()
N_HOP_A, N_HOP_B = NAMES.take(), NAMES.take()
N_LEFT_A, N_LEFT_B = NAMES.take(), NAMES.take()
N_RIGHT_A, N_RIGHT_B = NAMES.take(), NAMES.take()
G_LEFT_A, G_LEFT_B = NAMES.take(), NAMES.take()
G_RIGHT_A, G_RIGHT_B = NAMES.take(), NAMES.take()
G_OPP_A, G_OPP_B = NAMES.take(), NAMES.take()
N_CORE = NAMES.take(4)
G_CORE = NAMES.take(4)
GRAM_SUM = NAMES.take(15)
GRAM_X = NAMES.take(3)
GRAM_ALL = NAMES.take(15)
SQ = NAMES.take(7)
GRAM_CORE = NAMES.take()
W_HOP = NAMES.take(8)
W_NEXT = NAMES.take(16)
W_RING = NAMES.take(16)
W_FAR = NAMES.take(8)
W_SUB = NAMES.take(12)
W_ALL = NAMES.take(12)


def nn(a, b, precision=None):
    return lax.dot_general(
        a, b, (((1,), (0,)), ((), ())), precision=precision, preferred_element_type=F32
    )


def tn(a, b, precision=None):
    return lax.dot_general(
        a, b, (((0,), (0,)), ((), ())), precision=precision, preferred_element_type=F32
    )


def nt(a, b, precision=None):
    return lax.dot_general(
        a, b, (((1,), (1,)), ((), ())), precision=precision, preferred_element_type=F32
    )


def pick(index, values):
    out = values[0]
    for at in range(1, len(values)):
        out = out + (values[at] - values[at - 1]) * ((index + len(values) - at) // len(values))
    return out


def split(x):
    hi = x.astype(BF16)
    return hi, (x - hi.astype(F32)).astype(BF16)


def row_copy(x, j):
    return jnp.broadcast_to(x[j : j + 1, :], (8, 128))


def inverse_factor(x):
    n = len(x)
    sub = lax.broadcasted_iota(jnp.int32, (8, 128), 0)
    lane = lax.broadcasted_iota(jnp.int32, (8, 128), 1)
    col = [
        [None if i < k // 8 else jnp.broadcast_to(x[i][:, k : k + 1], (8, 128)) for i in range(n)]
        for k in range(8 * n)
    ]
    inverse = [jnp.where(lane == sub + 8 * i, 1.0, 0.0) for i in range(n)]
    for g in range(n):
        entry = [[row_copy(col[8 * g + j][g], i) for j in range(i + 1)] for i in range(8)]
        rows = [row_copy(inverse[g], j) for j in range(8)]
        inv, mult = [], [[None] * 8 for _ in range(8)]
        for j in range(8):
            inv.append(1.0 / entry[j][j])
            for k in range(j + 1, 8):
                mult[k][j] = entry[k][j] * inv[j]
                for i in range(k, 8):
                    entry[i][k] = entry[i][k] - entry[i][j] * mult[k][j]
                rows[k] = rows[k] - mult[k][j] * rows[j]
        final = jnp.zeros((8, 128), F32)
        for j in range(8):
            final = jnp.where(sub == j, rows[j] * lax.rsqrt(entry[j][j]), final)
        inverse[g] = final
        below = {}
        for i in range(g + 1, n):
            c = [col[8 * g + j][i] for j in range(8)]
            for j in range(8):
                for k in range(j + 1, 8):
                    c[k] = c[k] - c[j] * mult[k][j]
            below[i] = (c, [c[j] * inv[j] for j in range(8)])
        for k in range(8 * g + 8, 8 * n):
            across = [row_copy(below[k // 8][0][j], k % 8) for j in range(8)]
            for i in range(k // 8, n):
                for j in range(8):
                    col[k][i] = col[k][i] - below[i][1][j] * across[j]
        for i in range(g + 1, n):
            for j in range(8):
                inverse[i] = inverse[i] - below[i][1][j] * rows[j]
    return jnp.concatenate(inverse, axis=0)


def split3(x):
    first = x.astype(BF16)
    rest = x - first.astype(F32)
    second = rest.astype(BF16)
    return first, second, (rest - second.astype(F32)).astype(BF16)


def eliminate(k, half, m_ref):
    left = 128 * half
    cols = slice(left, left + 384)
    rows = pl.ds(pl.multiple_of(32 * k, 32), 32)
    d = pltpu.roll(m_ref[rows, left : left + 128], (128 - 32 * (k % 4)) % 128, 1)
    inverse = inverse_factor([d[8 * i : 8 * i + 8] for i in range(4)])
    scaled = nn(inverse[:, :32], m_ref[rows, cols], HIGH)
    m_ref[rows, cols] = scaled

    @pl.when(k < 7)
    def _():
        lane = lax.broadcasted_iota(jnp.int32, (32, RANK - left), 1)
        lower = jnp.where(lane >= 32 * k + 32 - left, scaled[:, : RANK - left], 0.0)
        a, b, c = split3(lower)
        d, e, f = split3(scaled)
        m_ref[left:, cols] -= tn(
            jnp.concatenate([a, a, b, a, b, c], axis=0), jnp.concatenate([d, e, d, f, e, d], axis=0)
        )


def main_kernel(
    grad,
    mom,
    basis,
    blend_out,
    ortho_out,
    back_out,
    norm_out,
    grad_v,
    basis_v,
    bases,
    hi_v,
    lo_v,
    part_v,
    from_core,
    hop_v,
    side_v,
    proj,
    gram_part,
    gram_in,
    gram_x,
    gram,
    elim,
    turned,
    w,
    w_hop,
    w_side,
    w_sub,
    w_full,
    sq_v,
    load_sem,
    send_sem,
    recv_sem,
):
    f = lax.axis_index("fsdp")
    t = lax.axis_index("tp")
    x, c = t // 2, t % 2
    z, y = f // 4, f % 4

    def tp_dev(xx, cc):
        return {"fsdp": f, "tp": xx * 2 + cc}

    def f_dev(ff):
        return {"fsdp": ff, "tp": t}

    right = tp_dev((x + 1) % 4, c)
    left = tp_dev((x + 3) % 4, c)
    twin = tp_dev(x, 1 - c)

    def remote(src, dst, number, device):
        return pltpu.make_async_remote_copy(
            src_ref=src,
            dst_ref=dst,
            send_sem=send_sem.at[number],
            recv_sem=recv_sem.at[number],
            device_id=device,
            device_id_type=MESH,
        )

    def send(src, dst, number, device):
        remote(src, dst, number, device).start()

    def arrive(dst, number):
        remote(dst, dst, number, twin).wait_recv()

    def all_sent(first, many, ref):
        @pl.loop(first, first + many)
        def _(number):
            remote(ref, ref, number, twin).wait_send()

    def piece_row(core, chip):
        return pl.multiple_of(core * HALF + chip * PIECE, 32)

    def chunk_row(i):
        g = 3 - i // 2
        d = g + (g // 2) * (1 - 2 * (g % 2))
        core = (1 - c) * (1 - i % 2) + c * (i % 2)
        return piece_row(core, (x + d) % 4)

    def load(i):
        rows = pl.ds(chunk_row(i), PIECE)
        return (
            pltpu.make_async_copy(mom.at[rows], blend_out.at[rows], load_sem.at[2 * i]),
            pltpu.make_async_copy(grad.at[rows], grad_v.at[i % 4], load_sem.at[2 * i + 1]),
        )

    basis_copy = pltpu.make_async_copy(basis, basis_v, load_sem.at[16])
    basis_copy.start()

    @pl.loop(0, 3)
    def _(i):
        for copy in load(i):
            copy.start()

    barrier = pltpu.get_barrier_semaphore()

    @pl.loop(1, 16)
    def _(d):
        pl.semaphore_signal(barrier, inc=1, device_id=f_dev((f + d) % 16), device_id_type=MESH)

    @pl.loop(1, 8)
    def _(d):
        pl.semaphore_signal(
            barrier, inc=1, device_id={"fsdp": f, "tp": (t + d) % 8}, device_id_type=MESH
        )

    basis_copy.wait()
    basis_hi, basis_lo = split(basis_v[...])
    bases[:LOCAL_COLS] = basis_hi
    bases[LOCAL_COLS:] = basis_lo
    turned[...] = jnp.zeros_like(turned)
    hi_v[LOCAL_ROWS:, :] = jnp.zeros((32, LOCAL_COLS), BF16)
    lo_v[LOCAL_ROWS:, :] = jnp.zeros((32, LOCAL_COLS), BF16)

    def partial(i):
        for copy in load(i):
            copy.wait()
        rows = pl.ds(chunk_row(i), PIECE)

        @pl.when(i < 5)
        def _():
            for copy in load(i + 3):
                copy.start()

        blend = blend_out[rows, :] + grad_v[i % 4].astype(F32)
        blend_out[rows, :] = blend
        hi, lo = split(blend)
        hi_v[rows, :] = hi
        lo_v[rows, :] = lo
        first, second = bases[:LOCAL_COLS], bases[LOCAL_COLS:]
        return nn(hi, first) + nn(hi, second) + nn(lo, first)

    a_rows, b_rows = pl.ds(0, PART), pl.ds(PART, PART)

    def add_core(j):
        arrive(from_core.at[j], N_CORE + j)
        part_v[2 * j + 1] += from_core[j]

    @pl.loop(0, 8)
    def _(i):
        part_v[i] = partial(i)
        j = i // 2
        core = remote(part_v.at[i], from_core.at[j], N_CORE + j, twin)

        @pl.when(i == 0)
        def _():
            pl.semaphore_wait(barrier, 22)

        @pl.when(i % 2 == 0)
        def _():
            core.start()

        @pl.when(i == 2)
        def _():
            add_core(0)
            send(part_v.at[1, a_rows], hop_v.at[0], N_HOP_A, right)
            send(part_v.at[1, b_rows], hop_v.at[1], N_HOP_B, left)

        @pl.when(i == 4)
        def _():
            add_core(1)
            send(part_v.at[3, a_rows], side_v.at[2], N_RIGHT_A, left)

        @pl.when(i == 6)
        def _():
            add_core(2)
            send(part_v.at[5, b_rows], side_v.at[1], N_LEFT_B, right)
            arrive(hop_v.at[0], N_HOP_A)
            part_v[5, a_rows] += hop_v[0]
            send(part_v.at[5, a_rows], side_v.at[0], N_LEFT_A, right)
            arrive(hop_v.at[1], N_HOP_B)
            part_v[3, b_rows] += hop_v[1]
            send(part_v.at[3, b_rows], side_v.at[3], N_RIGHT_B, left)

    add_core(3)
    my_row = piece_row(c, x)
    arrive(side_v.at[2], N_RIGHT_A)
    arrive(side_v.at[0], N_LEFT_A)
    proj[pl.ds(my_row, PART), :] = part_v[7, a_rows] + (side_v[0] + side_v[2])
    arrive(side_v.at[1], N_LEFT_B)
    arrive(side_v.at[3], N_RIGHT_B)
    proj[pl.ds(my_row + PART, PART), :] = part_v[7, b_rows] + (side_v[1] + side_v[3])

    def part_of(core, chip, b):
        return proj.at[pl.ds(pl.multiple_of(piece_row(core, chip) + b * PART, 16), PART)]

    def whole_of(core, chip):
        return proj.at[pl.ds(piece_row(core, chip), PIECE)]

    def send_part(chip, b, number, device):
        send(part_of(c, chip, b), part_of(c, chip, b), number, device)

    def send_whole(chip, number):
        send(whole_of(c, chip), whole_of(c, chip), number, twin)

    xl, xr, xo = (x + 3) % 4, (x + 1) % 4, (x + 2) % 4
    send_part(x, 0, G_LEFT_A, right)
    send_part(x, 1, G_RIGHT_B, left)
    send_whole(x, G_CORE)
    send_part(x, 1, G_LEFT_B, right)
    send_part(x, 0, G_RIGHT_A, left)

    half_cols = pl.ds(pl.multiple_of(c * 128, 128), 128)

    def eight(row):
        return pl.ds(pl.multiple_of(row * 8, 8), 8)

    def gram_start():
        halves = []
        for core in range(2):
            rows = pl.ds(piece_row(core, x), PIECE)
            a, b, d = split3(proj[rows, half_cols])
            left = jnp.concatenate([a, a, b, a, b, d], axis=0)
            a, b, d = split3(proj[rows, :])
            halves.append(tn(left, jnp.concatenate([a, b, a, d, b, a], axis=0)))
        gram_part[...] = halves[0] + halves[1]

        @pl.loop(1, 16)
        def _(d):
            to = (f + d) % 16
            send(gram_part.at[eight(to)], gram_in.at[d], GRAM_SUM + d - 1, f_dev(to))

    def gram_across():
        gram_in[0] = gram_part[eight(f), :]

        @pl.loop(1, 16)
        def _(d):
            arrive(gram_in.at[d], GRAM_SUM + d - 1)

        gram_x[x] = jnp.sum(gram_in[...], axis=0)

        @pl.loop(1, 4)
        def _(d):
            send(gram_x.at[x], gram_x.at[x], GRAM_X + d - 1, tp_dev((x + d) % 4, c))

    def gram_row(ff):
        return pl.ds(pl.multiple_of(c * 128 + ff * 8, 8), 8)

    def gram_round():
        @pl.loop(1, 4)
        def _(d):
            arrive(gram_x.at[(x + 4 - d) % 4], GRAM_X + d - 1)

        gram[gram_row(f), :] = (gram_x[0] + gram_x[1]) + (gram_x[2] + gram_x[3])

        @pl.loop(1, 16)
        def _(d):
            mine = gram.at[gram_row(f)]
            send(mine, mine, GRAM_ALL + d - 1, f_dev((f + d) % 16))

    def gram_half(core):
        return gram.at[pl.ds(pl.multiple_of(core * 128, 128), 128)]

    def gram_pair():
        @pl.loop(1, 16)
        def _(d):
            arrive(gram.at[gram_row((f + 16 - d) % 16)], GRAM_ALL + d - 1)

        send(gram_half(c), gram_half(c), GRAM_CORE, twin)

    w[...] = jnp.zeros_like(w)

    @pl.loop(0, 8)
    def _(g):
        core = (c + pick(g, (0, 1, 0, 0, 0, 1, 1, 1))) % 2
        chip = (x + pick(g, (0, 0, 1, 3, 2, 1, 3, 2))) % 4

        @pl.when(g == 1)
        def _():
            arrive(whole_of(1 - c, x), G_CORE)
            gram_start()

        @pl.when(g == 2)
        def _():
            arrive(part_of(c, xl, 0), G_LEFT_A)
            send_part(xl, 0, G_OPP_A, right)
            arrive(part_of(c, xr, 1), G_RIGHT_B)
            send_part(xr, 1, G_OPP_B, left)
            gram_across()
            arrive(part_of(c, xr, 0), G_RIGHT_A)
            send_whole(xr, G_CORE + 1)
            arrive(part_of(c, xl, 1), G_LEFT_B)
            send_whole(xl, G_CORE + 2)

        @pl.when(g == 4)
        def _():
            arrive(part_of(c, xo, 0), G_OPP_A)
            arrive(part_of(c, xo, 1), G_OPP_B)
            send_whole(xo, G_CORE + 3)
            gram_round()

        @pl.when(g == 5)
        def _():
            arrive(whole_of(1 - c, xr), G_CORE + 1)

        @pl.when(g == 6)
        def _():
            arrive(whole_of(1 - c, xl), G_CORE + 2)

        @pl.when(g == 7)
        def _():
            arrive(whole_of(1 - c, xo), G_CORE + 3)

        rows = pl.ds(piece_row(core, chip), PIECE)
        p_hi, p_lo = split(proj[rows, :].T)
        turned[:, :PIECE] = p_hi
        turned[:, 256 : 256 + PIECE] = p_hi
        turned[:, 512 : 512 + PIECE] = p_lo
        more = pl.ds(piece_row(core, chip), 256)
        for n in range(4):
            cols = slice(256 * n, 256 * n + 256)
            hi = hi_v[more, cols]
            w[:, cols] += nn(turned[...], jnp.concatenate([hi, lo_v[more, cols], hi], axis=0))

    def places(u):
        k, q = y + u * (z - y), z + u * (y - z)

        def first(kk):
            return f_dev(z * 4 + kk + u * (kk * 4 + y - z * 4 - kk))

        def second(qq):
            return f_dev(qq * 4 + y + u * (z * 4 + qq - qq * 4 - y))

        return k, q, first, second

    def cols_ab(u):
        start = pl.multiple_of(WIDE * u, WIDE)
        return pl.ds(start, 256), pl.ds(pl.multiple_of(start + 256, 256), 256)

    def cols_u(u):
        return pl.ds(pl.multiple_of(WIDE * u, WIDE), WIDE)

    def rows32(h, k):
        return pl.ds(pl.multiple_of(128 * h + 32 * k, 32), 32)

    def rows8(h, k, q):
        return pl.ds(pl.multiple_of(128 * h + 32 * k + 8 * q, 8), 8)

    def w_step_1(h, u):
        k, q, first, _ = places(u)
        ca, cb = cols_ab(u)
        i = 2 * h + u
        kr, kl, ko = (k + 1) % 4, (k + 3) % 4, (k + 2) % 4
        send(w.at[rows32(h, ko), ca], w_hop.at[2 * i], W_HOP + 2 * i, first(kr))
        send(w.at[rows32(h, ko), cb], w_hop.at[2 * i + 1], W_HOP + 2 * i + 1, first(kl))
        send(w.at[rows32(h, kr), cb], w_side.at[4 * i + 1], W_NEXT + 4 * i + 1, first(kr))
        send(w.at[rows32(h, kl), ca], w_side.at[4 * i + 2], W_NEXT + 4 * i + 2, first(kl))

    def w_step_2(h, u):
        k, q, first, _ = places(u)
        ca, cb = cols_ab(u)
        i = 2 * h + u
        kr, kl = (k + 1) % 4, (k + 3) % 4
        arrive(w_hop.at[2 * i], W_HOP + 2 * i)
        w[rows32(h, kr), ca] += w_hop[2 * i]
        send(w.at[rows32(h, kr), ca], w_side.at[4 * i], W_NEXT + 4 * i, first(kr))
        arrive(w_hop.at[2 * i + 1], W_HOP + 2 * i + 1)
        w[rows32(h, kl), cb] += w_hop[2 * i + 1]
        send(w.at[rows32(h, kl), cb], w_side.at[4 * i + 3], W_NEXT + 4 * i + 3, first(kl))

    def w_step_3(h, u):
        k, q, _, second = places(u)
        ca, cb = cols_ab(u)
        i = 2 * h + u
        for s in range(4):
            arrive(w_side.at[4 * i + s], W_NEXT + 4 * i + s)
        w[rows32(h, k), ca] += w_side[4 * i] + w_side[4 * i + 2]
        w[rows32(h, k), cb] += w_side[4 * i + 1] + w_side[4 * i + 3]

        @pl.loop(1, 4)
        def _(d):
            to, slot = (q + d) % 4, 3 * i + d - 1
            send(w.at[rows8(h, k, to), cols_u(u)], w_sub.at[slot], W_SUB + slot, second(to))

    def w_step_4(h, u):
        k, q, _, second = places(u)
        i = 2 * h + u

        @pl.loop(0, 3)
        def _(d):
            arrive(w_sub.at[3 * i + d], W_SUB + 3 * i + d)

        w_full[rows8(h, k, q), cols_u(u)] = (w[rows8(h, k, q), cols_u(u)] + w_sub[3 * i]) + (
            w_sub[3 * i + 1] + w_sub[3 * i + 2]
        )

        @pl.loop(1, 4)
        def _(d):
            mine = w_full.at[rows8(h, k, q), cols_u(u)]
            send(mine, mine, W_ALL + 3 * i + d - 1, second((q + d) % 4))

    def w_step_5(h, u):
        k, q, first, _ = places(u)
        ca, cb = cols_ab(u)
        i = 2 * h + u
        dr, dl = first((k + 1) % 4), first((k + 3) % 4)

        @pl.loop(1, 4)
        def _(d):
            arrive(w_full.at[rows8(h, k, (q + 4 - d) % 4), cols_u(u)], W_ALL + 3 * i + d - 1)

        mine_a, mine_b = w_full.at[rows32(h, k), ca], w_full.at[rows32(h, k), cb]
        send(mine_a, mine_a, W_RING + 4 * i, dr)
        send(mine_b, mine_b, W_RING + 4 * i + 3, dl)
        send(mine_b, mine_b, W_RING + 4 * i + 1, dr)
        send(mine_a, mine_a, W_RING + 4 * i + 2, dl)

    def w_step_6(h, u):
        k, q, first, _ = places(u)
        ca, cb = cols_ab(u)
        i = 2 * h + u
        kr, kl = (k + 1) % 4, (k + 3) % 4
        from_left = w_full.at[rows32(h, kl), ca]
        arrive(from_left, W_RING + 4 * i)
        send(from_left, from_left, W_FAR + 2 * i, first(kr))
        from_right = w_full.at[rows32(h, kr), cb]
        arrive(from_right, W_RING + 4 * i + 3)
        send(from_right, from_right, W_FAR + 2 * i + 1, first(kl))

    def w_step_7(h, u):
        k = places(u)[0]
        ca, cb = cols_ab(u)
        i = 2 * h + u
        kr, kl, ko = (k + 1) % 4, (k + 3) % 4, (k + 2) % 4
        arrive(w_full.at[rows32(h, kl), cb], W_RING + 4 * i + 1)
        arrive(w_full.at[rows32(h, kr), ca], W_RING + 4 * i + 2)
        arrive(w_full.at[rows32(h, ko), ca], W_FAR + 2 * i)
        arrive(w_full.at[rows32(h, ko), cb], W_FAR + 2 * i + 1)

    def all_parts(step):
        @pl.loop(0, 4)
        def _(i):
            step(i // 2, i % 2)

    all_parts(w_step_1)
    gram_pair()
    all_parts(w_step_2)
    w_steps_at = (w_step_3, None, w_step_4, None, w_step_5, None, w_step_6, w_step_7)

    arrive(gram_half(1 - c), GRAM_CORE)
    elim[:, :RANK] = gram[...]
    rr = lax.broadcasted_iota(jnp.int32, (RANK, RANK), 0)
    cc = lax.broadcasted_iota(jnp.int32, (RANK, RANK), 1)
    elim[:, RANK:] = jnp.where(rr == cc, 1.0, 0.0).astype(F32)

    for half in range(2):

        @pl.loop(4 * half, 4 * half + 4)
        def _(k):
            eliminate(k, half, elim)
            for at in range(4 * half, 4 * half + 4):
                if w_steps_at[at] is not None:

                    @pl.when(k == at)
                    def _():
                        all_parts(w_steps_at[at])

    f_hi, f_lo = split(elim[:, RANK:])
    factor = jnp.concatenate([f_hi, f_hi, f_lo], axis=1)
    squares = jnp.zeros((RANK, 128), F32)
    for n in range(4):
        cols = slice(256 * n, 256 * n + 256)
        w_hi, w_lo = split(w_full[:, cols])
        back = nn(factor, jnp.concatenate([w_hi, w_lo, w_hi], axis=0))
        back_out[:, cols] = back
        squares = squares + (back[:, :128] * back[:, :128] + back[:, 128:] * back[:, 128:])
    sq_v[t] = nt(jnp.ones((8, 128), F32), squares, HIGH)

    @pl.loop(1, 8)
    def _(d):
        send(sq_v.at[t], sq_v.at[t], SQ + d - 1, {"fsdp": f, "tp": (t + d) % 8})


    t_hi, t_lo = split(elim[:, RANK:].T)
    turned[:, :256] = t_hi
    turned[:, 256:512] = t_lo

    @pl.loop(0, LOCAL_ROWS // STEP)
    def _(i):
        rows = pl.ds(pl.multiple_of(i * STEP, 64), STEP)
        hi, lo = split(proj[rows, :])
        first, second = turned[:, :256], turned[:, 256:512]
        ortho_out[rows, :] = nn(hi, first) + nn(hi, second) + nn(lo, first)

    all_sent(N_HOP_A, 12, side_v.at[0])
    all_sent(N_CORE, 8, part_v.at[0])
    all_sent(GRAM_SUM, 33, sq_v.at[0])
    all_sent(GRAM_CORE, 1, gram_part)
    all_sent(W_HOP, 48, w_hop.at[0])
    all_sent(W_SUB, 24, w_sub.at[0])

    @pl.loop(1, 8)
    def _(d):
        arrive(sq_v.at[(t + 8 - d) % 8], SQ + d - 1)

    norm_out[...] = lax.rsqrt(jnp.sum(sq_v[...], axis=0) + 1e-06)
    all_sent(SQ, 7, sq_v.at[0])


def write_kernel(
    blend, ortho, back, norm, mom_out, basis_out, update_out, backs, mom_v, basis_v, update_v, sems
):
    hi, lo = split(back[...])
    backs[:RANK] = hi
    backs[RANK : 2 * RANK] = lo
    backs[2 * RANK :] = hi
    scale = (ROWS * COLS / RANK) ** 0.5
    norms = norm[0:1, :]

    def copies(i):
        slot = i % 2
        found = []
        for p in range(2):
            rows = pl.ds(pl.multiple_of(i * STEP + p * PIECE, 32), PIECE)
            here = pl.ds(p * PIECE, PIECE)
            found.append(pltpu.make_async_copy(mom_v.at[slot, here], mom_out.at[rows], sems.at[slot, p]))
            found.append(
                pltpu.make_async_copy(update_v.at[slot, here], update_out.at[rows], sems.at[slot, 2 + p])
            )
        rank_rows = pl.ds(pl.multiple_of(i * 256, 256), 256)
        found.append(pltpu.make_async_copy(basis_v.at[slot], basis_out.at[rank_rows], sems.at[slot, 4]))
        return found

    @pl.loop(0, LOCAL_ROWS // STEP)
    def _(i):
        slot = i % 2

        @pl.when(i >= 2)
        def _():
            for copy in copies(i - 2):
                copy.wait()

        rows = pl.ds(pl.multiple_of(i * STEP, 64), STEP)
        cols = pl.ds(pl.multiple_of(i * 256, 256), 256)
        basis_v[slot] = back[:, cols].T * norms
        plain = ortho[rows, :]
        mom_v[slot] = blend[rows, :] - nn((0.05 * plain).astype(BF16), backs[:RANK])
        mom_a, update_a, mom_b, update_b, basis_copy = copies(i)
        mom_a.start()
        mom_b.start(priority=1)
        basis_copy.start()
        hi, lo = split(plain * (scale * norms))
        update_v[slot] = nn(jnp.concatenate([hi, hi, lo], axis=1), backs[...]).astype(BF16)
        update_a.start()
        update_b.start(priority=1)

    for i in (2, 3):
        for copy in copies(i):
            copy.wait()


def body(gradient, momentum, basis):
    anywhere = pl.BlockSpec(memory_space=pl.ANY)
    inside = pl.BlockSpec(memory_space=pltpu.VMEM)
    vmem = pltpu.VMEM
    fixed = [pltpu.with_memory_space_constraint(a, pltpu.HBM) for a in (gradient, momentum, basis)]
    results = pl.pallas_call(
        main_kernel,
        out_shape=(
            vmem((LOCAL_ROWS, LOCAL_COLS), F32),
            vmem((LOCAL_ROWS, RANK), F32),
            vmem((RANK, LOCAL_COLS), F32),
            vmem((8, RANK), F32),
        ),
        in_specs=[anywhere] * 3,
        out_specs=(inside,) * 4,
        scratch_shapes=[
            vmem((4, PIECE, LOCAL_COLS), BF16),
            vmem((LOCAL_COLS, RANK), F32),
            vmem((2 * LOCAL_COLS, RANK), BF16),
            vmem((LOCAL_ROWS + 32, LOCAL_COLS), BF16),
            vmem((LOCAL_ROWS + 32, LOCAL_COLS), BF16),
            vmem((8, PIECE, RANK), F32),
            vmem((4, PIECE, RANK), F32),
            vmem((2, PART, RANK), F32),
            vmem((4, PART, RANK), F32),
            vmem((LOCAL_ROWS, RANK), F32),
            vmem((128, RANK), F32),
            vmem((16, 8, RANK), F32),
            vmem((4, 8, RANK), F32),
            vmem((RANK, RANK), F32),
            vmem((RANK, 2 * RANK), F32),
            vmem((RANK, 3 * 256), BF16),
            vmem((RANK, LOCAL_COLS), F32),
            vmem((8, 32, 256), F32),
            vmem((16, 32, 256), F32),
            vmem((12, 8, WIDE), F32),
            vmem((RANK, LOCAL_COLS), F32),
            vmem((8, 8, RANK), F32),
            pltpu.SemaphoreType.DMA((17,)),
            pltpu.SemaphoreType.DMA((NAMES.count,)),
            pltpu.SemaphoreType.DMA((NAMES.count,)),
        ],
        compiler_params=pltpu.CompilerParams(
            collective_id=0, has_side_effects=True, vmem_limit_bytes=44 * 2**20
        ),
        name="transfers",
    )(*fixed)
    results = [pltpu.with_memory_space_constraint(a, pltpu.VMEM) for a in results]

    return pl.pallas_call(
        write_kernel,
        out_shape=(
            jax.ShapeDtypeStruct((LOCAL_ROWS, LOCAL_COLS), F32),
            jax.ShapeDtypeStruct((LOCAL_COLS, RANK), F32),
            jax.ShapeDtypeStruct((LOCAL_ROWS, LOCAL_COLS), BF16),
        ),
        in_specs=[inside] * 4,
        out_specs=(anywhere,) * 3,
        scratch_shapes=[
            vmem((3 * RANK, LOCAL_COLS), BF16),
            vmem((2, STEP, LOCAL_COLS), F32),
            vmem((2, 256, RANK), F32),
            vmem((2, STEP, LOCAL_COLS), BF16),
            pltpu.SemaphoreType.DMA((2, 5)),
        ],
        compiler_params=pltpu.CompilerParams(vmem_limit_bytes=32 * 2**20),
        name="outputs",
    )(*results)


def solution(mesh):
    placed = (P("fsdp", "tp"), P("fsdp", "tp"), P("tp", None))
    return jax.shard_map(
        body,
        mesh=mesh,
        in_specs=placed,
        out_specs=(P("fsdp", "tp"), P("tp", None), P("fsdp", "tp")),
        check_vma=False,
    )
```

```python
import functools

import jax
import jax.numpy as jnp
from jax import lax
from jax.experimental import pallas as pl
from jax.experimental.pallas import tpu as pltpu
from jax.sharding import PartitionSpec as P

ROWS = 28672
COLS = 8192
RANK = 256

F32 = jnp.float32
BF16 = jnp.bfloat16
HIGH = lax.Precision.HIGHEST
MESH = pl.DeviceIdType.MESH

LOCAL_ROWS = 1792
LOCAL_COLS = 1024
HALF = 896
PIECE = 224
PART = 112
STEP = 448
WIDE = 512


class Names:
    def __init__(self):
        self.count = 0

    def take(self, many=1):
        first = self.count
        self.count += many
        return first


NAMES = Names()
N_HOP_A, N_HOP_B = NAMES.take(), NAMES.take()
N_LEFT_A, N_LEFT_B = NAMES.take(), NAMES.take()
N_RIGHT_A, N_RIGHT_B = NAMES.take(), NAMES.take()
G_LEFT_A, G_LEFT_B = NAMES.take(), NAMES.take()
G_RIGHT_A, G_RIGHT_B = NAMES.take(), NAMES.take()
G_OPP_A, G_OPP_B = NAMES.take(), NAMES.take()
N_CORE = NAMES.take(4)
G_CORE = NAMES.take(4)
GRAM_SUM = NAMES.take(15)
GRAM_X = NAMES.take(3)
GRAM_ALL = NAMES.take(15)
SQ = NAMES.take(7)
GRAM_CORE = NAMES.take()
W_HOP = NAMES.take(8)
W_NEXT = NAMES.take(16)
W_RING = NAMES.take(16)
W_FAR = NAMES.take(8)
W_SUB = NAMES.take(12)
W_ALL = NAMES.take(12)


def nn(a, b, precision=None):
    return lax.dot_general(
        a, b, (((1,), (0,)), ((), ())), precision=precision, preferred_element_type=F32
    )


def tn(a, b, precision=None):
    return lax.dot_general(
        a, b, (((0,), (0,)), ((), ())), precision=precision, preferred_element_type=F32
    )


def nt(a, b, precision=None):
    return lax.dot_general(
        a, b, (((1,), (1,)), ((), ())), precision=precision, preferred_element_type=F32
    )


def pick(index, values):
    out = values[0]
    for at in range(1, len(values)):
        out = out + (values[at] - values[at - 1]) * ((index + len(values) - at) // len(values))
    return out


def split(x):
    hi = x.astype(BF16)
    return hi, (x - hi.astype(F32)).astype(BF16)


def row_copy(x, j):
    return jnp.broadcast_to(x[j : j + 1, :], (8, 128))


def inverse_factor(x):
    x = list(x)
    n = len(x)
    sub = lax.broadcasted_iota(jnp.int32, (8, 128), 0)
    for g in range(n):
        lanes = [32 + 8 * g + j for j in range(8)]
        col = {i: [jnp.broadcast_to(x[i][:, at : at + 1], (8, 128)) for at in lanes] for i in range(g, n)}
        entry = [[row_copy(col[g][j], i) for j in range(i + 1)] for i in range(8)]
        rows = [row_copy(x[g], j) for j in range(8)]
        inv, mult = [], [[None] * 8 for _ in range(8)]
        for j in range(8):
            inv.append(1.0 / entry[j][j])
            for k in range(j + 1, 8):
                mult[k][j] = entry[k][j] * inv[j]
                for i in range(k, 8):
                    entry[i][k] = entry[i][k] - entry[i][j] * mult[k][j]
                rows[k] = rows[k] - mult[k][j] * rows[j]
        for i in range(g + 1, n):
            c = col[i]
            for j in range(8):
                for k in range(j + 1, 8):
                    c[k] = c[k] - c[j] * mult[k][j]
                x[i] = x[i] - (c[j] * inv[j]) * rows[j]
        final = jnp.zeros((8, 128), F32)
        for j in range(8):
            final = jnp.where(sub == j, rows[j] * lax.rsqrt(entry[j][j]), final)
        x[g] = final
    return jnp.concatenate(x, axis=0)


def split3(x):
    first = x.astype(BF16)
    rest = x - first.astype(F32)
    second = rest.astype(BF16)
    return first, second, (rest - second.astype(F32)).astype(BF16)


def eliminate(k, half, m_ref):
    left = 128 * half
    cols = slice(left, left + 384)
    rows = pl.ds(pl.multiple_of(32 * k, 32), 32)
    lane = lax.broadcasted_iota(jnp.int32, (32, 128), 1)
    subl = lax.broadcasted_iota(jnp.int32, (32, 128), 0)
    d = pltpu.roll(m_ref[rows, left : left + 128], (160 - 32 * (k % 4)) % 128, 1)
    x = jnp.where(lane < 32, jnp.where(lane == subl, 1.0, 0.0), d)
    inverse = inverse_factor([x[8 * i : 8 * i + 8] for i in range(4)])
    scaled = nn(inverse[:, :32], m_ref[rows, cols], HIGH)
    m_ref[rows, cols] = scaled

    @pl.when(k < 7)
    def _():
        lane = lax.broadcasted_iota(jnp.int32, (32, RANK - left), 1)
        lower = jnp.where(lane >= 32 * k + 32 - left, scaled[:, : RANK - left], 0.0)
        a, b, c = split3(lower)
        d, e, f = split3(scaled)
        m_ref[left:, cols] -= tn(
            jnp.concatenate([a, a, b, a, b, c], axis=0), jnp.concatenate([d, e, d, f, e, d], axis=0)
        )


def main_kernel(
    grad,
    mom,
    basis,
    blend_out,
    ortho_out,
    back_out,
    norm_out,
    grad_v,
    basis_v,
    bases,
    hi_v,
    lo_v,
    part_v,
    from_core,
    hop_v,
    side_v,
    proj,
    gram_part,
    gram_in,
    gram_x,
    gram,
    elim,
    turned,
    w,
    w_hop,
    w_side,
    w_sub,
    w_full,
    sq_v,
    load_sem,
    send_sem,
    recv_sem,
):
    f = lax.axis_index("fsdp")
    t = lax.axis_index("tp")
    x, c = t // 2, t % 2
    z, y = f // 4, f % 4

    def tp_dev(xx, cc):
        return {"fsdp": f, "tp": xx * 2 + cc}

    def f_dev(ff):
        return {"fsdp": ff, "tp": t}

    right = tp_dev((x + 1) % 4, c)
    left = tp_dev((x + 3) % 4, c)
    twin = tp_dev(x, 1 - c)

    def remote(src, dst, number, device):
        return pltpu.make_async_remote_copy(
            src_ref=src,
            dst_ref=dst,
            send_sem=send_sem.at[number],
            recv_sem=recv_sem.at[number],
            device_id=device,
            device_id_type=MESH,
        )

    def send(src, dst, number, device):
        remote(src, dst, number, device).start()

    def arrive(dst, number):
        remote(dst, dst, number, twin).wait_recv()

    def all_sent(first, many, ref):
        @pl.loop(first, first + many)
        def _(number):
            remote(ref, ref, number, twin).wait_send()

    def piece_row(core, chip):
        return pl.multiple_of(core * HALF + chip * PIECE, 32)

    def chunk_row(i):
        g = 3 - i // 2
        d = g + (g // 2) * (1 - 2 * (g % 2))
        core = (1 - c) * (1 - i % 2) + c * (i % 2)
        return piece_row(core, (x + d) % 4)

    def load(i):
        rows = pl.ds(chunk_row(i), PIECE)
        return (
            pltpu.make_async_copy(mom.at[rows], blend_out.at[rows], load_sem.at[2 * i]),
            pltpu.make_async_copy(grad.at[rows], grad_v.at[i % 4], load_sem.at[2 * i + 1]),
        )

    basis_copy = pltpu.make_async_copy(basis, basis_v, load_sem.at[16])
    basis_copy.start()

    @pl.loop(0, 3)
    def _(i):
        for copy in load(i):
            copy.start()

    barrier = pltpu.get_barrier_semaphore()

    @pl.loop(1, 16)
    def _(d):
        pl.semaphore_signal(barrier, inc=1, device_id=f_dev((f + d) % 16), device_id_type=MESH)

    @pl.loop(1, 8)
    def _(d):
        pl.semaphore_signal(
            barrier, inc=1, device_id={"fsdp": f, "tp": (t + d) % 8}, device_id_type=MESH
        )

    basis_copy.wait()
    basis_hi, basis_lo = split(basis_v[...])
    bases[:LOCAL_COLS] = basis_hi
    bases[LOCAL_COLS:] = basis_lo
    turned[...] = jnp.zeros_like(turned)
    hi_v[LOCAL_ROWS:, :] = jnp.zeros((32, LOCAL_COLS), BF16)
    lo_v[LOCAL_ROWS:, :] = jnp.zeros((32, LOCAL_COLS), BF16)

    def partial(i):
        for copy in load(i):
            copy.wait()
        rows = pl.ds(chunk_row(i), PIECE)

        @pl.when(i < 5)
        def _():
            for copy in load(i + 3):
                copy.start()

        blend = blend_out[rows, :] + grad_v[i % 4].astype(F32)
        blend_out[rows, :] = blend
        hi, lo = split(blend)
        hi_v[rows, :] = hi
        lo_v[rows, :] = lo
        first, second = bases[:LOCAL_COLS], bases[LOCAL_COLS:]
        return nn(hi, first) + nn(hi, second) + nn(lo, first)

    a_rows, b_rows = pl.ds(0, PART), pl.ds(PART, PART)

    def add_core(j):
        arrive(from_core.at[j], N_CORE + j)
        part_v[2 * j + 1] += from_core[j]

    @pl.loop(0, 8)
    def _(i):
        part_v[i] = partial(i)
        j = i // 2
        core = remote(part_v.at[i], from_core.at[j], N_CORE + j, twin)

        @pl.when(i == 0)
        def _():
            pl.semaphore_wait(barrier, 22)

        @pl.when(i % 2 == 0)
        def _():
            core.start()

        @pl.when(i == 2)
        def _():
            add_core(0)
            send(part_v.at[1, a_rows], hop_v.at[0], N_HOP_A, right)
            send(part_v.at[1, b_rows], hop_v.at[1], N_HOP_B, left)

        @pl.when(i == 4)
        def _():
            add_core(1)
            send(part_v.at[3, a_rows], side_v.at[2], N_RIGHT_A, left)

        @pl.when(i == 6)
        def _():
            add_core(2)
            send(part_v.at[5, b_rows], side_v.at[1], N_LEFT_B, right)
            arrive(hop_v.at[0], N_HOP_A)
            part_v[5, a_rows] += hop_v[0]
            send(part_v.at[5, a_rows], side_v.at[0], N_LEFT_A, right)
            arrive(hop_v.at[1], N_HOP_B)
            part_v[3, b_rows] += hop_v[1]
            send(part_v.at[3, b_rows], side_v.at[3], N_RIGHT_B, left)

    add_core(3)
    my_row = piece_row(c, x)
    arrive(side_v.at[2], N_RIGHT_A)
    arrive(side_v.at[0], N_LEFT_A)
    proj[pl.ds(my_row, PART), :] = part_v[7, a_rows] + (side_v[0] + side_v[2])
    arrive(side_v.at[1], N_LEFT_B)
    arrive(side_v.at[3], N_RIGHT_B)
    proj[pl.ds(my_row + PART, PART), :] = part_v[7, b_rows] + (side_v[1] + side_v[3])

    def part_of(core, chip, b):
        return proj.at[pl.ds(pl.multiple_of(piece_row(core, chip) + b * PART, 16), PART)]

    def whole_of(core, chip):
        return proj.at[pl.ds(piece_row(core, chip), PIECE)]

    def send_part(chip, b, number, device):
        send(part_of(c, chip, b), part_of(c, chip, b), number, device)

    def send_whole(chip, number):
        send(whole_of(c, chip), whole_of(c, chip), number, twin)

    xl, xr, xo = (x + 3) % 4, (x + 1) % 4, (x + 2) % 4
    send_part(x, 0, G_LEFT_A, right)
    send_part(x, 1, G_RIGHT_B, left)
    send_whole(x, G_CORE)
    send_part(x, 1, G_LEFT_B, right)
    send_part(x, 0, G_RIGHT_A, left)

    half_cols = pl.ds(pl.multiple_of(c * 128, 128), 128)

    def eight(row):
        return pl.ds(pl.multiple_of(row * 8, 8), 8)

    def gram_start():
        halves = []
        for core in range(2):
            rows = pl.ds(piece_row(core, x), PIECE)
            a, b, d = split3(proj[rows, half_cols])
            left = jnp.concatenate([a, a, b, a, b, d], axis=0)
            a, b, d = split3(proj[rows, :])
            halves.append(tn(left, jnp.concatenate([a, b, a, d, b, a], axis=0)))
        gram_part[...] = halves[0] + halves[1]

        @pl.loop(1, 16)
        def _(d):
            to = (f + d) % 16
            send(gram_part.at[eight(to)], gram_in.at[d], GRAM_SUM + d - 1, f_dev(to))

    def gram_across():
        gram_in[0] = gram_part[eight(f), :]

        @pl.loop(1, 16)
        def _(d):
            arrive(gram_in.at[d], GRAM_SUM + d - 1)

        gram_x[x] = jnp.sum(gram_in[...], axis=0)

        @pl.loop(1, 4)
        def _(d):
            send(gram_x.at[x], gram_x.at[x], GRAM_X + d - 1, tp_dev((x + d) % 4, c))

    def gram_row(ff):
        return pl.ds(pl.multiple_of(c * 128 + ff * 8, 8), 8)

    def gram_round():
        @pl.loop(1, 4)
        def _(d):
            arrive(gram_x.at[(x + 4 - d) % 4], GRAM_X + d - 1)

        gram[gram_row(f), :] = (gram_x[0] + gram_x[1]) + (gram_x[2] + gram_x[3])

        @pl.loop(1, 16)
        def _(d):
            mine = gram.at[gram_row(f)]
            send(mine, mine, GRAM_ALL + d - 1, f_dev((f + d) % 16))

    def gram_half(core):
        return gram.at[pl.ds(pl.multiple_of(core * 128, 128), 128)]

    def gram_pair():
        @pl.loop(1, 16)
        def _(d):
            arrive(gram.at[gram_row((f + 16 - d) % 16)], GRAM_ALL + d - 1)

        send(gram_half(c), gram_half(c), GRAM_CORE, twin)

    w[...] = jnp.zeros_like(w)

    @pl.loop(0, 8)
    def _(g):
        core = (c + pick(g, (0, 1, 0, 0, 0, 1, 1, 1))) % 2
        chip = (x + pick(g, (0, 0, 1, 3, 2, 1, 3, 2))) % 4

        @pl.when(g == 1)
        def _():
            arrive(whole_of(1 - c, x), G_CORE)
            gram_start()

        @pl.when(g == 2)
        def _():
            arrive(part_of(c, xl, 0), G_LEFT_A)
            send_part(xl, 0, G_OPP_A, right)
            arrive(part_of(c, xr, 1), G_RIGHT_B)
            send_part(xr, 1, G_OPP_B, left)
            gram_across()
            arrive(part_of(c, xr, 0), G_RIGHT_A)
            send_whole(xr, G_CORE + 1)
            arrive(part_of(c, xl, 1), G_LEFT_B)
            send_whole(xl, G_CORE + 2)

        @pl.when(g == 4)
        def _():
            arrive(part_of(c, xo, 0), G_OPP_A)
            arrive(part_of(c, xo, 1), G_OPP_B)
            send_whole(xo, G_CORE + 3)
            gram_round()

        @pl.when(g == 5)
        def _():
            arrive(whole_of(1 - c, xr), G_CORE + 1)

        @pl.when(g == 6)
        def _():
            arrive(whole_of(1 - c, xl), G_CORE + 2)

        @pl.when(g == 7)
        def _():
            arrive(whole_of(1 - c, xo), G_CORE + 3)

        rows = pl.ds(piece_row(core, chip), PIECE)
        p_hi, p_lo = split(proj[rows, :].T)
        turned[:, :PIECE] = p_hi
        turned[:, 256 : 256 + PIECE] = p_hi
        turned[:, 512 : 512 + PIECE] = p_lo
        more = pl.ds(piece_row(core, chip), 256)
        for n in range(4):
            cols = slice(256 * n, 256 * n + 256)
            hi = hi_v[more, cols]
            w[:, cols] += nn(turned[...], jnp.concatenate([hi, lo_v[more, cols], hi], axis=0))

    def places(u):
        k, q = y + u * (z - y), z + u * (y - z)

        def first(kk):
            return f_dev(z * 4 + kk + u * (kk * 4 + y - z * 4 - kk))

        def second(qq):
            return f_dev(qq * 4 + y + u * (z * 4 + qq - qq * 4 - y))

        return k, q, first, second

    def cols_ab(u):
        start = pl.multiple_of(WIDE * u, WIDE)
        return pl.ds(start, 256), pl.ds(pl.multiple_of(start + 256, 256), 256)

    def cols_u(u):
        return pl.ds(pl.multiple_of(WIDE * u, WIDE), WIDE)

    def rows32(h, k):
        return pl.ds(pl.multiple_of(128 * h + 32 * k, 32), 32)

    def rows8(h, k, q):
        return pl.ds(pl.multiple_of(128 * h + 32 * k + 8 * q, 8), 8)

    def w_step_1(h, u):
        k, q, first, _ = places(u)
        ca, cb = cols_ab(u)
        i = 2 * h + u
        kr, kl, ko = (k + 1) % 4, (k + 3) % 4, (k + 2) % 4
        send(w.at[rows32(h, ko), ca], w_hop.at[2 * i], W_HOP + 2 * i, first(kr))
        send(w.at[rows32(h, ko), cb], w_hop.at[2 * i + 1], W_HOP + 2 * i + 1, first(kl))
        send(w.at[rows32(h, kr), cb], w_side.at[4 * i + 1], W_NEXT + 4 * i + 1, first(kr))
        send(w.at[rows32(h, kl), ca], w_side.at[4 * i + 2], W_NEXT + 4 * i + 2, first(kl))

    def w_step_2(h, u):
        k, q, first, _ = places(u)
        ca, cb = cols_ab(u)
        i = 2 * h + u
        kr, kl = (k + 1) % 4, (k + 3) % 4
        arrive(w_hop.at[2 * i], W_HOP + 2 * i)
        w[rows32(h, kr), ca] += w_hop[2 * i]
        send(w.at[rows32(h, kr), ca], w_side.at[4 * i], W_NEXT + 4 * i, first(kr))
        arrive(w_hop.at[2 * i + 1], W_HOP + 2 * i + 1)
        w[rows32(h, kl), cb] += w_hop[2 * i + 1]
        send(w.at[rows32(h, kl), cb], w_side.at[4 * i + 3], W_NEXT + 4 * i + 3, first(kl))

    def w_step_3(h, u):
        k, q, _, second = places(u)
        ca, cb = cols_ab(u)
        i = 2 * h + u
        for s in range(4):
            arrive(w_side.at[4 * i + s], W_NEXT + 4 * i + s)
        w[rows32(h, k), ca] += w_side[4 * i] + w_side[4 * i + 2]
        w[rows32(h, k), cb] += w_side[4 * i + 1] + w_side[4 * i + 3]

        @pl.loop(1, 4)
        def _(d):
            to, slot = (q + d) % 4, 3 * i + d - 1
            send(w.at[rows8(h, k, to), cols_u(u)], w_sub.at[slot], W_SUB + slot, second(to))

    def w_step_4(h, u):
        k, q, _, second = places(u)
        i = 2 * h + u

        @pl.loop(0, 3)
        def _(d):
            arrive(w_sub.at[3 * i + d], W_SUB + 3 * i + d)

        w_full[rows8(h, k, q), cols_u(u)] = (w[rows8(h, k, q), cols_u(u)] + w_sub[3 * i]) + (
            w_sub[3 * i + 1] + w_sub[3 * i + 2]
        )

        @pl.loop(1, 4)
        def _(d):
            mine = w_full.at[rows8(h, k, q), cols_u(u)]
            send(mine, mine, W_ALL + 3 * i + d - 1, second((q + d) % 4))

    def w_step_5(h, u):
        k, q, first, _ = places(u)
        ca, cb = cols_ab(u)
        i = 2 * h + u
        dr, dl = first((k + 1) % 4), first((k + 3) % 4)

        @pl.loop(1, 4)
        def _(d):
            arrive(w_full.at[rows8(h, k, (q + 4 - d) % 4), cols_u(u)], W_ALL + 3 * i + d - 1)

        mine_a, mine_b = w_full.at[rows32(h, k), ca], w_full.at[rows32(h, k), cb]
        send(mine_a, mine_a, W_RING + 4 * i, dr)
        send(mine_b, mine_b, W_RING + 4 * i + 3, dl)
        send(mine_b, mine_b, W_RING + 4 * i + 1, dr)
        send(mine_a, mine_a, W_RING + 4 * i + 2, dl)

    def w_step_6(h, u):
        k, q, first, _ = places(u)
        ca, cb = cols_ab(u)
        i = 2 * h + u
        kr, kl = (k + 1) % 4, (k + 3) % 4
        from_left = w_full.at[rows32(h, kl), ca]
        arrive(from_left, W_RING + 4 * i)
        send(from_left, from_left, W_FAR + 2 * i, first(kr))
        from_right = w_full.at[rows32(h, kr), cb]
        arrive(from_right, W_RING + 4 * i + 3)
        send(from_right, from_right, W_FAR + 2 * i + 1, first(kl))

    def w_step_7(h, u):
        k = places(u)[0]
        ca, cb = cols_ab(u)
        i = 2 * h + u
        kr, kl, ko = (k + 1) % 4, (k + 3) % 4, (k + 2) % 4
        arrive(w_full.at[rows32(h, kl), cb], W_RING + 4 * i + 1)
        arrive(w_full.at[rows32(h, kr), ca], W_RING + 4 * i + 2)
        arrive(w_full.at[rows32(h, ko), ca], W_FAR + 2 * i)
        arrive(w_full.at[rows32(h, ko), cb], W_FAR + 2 * i + 1)

    def all_parts(step):
        @pl.loop(0, 4)
        def _(i):
            step(i // 2, i % 2)

    all_parts(w_step_1)
    gram_pair()
    all_parts(w_step_2)
    w_steps_at = (w_step_3, None, w_step_4, None, w_step_5, None, w_step_6, w_step_7)

    arrive(gram_half(1 - c), GRAM_CORE)
    elim[:, :RANK] = gram[...]
    rr = lax.broadcasted_iota(jnp.int32, (RANK, RANK), 0)
    cc = lax.broadcasted_iota(jnp.int32, (RANK, RANK), 1)
    elim[:, RANK:] = jnp.where(rr == cc, 1.0, 0.0).astype(F32)

    for half in range(2):

        @pl.loop(4 * half, 4 * half + 4)
        def _(k):
            eliminate(k, half, elim)
            for at in range(4 * half, 4 * half + 4):
                if w_steps_at[at] is not None:

                    @pl.when(k == at)
                    def _():
                        all_parts(w_steps_at[at])

    f_hi, f_lo = split(elim[:, RANK:])
    factor = jnp.concatenate([f_hi, f_hi, f_lo], axis=1)
    squares = jnp.zeros((RANK, 128), F32)
    for n in range(4):
        cols = slice(256 * n, 256 * n + 256)
        w_hi, w_lo = split(w_full[:, cols])
        back = nn(factor, jnp.concatenate([w_hi, w_lo, w_hi], axis=0))
        back_out[:, cols] = back
        squares = squares + (back[:, :128] * back[:, :128] + back[:, 128:] * back[:, 128:])
    sq_v[t] = nt(jnp.ones((8, 128), F32), squares, HIGH)

    @pl.loop(1, 8)
    def _(d):
        send(sq_v.at[t], sq_v.at[t], SQ + d - 1, {"fsdp": f, "tp": (t + d) % 8})


    t_hi, t_lo = split(elim[:, RANK:].T)
    turned[:, :256] = t_hi
    turned[:, 256:512] = t_lo

    @pl.loop(0, LOCAL_ROWS // STEP)
    def _(i):
        rows = pl.ds(pl.multiple_of(i * STEP, 64), STEP)
        hi, lo = split(proj[rows, :])
        first, second = turned[:, :256], turned[:, 256:512]
        ortho_out[rows, :] = nn(hi, first) + nn(hi, second) + nn(lo, first)

    all_sent(N_HOP_A, 12, side_v.at[0])
    all_sent(N_CORE, 8, part_v.at[0])
    all_sent(GRAM_SUM, 33, sq_v.at[0])
    all_sent(GRAM_CORE, 1, gram_part)
    all_sent(W_HOP, 48, w_hop.at[0])
    all_sent(W_SUB, 24, w_sub.at[0])

    @pl.loop(1, 8)
    def _(d):
        arrive(sq_v.at[(t + 8 - d) % 8], SQ + d - 1)

    norm_out[...] = lax.rsqrt(jnp.sum(sq_v[...], axis=0) + 1e-06)
    all_sent(SQ, 7, sq_v.at[0])


def write_kernel(
    blend, ortho, back, norm, mom_out, basis_out, update_out, backs, mom_v, basis_v, update_v, sems
):
    hi, lo = split(back[...])
    backs[:RANK] = hi
    backs[RANK : 2 * RANK] = lo
    backs[2 * RANK :] = hi
    scale = (ROWS * COLS / RANK) ** 0.5
    norms = norm[0:1, :]

    def copies(i):
        slot = i % 2
        found = []
        for p in range(2):
            rows = pl.ds(pl.multiple_of(i * STEP + p * PIECE, 32), PIECE)
            here = pl.ds(p * PIECE, PIECE)
            found.append(pltpu.make_async_copy(mom_v.at[slot, here], mom_out.at[rows], sems.at[slot, p]))
            found.append(
                pltpu.make_async_copy(update_v.at[slot, here], update_out.at[rows], sems.at[slot, 2 + p])
            )
        rank_rows = pl.ds(pl.multiple_of(i * 256, 256), 256)
        found.append(pltpu.make_async_copy(basis_v.at[slot], basis_out.at[rank_rows], sems.at[slot, 4]))
        return found

    @pl.loop(0, LOCAL_ROWS // STEP)
    def _(i):
        slot = i % 2

        @pl.when(i >= 2)
        def _():
            for copy in copies(i - 2):
                copy.wait()

        rows = pl.ds(pl.multiple_of(i * STEP, 64), STEP)
        cols = pl.ds(pl.multiple_of(i * 256, 256), 256)
        basis_v[slot] = back[:, cols].T * norms
        plain = ortho[rows, :]
        mom_v[slot] = blend[rows, :] - nn((0.05 * plain).astype(BF16), backs[:RANK])
        mom_a, update_a, mom_b, update_b, basis_copy = copies(i)
        mom_a.start()
        mom_b.start(priority=1)
        basis_copy.start()
        hi, lo = split(plain * (scale * norms))
        update_v[slot] = nn(jnp.concatenate([hi, hi, lo], axis=1), backs[...]).astype(BF16)
        update_a.start()
        update_b.start(priority=1)

    for i in (2, 3):
        for copy in copies(i):
            copy.wait()


def body(gradient, momentum, basis):
    anywhere = pl.BlockSpec(memory_space=pl.ANY)
    inside = pl.BlockSpec(memory_space=pltpu.VMEM)
    vmem = pltpu.VMEM
    fixed = [pltpu.with_memory_space_constraint(a, pltpu.HBM) for a in (gradient, momentum, basis)]
    results = pl.pallas_call(
        main_kernel,
        out_shape=(
            vmem((LOCAL_ROWS, LOCAL_COLS), F32),
            vmem((LOCAL_ROWS, RANK), F32),
            vmem((RANK, LOCAL_COLS), F32),
            vmem((8, RANK), F32),
        ),
        in_specs=[anywhere] * 3,
        out_specs=(inside,) * 4,
        scratch_shapes=[
            vmem((4, PIECE, LOCAL_COLS), BF16),
            vmem((LOCAL_COLS, RANK), F32),
            vmem((2 * LOCAL_COLS, RANK), BF16),
            vmem((LOCAL_ROWS + 32, LOCAL_COLS), BF16),
            vmem((LOCAL_ROWS + 32, LOCAL_COLS), BF16),
            vmem((8, PIECE, RANK), F32),
            vmem((4, PIECE, RANK), F32),
            vmem((2, PART, RANK), F32),
            vmem((4, PART, RANK), F32),
            vmem((LOCAL_ROWS, RANK), F32),
            vmem((128, RANK), F32),
            vmem((16, 8, RANK), F32),
            vmem((4, 8, RANK), F32),
            vmem((RANK, RANK), F32),
            vmem((RANK, 2 * RANK), F32),
            vmem((RANK, 3 * 256), BF16),
            vmem((RANK, LOCAL_COLS), F32),
            vmem((8, 32, 256), F32),
            vmem((16, 32, 256), F32),
            vmem((12, 8, WIDE), F32),
            vmem((RANK, LOCAL_COLS), F32),
            vmem((8, 8, RANK), F32),
            pltpu.SemaphoreType.DMA((17,)),
            pltpu.SemaphoreType.DMA((NAMES.count,)),
            pltpu.SemaphoreType.DMA((NAMES.count,)),
        ],
        compiler_params=pltpu.CompilerParams(
            collective_id=0, has_side_effects=True, vmem_limit_bytes=44 * 2**20
        ),
        name="transfers",
    )(*fixed)
    results = [pltpu.with_memory_space_constraint(a, pltpu.VMEM) for a in results]

    return pl.pallas_call(
        write_kernel,
        out_shape=(
            jax.ShapeDtypeStruct((LOCAL_ROWS, LOCAL_COLS), F32),
            jax.ShapeDtypeStruct((LOCAL_COLS, RANK), F32),
            jax.ShapeDtypeStruct((LOCAL_ROWS, LOCAL_COLS), BF16),
        ),
        in_specs=[inside] * 4,
        out_specs=(anywhere,) * 3,
        scratch_shapes=[
            vmem((3 * RANK, LOCAL_COLS), BF16),
            vmem((2, STEP, LOCAL_COLS), F32),
            vmem((2, 256, RANK), F32),
            vmem((2, STEP, LOCAL_COLS), BF16),
            pltpu.SemaphoreType.DMA((2, 5)),
        ],
        compiler_params=pltpu.CompilerParams(vmem_limit_bytes=32 * 2**20),
        name="outputs",
    )(*results)


def solution(mesh):
    placed = (P("fsdp", "tp"), P("fsdp", "tp"), P("tp", None))
    return jax.shard_map(
        body,
        mesh=mesh,
        in_specs=placed,
        out_specs=(P("fsdp", "tp"), P("tp", None), P("fsdp", "tp")),
        check_vma=False,
    )
```

```python
import functools

import jax
import jax.numpy as jnp
from jax import lax
from jax.experimental import pallas as pl
from jax.experimental.pallas import tpu as pltpu
from jax.sharding import PartitionSpec as P

ROWS = 28672
COLS = 8192
RANK = 256

F32 = jnp.float32
BF16 = jnp.bfloat16
HIGH = lax.Precision.HIGHEST
MESH = pl.DeviceIdType.MESH

LOCAL_ROWS = 1792
LOCAL_COLS = 1024
HALF = 896
PIECE = 224
PART = 112
STEP = 448
WIDE = 512


class Names:
    def __init__(self):
        self.count = 0

    def take(self, many=1):
        first = self.count
        self.count += many
        return first


NAMES = Names()
N_HOP_A, N_HOP_B = NAMES.take(), NAMES.take()
N_LEFT_A, N_LEFT_B = NAMES.take(), NAMES.take()
N_RIGHT_A, N_RIGHT_B = NAMES.take(), NAMES.take()
G_LEFT_A, G_LEFT_B = NAMES.take(), NAMES.take()
G_RIGHT_A, G_RIGHT_B = NAMES.take(), NAMES.take()
G_OPP_A, G_OPP_B = NAMES.take(), NAMES.take()
N_CORE = NAMES.take(4)
G_CORE = NAMES.take(4)
GRAM_SUM = NAMES.take(15)
GRAM_X = NAMES.take(3)
GRAM_ALL = NAMES.take(15)
SQ = NAMES.take(7)
GRAM_CORE = NAMES.take()
W_HOP = NAMES.take(4)
W_NEXT = NAMES.take(8)
W_RING = NAMES.take(8)
W_FAR = NAMES.take(4)
W_SUB = NAMES.take(6)
W_ALL = NAMES.take(6)


def nn(a, b, precision=None):
    return lax.dot_general(
        a, b, (((1,), (0,)), ((), ())), precision=precision, preferred_element_type=F32
    )


def tn(a, b, precision=None):
    return lax.dot_general(
        a, b, (((0,), (0,)), ((), ())), precision=precision, preferred_element_type=F32
    )


def nt(a, b, precision=None):
    return lax.dot_general(
        a, b, (((1,), (1,)), ((), ())), precision=precision, preferred_element_type=F32
    )


def pick(index, values):
    out = values[0]
    for at in range(1, len(values)):
        out = out + (values[at] - values[at - 1]) * ((index + len(values) - at) // len(values))
    return out


def split(x):
    hi = x.astype(BF16)
    return hi, (x - hi.astype(F32)).astype(BF16)


def row_copy(x, j):
    return jnp.broadcast_to(x[j : j + 1, :], (8, 128))


def inverse_factor(x):
    x = list(x)
    n = len(x)
    sub = lax.broadcasted_iota(jnp.int32, (8, 128), 0)
    for g in range(n):
        lanes = [32 + 8 * g + j for j in range(8)]
        col = {i: [jnp.broadcast_to(x[i][:, at : at + 1], (8, 128)) for at in lanes] for i in range(g, n)}
        entry = [[row_copy(col[g][j], i) for j in range(i + 1)] for i in range(8)]
        rows = [row_copy(x[g], j) for j in range(8)]
        inv, mult = [], [[None] * 8 for _ in range(8)]
        for j in range(8):
            inv.append(1.0 / entry[j][j])
            for k in range(j + 1, 8):
                mult[k][j] = entry[k][j] * inv[j]
                for i in range(k, 8):
                    entry[i][k] = entry[i][k] - entry[i][j] * mult[k][j]
                rows[k] = rows[k] - mult[k][j] * rows[j]
        for i in range(g + 1, n):
            c = col[i]
            for j in range(8):
                for k in range(j + 1, 8):
                    c[k] = c[k] - c[j] * mult[k][j]
                x[i] = x[i] - (c[j] * inv[j]) * rows[j]
        final = jnp.zeros((8, 128), F32)
        for j in range(8):
            final = jnp.where(sub == j, rows[j] * lax.rsqrt(entry[j][j]), final)
        x[g] = final
    return jnp.concatenate(x, axis=0)


def split3(x):
    first = x.astype(BF16)
    rest = x - first.astype(F32)
    second = rest.astype(BF16)
    return first, second, (rest - second.astype(F32)).astype(BF16)


def eliminate(k, half, m_ref):
    left = 128 * half
    cols = slice(left, left + 384)
    rows = pl.ds(pl.multiple_of(32 * k, 32), 32)
    lane = lax.broadcasted_iota(jnp.int32, (32, 128), 1)
    subl = lax.broadcasted_iota(jnp.int32, (32, 128), 0)
    d = pltpu.roll(m_ref[rows, left : left + 128], (160 - 32 * (k % 4)) % 128, 1)
    x = jnp.where(lane < 32, jnp.where(lane == subl, 1.0, 0.0), d)
    inverse = inverse_factor([x[8 * i : 8 * i + 8] for i in range(4)])
    scaled = nn(inverse[:, :32], m_ref[rows, cols], HIGH)
    m_ref[rows, cols] = scaled

    @pl.when(k < 7)
    def _():
        lane = lax.broadcasted_iota(jnp.int32, (32, RANK - left), 1)
        lower = jnp.where(lane >= 32 * k + 32 - left, scaled[:, : RANK - left], 0.0)
        a, b, c = split3(lower)
        d, e, f = split3(scaled)
        m_ref[left:, cols] -= tn(
            jnp.concatenate([a, a, b, a, b, c], axis=0), jnp.concatenate([d, e, d, f, e, d], axis=0)
        )


def main_kernel(
    grad,
    mom,
    basis,
    blend_out,
    ortho_out,
    back_out,
    norm_out,
    grad_v,
    basis_v,
    bases,
    hi_v,
    lo_v,
    part_v,
    from_core,
    hop_v,
    side_v,
    proj,
    gram_part,
    gram_in,
    gram_x,
    gram,
    elim,
    turned,
    w,
    w_hop,
    w_side,
    w_sub,
    w_full,
    sq_v,
    load_sem,
    send_sem,
    recv_sem,
):
    f = lax.axis_index("fsdp")
    t = lax.axis_index("tp")
    x, c = t // 2, t % 2
    z, y = f // 4, f % 4

    def tp_dev(xx, cc):
        return {"fsdp": f, "tp": xx * 2 + cc}

    def f_dev(ff):
        return {"fsdp": ff, "tp": t}

    right = tp_dev((x + 1) % 4, c)
    left = tp_dev((x + 3) % 4, c)
    twin = tp_dev(x, 1 - c)

    def remote(src, dst, number, device):
        return pltpu.make_async_remote_copy(
            src_ref=src,
            dst_ref=dst,
            send_sem=send_sem.at[number],
            recv_sem=recv_sem.at[number],
            device_id=device,
            device_id_type=MESH,
        )

    def send(src, dst, number, device):
        remote(src, dst, number, device).start()

    def arrive(dst, number):
        remote(dst, dst, number, twin).wait_recv()

    def all_sent(first, many, ref):
        @pl.loop(first, first + many)
        def _(number):
            remote(ref, ref, number, twin).wait_send()

    def piece_row(core, chip):
        return pl.multiple_of(core * HALF + chip * PIECE, 32)

    def chunk_row(i):
        g = 3 - i // 2
        d = g + (g // 2) * (1 - 2 * (g % 2))
        core = (1 - c) * (1 - i % 2) + c * (i % 2)
        return piece_row(core, (x + d) % 4)

    def load(i):
        rows = pl.ds(chunk_row(i), PIECE)
        return (
            pltpu.make_async_copy(mom.at[rows], blend_out.at[rows], load_sem.at[2 * i]),
            pltpu.make_async_copy(grad.at[rows], grad_v.at[i % 4], load_sem.at[2 * i + 1]),
        )

    basis_copy = pltpu.make_async_copy(basis, basis_v, load_sem.at[16])
    basis_copy.start()

    @pl.loop(0, 3)
    def _(i):
        for copy in load(i):
            copy.start()

    barrier = pltpu.get_barrier_semaphore()

    @pl.loop(1, 16)
    def _(d):
        pl.semaphore_signal(barrier, inc=1, device_id=f_dev((f + d) % 16), device_id_type=MESH)

    @pl.loop(1, 8)
    def _(d):
        pl.semaphore_signal(
            barrier, inc=1, device_id={"fsdp": f, "tp": (t + d) % 8}, device_id_type=MESH
        )

    basis_copy.wait()
    basis_hi, basis_lo = split(basis_v[...])
    bases[:LOCAL_COLS] = basis_hi
    bases[LOCAL_COLS:] = basis_lo
    turned[...] = jnp.zeros_like(turned)
    hi_v[LOCAL_ROWS:, :] = jnp.zeros((32, LOCAL_COLS), BF16)
    lo_v[LOCAL_ROWS:, :] = jnp.zeros((32, LOCAL_COLS), BF16)

    def partial(i):
        for copy in load(i):
            copy.wait()
        rows = pl.ds(chunk_row(i), PIECE)

        @pl.when(i < 5)
        def _():
            for copy in load(i + 3):
                copy.start()

        blend = blend_out[rows, :] + grad_v[i % 4].astype(F32)
        blend_out[rows, :] = blend
        hi, lo = split(blend)
        hi_v[rows, :] = hi
        lo_v[rows, :] = lo
        first, second = bases[:LOCAL_COLS], bases[LOCAL_COLS:]
        return nn(hi, first) + nn(hi, second) + nn(lo, first)

    a_rows, b_rows = pl.ds(0, PART), pl.ds(PART, PART)

    def add_core(j):
        arrive(from_core.at[j], N_CORE + j)
        part_v[2 * j + 1] += from_core[j]

    @pl.loop(0, 8)
    def _(i):
        part_v[i] = partial(i)
        j = i // 2
        core = remote(part_v.at[i], from_core.at[j], N_CORE + j, twin)

        @pl.when(i == 0)
        def _():
            pl.semaphore_wait(barrier, 22)

        @pl.when(i % 2 == 0)
        def _():
            core.start()

        @pl.when(i == 2)
        def _():
            add_core(0)
            send(part_v.at[1, a_rows], hop_v.at[0], N_HOP_A, right)
            send(part_v.at[1, b_rows], hop_v.at[1], N_HOP_B, left)

        @pl.when(i == 4)
        def _():
            add_core(1)
            send(part_v.at[3, a_rows], side_v.at[2], N_RIGHT_A, left)

        @pl.when(i == 6)
        def _():
            add_core(2)
            send(part_v.at[5, b_rows], side_v.at[1], N_LEFT_B, right)
            arrive(hop_v.at[0], N_HOP_A)
            part_v[5, a_rows] += hop_v[0]
            send(part_v.at[5, a_rows], side_v.at[0], N_LEFT_A, right)
            arrive(hop_v.at[1], N_HOP_B)
            part_v[3, b_rows] += hop_v[1]
            send(part_v.at[3, b_rows], side_v.at[3], N_RIGHT_B, left)

    add_core(3)
    my_row = piece_row(c, x)
    arrive(side_v.at[2], N_RIGHT_A)
    arrive(side_v.at[0], N_LEFT_A)
    proj[pl.ds(my_row, PART), :] = part_v[7, a_rows] + (side_v[0] + side_v[2])
    arrive(side_v.at[1], N_LEFT_B)
    arrive(side_v.at[3], N_RIGHT_B)
    proj[pl.ds(my_row + PART, PART), :] = part_v[7, b_rows] + (side_v[1] + side_v[3])

    def part_of(core, chip, b):
        return proj.at[pl.ds(pl.multiple_of(piece_row(core, chip) + b * PART, 16), PART)]

    def whole_of(core, chip):
        return proj.at[pl.ds(piece_row(core, chip), PIECE)]

    def send_part(chip, b, number, device):
        send(part_of(c, chip, b), part_of(c, chip, b), number, device)

    def send_whole(chip, number):
        send(whole_of(c, chip), whole_of(c, chip), number, twin)

    xl, xr, xo = (x + 3) % 4, (x + 1) % 4, (x + 2) % 4
    send_part(x, 0, G_LEFT_A, right)
    send_part(x, 1, G_RIGHT_B, left)
    send_whole(x, G_CORE)
    send_part(x, 1, G_LEFT_B, right)
    send_part(x, 0, G_RIGHT_A, left)

    half_cols = pl.ds(pl.multiple_of(c * 128, 128), 128)

    def eight(row):
        return pl.ds(pl.multiple_of(row * 8, 8), 8)

    def gram_start():
        left, right = [], []
        for core in range(2):
            rows = pl.ds(piece_row(core, x), PIECE)
            a, b, d = split3(proj[rows, half_cols])
            left += [a, a, b, a, b, d]
            a, b, d = split3(proj[rows, :])
            right += [a, b, a, d, b, a]
        gram_part[...] = tn(jnp.concatenate(left, axis=0), jnp.concatenate(right, axis=0))

        @pl.loop(1, 16)
        def _(d):
            to = (f + d) % 16
            send(gram_part.at[eight(to)], gram_in.at[d], GRAM_SUM + d - 1, f_dev(to))

    def gram_across():
        gram_in[0] = gram_part[eight(f), :]

        @pl.loop(1, 16)
        def _(d):
            arrive(gram_in.at[d], GRAM_SUM + d - 1)

        gram_x[x] = jnp.sum(gram_in[...], axis=0)

        @pl.loop(1, 4)
        def _(d):
            send(gram_x.at[x], gram_x.at[x], GRAM_X + d - 1, tp_dev((x + d) % 4, c))

    def gram_row(ff):
        return pl.ds(pl.multiple_of(c * 128 + ff * 8, 8), 8)

    def gram_round():
        @pl.loop(1, 4)
        def _(d):
            arrive(gram_x.at[(x + 4 - d) % 4], GRAM_X + d - 1)

        gram[gram_row(f), :] = (gram_x[0] + gram_x[1]) + (gram_x[2] + gram_x[3])

        @pl.loop(1, 16)
        def _(d):
            mine = gram.at[gram_row(f)]
            send(mine, mine, GRAM_ALL + d - 1, f_dev((f + d) % 16))

    def gram_half(core):
        return gram.at[pl.ds(pl.multiple_of(core * 128, 128), 128)]

    def gram_pair():
        @pl.loop(1, 16)
        def _(d):
            arrive(gram.at[gram_row((f + 16 - d) % 16)], GRAM_ALL + d - 1)

        send(gram_half(c), gram_half(c), GRAM_CORE, twin)

    w[...] = jnp.zeros_like(w)

    @pl.loop(0, 8)
    def _(g):
        core = (c + pick(g, (0, 1, 0, 0, 0, 1, 1, 1))) % 2
        chip = (x + pick(g, (0, 0, 1, 3, 2, 1, 3, 2))) % 4

        @pl.when(g == 1)
        def _():
            arrive(whole_of(1 - c, x), G_CORE)
            gram_start()

        @pl.when(g == 2)
        def _():
            arrive(part_of(c, xl, 0), G_LEFT_A)
            send_part(xl, 0, G_OPP_A, right)
            arrive(part_of(c, xr, 1), G_RIGHT_B)
            send_part(xr, 1, G_OPP_B, left)
            arrive(part_of(c, xr, 0), G_RIGHT_A)
            send_whole(xr, G_CORE + 1)
            arrive(part_of(c, xl, 1), G_LEFT_B)
            send_whole(xl, G_CORE + 2)

        @pl.when(g == 3)
        def _():
            gram_across()

        @pl.when(g == 4)
        def _():
            arrive(part_of(c, xo, 0), G_OPP_A)
            arrive(part_of(c, xo, 1), G_OPP_B)
            send_whole(xo, G_CORE + 3)

        @pl.when(g == 5)
        def _():
            arrive(whole_of(1 - c, xr), G_CORE + 1)

        @pl.when(g == 6)
        def _():
            gram_round()
            arrive(whole_of(1 - c, xl), G_CORE + 2)

        @pl.when(g == 7)
        def _():
            arrive(whole_of(1 - c, xo), G_CORE + 3)

        rows = pl.ds(piece_row(core, chip), PIECE)
        p_hi, p_lo = split(proj[rows, :].T)
        turned[:, :PIECE] = p_hi
        turned[:, 256 : 256 + PIECE] = p_hi
        turned[:, 512 : 512 + PIECE] = p_lo
        more = pl.ds(piece_row(core, chip), 256)
        for n in range(4):
            cols = slice(256 * n, 256 * n + 256)
            hi = hi_v[more, cols]
            w[:, cols] += nn(turned[...], jnp.concatenate([hi, lo_v[more, cols], hi], axis=0))

    def places(h):
        k, q = y + h * (z - y), z + h * (y - z)

        def first(kk):
            return f_dev(z * 4 + kk + h * (kk * 4 + y - z * 4 - kk))

        def second(qq):
            return f_dev(qq * 4 + y + h * (z * 4 + qq - qq * 4 - y))

        return k, q, first, second

    ca, cb = pl.ds(0, WIDE), pl.ds(WIDE, WIDE)

    def rows32(h, k):
        return pl.ds(pl.multiple_of(128 * h + 32 * k, 32), 32)

    def rows8(h, k, q):
        return pl.ds(pl.multiple_of(128 * h + 32 * k + 8 * q, 8), 8)

    def w_step_1(h):
        k, q, first, _ = places(h)
        kr, kl, ko = (k + 1) % 4, (k + 3) % 4, (k + 2) % 4
        send(w.at[rows32(h, ko), ca], w_hop.at[2 * h], W_HOP + 2 * h, first(kr))
        send(w.at[rows32(h, ko), cb], w_hop.at[2 * h + 1], W_HOP + 2 * h + 1, first(kl))

    def w_step_1b(h):
        k, q, first, _ = places(h)
        kr, kl = (k + 1) % 4, (k + 3) % 4
        send(w.at[rows32(h, kr), cb], w_side.at[4 * h + 1], W_NEXT + 4 * h + 1, first(kr))
        send(w.at[rows32(h, kl), ca], w_side.at[4 * h + 2], W_NEXT + 4 * h + 2, first(kl))

    def w_step_2(h):
        k, q, first, _ = places(h)
        kr, kl = (k + 1) % 4, (k + 3) % 4
        arrive(w_hop.at[2 * h], W_HOP + 2 * h)
        w[rows32(h, kr), ca] += w_hop[2 * h]
        send(w.at[rows32(h, kr), ca], w_side.at[4 * h], W_NEXT + 4 * h, first(kr))
        arrive(w_hop.at[2 * h + 1], W_HOP + 2 * h + 1)
        w[rows32(h, kl), cb] += w_hop[2 * h + 1]
        send(w.at[rows32(h, kl), cb], w_side.at[4 * h + 3], W_NEXT + 4 * h + 3, first(kl))

    def w_step_3(h):
        k, q, _, second = places(h)
        for s in range(4):
            arrive(w_side.at[4 * h + s], W_NEXT + 4 * h + s)
        w[rows32(h, k), ca] += w_side[4 * h] + w_side[4 * h + 2]
        w[rows32(h, k), cb] += w_side[4 * h + 1] + w_side[4 * h + 3]

        @pl.loop(1, 4)
        def _(d):
            to, slot = (q + d) % 4, 3 * h + d - 1
            send(w.at[rows8(h, k, to)], w_sub.at[slot], W_SUB + slot, second(to))

    def w_step_4(h):
        k, q, _, second = places(h)

        @pl.loop(0, 3)
        def _(d):
            arrive(w_sub.at[3 * h + d], W_SUB + 3 * h + d)

        w_full[rows8(h, k, q), :] = (w[rows8(h, k, q), :] + w_sub[3 * h]) + (
            w_sub[3 * h + 1] + w_sub[3 * h + 2]
        )

        @pl.loop(1, 4)
        def _(d):
            mine = w_full.at[rows8(h, k, q)]
            send(mine, mine, W_ALL + 3 * h + d - 1, second((q + d) % 4))

    def w_step_5(h):
        k, q, first, _ = places(h)
        dr, dl = first((k + 1) % 4), first((k + 3) % 4)

        @pl.loop(1, 4)
        def _(d):
            arrive(w_full.at[rows8(h, k, (q + 4 - d) % 4)], W_ALL + 3 * h + d - 1)

        mine_a, mine_b = w_full.at[rows32(h, k), ca], w_full.at[rows32(h, k), cb]
        send(mine_a, mine_a, W_RING + 4 * h, dr)
        send(mine_b, mine_b, W_RING + 4 * h + 3, dl)
        send(mine_b, mine_b, W_RING + 4 * h + 1, dr)
        send(mine_a, mine_a, W_RING + 4 * h + 2, dl)

    def w_step_6(h):
        k, q, first, _ = places(h)
        kr, kl = (k + 1) % 4, (k + 3) % 4
        from_left = w_full.at[rows32(h, kl), ca]
        arrive(from_left, W_RING + 4 * h)
        send(from_left, from_left, W_FAR + 2 * h, first(kr))
        from_right = w_full.at[rows32(h, kr), cb]
        arrive(from_right, W_RING + 4 * h + 3)
        send(from_right, from_right, W_FAR + 2 * h + 1, first(kl))

    def w_step_7(h):
        k = places(h)[0]
        kr, kl, ko = (k + 1) % 4, (k + 3) % 4, (k + 2) % 4
        arrive(w_full.at[rows32(h, kl), cb], W_RING + 4 * h + 1)
        arrive(w_full.at[rows32(h, kr), ca], W_RING + 4 * h + 2)
        arrive(w_full.at[rows32(h, ko), ca], W_FAR + 2 * h)
        arrive(w_full.at[rows32(h, ko), cb], W_FAR + 2 * h + 1)

    def both_halves(step):
        for h in range(2):
            step(h)

    both_halves(w_step_1)
    both_halves(w_step_1b)
    both_halves(w_step_2)
    gram_pair()
    both_halves(w_step_3)
    w_steps_at = (w_step_4, None, w_step_5, None, w_step_6, None, w_step_7, None)

    arrive(gram_half(1 - c), GRAM_CORE)
    elim[:, :RANK] = gram[...]
    rr = lax.broadcasted_iota(jnp.int32, (RANK, RANK), 0)
    cc = lax.broadcasted_iota(jnp.int32, (RANK, RANK), 1)
    elim[:, RANK:] = jnp.where(rr == cc, 1.0, 0.0).astype(F32)

    for half in range(2):

        @pl.loop(4 * half, 4 * half + 4)
        def _(k):
            eliminate(k, half, elim)
            for at in range(4 * half, 4 * half + 4):
                if w_steps_at[at] is not None:

                    @pl.when(k == at)
                    def _():
                        both_halves(w_steps_at[at])

    f_hi, f_lo = split(elim[:, RANK:])
    factor = jnp.concatenate([f_hi, f_hi, f_lo], axis=1)
    squares = jnp.zeros((RANK, 128), F32)
    for n in range(4):
        cols = slice(256 * n, 256 * n + 256)
        w_hi, w_lo = split(w_full[:, cols])
        back = nn(factor, jnp.concatenate([w_hi, w_lo, w_hi], axis=0))
        back_out[:, cols] = back
        squares = squares + (back[:, :128] * back[:, :128] + back[:, 128:] * back[:, 128:])
    sq_v[t] = nt(jnp.ones((8, 128), F32), squares, HIGH)

    @pl.loop(1, 8)
    def _(d):
        send(sq_v.at[t], sq_v.at[t], SQ + d - 1, {"fsdp": f, "tp": (t + d) % 8})


    t_hi, t_lo = split(elim[:, RANK:].T)
    turned[:, :256] = t_hi
    turned[:, 256:512] = t_lo

    @pl.loop(0, LOCAL_ROWS // STEP)
    def _(i):
        rows = pl.ds(pl.multiple_of(i * STEP, 64), STEP)
        hi, lo = split(proj[rows, :])
        first, second = turned[:, :256], turned[:, 256:512]
        ortho_out[rows, :] = nn(hi, first) + nn(hi, second) + nn(lo, first)

    all_sent(N_HOP_A, 12, side_v.at[0])
    all_sent(N_CORE, 8, part_v.at[0])
    all_sent(GRAM_SUM, 33, sq_v.at[0])
    all_sent(GRAM_CORE, 1, gram_part)
    all_sent(W_HOP, 24, w_hop.at[0])
    all_sent(W_SUB, 12, w_sub.at[0])

    @pl.loop(1, 8)
    def _(d):
        arrive(sq_v.at[(t + 8 - d) % 8], SQ + d - 1)

    norm_out[...] = lax.rsqrt(jnp.sum(sq_v[...], axis=0) + 1e-06)
    all_sent(SQ, 7, sq_v.at[0])


def write_kernel(
    blend, ortho, back, norm, mom_out, basis_out, update_out, backs, mom_v, basis_v, update_v, sems
):
    hi, lo = split(back[...])
    backs[:RANK] = hi
    backs[RANK : 2 * RANK] = lo
    backs[2 * RANK :] = hi
    scale = (ROWS * COLS / RANK) ** 0.5
    norms = norm[0:1, :]

    def copies(i):
        slot = i % 2
        found = []
        for p in range(2):
            rows = pl.ds(pl.multiple_of(i * STEP + p * PIECE, 32), PIECE)
            here = pl.ds(p * PIECE, PIECE)
            found.append(pltpu.make_async_copy(mom_v.at[slot, here], mom_out.at[rows], sems.at[slot, p]))
            found.append(
                pltpu.make_async_copy(update_v.at[slot, here], update_out.at[rows], sems.at[slot, 2 + p])
            )
        rank_rows = pl.ds(pl.multiple_of(i * 256, 256), 256)
        found.append(pltpu.make_async_copy(basis_v.at[slot], basis_out.at[rank_rows], sems.at[slot, 4]))
        return found

    @pl.loop(0, LOCAL_ROWS // STEP)
    def _(i):
        slot = i % 2

        @pl.when(i >= 2)
        def _():
            for copy in copies(i - 2):
                copy.wait()

        rows = pl.ds(pl.multiple_of(i * STEP, 64), STEP)
        cols = pl.ds(pl.multiple_of(i * 256, 256), 256)
        basis_v[slot] = back[:, cols].T * norms
        plain = ortho[rows, :]
        mom_v[slot] = blend[rows, :] - nn((0.05 * plain).astype(BF16), backs[:RANK])
        mom_a, update_a, mom_b, update_b, basis_copy = copies(i)
        mom_a.start()
        mom_b.start(priority=1)
        basis_copy.start()
        hi, lo = split(plain * (scale * norms))
        update_v[slot] = nn(jnp.concatenate([hi, hi, lo], axis=1), backs[...]).astype(BF16)
        update_a.start()
        update_b.start(priority=1)

    for i in (2, 3):
        for copy in copies(i):
            copy.wait()


def body(gradient, momentum, basis):
    anywhere = pl.BlockSpec(memory_space=pl.ANY)
    inside = pl.BlockSpec(memory_space=pltpu.VMEM)
    vmem = pltpu.VMEM
    fixed = [pltpu.with_memory_space_constraint(a, pltpu.HBM) for a in (gradient, momentum, basis)]
    results = pl.pallas_call(
        main_kernel,
        out_shape=(
            vmem((LOCAL_ROWS, LOCAL_COLS), F32),
            vmem((LOCAL_ROWS, RANK), F32),
            vmem((RANK, LOCAL_COLS), F32),
            vmem((8, RANK), F32),
        ),
        in_specs=[anywhere] * 3,
        out_specs=(inside,) * 4,
        scratch_shapes=[
            vmem((4, PIECE, LOCAL_COLS), BF16),
            vmem((LOCAL_COLS, RANK), F32),
            vmem((2 * LOCAL_COLS, RANK), BF16),
            vmem((LOCAL_ROWS + 32, LOCAL_COLS), BF16),
            vmem((LOCAL_ROWS + 32, LOCAL_COLS), BF16),
            vmem((8, PIECE, RANK), F32),
            vmem((4, PIECE, RANK), F32),
            vmem((2, PART, RANK), F32),
            vmem((4, PART, RANK), F32),
            vmem((LOCAL_ROWS, RANK), F32),
            vmem((128, RANK), F32),
            vmem((16, 8, RANK), F32),
            vmem((4, 8, RANK), F32),
            vmem((RANK, RANK), F32),
            vmem((RANK, 2 * RANK), F32),
            vmem((RANK, 3 * 256), BF16),
            vmem((RANK, LOCAL_COLS), F32),
            vmem((4, 32, WIDE), F32),
            vmem((8, 32, WIDE), F32),
            vmem((6, 8, LOCAL_COLS), F32),
            vmem((RANK, LOCAL_COLS), F32),
            vmem((8, 8, RANK), F32),
            pltpu.SemaphoreType.DMA((17,)),
            pltpu.SemaphoreType.DMA((NAMES.count,)),
            pltpu.SemaphoreType.DMA((NAMES.count,)),
        ],
        compiler_params=pltpu.CompilerParams(
            collective_id=0, has_side_effects=True, vmem_limit_bytes=44 * 2**20
        ),
        name="transfers",
    )(*fixed)
    results = [pltpu.with_memory_space_constraint(a, pltpu.VMEM) for a in results]

    return pl.pallas_call(
        write_kernel,
        out_shape=(
            jax.ShapeDtypeStruct((LOCAL_ROWS, LOCAL_COLS), F32),
            jax.ShapeDtypeStruct((LOCAL_COLS, RANK), F32),
            jax.ShapeDtypeStruct((LOCAL_ROWS, LOCAL_COLS), BF16),
        ),
        in_specs=[inside] * 4,
        out_specs=(anywhere,) * 3,
        scratch_shapes=[
            vmem((3 * RANK, LOCAL_COLS), BF16),
            vmem((2, STEP, LOCAL_COLS), F32),
            vmem((2, 256, RANK), F32),
            vmem((2, STEP, LOCAL_COLS), BF16),
            pltpu.SemaphoreType.DMA((2, 5)),
        ],
        compiler_params=pltpu.CompilerParams(vmem_limit_bytes=32 * 2**20),
        name="outputs",
    )(*results)


def solution(mesh):
    placed = (P("fsdp", "tp"), P("fsdp", "tp"), P("tp", None))
    return jax.shard_map(
        body,
        mesh=mesh,
        in_specs=placed,
        out_specs=(P("fsdp", "tp"), P("tp", None), P("fsdp", "tp")),
        check_vma=False,
    )
```

```python
import functools

import jax
import jax.numpy as jnp
from jax import lax
from jax.experimental import pallas as pl
from jax.experimental.pallas import tpu as pltpu
from jax.sharding import PartitionSpec as P

ROWS = 28672
COLS = 8192
RANK = 256

F32 = jnp.float32
BF16 = jnp.bfloat16
HIGH = lax.Precision.HIGHEST
MESH = pl.DeviceIdType.MESH

LOCAL_ROWS = 1792
LOCAL_COLS = 1024
HALF = 896
PIECE = 224
PART = 112
STEP = 448
WIDE = 512


class Names:
    def __init__(self):
        self.count = 0

    def take(self, many=1):
        first = self.count
        self.count += many
        return first


NAMES = Names()
N_HOP_A, N_HOP_B = NAMES.take(), NAMES.take()
N_LEFT_A, N_LEFT_B = NAMES.take(), NAMES.take()
N_RIGHT_A, N_RIGHT_B = NAMES.take(), NAMES.take()
G_LEFT_A, G_LEFT_B = NAMES.take(), NAMES.take()
G_RIGHT_A, G_RIGHT_B = NAMES.take(), NAMES.take()
G_OPP_A, G_OPP_B = NAMES.take(), NAMES.take()
N_CORE = NAMES.take(4)
G_CORE = NAMES.take(4)
GRAM_SUM = NAMES.take(15)
GRAM_X = NAMES.take(3)
GRAM_ALL = NAMES.take(15)
SQ = NAMES.take(7)
GRAM_CORE = NAMES.take()
W_HOP = NAMES.take(8)
W_NEXT = NAMES.take(16)
W_RING = NAMES.take(16)
W_FAR = NAMES.take(8)
W_SUB = NAMES.take(12)
W_ALL = NAMES.take(12)


def nn(a, b, precision=None):
    return lax.dot_general(
        a, b, (((1,), (0,)), ((), ())), precision=precision, preferred_element_type=F32
    )


def tn(a, b, precision=None):
    return lax.dot_general(
        a, b, (((0,), (0,)), ((), ())), precision=precision, preferred_element_type=F32
    )


def nt(a, b, precision=None):
    return lax.dot_general(
        a, b, (((1,), (1,)), ((), ())), precision=precision, preferred_element_type=F32
    )


def pick(index, values):
    out = values[0]
    for at in range(1, len(values)):
        out = out + (values[at] - values[at - 1]) * ((index + len(values) - at) // len(values))
    return out


def split(x):
    hi = x.astype(BF16)
    return hi, (x - hi.astype(F32)).astype(BF16)


def row_copy(x, j):
    return jnp.broadcast_to(x[j : j + 1, :], (8, 128))


def inverse_factor(x):
    x = list(x)
    n = len(x)
    sub = lax.broadcasted_iota(jnp.int32, (8, 128), 0)
    for g in range(n):
        lanes = [32 + 8 * g + j for j in range(8)]
        col = {i: [jnp.broadcast_to(x[i][:, at : at + 1], (8, 128)) for at in lanes] for i in range(g, n)}
        entry = [[row_copy(col[g][j], i) for j in range(i + 1)] for i in range(8)]
        rows = [row_copy(x[g], j) for j in range(8)]
        inv, mult = [], [[None] * 8 for _ in range(8)]
        for j in range(8):
            inv.append(1.0 / entry[j][j])
            for k in range(j + 1, 8):
                mult[k][j] = entry[k][j] * inv[j]
                for i in range(k, 8):
                    entry[i][k] = entry[i][k] - entry[i][j] * mult[k][j]
                rows[k] = rows[k] - mult[k][j] * rows[j]
        for i in range(g + 1, n):
            c = col[i]
            for j in range(8):
                for k in range(j + 1, 8):
                    c[k] = c[k] - c[j] * mult[k][j]
                x[i] = x[i] - (c[j] * inv[j]) * rows[j]
        final = jnp.zeros((8, 128), F32)
        for j in range(8):
            final = jnp.where(sub == j, rows[j] * lax.rsqrt(entry[j][j]), final)
        x[g] = final
    return jnp.concatenate(x, axis=0)


def split3(x):
    first = x.astype(BF16)
    rest = x - first.astype(F32)
    second = rest.astype(BF16)
    return first, second, (rest - second.astype(F32)).astype(BF16)


def eliminate(k, half, m_ref):
    left = 128 * half
    cols = slice(left, left + 384)
    rows = pl.ds(pl.multiple_of(32 * k, 32), 32)
    lane = lax.broadcasted_iota(jnp.int32, (32, 128), 1)
    subl = lax.broadcasted_iota(jnp.int32, (32, 128), 0)
    d = pltpu.roll(m_ref[rows, left : left + 128], (160 - 32 * (k % 4)) % 128, 1)
    x = jnp.where(lane < 32, jnp.where(lane == subl, 1.0, 0.0), d)
    inverse = inverse_factor([x[8 * i : 8 * i + 8] for i in range(4)])
    scaled = nn(inverse[:, :32], m_ref[rows, cols], HIGH)
    m_ref[rows, cols] = scaled

    @pl.when(k < 7)
    def _():
        lane = lax.broadcasted_iota(jnp.int32, (32, RANK - left), 1)
        lower = jnp.where(lane >= 32 * k + 32 - left, scaled[:, : RANK - left], 0.0)
        a, b, c = split3(lower)
        d, e, f = split3(scaled)
        m_ref[left:, cols] -= tn(
            jnp.concatenate([a, a, b, a, b, c], axis=0), jnp.concatenate([d, e, d, f, e, d], axis=0)
        )


def main_kernel(
    grad,
    mom,
    basis,
    blend_out,
    ortho_out,
    back_out,
    norm_out,
    grad_v,
    basis_v,
    bases,
    hi_v,
    lo_v,
    part_v,
    from_core,
    hop_v,
    side_v,
    proj,
    gram_part,
    gram_in,
    gram_x,
    gram,
    elim,
    turned,
    w,
    w_hop,
    w_side,
    w_sub,
    w_full,
    sq_v,
    load_sem,
    send_sem,
    recv_sem,
):
    f = lax.axis_index("fsdp")
    t = lax.axis_index("tp")
    x, c = t // 2, t % 2
    z, y = f // 4, f % 4

    def tp_dev(xx, cc):
        return {"fsdp": f, "tp": xx * 2 + cc}

    def f_dev(ff):
        return {"fsdp": ff, "tp": t}

    right = tp_dev((x + 1) % 4, c)
    left = tp_dev((x + 3) % 4, c)
    twin = tp_dev(x, 1 - c)

    def remote(src, dst, number, device):
        return pltpu.make_async_remote_copy(
            src_ref=src,
            dst_ref=dst,
            send_sem=send_sem.at[number],
            recv_sem=recv_sem.at[number],
            device_id=device,
            device_id_type=MESH,
        )

    def send(src, dst, number, device):
        remote(src, dst, number, device).start()

    def arrive(dst, number):
        remote(dst, dst, number, twin).wait_recv()

    def all_sent(first, many, ref):
        @pl.loop(first, first + many)
        def _(number):
            remote(ref, ref, number, twin).wait_send()

    def piece_row(core, chip):
        return pl.multiple_of(core * HALF + chip * PIECE, 32)

    def chunk_row(i):
        g = 3 - i // 2
        d = g + (g // 2) * (1 - 2 * (g % 2))
        core = (1 - c) * (1 - i % 2) + c * (i % 2)
        return piece_row(core, (x + d) % 4)

    def load(i):
        rows = pl.ds(chunk_row(i), PIECE)
        return (
            pltpu.make_async_copy(mom.at[rows], blend_out.at[rows], load_sem.at[2 * i]),
            pltpu.make_async_copy(grad.at[rows], grad_v.at[i % 4], load_sem.at[2 * i + 1]),
        )

    basis_copy = pltpu.make_async_copy(basis, basis_v, load_sem.at[16])
    basis_copy.start()

    @pl.loop(0, 3)
    def _(i):
        for copy in load(i):
            copy.start()

    barrier = pltpu.get_barrier_semaphore()

    @pl.loop(1, 16)
    def _(d):
        pl.semaphore_signal(barrier, inc=1, device_id=f_dev((f + d) % 16), device_id_type=MESH)

    @pl.loop(1, 8)
    def _(d):
        pl.semaphore_signal(
            barrier, inc=1, device_id={"fsdp": f, "tp": (t + d) % 8}, device_id_type=MESH
        )

    basis_copy.wait()
    basis_hi, basis_lo = split(basis_v[...])
    bases[:LOCAL_COLS] = basis_hi
    bases[LOCAL_COLS:] = basis_lo
    turned[...] = jnp.zeros_like(turned)
    hi_v[LOCAL_ROWS:, :] = jnp.zeros((32, LOCAL_COLS), BF16)
    lo_v[LOCAL_ROWS:, :] = jnp.zeros((32, LOCAL_COLS), BF16)

    def partial(i):
        for copy in load(i):
            copy.wait()
        rows = pl.ds(chunk_row(i), PIECE)

        @pl.when(i < 5)
        def _():
            for copy in load(i + 3):
                copy.start()

        blend = blend_out[rows, :] + grad_v[i % 4].astype(F32)
        blend_out[rows, :] = blend
        hi, lo = split(blend)
        hi_v[rows, :] = hi
        lo_v[rows, :] = lo
        first, second = bases[:LOCAL_COLS], bases[LOCAL_COLS:]
        return nn(hi, first) + nn(hi, second) + nn(lo, first)

    a_rows, b_rows = pl.ds(0, PART), pl.ds(PART, PART)

    def add_core(j):
        arrive(from_core.at[j], N_CORE + j)
        part_v[2 * j + 1] += from_core[j]

    @pl.loop(0, 8)
    def _(i):
        part_v[i] = partial(i)
        j = i // 2
        core = remote(part_v.at[i], from_core.at[j], N_CORE + j, twin)

        @pl.when(i == 0)
        def _():
            pl.semaphore_wait(barrier, 22)

        @pl.when(i % 2 == 0)
        def _():
            core.start()

        @pl.when(i == 2)
        def _():
            add_core(0)
            send(part_v.at[1, a_rows], hop_v.at[0], N_HOP_A, right)
            send(part_v.at[1, b_rows], hop_v.at[1], N_HOP_B, left)

        @pl.when(i == 4)
        def _():
            add_core(1)
            send(part_v.at[3, a_rows], side_v.at[2], N_RIGHT_A, left)

        @pl.when(i == 6)
        def _():
            add_core(2)
            send(part_v.at[5, b_rows], side_v.at[1], N_LEFT_B, right)
            arrive(hop_v.at[0], N_HOP_A)
            part_v[5, a_rows] += hop_v[0]
            send(part_v.at[5, a_rows], side_v.at[0], N_LEFT_A, right)
            arrive(hop_v.at[1], N_HOP_B)
            part_v[3, b_rows] += hop_v[1]
            send(part_v.at[3, b_rows], side_v.at[3], N_RIGHT_B, left)

    add_core(3)
    my_row = piece_row(c, x)
    arrive(side_v.at[2], N_RIGHT_A)
    arrive(side_v.at[0], N_LEFT_A)
    proj[pl.ds(my_row, PART), :] = part_v[7, a_rows] + (side_v[0] + side_v[2])
    arrive(side_v.at[1], N_LEFT_B)
    arrive(side_v.at[3], N_RIGHT_B)
    proj[pl.ds(my_row + PART, PART), :] = part_v[7, b_rows] + (side_v[1] + side_v[3])

    def part_of(core, chip, b):
        return proj.at[pl.ds(pl.multiple_of(piece_row(core, chip) + b * PART, 16), PART)]

    def whole_of(core, chip):
        return proj.at[pl.ds(piece_row(core, chip), PIECE)]

    def send_part(chip, b, number, device):
        send(part_of(c, chip, b), part_of(c, chip, b), number, device)

    def send_whole(chip, number):
        send(whole_of(c, chip), whole_of(c, chip), number, twin)

    xl, xr, xo = (x + 3) % 4, (x + 1) % 4, (x + 2) % 4
    send_part(x, 0, G_LEFT_A, right)
    send_part(x, 1, G_RIGHT_B, left)
    send_whole(x, G_CORE)
    send_part(x, 1, G_LEFT_B, right)
    send_part(x, 0, G_RIGHT_A, left)

    half_cols = pl.ds(pl.multiple_of(c * 128, 128), 128)

    def eight(row):
        return pl.ds(pl.multiple_of(row * 8, 8), 8)

    def gram_start():
        halves = []
        for core in range(2):
            rows = pl.ds(piece_row(core, x), PIECE)
            a, b, d = split3(proj[rows, half_cols])
            left = jnp.concatenate([a, a, b, a, b, d], axis=0)
            a, b, d = split3(proj[rows, :])
            halves.append(tn(left, jnp.concatenate([a, b, a, d, b, a], axis=0)))
        gram_part[...] = halves[0] + halves[1]

        @pl.loop(1, 16)
        def _(d):
            to = (f + d) % 16
            send(gram_part.at[eight(to)], gram_in.at[d], GRAM_SUM + d - 1, f_dev(to))

    def gram_across():
        gram_in[0] = gram_part[eight(f), :]

        @pl.loop(1, 16)
        def _(d):
            arrive(gram_in.at[d], GRAM_SUM + d - 1)

        gram_x[x] = jnp.sum(gram_in[...], axis=0)

        @pl.loop(1, 4)
        def _(d):
            send(gram_x.at[x], gram_x.at[x], GRAM_X + d - 1, tp_dev((x + d) % 4, c))

    def gram_row(ff):
        return pl.ds(pl.multiple_of(c * 128 + ff * 8, 8), 8)

    def gram_round():
        @pl.loop(1, 4)
        def _(d):
            arrive(gram_x.at[(x + 4 - d) % 4], GRAM_X + d - 1)

        gram[gram_row(f), :] = (gram_x[0] + gram_x[1]) + (gram_x[2] + gram_x[3])

        @pl.loop(1, 16)
        def _(d):
            mine = gram.at[gram_row(f)]
            send(mine, mine, GRAM_ALL + d - 1, f_dev((f + d) % 16))

    def gram_half(core):
        return gram.at[pl.ds(pl.multiple_of(core * 128, 128), 128)]

    def gram_pair():
        @pl.loop(1, 16)
        def _(d):
            arrive(gram.at[gram_row((f + 16 - d) % 16)], GRAM_ALL + d - 1)

        send(gram_half(c), gram_half(c), GRAM_CORE, twin)

    w[...] = jnp.zeros_like(w)

    @pl.loop(0, 8)
    def _(g):
        core = (c + pick(g, (0, 1, 0, 0, 0, 1, 1, 1))) % 2
        chip = (x + pick(g, (0, 0, 1, 3, 2, 1, 3, 2))) % 4

        @pl.when(g == 1)
        def _():
            arrive(whole_of(1 - c, x), G_CORE)
            gram_start()

        @pl.when(g == 2)
        def _():
            arrive(part_of(c, xl, 0), G_LEFT_A)
            send_part(xl, 0, G_OPP_A, right)
            arrive(part_of(c, xr, 1), G_RIGHT_B)
            send_part(xr, 1, G_OPP_B, left)
            gram_across()
            arrive(part_of(c, xr, 0), G_RIGHT_A)
            send_whole(xr, G_CORE + 1)
            arrive(part_of(c, xl, 1), G_LEFT_B)
            send_whole(xl, G_CORE + 2)

        @pl.when(g == 4)
        def _():
            gram_round()
            arrive(part_of(c, xo, 0), G_OPP_A)
            arrive(part_of(c, xo, 1), G_OPP_B)
            send_whole(xo, G_CORE + 3)

        @pl.when(g == 5)
        def _():
            arrive(whole_of(1 - c, xr), G_CORE + 1)

        @pl.when(g == 6)
        def _():
            arrive(whole_of(1 - c, xl), G_CORE + 2)

        @pl.when(g == 7)
        def _():
            gram_pair()
            arrive(whole_of(1 - c, xo), G_CORE + 3)

        rows = pl.ds(piece_row(core, chip), PIECE)
        p_hi, p_lo = split(proj[rows, :].T)
        turned[:, :PIECE] = p_hi
        turned[:, 256 : 256 + PIECE] = p_hi
        turned[:, 512 : 512 + PIECE] = p_lo
        more = pl.ds(piece_row(core, chip), 256)
        for n in range(4):
            cols = slice(256 * n, 256 * n + 256)
            hi = hi_v[more, cols]
            w[:, cols] += nn(turned[...], jnp.concatenate([hi, lo_v[more, cols], hi], axis=0))

    def places(u):
        k, q = y + u * (z - y), z + u * (y - z)

        def first(kk):
            return f_dev(z * 4 + kk + u * (kk * 4 + y - z * 4 - kk))

        def second(qq):
            return f_dev(qq * 4 + y + u * (z * 4 + qq - qq * 4 - y))

        return k, q, first, second

    def cols_ab(u):
        start = pl.multiple_of(WIDE * u, WIDE)
        return pl.ds(start, 256), pl.ds(pl.multiple_of(start + 256, 256), 256)

    def cols_u(u):
        return pl.ds(pl.multiple_of(WIDE * u, WIDE), WIDE)

    def rows32(h, k):
        return pl.ds(pl.multiple_of(128 * h + 32 * k, 32), 32)

    def rows8(h, k, q):
        return pl.ds(pl.multiple_of(128 * h + 32 * k + 8 * q, 8), 8)

    def w_step_1(h, u):
        k, q, first, _ = places(u)
        ca, cb = cols_ab(u)
        i = 2 * h + u
        kr, kl, ko = (k + 1) % 4, (k + 3) % 4, (k + 2) % 4
        send(w.at[rows32(h, ko), ca], w_hop.at[2 * i], W_HOP + 2 * i, first(kr))
        send(w.at[rows32(h, ko), cb], w_hop.at[2 * i + 1], W_HOP + 2 * i + 1, first(kl))
        send(w.at[rows32(h, kr), cb], w_side.at[4 * i + 1], W_NEXT + 4 * i + 1, first(kr))
        send(w.at[rows32(h, kl), ca], w_side.at[4 * i + 2], W_NEXT + 4 * i + 2, first(kl))

    def w_step_2(h, u):
        k, q, first, _ = places(u)
        ca, cb = cols_ab(u)
        i = 2 * h + u
        kr, kl = (k + 1) % 4, (k + 3) % 4
        arrive(w_hop.at[2 * i], W_HOP + 2 * i)
        w[rows32(h, kr), ca] += w_hop[2 * i]
        send(w.at[rows32(h, kr), ca], w_side.at[4 * i], W_NEXT + 4 * i, first(kr))
        arrive(w_hop.at[2 * i + 1], W_HOP + 2 * i + 1)
        w[rows32(h, kl), cb] += w_hop[2 * i + 1]
        send(w.at[rows32(h, kl), cb], w_side.at[4 * i + 3], W_NEXT + 4 * i + 3, first(kl))

    def w_step_3(h, u):
        k, q, _, second = places(u)
        ca, cb = cols_ab(u)
        i = 2 * h + u
        for s in range(4):
            arrive(w_side.at[4 * i + s], W_NEXT + 4 * i + s)
        w[rows32(h, k), ca] += w_side[4 * i] + w_side[4 * i + 2]
        w[rows32(h, k), cb] += w_side[4 * i + 1] + w_side[4 * i + 3]

        @pl.loop(1, 4)
        def _(d):
            to, slot = (q + d) % 4, 3 * i + d - 1
            send(w.at[rows8(h, k, to), cols_u(u)], w_sub.at[slot], W_SUB + slot, second(to))

    def w_step_4(h, u):
        k, q, _, second = places(u)
        i = 2 * h + u

        @pl.loop(0, 3)
        def _(d):
            arrive(w_sub.at[3 * i + d], W_SUB + 3 * i + d)

        w_full[rows8(h, k, q), cols_u(u)] = (w[rows8(h, k, q), cols_u(u)] + w_sub[3 * i]) + (
            w_sub[3 * i + 1] + w_sub[3 * i + 2]
        )

        @pl.loop(1, 4)
        def _(d):
            mine = w_full.at[rows8(h, k, q), cols_u(u)]
            send(mine, mine, W_ALL + 3 * i + d - 1, second((q + d) % 4))

    def w_step_5(h, u):
        k, q, first, _ = places(u)
        ca, cb = cols_ab(u)
        i = 2 * h + u
        dr, dl = first((k + 1) % 4), first((k + 3) % 4)

        @pl.loop(1, 4)
        def _(d):
            arrive(w_full.at[rows8(h, k, (q + 4 - d) % 4), cols_u(u)], W_ALL + 3 * i + d - 1)

        mine_a, mine_b = w_full.at[rows32(h, k), ca], w_full.at[rows32(h, k), cb]
        send(mine_a, mine_a, W_RING + 4 * i, dr)
        send(mine_b, mine_b, W_RING + 4 * i + 3, dl)
        send(mine_b, mine_b, W_RING + 4 * i + 1, dr)
        send(mine_a, mine_a, W_RING + 4 * i + 2, dl)

    def w_step_6(h, u):
        k, q, first, _ = places(u)
        ca, cb = cols_ab(u)
        i = 2 * h + u
        kr, kl = (k + 1) % 4, (k + 3) % 4
        from_left = w_full.at[rows32(h, kl), ca]
        arrive(from_left, W_RING + 4 * i)
        send(from_left, from_left, W_FAR + 2 * i, first(kr))
        from_right = w_full.at[rows32(h, kr), cb]
        arrive(from_right, W_RING + 4 * i + 3)
        send(from_right, from_right, W_FAR + 2 * i + 1, first(kl))

    def w_step_7(h, u):
        k = places(u)[0]
        ca, cb = cols_ab(u)
        i = 2 * h + u
        kr, kl, ko = (k + 1) % 4, (k + 3) % 4, (k + 2) % 4
        arrive(w_full.at[rows32(h, kl), cb], W_RING + 4 * i + 1)
        arrive(w_full.at[rows32(h, kr), ca], W_RING + 4 * i + 2)
        arrive(w_full.at[rows32(h, ko), ca], W_FAR + 2 * i)
        arrive(w_full.at[rows32(h, ko), cb], W_FAR + 2 * i + 1)

    def all_parts(step):
        @pl.loop(0, 4)
        def _(i):
            step(i // 2, i % 2)

    all_parts(w_step_1)
    all_parts(w_step_2)
    w_steps_at = (w_step_3, None, w_step_4, None, w_step_5, None, w_step_6, w_step_7)

    arrive(gram_half(1 - c), GRAM_CORE)
    elim[:, :RANK] = gram[...]
    rr = lax.broadcasted_iota(jnp.int32, (RANK, RANK), 0)
    cc = lax.broadcasted_iota(jnp.int32, (RANK, RANK), 1)
    elim[:, RANK:] = jnp.where(rr == cc, 1.0, 0.0).astype(F32)

    for half in range(2):

        @pl.loop(4 * half, 4 * half + 4)
        def _(k):
            eliminate(k, half, elim)
            for at in range(4 * half, 4 * half + 4):
                if w_steps_at[at] is not None:

                    @pl.when(k == at)
                    def _():
                        all_parts(w_steps_at[at])

    f_hi, f_lo = split(elim[:, RANK:])
    factor = jnp.concatenate([f_hi, f_hi, f_lo], axis=1)
    squares = jnp.zeros((RANK, 128), F32)
    for n in range(4):
        cols = slice(256 * n, 256 * n + 256)
        w_hi, w_lo = split(w_full[:, cols])
        back = nn(factor, jnp.concatenate([w_hi, w_lo, w_hi], axis=0))
        back_out[:, cols] = back
        squares = squares + (back[:, :128] * back[:, :128] + back[:, 128:] * back[:, 128:])
    sq_v[t] = nt(jnp.ones((8, 128), F32), squares, HIGH)

    @pl.loop(1, 8)
    def _(d):
        send(sq_v.at[t], sq_v.at[t], SQ + d - 1, {"fsdp": f, "tp": (t + d) % 8})


    t_hi, t_lo = split(elim[:, RANK:].T)
    turned[:, :256] = t_hi
    turned[:, 256:512] = t_lo

    @pl.loop(0, LOCAL_ROWS // STEP)
    def _(i):
        rows = pl.ds(pl.multiple_of(i * STEP, 64), STEP)
        hi, lo = split(proj[rows, :])
        first, second = turned[:, :256], turned[:, 256:512]
        ortho_out[rows, :] = nn(hi, first) + nn(hi, second) + nn(lo, first)

    all_sent(N_HOP_A, 12, side_v.at[0])
    all_sent(N_CORE, 8, part_v.at[0])
    all_sent(GRAM_SUM, 33, sq_v.at[0])
    all_sent(GRAM_CORE, 1, gram_part)
    all_sent(W_HOP, 48, w_hop.at[0])
    all_sent(W_SUB, 24, w_sub.at[0])

    @pl.loop(1, 8)
    def _(d):
        arrive(sq_v.at[(t + 8 - d) % 8], SQ + d - 1)

    norm_out[...] = lax.rsqrt(jnp.sum(sq_v[...], axis=0) + 1e-06)
    all_sent(SQ, 7, sq_v.at[0])


def write_kernel(
    blend, ortho, back, norm, mom_out, basis_out, update_out, backs, mom_v, basis_v, update_v, sems
):
    hi, lo = split(back[...])
    backs[:RANK] = hi
    backs[RANK : 2 * RANK] = lo
    backs[2 * RANK :] = hi
    scale = (ROWS * COLS / RANK) ** 0.5
    norms = norm[0:1, :]

    def copies(i):
        slot = i % 2
        found = []
        for p in range(2):
            rows = pl.ds(pl.multiple_of(i * STEP + p * PIECE, 32), PIECE)
            here = pl.ds(p * PIECE, PIECE)
            found.append(pltpu.make_async_copy(mom_v.at[slot, here], mom_out.at[rows], sems.at[slot, p]))
            found.append(
                pltpu.make_async_copy(update_v.at[slot, here], update_out.at[rows], sems.at[slot, 2 + p])
            )
        rank_rows = pl.ds(pl.multiple_of(i * 256, 256), 256)
        found.append(pltpu.make_async_copy(basis_v.at[slot], basis_out.at[rank_rows], sems.at[slot, 4]))
        return found

    @pl.loop(0, LOCAL_ROWS // STEP)
    def _(i):
        slot = i % 2

        @pl.when(i >= 2)
        def _():
            for copy in copies(i - 2):
                copy.wait()

        rows = pl.ds(pl.multiple_of(i * STEP, 64), STEP)
        cols = pl.ds(pl.multiple_of(i * 256, 256), 256)
        basis_v[slot] = back[:, cols].T * norms
        plain = ortho[rows, :]
        mom_v[slot] = blend[rows, :] - nn((0.05 * plain).astype(BF16), backs[:RANK])
        mom_a, update_a, mom_b, update_b, basis_copy = copies(i)
        mom_a.start()
        mom_b.start(priority=1)
        basis_copy.start()
        hi, lo = split(plain * (scale * norms))
        update_v[slot] = nn(jnp.concatenate([hi, hi, lo], axis=1), backs[...]).astype(BF16)
        update_a.start()
        update_b.start(priority=1)

    for i in (2, 3):
        for copy in copies(i):
            copy.wait()


def body(gradient, momentum, basis):
    anywhere = pl.BlockSpec(memory_space=pl.ANY)
    inside = pl.BlockSpec(memory_space=pltpu.VMEM)
    vmem = pltpu.VMEM
    fixed = [pltpu.with_memory_space_constraint(a, pltpu.HBM) for a in (gradient, momentum, basis)]
    results = pl.pallas_call(
        main_kernel,
        out_shape=(
            vmem((LOCAL_ROWS, LOCAL_COLS), F32),
            vmem((LOCAL_ROWS, RANK), F32),
            vmem((RANK, LOCAL_COLS), F32),
            vmem((8, RANK), F32),
        ),
        in_specs=[anywhere] * 3,
        out_specs=(inside,) * 4,
        scratch_shapes=[
            vmem((4, PIECE, LOCAL_COLS), BF16),
            vmem((LOCAL_COLS, RANK), F32),
            vmem((2 * LOCAL_COLS, RANK), BF16),
            vmem((LOCAL_ROWS + 32, LOCAL_COLS), BF16),
            vmem((LOCAL_ROWS + 32, LOCAL_COLS), BF16),
            vmem((8, PIECE, RANK), F32),
            vmem((4, PIECE, RANK), F32),
            vmem((2, PART, RANK), F32),
            vmem((4, PART, RANK), F32),
            vmem((LOCAL_ROWS, RANK), F32),
            vmem((128, RANK), F32),
            vmem((16, 8, RANK), F32),
            vmem((4, 8, RANK), F32),
            vmem((RANK, RANK), F32),
            vmem((RANK, 2 * RANK), F32),
            vmem((RANK, 3 * 256), BF16),
            vmem((RANK, LOCAL_COLS), F32),
            vmem((8, 32, 256), F32),
            vmem((16, 32, 256), F32),
            vmem((12, 8, WIDE), F32),
            vmem((RANK, LOCAL_COLS), F32),
            vmem((8, 8, RANK), F32),
            pltpu.SemaphoreType.DMA((17,)),
            pltpu.SemaphoreType.DMA((NAMES.count,)),
            pltpu.SemaphoreType.DMA((NAMES.count,)),
        ],
        compiler_params=pltpu.CompilerParams(
            collective_id=0, has_side_effects=True, vmem_limit_bytes=44 * 2**20
        ),
        name="transfers",
    )(*fixed)
    results = [pltpu.with_memory_space_constraint(a, pltpu.VMEM) for a in results]

    return pl.pallas_call(
        write_kernel,
        out_shape=(
            jax.ShapeDtypeStruct((LOCAL_ROWS, LOCAL_COLS), F32),
            jax.ShapeDtypeStruct((LOCAL_COLS, RANK), F32),
            jax.ShapeDtypeStruct((LOCAL_ROWS, LOCAL_COLS), BF16),
        ),
        in_specs=[inside] * 4,
        out_specs=(anywhere,) * 3,
        scratch_shapes=[
            vmem((3 * RANK, LOCAL_COLS), BF16),
            vmem((2, STEP, LOCAL_COLS), F32),
            vmem((2, 256, RANK), F32),
            vmem((2, STEP, LOCAL_COLS), BF16),
            pltpu.SemaphoreType.DMA((2, 5)),
        ],
        compiler_params=pltpu.CompilerParams(vmem_limit_bytes=32 * 2**20),
        name="outputs",
    )(*results)


def solution(mesh):
    placed = (P("fsdp", "tp"), P("fsdp", "tp"), P("tp", None))
    return jax.shard_map(
        body,
        mesh=mesh,
        in_specs=placed,
        out_specs=(P("fsdp", "tp"), P("tp", None), P("fsdp", "tp")),
        check_vma=False,
    )
```

```python
import functools

import jax
import jax.numpy as jnp
from jax import lax
from jax.experimental import pallas as pl
from jax.experimental.pallas import tpu as pltpu
from jax.sharding import PartitionSpec as P

ROWS = 28672
COLS = 8192
RANK = 256

F32 = jnp.float32
BF16 = jnp.bfloat16
HIGH = lax.Precision.HIGHEST
MESH = pl.DeviceIdType.MESH

LOCAL_ROWS = 1792
LOCAL_COLS = 1024
HALF = 896
PIECE = 224
PART = 112
STEP = 448
WIDE = 512


class Names:
    def __init__(self):
        self.count = 0

    def take(self, many=1):
        first = self.count
        self.count += many
        return first


NAMES = Names()
N_HOP_A, N_HOP_B = NAMES.take(), NAMES.take()
N_LEFT_A, N_LEFT_B = NAMES.take(), NAMES.take()
N_RIGHT_A, N_RIGHT_B = NAMES.take(), NAMES.take()
G_LEFT_A, G_LEFT_B = NAMES.take(), NAMES.take()
G_RIGHT_A, G_RIGHT_B = NAMES.take(), NAMES.take()
G_OPP_A, G_OPP_B = NAMES.take(), NAMES.take()
N_CORE = NAMES.take(4)
G_CORE = NAMES.take(4)
GRAM_SUM = NAMES.take(15)
GRAM_X = NAMES.take(3)
GRAM_ALL = NAMES.take(15)
SQ = NAMES.take(7)
GRAM_CORE = NAMES.take()
W_HOP = NAMES.take(8)
W_NEXT = NAMES.take(16)
W_RING = NAMES.take(16)
W_FAR = NAMES.take(8)
W_SUB = NAMES.take(12)
W_ALL = NAMES.take(12)


def nn(a, b, precision=None):
    return lax.dot_general(
        a, b, (((1,), (0,)), ((), ())), precision=precision, preferred_element_type=F32
    )


def tn(a, b, precision=None):
    return lax.dot_general(
        a, b, (((0,), (0,)), ((), ())), precision=precision, preferred_element_type=F32
    )


def nt(a, b, precision=None):
    return lax.dot_general(
        a, b, (((1,), (1,)), ((), ())), precision=precision, preferred_element_type=F32
    )


def pick(index, values):
    out = values[0]
    for at in range(1, len(values)):
        out = out + (values[at] - values[at - 1]) * ((index + len(values) - at) // len(values))
    return out


def split(x):
    hi = x.astype(BF16)
    return hi, (x - hi.astype(F32)).astype(BF16)


def row_copy(x, j):
    return jnp.broadcast_to(x[j : j + 1, :], (8, 128))


def inverse_factor(x):
    n = len(x)
    sub = lax.broadcasted_iota(jnp.int32, (8, 128), 0)
    lane = lax.broadcasted_iota(jnp.int32, (8, 128), 1)
    col = [
        [None if i < k // 8 else jnp.broadcast_to(x[i][:, k : k + 1], (8, 128)) for i in range(n)]
        for k in range(8 * n)
    ]
    inverse = [jnp.where(lane == sub + 8 * i, 1.0, 0.0) for i in range(n)]
    for g in range(n):
        entry = [[row_copy(col[8 * g + j][g], i) for j in range(i + 1)] for i in range(8)]
        rows = [row_copy(inverse[g], j) for j in range(8)]
        inv, mult = [], [[None] * 8 for _ in range(8)]
        for j in range(8):
            inv.append(1.0 / entry[j][j])
            for k in range(j + 1, 8):
                mult[k][j] = entry[k][j] * inv[j]
                for i in range(k, 8):
                    entry[i][k] = entry[i][k] - entry[i][j] * mult[k][j]
                rows[k] = rows[k] - mult[k][j] * rows[j]
        final = jnp.zeros((8, 128), F32)
        for j in range(8):
            final = jnp.where(sub == j, rows[j] * lax.rsqrt(entry[j][j]), final)
        inverse[g] = final
        below = {}
        for i in range(g + 1, n):
            c = [col[8 * g + j][i] for j in range(8)]
            for j in range(8):
                for k in range(j + 1, 8):
                    c[k] = c[k] - c[j] * mult[k][j]
            below[i] = (c, [c[j] * inv[j] for j in range(8)])
        for k in range(8 * g + 8, 8 * n):
            across = [row_copy(below[k // 8][0][j], k % 8) for j in range(8)]
            for i in range(k // 8, n):
                for j in range(8):
                    col[k][i] = col[k][i] - below[i][1][j] * across[j]
        for i in range(g + 1, n):
            for j in range(8):
                inverse[i] = inverse[i] - below[i][1][j] * rows[j]
    return jnp.concatenate(inverse, axis=0)


def split3(x):
    first = x.astype(BF16)
    rest = x - first.astype(F32)
    second = rest.astype(BF16)
    return first, second, (rest - second.astype(F32)).astype(BF16)


def eliminate(k, half, m_ref):
    left = 128 * half
    cols = slice(left, left + 384)
    rows = pl.ds(pl.multiple_of(32 * k, 32), 32)
    d = pltpu.roll(m_ref[rows, left : left + 128], (128 - 32 * (k % 4)) % 128, 1)
    inverse = inverse_factor([d[8 * i : 8 * i + 8] for i in range(4)])
    scaled = nn(inverse[:, :32], m_ref[rows, cols], HIGH)
    m_ref[rows, cols] = scaled

    @pl.when(k < 7)
    def _():
        lane = lax.broadcasted_iota(jnp.int32, (32, RANK - left), 1)
        lower = jnp.where(lane >= 32 * k + 32 - left, scaled[:, : RANK - left], 0.0)
        a, b, c = split3(lower)
        d, e, f = split3(scaled)
        m_ref[left:, cols] -= tn(
            jnp.concatenate([a, a, b, a, b, c], axis=0), jnp.concatenate([d, e, d, f, e, d], axis=0)
        )


def main_kernel(
    grad,
    mom,
    basis,
    blend_out,
    ortho_out,
    back_out,
    norm_out,
    grad_v,
    basis_v,
    bases,
    hi_v,
    lo_v,
    part_v,
    from_core,
    hop_v,
    side_v,
    proj,
    gram_part,
    gram_in,
    gram_x,
    gram,
    elim,
    turned,
    w,
    w_hop,
    w_side,
    w_sub,
    w_full,
    sq_v,
    load_sem,
    send_sem,
    recv_sem,
):
    f = lax.axis_index("fsdp")
    t = lax.axis_index("tp")
    x, c = t // 2, t % 2
    z, y = f // 4, f % 4

    def tp_dev(xx, cc):
        return {"fsdp": f, "tp": xx * 2 + cc}

    def f_dev(ff):
        return {"fsdp": ff, "tp": t}

    right = tp_dev((x + 1) % 4, c)
    left = tp_dev((x + 3) % 4, c)
    twin = tp_dev(x, 1 - c)

    def remote(src, dst, number, device):
        return pltpu.make_async_remote_copy(
            src_ref=src,
            dst_ref=dst,
            send_sem=send_sem.at[number],
            recv_sem=recv_sem.at[number],
            device_id=device,
            device_id_type=MESH,
        )

    def send(src, dst, number, device):
        remote(src, dst, number, device).start()

    def arrive(dst, number):
        remote(dst, dst, number, twin).wait_recv()

    def all_sent(first, many, ref):
        @pl.loop(first, first + many)
        def _(number):
            remote(ref, ref, number, twin).wait_send()

    def piece_row(core, chip):
        return pl.multiple_of(core * HALF + chip * PIECE, 32)

    def chunk_row(i):
        g = 3 - i // 2
        d = g + (g // 2) * (1 - 2 * (g % 2))
        core = (1 - c) * (1 - i % 2) + c * (i % 2)
        return piece_row(core, (x + d) % 4)

    def load(i):
        rows = pl.ds(chunk_row(i), PIECE)
        return (
            pltpu.make_async_copy(mom.at[rows], blend_out.at[rows], load_sem.at[2 * i]),
            pltpu.make_async_copy(grad.at[rows], grad_v.at[i % 4], load_sem.at[2 * i + 1]),
        )

    basis_copy = pltpu.make_async_copy(basis, basis_v, load_sem.at[16])
    basis_copy.start()

    @pl.loop(0, 3)
    def _(i):
        for copy in load(i):
            copy.start()

    barrier = pltpu.get_barrier_semaphore()

    @pl.loop(1, 16)
    def _(d):
        pl.semaphore_signal(barrier, inc=1, device_id=f_dev((f + d) % 16), device_id_type=MESH)

    @pl.loop(1, 8)
    def _(d):
        pl.semaphore_signal(
            barrier, inc=1, device_id={"fsdp": f, "tp": (t + d) % 8}, device_id_type=MESH
        )

    basis_copy.wait()
    basis_hi, basis_lo = split(basis_v[...])
    bases[:LOCAL_COLS] = basis_hi
    bases[LOCAL_COLS:] = basis_lo
    turned[...] = jnp.zeros_like(turned)
    hi_v[LOCAL_ROWS:, :] = jnp.zeros((32, LOCAL_COLS), BF16)
    lo_v[LOCAL_ROWS:, :] = jnp.zeros((32, LOCAL_COLS), BF16)

    def partial(i):
        for copy in load(i):
            copy.wait()
        rows = pl.ds(chunk_row(i), PIECE)

        @pl.when(i < 5)
        def _():
            for copy in load(i + 3):
                copy.start()

        blend = blend_out[rows, :] + grad_v[i % 4].astype(F32)
        blend_out[rows, :] = blend
        hi, lo = split(blend)
        hi_v[rows, :] = hi
        lo_v[rows, :] = lo
        first, second = bases[:LOCAL_COLS], bases[LOCAL_COLS:]
        return nn(hi, first) + nn(hi, second) + nn(lo, first)

    a_rows, b_rows = pl.ds(0, PART), pl.ds(PART, PART)

    def add_core(j):
        arrive(from_core.at[j], N_CORE + j)
        part_v[2 * j + 1] += from_core[j]

    @pl.loop(0, 8)
    def _(i):
        part_v[i] = partial(i)
        j = i // 2
        core = remote(part_v.at[i], from_core.at[j], N_CORE + j, twin)

        @pl.when(i == 0)
        def _():
            pl.semaphore_wait(barrier, 22)

        @pl.when(i % 2 == 0)
        def _():
            core.start()

        @pl.when(i == 2)
        def _():
            add_core(0)
            send(part_v.at[1, a_rows], hop_v.at[0], N_HOP_A, right)
            send(part_v.at[1, b_rows], hop_v.at[1], N_HOP_B, left)

        @pl.when(i == 4)
        def _():
            add_core(1)
            send(part_v.at[3, a_rows], side_v.at[2], N_RIGHT_A, left)

        @pl.when(i == 6)
        def _():
            add_core(2)
            send(part_v.at[5, b_rows], side_v.at[1], N_LEFT_B, right)
            arrive(hop_v.at[0], N_HOP_A)
            part_v[5, a_rows] += hop_v[0]
            send(part_v.at[5, a_rows], side_v.at[0], N_LEFT_A, right)
            arrive(hop_v.at[1], N_HOP_B)
            part_v[3, b_rows] += hop_v[1]
            send(part_v.at[3, b_rows], side_v.at[3], N_RIGHT_B, left)

    add_core(3)
    my_row = piece_row(c, x)
    arrive(side_v.at[2], N_RIGHT_A)
    arrive(side_v.at[0], N_LEFT_A)
    proj[pl.ds(my_row, PART), :] = part_v[7, a_rows] + (side_v[0] + side_v[2])
    arrive(side_v.at[1], N_LEFT_B)
    arrive(side_v.at[3], N_RIGHT_B)
    proj[pl.ds(my_row + PART, PART), :] = part_v[7, b_rows] + (side_v[1] + side_v[3])

    def part_of(core, chip, b):
        return proj.at[pl.ds(pl.multiple_of(piece_row(core, chip) + b * PART, 16), PART)]

    def whole_of(core, chip):
        return proj.at[pl.ds(piece_row(core, chip), PIECE)]

    def send_part(chip, b, number, device):
        send(part_of(c, chip, b), part_of(c, chip, b), number, device)

    def send_whole(chip, number):
        send(whole_of(c, chip), whole_of(c, chip), number, twin)

    xl, xr, xo = (x + 3) % 4, (x + 1) % 4, (x + 2) % 4
    send_part(x, 0, G_LEFT_A, right)
    send_part(x, 1, G_RIGHT_B, left)
    send_whole(x, G_CORE)
    send_part(x, 1, G_LEFT_B, right)
    send_part(x, 0, G_RIGHT_A, left)

    half_cols = pl.ds(pl.multiple_of(c * 128, 128), 128)

    def eight(row):
        return pl.ds(pl.multiple_of(row * 8, 8), 8)

    def gram_start():
        halves = []
        for core in range(2):
            rows = pl.ds(piece_row(core, x), PIECE)
            a, b, d = split3(proj[rows, half_cols])
            left = jnp.concatenate([a, a, b, a, b, d], axis=0)
            a, b, d = split3(proj[rows, :])
            halves.append(tn(left, jnp.concatenate([a, b, a, d, b, a], axis=0)))
        gram_part[...] = halves[0] + halves[1]

        @pl.loop(1, 16)
        def _(d):
            to = (f + d) % 16
            send(gram_part.at[eight(to)], gram_in.at[d], GRAM_SUM + d - 1, f_dev(to))

    def gram_across():
        gram_in[0] = gram_part[eight(f), :]

        @pl.loop(1, 16)
        def _(d):
            arrive(gram_in.at[d], GRAM_SUM + d - 1)

        gram_x[x] = jnp.sum(gram_in[...], axis=0)

        @pl.loop(1, 4)
        def _(d):
            send(gram_x.at[x], gram_x.at[x], GRAM_X + d - 1, tp_dev((x + d) % 4, c))

    def gram_row(ff):
        return pl.ds(pl.multiple_of(c * 128 + ff * 8, 8), 8)

    def gram_round():
        @pl.loop(1, 4)
        def _(d):
            arrive(gram_x.at[(x + 4 - d) % 4], GRAM_X + d - 1)

        gram[gram_row(f), :] = (gram_x[0] + gram_x[1]) + (gram_x[2] + gram_x[3])

        @pl.loop(1, 16)
        def _(d):
            mine = gram.at[gram_row(f)]
            send(mine, mine, GRAM_ALL + d - 1, f_dev((f + d) % 16))

    def gram_half(core):
        return gram.at[pl.ds(pl.multiple_of(core * 128, 128), 128)]

    def gram_pair():
        @pl.loop(1, 16)
        def _(d):
            arrive(gram.at[gram_row((f + 16 - d) % 16)], GRAM_ALL + d - 1)

        send(gram_half(c), gram_half(c), GRAM_CORE, twin)

    w[...] = jnp.zeros_like(w)

    @pl.loop(0, 8)
    def _(g):
        core = (c + pick(g, (0, 1, 0, 0, 0, 1, 1, 1))) % 2
        chip = (x + pick(g, (0, 0, 1, 3, 2, 1, 3, 2))) % 4

        @pl.when(g == 1)
        def _():
            arrive(whole_of(1 - c, x), G_CORE)
            gram_start()

        @pl.when(g == 2)
        def _():
            arrive(part_of(c, xl, 0), G_LEFT_A)
            send_part(xl, 0, G_OPP_A, right)
            arrive(part_of(c, xr, 1), G_RIGHT_B)
            send_part(xr, 1, G_OPP_B, left)
            gram_across()
            arrive(part_of(c, xr, 0), G_RIGHT_A)
            send_whole(xr, G_CORE + 1)
            arrive(part_of(c, xl, 1), G_LEFT_B)
            send_whole(xl, G_CORE + 2)

        @pl.when(g == 4)
        def _():
            arrive(part_of(c, xo, 0), G_OPP_A)
            arrive(part_of(c, xo, 1), G_OPP_B)
            send_whole(xo, G_CORE + 3)
            gram_round()

        @pl.when(g == 5)
        def _():
            arrive(whole_of(1 - c, xr), G_CORE + 1)

        @pl.when(g == 6)
        def _():
            arrive(whole_of(1 - c, xl), G_CORE + 2)

        @pl.when(g == 7)
        def _():
            arrive(whole_of(1 - c, xo), G_CORE + 3)

        rows = pl.ds(piece_row(core, chip), PIECE)
        p_hi, p_lo = split(proj[rows, :].T)
        turned[:, :PIECE] = p_hi
        turned[:, 256 : 256 + PIECE] = p_hi
        turned[:, 512 : 512 + PIECE] = p_lo
        more = pl.ds(piece_row(core, chip), 256)
        for n in range(4):
            cols = slice(256 * n, 256 * n + 256)
            hi = hi_v[more, cols]
            w[:, cols] += nn(turned[...], jnp.concatenate([hi, lo_v[more, cols], hi], axis=0))

    def places(u):
        k, q = y + u * (z - y), z + u * (y - z)

        def first(kk):
            return f_dev(z * 4 + kk + u * (kk * 4 + y - z * 4 - kk))

        def second(qq):
            return f_dev(qq * 4 + y + u * (z * 4 + qq - qq * 4 - y))

        return k, q, first, second

    def cols_ab(u):
        start = pl.multiple_of(WIDE * u, WIDE)
        return pl.ds(start, 256), pl.ds(pl.multiple_of(start + 256, 256), 256)

    def cols_u(u):
        return pl.ds(pl.multiple_of(WIDE * u, WIDE), WIDE)

    def rows32(h, k):
        return pl.ds(pl.multiple_of(128 * h + 32 * k, 32), 32)

    def rows8(h, k, q):
        return pl.ds(pl.multiple_of(128 * h + 32 * k + 8 * q, 8), 8)

    def w_step_1(h, u):
        k, q, first, _ = places(u)
        ca, cb = cols_ab(u)
        i = 2 * h + u
        kr, kl, ko = (k + 1) % 4, (k + 3) % 4, (k + 2) % 4
        send(w.at[rows32(h, ko), ca], w_hop.at[2 * i], W_HOP + 2 * i, first(kr))
        send(w.at[rows32(h, ko), cb], w_hop.at[2 * i + 1], W_HOP + 2 * i + 1, first(kl))
        send(w.at[rows32(h, kr), cb], w_side.at[4 * i + 1], W_NEXT + 4 * i + 1, first(kr))
        send(w.at[rows32(h, kl), ca], w_side.at[4 * i + 2], W_NEXT + 4 * i + 2, first(kl))

    def w_step_2(h, u):
        k, q, first, _ = places(u)
        ca, cb = cols_ab(u)
        i = 2 * h + u
        kr, kl = (k + 1) % 4, (k + 3) % 4
        arrive(w_hop.at[2 * i], W_HOP + 2 * i)
        w[rows32(h, kr), ca] += w_hop[2 * i]
        send(w.at[rows32(h, kr), ca], w_side.at[4 * i], W_NEXT + 4 * i, first(kr))
        arrive(w_hop.at[2 * i + 1], W_HOP + 2 * i + 1)
        w[rows32(h, kl), cb] += w_hop[2 * i + 1]
        send(w.at[rows32(h, kl), cb], w_side.at[4 * i + 3], W_NEXT + 4 * i + 3, first(kl))

    def w_step_3(h, u):
        k, q, _, second = places(u)
        ca, cb = cols_ab(u)
        i = 2 * h + u
        for s in range(4):
            arrive(w_side.at[4 * i + s], W_NEXT + 4 * i + s)
        w[rows32(h, k), ca] += w_side[4 * i] + w_side[4 * i + 2]
        w[rows32(h, k), cb] += w_side[4 * i + 1] + w_side[4 * i + 3]

        @pl.loop(1, 4)
        def _(d):
            to, slot = (q + d) % 4, 3 * i + d - 1
            send(w.at[rows8(h, k, to), cols_u(u)], w_sub.at[slot], W_SUB + slot, second(to))

    def w_step_4(h, u):
        k, q, _, second = places(u)
        i = 2 * h + u

        @pl.loop(0, 3)
        def _(d):
            arrive(w_sub.at[3 * i + d], W_SUB + 3 * i + d)

        w_full[rows8(h, k, q), cols_u(u)] = (w[rows8(h, k, q), cols_u(u)] + w_sub[3 * i]) + (
            w_sub[3 * i + 1] + w_sub[3 * i + 2]
        )

        @pl.loop(1, 4)
        def _(d):
            mine = w_full.at[rows8(h, k, q), cols_u(u)]
            send(mine, mine, W_ALL + 3 * i + d - 1, second((q + d) % 4))

    def w_step_5(h, u):
        k, q, first, _ = places(u)
        ca, cb = cols_ab(u)
        i = 2 * h + u
        dr, dl = first((k + 1) % 4), first((k + 3) % 4)

        @pl.loop(1, 4)
        def _(d):
            arrive(w_full.at[rows8(h, k, (q + 4 - d) % 4), cols_u(u)], W_ALL + 3 * i + d - 1)

        mine_a, mine_b = w_full.at[rows32(h, k), ca], w_full.at[rows32(h, k), cb]
        send(mine_a, mine_a, W_RING + 4 * i, dr)
        send(mine_b, mine_b, W_RING + 4 * i + 3, dl)
        send(mine_b, mine_b, W_RING + 4 * i + 1, dr)
        send(mine_a, mine_a, W_RING + 4 * i + 2, dl)

    def w_step_6(h, u):
        k, q, first, _ = places(u)
        ca, cb = cols_ab(u)
        i = 2 * h + u
        kr, kl = (k + 1) % 4, (k + 3) % 4
        from_left = w_full.at[rows32(h, kl), ca]
        arrive(from_left, W_RING + 4 * i)
        send(from_left, from_left, W_FAR + 2 * i, first(kr))
        from_right = w_full.at[rows32(h, kr), cb]
        arrive(from_right, W_RING + 4 * i + 3)
        send(from_right, from_right, W_FAR + 2 * i + 1, first(kl))

    def w_step_7(h, u):
        k = places(u)[0]
        ca, cb = cols_ab(u)
        i = 2 * h + u
        kr, kl, ko = (k + 1) % 4, (k + 3) % 4, (k + 2) % 4
        arrive(w_full.at[rows32(h, kl), cb], W_RING + 4 * i + 1)
        arrive(w_full.at[rows32(h, kr), ca], W_RING + 4 * i + 2)
        arrive(w_full.at[rows32(h, ko), ca], W_FAR + 2 * i)
        arrive(w_full.at[rows32(h, ko), cb], W_FAR + 2 * i + 1)

    def all_parts(step):
        @pl.loop(0, 4)
        def _(i):
            step(i // 2, i % 2)

    all_parts(w_step_1)
    gram_pair()
    all_parts(w_step_2)
    w_steps_at = (None, w_step_4, None, w_step_5, None, w_step_6, None, w_step_7)

    arrive(gram_half(1 - c), GRAM_CORE)
    all_parts(w_step_3)
    elim[:, :RANK] = gram[...]
    rr = lax.broadcasted_iota(jnp.int32, (RANK, RANK), 0)
    cc = lax.broadcasted_iota(jnp.int32, (RANK, RANK), 1)
    elim[:, RANK:] = jnp.where(rr == cc, 1.0, 0.0).astype(F32)

    for half in range(2):

        @pl.loop(4 * half, 4 * half + 4)
        def _(k):
            eliminate(k, half, elim)
            for at in range(4 * half, 4 * half + 4):
                if w_steps_at[at] is not None:

                    @pl.when(k == at)
                    def _():
                        all_parts(w_steps_at[at])

    f_hi, f_lo = split(elim[:, RANK:])
    factor = jnp.concatenate([f_hi, f_hi, f_lo], axis=1)
    squares = jnp.zeros((RANK, 128), F32)
    for n in range(4):
        cols = slice(256 * n, 256 * n + 256)
        w_hi, w_lo = split(w_full[:, cols])
        back = nn(factor, jnp.concatenate([w_hi, w_lo, w_hi], axis=0))
        back_out[:, cols] = back
        squares = squares + (back[:, :128] * back[:, :128] + back[:, 128:] * back[:, 128:])
    sq_v[t] = nt(jnp.ones((8, 128), F32), squares, HIGH)

    @pl.loop(1, 8)
    def _(d):
        send(sq_v.at[t], sq_v.at[t], SQ + d - 1, {"fsdp": f, "tp": (t + d) % 8})


    t_hi, t_lo = split(elim[:, RANK:].T)
    turned[:, :256] = t_hi
    turned[:, 256:512] = t_lo

    @pl.loop(0, LOCAL_ROWS // STEP)
    def _(i):
        rows = pl.ds(pl.multiple_of(i * STEP, 64), STEP)
        hi, lo = split(proj[rows, :])
        first, second = turned[:, :256], turned[:, 256:512]
        ortho_out[rows, :] = nn(hi, first) + nn(hi, second) + nn(lo, first)

    all_sent(N_HOP_A, 12, side_v.at[0])
    all_sent(N_CORE, 8, part_v.at[0])
    all_sent(GRAM_SUM, 33, sq_v.at[0])
    all_sent(GRAM_CORE, 1, gram_part)
    all_sent(W_HOP, 48, w_hop.at[0])
    all_sent(W_SUB, 24, w_sub.at[0])

    @pl.loop(1, 8)
    def _(d):
        arrive(sq_v.at[(t + 8 - d) % 8], SQ + d - 1)

    norm_out[...] = lax.rsqrt(jnp.sum(sq_v[...], axis=0) + 1e-06)
    all_sent(SQ, 7, sq_v.at[0])


def write_kernel(
    blend, ortho, back, norm, mom_out, basis_out, update_out, backs, mom_v, basis_v, update_v, sems
):
    hi, lo = split(back[...])
    backs[:RANK] = hi
    backs[RANK : 2 * RANK] = lo
    backs[2 * RANK :] = hi
    scale = (ROWS * COLS / RANK) ** 0.5
    norms = norm[0:1, :]

    def copies(i):
        slot = i % 2
        found = []
        for p in range(2):
            rows = pl.ds(pl.multiple_of(i * STEP + p * PIECE, 32), PIECE)
            here = pl.ds(p * PIECE, PIECE)
            found.append(pltpu.make_async_copy(mom_v.at[slot, here], mom_out.at[rows], sems.at[slot, p]))
            found.append(
                pltpu.make_async_copy(update_v.at[slot, here], update_out.at[rows], sems.at[slot, 2 + p])
            )
        rank_rows = pl.ds(pl.multiple_of(i * 256, 256), 256)
        found.append(pltpu.make_async_copy(basis_v.at[slot], basis_out.at[rank_rows], sems.at[slot, 4]))
        return found

    @pl.loop(0, LOCAL_ROWS // STEP)
    def _(i):
        slot = i % 2

        @pl.when(i >= 2)
        def _():
            for copy in copies(i - 2):
                copy.wait()

        rows = pl.ds(pl.multiple_of(i * STEP, 64), STEP)
        cols = pl.ds(pl.multiple_of(i * 256, 256), 256)
        basis_v[slot] = back[:, cols].T * norms
        plain = ortho[rows, :]
        mom_v[slot] = blend[rows, :] - nn((0.05 * plain).astype(BF16), backs[:RANK])
        mom_a, update_a, mom_b, update_b, basis_copy = copies(i)
        mom_a.start()
        mom_b.start(priority=1)
        basis_copy.start()
        hi, lo = split(plain * (scale * norms))
        update_v[slot] = nn(jnp.concatenate([hi, hi, lo], axis=1), backs[...]).astype(BF16)
        update_a.start()
        update_b.start(priority=1)

    for i in (2, 3):
        for copy in copies(i):
            copy.wait()


def body(gradient, momentum, basis):
    anywhere = pl.BlockSpec(memory_space=pl.ANY)
    inside = pl.BlockSpec(memory_space=pltpu.VMEM)
    vmem = pltpu.VMEM
    fixed = [pltpu.with_memory_space_constraint(a, pltpu.HBM) for a in (gradient, momentum, basis)]
    results = pl.pallas_call(
        main_kernel,
        out_shape=(
            vmem((LOCAL_ROWS, LOCAL_COLS), F32),
            vmem((LOCAL_ROWS, RANK), F32),
            vmem((RANK, LOCAL_COLS), F32),
            vmem((8, RANK), F32),
        ),
        in_specs=[anywhere] * 3,
        out_specs=(inside,) * 4,
        scratch_shapes=[
            vmem((4, PIECE, LOCAL_COLS), BF16),
            vmem((LOCAL_COLS, RANK), F32),
            vmem((2 * LOCAL_COLS, RANK), BF16),
            vmem((LOCAL_ROWS + 32, LOCAL_COLS), BF16),
            vmem((LOCAL_ROWS + 32, LOCAL_COLS), BF16),
            vmem((8, PIECE, RANK), F32),
            vmem((4, PIECE, RANK), F32),
            vmem((2, PART, RANK), F32),
            vmem((4, PART, RANK), F32),
            vmem((LOCAL_ROWS, RANK), F32),
            vmem((128, RANK), F32),
            vmem((16, 8, RANK), F32),
            vmem((4, 8, RANK), F32),
            vmem((RANK, RANK), F32),
            vmem((RANK, 2 * RANK), F32),
            vmem((RANK, 3 * 256), BF16),
            vmem((RANK, LOCAL_COLS), F32),
            vmem((8, 32, 256), F32),
            vmem((16, 32, 256), F32),
            vmem((12, 8, WIDE), F32),
            vmem((RANK, LOCAL_COLS), F32),
            vmem((8, 8, RANK), F32),
            pltpu.SemaphoreType.DMA((17,)),
            pltpu.SemaphoreType.DMA((NAMES.count,)),
            pltpu.SemaphoreType.DMA((NAMES.count,)),
        ],
        compiler_params=pltpu.CompilerParams(
            collective_id=0, has_side_effects=True, vmem_limit_bytes=44 * 2**20
        ),
        name="transfers",
    )(*fixed)
    results = [pltpu.with_memory_space_constraint(a, pltpu.VMEM) for a in results]

    return pl.pallas_call(
        write_kernel,
        out_shape=(
            jax.ShapeDtypeStruct((LOCAL_ROWS, LOCAL_COLS), F32),
            jax.ShapeDtypeStruct((LOCAL_COLS, RANK), F32),
            jax.ShapeDtypeStruct((LOCAL_ROWS, LOCAL_COLS), BF16),
        ),
        in_specs=[inside] * 4,
        out_specs=(anywhere,) * 3,
        scratch_shapes=[
            vmem((3 * RANK, LOCAL_COLS), BF16),
            vmem((2, STEP, LOCAL_COLS), F32),
            vmem((2, 256, RANK), F32),
            vmem((2, STEP, LOCAL_COLS), BF16),
            pltpu.SemaphoreType.DMA((2, 5)),
        ],
        compiler_params=pltpu.CompilerParams(vmem_limit_bytes=32 * 2**20),
        name="outputs",
    )(*results)


def solution(mesh):
    placed = (P("fsdp", "tp"), P("fsdp", "tp"), P("tp", None))
    return jax.shard_map(
        body,
        mesh=mesh,
        in_specs=placed,
        out_specs=(P("fsdp", "tp"), P("tp", None), P("fsdp", "tp")),
        check_vma=False,
    )
```

```python
import functools

import jax
import jax.numpy as jnp
from jax import lax
from jax.experimental import pallas as pl
from jax.experimental.pallas import tpu as pltpu
from jax.sharding import PartitionSpec as P

ROWS = 28672
COLS = 8192
RANK = 256

F32 = jnp.float32
BF16 = jnp.bfloat16
HIGH = lax.Precision.HIGHEST
MESH = pl.DeviceIdType.MESH

LOCAL_ROWS = 1792
LOCAL_COLS = 1024
HALF = 896
PIECE = 224
PART = 112
STEP = 448
WIDE = 512


class Names:
    def __init__(self):
        self.count = 0

    def take(self, many=1):
        first = self.count
        self.count += many
        return first


NAMES = Names()
N_HOP_A, N_HOP_B = NAMES.take(), NAMES.take()
N_LEFT_A, N_LEFT_B = NAMES.take(), NAMES.take()
N_RIGHT_A, N_RIGHT_B = NAMES.take(), NAMES.take()
G_LEFT_A, G_LEFT_B = NAMES.take(), NAMES.take()
G_RIGHT_A, G_RIGHT_B = NAMES.take(), NAMES.take()
G_OPP_A, G_OPP_B = NAMES.take(), NAMES.take()
N_CORE = NAMES.take(4)
G_CORE = NAMES.take(4)
GRAM_SUM = NAMES.take(15)
GRAM_X = NAMES.take(3)
GRAM_ALL = NAMES.take(15)
SQ = NAMES.take(7)
GRAM_CORE = NAMES.take()
W_HOP = NAMES.take(8)
W_NEXT = NAMES.take(16)
W_RING = NAMES.take(16)
W_FAR = NAMES.take(8)
W_SUB = NAMES.take(12)
W_ALL = NAMES.take(12)


def nn(a, b, precision=None):
    return lax.dot_general(
        a, b, (((1,), (0,)), ((), ())), precision=precision, preferred_element_type=F32
    )


def tn(a, b, precision=None):
    return lax.dot_general(
        a, b, (((0,), (0,)), ((), ())), precision=precision, preferred_element_type=F32
    )


def nt(a, b, precision=None):
    return lax.dot_general(
        a, b, (((1,), (1,)), ((), ())), precision=precision, preferred_element_type=F32
    )


def pick(index, values):
    out = values[0]
    for at in range(1, len(values)):
        out = out + (values[at] - values[at - 1]) * ((index + len(values) - at) // len(values))
    return out


def split(x):
    hi = x.astype(BF16)
    return hi, (x - hi.astype(F32)).astype(BF16)


def row_copy(x, j):
    return jnp.broadcast_to(x[j : j + 1, :], (8, 128))


def inverse_factor(x):
    x = list(x)
    n = len(x)
    sub = lax.broadcasted_iota(jnp.int32, (8, 128), 0)
    for g in range(n):
        lanes = [32 + 8 * g + j for j in range(8)]
        col = {i: [jnp.broadcast_to(x[i][:, at : at + 1], (8, 128)) for at in lanes] for i in range(g, n)}
        entry = [[row_copy(col[g][j], i) for j in range(i + 1)] for i in range(8)]
        rows = [row_copy(x[g], j) for j in range(8)]
        inv, mult = [], [[None] * 8 for _ in range(8)]
        for j in range(8):
            inv.append(1.0 / entry[j][j])
            for k in range(j + 1, 8):
                mult[k][j] = entry[k][j] * inv[j]
                for i in range(k, 8):
                    entry[i][k] = entry[i][k] - entry[i][j] * mult[k][j]
                rows[k] = rows[k] - mult[k][j] * rows[j]
        for i in range(g + 1, n):
            c = col[i]
            for j in range(8):
                for k in range(j + 1, 8):
                    c[k] = c[k] - c[j] * mult[k][j]
                x[i] = x[i] - (c[j] * inv[j]) * rows[j]
        final = jnp.zeros((8, 128), F32)
        for j in range(8):
            final = jnp.where(sub == j, rows[j] * lax.rsqrt(entry[j][j]), final)
        x[g] = final
    return jnp.concatenate(x, axis=0)


def split3(x):
    first = x.astype(BF16)
    rest = x - first.astype(F32)
    second = rest.astype(BF16)
    return first, second, (rest - second.astype(F32)).astype(BF16)


def eliminate(k, half, m_ref):
    left = 128 * half
    cols = slice(left, left + 384)
    rows = pl.ds(pl.multiple_of(32 * k, 32), 32)
    lane = lax.broadcasted_iota(jnp.int32, (32, 128), 1)
    subl = lax.broadcasted_iota(jnp.int32, (32, 128), 0)
    d = pltpu.roll(m_ref[rows, left : left + 128], (160 - 32 * (k % 4)) % 128, 1)
    x = jnp.where(lane < 32, jnp.where(lane == subl, 1.0, 0.0), d)
    inverse = inverse_factor([x[8 * i : 8 * i + 8] for i in range(4)])
    scaled = nn(inverse[:, :32], m_ref[rows, cols], HIGH)
    m_ref[rows, cols] = scaled

    @pl.when(k < 7)
    def _():
        lane = lax.broadcasted_iota(jnp.int32, (32, RANK - left), 1)
        lower = jnp.where(lane >= 32 * k + 32 - left, scaled[:, : RANK - left], 0.0)
        a, b, c = split3(lower)
        d, e, f = split3(scaled)
        m_ref[left:, cols] -= tn(
            jnp.concatenate([a, a, b, a, b, c], axis=0), jnp.concatenate([d, e, d, f, e, d], axis=0)
        )


def main_kernel(
    grad,
    mom,
    basis,
    blend_out,
    ortho_out,
    back_out,
    norm_out,
    grad_v,
    basis_v,
    bases,
    hi_v,
    lo_v,
    part_v,
    from_core,
    hop_v,
    side_v,
    proj,
    gram_part,
    gram_in,
    gram_x,
    gram,
    elim,
    turned,
    w,
    w_hop,
    w_side,
    w_sub,
    w_full,
    sq_v,
    load_sem,
    send_sem,
    recv_sem,
):
    f = lax.axis_index("fsdp")
    t = lax.axis_index("tp")
    x, c = t // 2, t % 2
    z, y = f // 4, f % 4

    def tp_dev(xx, cc):
        return {"fsdp": f, "tp": xx * 2 + cc}

    def f_dev(ff):
        return {"fsdp": ff, "tp": t}

    right = tp_dev((x + 1) % 4, c)
    left = tp_dev((x + 3) % 4, c)
    twin = tp_dev(x, 1 - c)

    def remote(src, dst, number, device):
        return pltpu.make_async_remote_copy(
            src_ref=src,
            dst_ref=dst,
            send_sem=send_sem.at[number],
            recv_sem=recv_sem.at[number],
            device_id=device,
            device_id_type=MESH,
        )

    def send(src, dst, number, device):
        remote(src, dst, number, device).start()

    def arrive(dst, number):
        remote(dst, dst, number, twin).wait_recv()

    def all_sent(first, many, ref):
        @pl.loop(first, first + many)
        def _(number):
            remote(ref, ref, number, twin).wait_send()

    def piece_row(core, chip):
        return pl.multiple_of(core * HALF + chip * PIECE, 32)

    def chunk_row(i):
        g = 3 - i // 2
        d = g + (g // 2) * (1 - 2 * (g % 2))
        core = (1 - c) * (1 - i % 2) + c * (i % 2)
        return piece_row(core, (x + d) % 4)

    def load(i):
        rows = pl.ds(chunk_row(i), PIECE)
        return (
            pltpu.make_async_copy(mom.at[rows], blend_out.at[rows], load_sem.at[2 * i]),
            pltpu.make_async_copy(grad.at[rows], grad_v.at[i % 4], load_sem.at[2 * i + 1]),
        )

    basis_copy = pltpu.make_async_copy(basis, basis_v, load_sem.at[16])
    basis_copy.start()

    @pl.loop(0, 3)
    def _(i):
        for copy in load(i):
            copy.start()

    barrier = pltpu.get_barrier_semaphore()

    @pl.loop(1, 16)
    def _(d):
        pl.semaphore_signal(barrier, inc=1, device_id=f_dev((f + d) % 16), device_id_type=MESH)

    @pl.loop(1, 8)
    def _(d):
        pl.semaphore_signal(
            barrier, inc=1, device_id={"fsdp": f, "tp": (t + d) % 8}, device_id_type=MESH
        )

    basis_copy.wait()
    basis_hi, basis_lo = split(basis_v[...])
    bases[:LOCAL_COLS] = basis_hi
    bases[LOCAL_COLS:] = basis_lo
    turned[...] = jnp.zeros_like(turned)
    hi_v[LOCAL_ROWS:, :] = jnp.zeros((32, LOCAL_COLS), BF16)
    lo_v[LOCAL_ROWS:, :] = jnp.zeros((32, LOCAL_COLS), BF16)

    def partial(i):
        for copy in load(i):
            copy.wait()
        rows = pl.ds(chunk_row(i), PIECE)

        @pl.when(i < 5)
        def _():
            for copy in load(i + 3):
                copy.start()

        blend = blend_out[rows, :] + grad_v[i % 4].astype(F32)
        blend_out[rows, :] = blend
        hi, lo = split(blend)
        hi_v[rows, :] = hi
        lo_v[rows, :] = lo
        first, second = bases[:LOCAL_COLS], bases[LOCAL_COLS:]
        return nn(hi, first) + nn(hi, second) + nn(lo, first)

    a_rows, b_rows = pl.ds(0, PART), pl.ds(PART, PART)

    def add_core(j):
        arrive(from_core.at[j], N_CORE + j)
        part_v[2 * j + 1] += from_core[j]

    @pl.loop(0, 8)
    def _(i):
        part_v[i] = partial(i)
        j = i // 2
        core = remote(part_v.at[i], from_core.at[j], N_CORE + j, twin)

        @pl.when(i == 0)
        def _():
            pl.semaphore_wait(barrier, 22)

        @pl.when(i % 2 == 0)
        def _():
            core.start()

        @pl.when(i == 2)
        def _():
            add_core(0)
            send(part_v.at[1, a_rows], hop_v.at[0], N_HOP_A, right)
            send(part_v.at[1, b_rows], hop_v.at[1], N_HOP_B, left)

        @pl.when(i == 4)
        def _():
            add_core(1)
            send(part_v.at[3, a_rows], side_v.at[2], N_RIGHT_A, left)

        @pl.when(i == 6)
        def _():
            add_core(2)
            send(part_v.at[5, b_rows], side_v.at[1], N_LEFT_B, right)
            arrive(hop_v.at[0], N_HOP_A)
            part_v[5, a_rows] += hop_v[0]
            send(part_v.at[5, a_rows], side_v.at[0], N_LEFT_A, right)
            arrive(hop_v.at[1], N_HOP_B)
            part_v[3, b_rows] += hop_v[1]
            send(part_v.at[3, b_rows], side_v.at[3], N_RIGHT_B, left)

    add_core(3)
    my_row = piece_row(c, x)
    arrive(side_v.at[2], N_RIGHT_A)
    arrive(side_v.at[0], N_LEFT_A)
    proj[pl.ds(my_row, PART), :] = part_v[7, a_rows] + (side_v[0] + side_v[2])
    arrive(side_v.at[1], N_LEFT_B)
    arrive(side_v.at[3], N_RIGHT_B)
    proj[pl.ds(my_row + PART, PART), :] = part_v[7, b_rows] + (side_v[1] + side_v[3])

    def part_of(core, chip, b):
        return proj.at[pl.ds(pl.multiple_of(piece_row(core, chip) + b * PART, 16), PART)]

    def whole_of(core, chip):
        return proj.at[pl.ds(piece_row(core, chip), PIECE)]

    def send_part(chip, b, number, device):
        send(part_of(c, chip, b), part_of(c, chip, b), number, device)

    def send_whole(chip, number):
        send(whole_of(c, chip), whole_of(c, chip), number, twin)

    xl, xr, xo = (x + 3) % 4, (x + 1) % 4, (x + 2) % 4
    send_part(x, 0, G_LEFT_A, right)
    send_part(x, 1, G_RIGHT_B, left)
    send_whole(x, G_CORE)
    send_part(x, 1, G_LEFT_B, right)
    send_part(x, 0, G_RIGHT_A, left)

    half_cols = pl.ds(pl.multiple_of(c * 128, 128), 128)

    def eight(row):
        return pl.ds(pl.multiple_of(row * 8, 8), 8)

    def gram_start():
        halves = []
        for core in range(2):
            rows = pl.ds(piece_row(core, x), PIECE)
            a, b, d = split3(proj[rows, half_cols])
            left = jnp.concatenate([a, a, b, a, b, d], axis=0)
            a, b, d = split3(proj[rows, :])
            halves.append(tn(left, jnp.concatenate([a, b, a, d, b, a], axis=0)))
        gram_part[...] = halves[0] + halves[1]

        @pl.loop(1, 16)
        def _(d):
            to = (f + d) % 16
            send(gram_part.at[eight(to)], gram_in.at[d], GRAM_SUM + d - 1, f_dev(to))

    def gram_across():
        gram_in[0] = gram_part[eight(f), :]

        @pl.loop(1, 16)
        def _(d):
            arrive(gram_in.at[d], GRAM_SUM + d - 1)

        gram_x[x] = jnp.sum(gram_in[...], axis=0)

        @pl.loop(1, 4)
        def _(d):
            send(gram_x.at[x], gram_x.at[x], GRAM_X + d - 1, tp_dev((x + d) % 4, c))

    def gram_row(ff):
        return pl.ds(pl.multiple_of(c * 128 + ff * 8, 8), 8)

    def gram_round():
        @pl.loop(1, 4)
        def _(d):
            arrive(gram_x.at[(x + 4 - d) % 4], GRAM_X + d - 1)

        gram[gram_row(f), :] = (gram_x[0] + gram_x[1]) + (gram_x[2] + gram_x[3])

        @pl.loop(1, 16)
        def _(d):
            mine = gram.at[gram_row(f)]
            send(mine, mine, GRAM_ALL + d - 1, f_dev((f + d) % 16))

    def gram_half(core):
        return gram.at[pl.ds(pl.multiple_of(core * 128, 128), 128)]

    def gram_pair():
        @pl.loop(1, 16)
        def _(d):
            arrive(gram.at[gram_row((f + 16 - d) % 16)], GRAM_ALL + d - 1)

        send(gram_half(c), gram_half(c), GRAM_CORE, twin)

    w[...] = jnp.zeros_like(w)

    @pl.loop(0, 8)
    def _(g):
        core = (c + pick(g, (0, 1, 0, 0, 0, 1, 1, 1))) % 2
        chip = (x + pick(g, (0, 0, 1, 3, 2, 1, 3, 2))) % 4

        @pl.when(g == 1)
        def _():
            arrive(whole_of(1 - c, x), G_CORE)
            gram_start()

        @pl.when(g == 2)
        def _():
            arrive(part_of(c, xl, 0), G_LEFT_A)
            send_part(xl, 0, G_OPP_A, right)
            arrive(part_of(c, xr, 1), G_RIGHT_B)
            send_part(xr, 1, G_OPP_B, left)
            gram_across()
            arrive(part_of(c, xr, 0), G_RIGHT_A)
            send_whole(xr, G_CORE + 1)
            arrive(part_of(c, xl, 1), G_LEFT_B)
            send_whole(xl, G_CORE + 2)

        @pl.when(g == 4)
        def _():
            arrive(part_of(c, xo, 0), G_OPP_A)
            arrive(part_of(c, xo, 1), G_OPP_B)
            send_whole(xo, G_CORE + 3)
            gram_round()

        @pl.when(g == 5)
        def _():
            arrive(whole_of(1 - c, xr), G_CORE + 1)

        @pl.when(g == 6)
        def _():
            arrive(whole_of(1 - c, xl), G_CORE + 2)

        @pl.when(g == 7)
        def _():
            arrive(whole_of(1 - c, xo), G_CORE + 3)

        rows = pl.ds(piece_row(core, chip), PIECE)
        p_hi, p_lo = split(proj[rows, :].T)
        turned[:, :PIECE] = p_hi
        turned[:, 256 : 256 + PIECE] = p_hi
        turned[:, 512 : 512 + PIECE] = p_lo
        more = pl.ds(piece_row(core, chip), 256)
        for n in range(4):
            cols = slice(256 * n, 256 * n + 256)
            hi = hi_v[more, cols]
            w[:, cols] += nn(turned[...], jnp.concatenate([hi, lo_v[more, cols], hi], axis=0))

    def places(u):
        k, q = y + u * (z - y), z + u * (y - z)

        def first(kk):
            return f_dev(z * 4 + kk + u * (kk * 4 + y - z * 4 - kk))

        def second(qq):
            return f_dev(qq * 4 + y + u * (z * 4 + qq - qq * 4 - y))

        return k, q, first, second

    def cols_ab(u):
        start = pl.multiple_of(WIDE * u, WIDE)
        return pl.ds(start, 256), pl.ds(pl.multiple_of(start + 256, 256), 256)

    def cols_u(u):
        return pl.ds(pl.multiple_of(WIDE * u, WIDE), WIDE)

    def rows32(h, k):
        return pl.ds(pl.multiple_of(128 * h + 32 * k, 32), 32)

    def rows8(h, k, q):
        return pl.ds(pl.multiple_of(128 * h + 32 * k + 8 * q, 8), 8)

    def w_step_1(h, u):
        k, q, first, _ = places(u)
        ca, cb = cols_ab(u)
        i = 2 * h + u
        kr, kl, ko = (k + 1) % 4, (k + 3) % 4, (k + 2) % 4
        send(w.at[rows32(h, ko), ca], w_hop.at[2 * i], W_HOP + 2 * i, first(kr))
        send(w.at[rows32(h, ko), cb], w_hop.at[2 * i + 1], W_HOP + 2 * i + 1, first(kl))
        send(w.at[rows32(h, kr), cb], w_side.at[4 * i + 1], W_NEXT + 4 * i + 1, first(kr))
        send(w.at[rows32(h, kl), ca], w_side.at[4 * i + 2], W_NEXT + 4 * i + 2, first(kl))

    def w_step_2(h, u):
        k, q, first, _ = places(u)
        ca, cb = cols_ab(u)
        i = 2 * h + u
        kr, kl = (k + 1) % 4, (k + 3) % 4
        arrive(w_hop.at[2 * i], W_HOP + 2 * i)
        w[rows32(h, kr), ca] += w_hop[2 * i]
        send(w.at[rows32(h, kr), ca], w_side.at[4 * i], W_NEXT + 4 * i, first(kr))
        arrive(w_hop.at[2 * i + 1], W_HOP + 2 * i + 1)
        w[rows32(h, kl), cb] += w_hop[2 * i + 1]
        send(w.at[rows32(h, kl), cb], w_side.at[4 * i + 3], W_NEXT + 4 * i + 3, first(kl))

    def w_step_3(h, u):
        k, q, _, second = places(u)
        ca, cb = cols_ab(u)
        i = 2 * h + u
        for s in range(4):
            arrive(w_side.at[4 * i + s], W_NEXT + 4 * i + s)
        w[rows32(h, k), ca] += w_side[4 * i] + w_side[4 * i + 2]
        w[rows32(h, k), cb] += w_side[4 * i + 1] + w_side[4 * i + 3]

        @pl.loop(1, 4)
        def _(d):
            to, slot = (q + d) % 4, 3 * i + d - 1
            send(w.at[rows8(h, k, to), cols_u(u)], w_sub.at[slot], W_SUB + slot, second(to))

    def w_step_4(h, u):
        k, q, _, second = places(u)
        i = 2 * h + u

        @pl.loop(0, 3)
        def _(d):
            arrive(w_sub.at[3 * i + d], W_SUB + 3 * i + d)

        w_full[rows8(h, k, q), cols_u(u)] = (w[rows8(h, k, q), cols_u(u)] + w_sub[3 * i]) + (
            w_sub[3 * i + 1] + w_sub[3 * i + 2]
        )

        @pl.loop(1, 4)
        def _(d):
            mine = w_full.at[rows8(h, k, q), cols_u(u)]
            send(mine, mine, W_ALL + 3 * i + d - 1, second((q + d) % 4))

    def w_step_5(h, u):
        k, q, first, _ = places(u)
        ca, cb = cols_ab(u)
        i = 2 * h + u
        dr, dl = first((k + 1) % 4), first((k + 3) % 4)

        @pl.loop(1, 4)
        def _(d):
            arrive(w_full.at[rows8(h, k, (q + 4 - d) % 4), cols_u(u)], W_ALL + 3 * i + d - 1)

        mine_a, mine_b = w_full.at[rows32(h, k), ca], w_full.at[rows32(h, k), cb]
        send(mine_a, mine_a, W_RING + 4 * i, dr)
        send(mine_b, mine_b, W_RING + 4 * i + 3, dl)
        send(mine_b, mine_b, W_RING + 4 * i + 1, dr)
        send(mine_a, mine_a, W_RING + 4 * i + 2, dl)

    def w_step_6(h, u):
        k, q, first, _ = places(u)
        ca, cb = cols_ab(u)
        i = 2 * h + u
        kr, kl = (k + 1) % 4, (k + 3) % 4
        from_left = w_full.at[rows32(h, kl), ca]
        arrive(from_left, W_RING + 4 * i)
        send(from_left, from_left, W_FAR + 2 * i, first(kr))
        from_right = w_full.at[rows32(h, kr), cb]
        arrive(from_right, W_RING + 4 * i + 3)
        send(from_right, from_right, W_FAR + 2 * i + 1, first(kl))

    def w_step_7(h, u):
        k = places(u)[0]
        ca, cb = cols_ab(u)
        i = 2 * h + u
        kr, kl, ko = (k + 1) % 4, (k + 3) % 4, (k + 2) % 4
        arrive(w_full.at[rows32(h, kl), cb], W_RING + 4 * i + 1)
        arrive(w_full.at[rows32(h, kr), ca], W_RING + 4 * i + 2)
        arrive(w_full.at[rows32(h, ko), ca], W_FAR + 2 * i)
        arrive(w_full.at[rows32(h, ko), cb], W_FAR + 2 * i + 1)

    def all_parts(step):
        @pl.loop(0, 4)
        def _(i):
            step(i // 2, i % 2)

    all_parts(w_step_1)
    gram_pair()
    all_parts(w_step_2)
    w_steps_at = (None, w_step_4, None, w_step_5, None, w_step_6, None, w_step_7)

    arrive(gram_half(1 - c), GRAM_CORE)
    all_parts(w_step_3)
    elim[:, :RANK] = gram[...]
    rr = lax.broadcasted_iota(jnp.int32, (RANK, RANK), 0)
    cc = lax.broadcasted_iota(jnp.int32, (RANK, RANK), 1)
    elim[:, RANK:] = jnp.where(rr == cc, 1.0, 0.0).astype(F32)

    for half in range(2):

        @pl.loop(4 * half, 4 * half + 4)
        def _(k):
            eliminate(k, half, elim)
            for at in range(4 * half, 4 * half + 4):
                if w_steps_at[at] is not None:

                    @pl.when(k == at)
                    def _():
                        all_parts(w_steps_at[at])

    f_hi, f_lo = split(elim[:, RANK:])
    factor = jnp.concatenate([f_hi, f_hi, f_lo], axis=1)
    squares = jnp.zeros((RANK, 128), F32)
    for n in range(4):
        cols = slice(256 * n, 256 * n + 256)
        w_hi, w_lo = split(w_full[:, cols])
        back = nn(factor, jnp.concatenate([w_hi, w_lo, w_hi], axis=0))
        back_out[:, cols] = back
        squares = squares + (back[:, :128] * back[:, :128] + back[:, 128:] * back[:, 128:])
    sq_v[t] = nt(jnp.ones((8, 128), F32), squares, HIGH)

    @pl.loop(1, 8)
    def _(d):
        send(sq_v.at[t], sq_v.at[t], SQ + d - 1, {"fsdp": f, "tp": (t + d) % 8})


    t_hi, t_lo = split(elim[:, RANK:].T)
    turned[:, :256] = t_hi
    turned[:, 256:512] = t_lo

    @pl.loop(0, LOCAL_ROWS // STEP)
    def _(i):
        rows = pl.ds(pl.multiple_of(i * STEP, 64), STEP)
        hi, lo = split(proj[rows, :])
        first, second = turned[:, :256], turned[:, 256:512]
        ortho_out[rows, :] = nn(hi, first) + nn(hi, second) + nn(lo, first)

    all_sent(N_HOP_A, 12, side_v.at[0])
    all_sent(N_CORE, 8, part_v.at[0])
    all_sent(GRAM_SUM, 33, sq_v.at[0])
    all_sent(GRAM_CORE, 1, gram_part)
    all_sent(W_HOP, 48, w_hop.at[0])
    all_sent(W_SUB, 24, w_sub.at[0])

    @pl.loop(1, 8)
    def _(d):
        arrive(sq_v.at[(t + 8 - d) % 8], SQ + d - 1)

    norm_out[...] = lax.rsqrt(jnp.sum(sq_v[...], axis=0) + 1e-06)
    all_sent(SQ, 7, sq_v.at[0])


def write_kernel(
    blend, ortho, back, norm, mom_out, basis_out, update_out, backs, mom_v, basis_v, update_v, sems
):
    hi, lo = split(back[...])
    backs[:RANK] = hi
    backs[RANK : 2 * RANK] = lo
    backs[2 * RANK :] = hi
    scale = (ROWS * COLS / RANK) ** 0.5
    norms = norm[0:1, :]

    def copies(i):
        slot = i % 2
        found = []
        for p in range(2):
            rows = pl.ds(pl.multiple_of(i * STEP + p * PIECE, 32), PIECE)
            here = pl.ds(p * PIECE, PIECE)
            found.append(pltpu.make_async_copy(mom_v.at[slot, here], mom_out.at[rows], sems.at[slot, p]))
            found.append(
                pltpu.make_async_copy(update_v.at[slot, here], update_out.at[rows], sems.at[slot, 2 + p])
            )
        rank_rows = pl.ds(pl.multiple_of(i * 256, 256), 256)
        found.append(pltpu.make_async_copy(basis_v.at[slot], basis_out.at[rank_rows], sems.at[slot, 4]))
        return found

    @pl.loop(0, LOCAL_ROWS // STEP)
    def _(i):
        slot = i % 2

        @pl.when(i >= 2)
        def _():
            for copy in copies(i - 2):
                copy.wait()

        rows = pl.ds(pl.multiple_of(i * STEP, 64), STEP)
        cols = pl.ds(pl.multiple_of(i * 256, 256), 256)
        basis_v[slot] = back[:, cols].T * norms
        plain = ortho[rows, :]
        mom_v[slot] = blend[rows, :] - nn((0.05 * plain).astype(BF16), backs[:RANK])
        mom_a, update_a, mom_b, update_b, basis_copy = copies(i)
        mom_a.start()
        mom_b.start(priority=1)
        basis_copy.start()
        hi, lo = split(plain * (scale * norms))
        update_v[slot] = nn(jnp.concatenate([hi, hi, lo], axis=1), backs[...]).astype(BF16)
        update_a.start()
        update_b.start(priority=1)

    for i in (2, 3):
        for copy in copies(i):
            copy.wait()


def body(gradient, momentum, basis):
    anywhere = pl.BlockSpec(memory_space=pl.ANY)
    inside = pl.BlockSpec(memory_space=pltpu.VMEM)
    vmem = pltpu.VMEM
    fixed = [pltpu.with_memory_space_constraint(a, pltpu.HBM) for a in (gradient, momentum, basis)]
    results = pl.pallas_call(
        main_kernel,
        out_shape=(
            vmem((LOCAL_ROWS, LOCAL_COLS), F32),
            vmem((LOCAL_ROWS, RANK), F32),
            vmem((RANK, LOCAL_COLS), F32),
            vmem((8, RANK), F32),
        ),
        in_specs=[anywhere] * 3,
        out_specs=(inside,) * 4,
        scratch_shapes=[
            vmem((4, PIECE, LOCAL_COLS), BF16),
            vmem((LOCAL_COLS, RANK), F32),
            vmem((2 * LOCAL_COLS, RANK), BF16),
            vmem((LOCAL_ROWS + 32, LOCAL_COLS), BF16),
            vmem((LOCAL_ROWS + 32, LOCAL_COLS), BF16),
            vmem((8, PIECE, RANK), F32),
            vmem((4, PIECE, RANK), F32),
            vmem((2, PART, RANK), F32),
            vmem((4, PART, RANK), F32),
            vmem((LOCAL_ROWS, RANK), F32),
            vmem((128, RANK), F32),
            vmem((16, 8, RANK), F32),
            vmem((4, 8, RANK), F32),
            vmem((RANK, RANK), F32),
            vmem((RANK, 2 * RANK), F32),
            vmem((RANK, 3 * 256), BF16),
            vmem((RANK, LOCAL_COLS), F32),
            vmem((8, 32, 256), F32),
            vmem((16, 32, 256), F32),
            vmem((12, 8, WIDE), F32),
            vmem((RANK, LOCAL_COLS), F32),
            vmem((8, 8, RANK), F32),
            pltpu.SemaphoreType.DMA((17,)),
            pltpu.SemaphoreType.DMA((NAMES.count,)),
            pltpu.SemaphoreType.DMA((NAMES.count,)),
        ],
        compiler_params=pltpu.CompilerParams(
            collective_id=0, has_side_effects=True, vmem_limit_bytes=44 * 2**20
        ),
        name="transfers",
    )(*fixed)
    results = [pltpu.with_memory_space_constraint(a, pltpu.VMEM) for a in results]

    return pl.pallas_call(
        write_kernel,
        out_shape=(
            jax.ShapeDtypeStruct((LOCAL_ROWS, LOCAL_COLS), F32),
            jax.ShapeDtypeStruct((LOCAL_COLS, RANK), F32),
            jax.ShapeDtypeStruct((LOCAL_ROWS, LOCAL_COLS), BF16),
        ),
        in_specs=[inside] * 4,
        out_specs=(anywhere,) * 3,
        scratch_shapes=[
            vmem((3 * RANK, LOCAL_COLS), BF16),
            vmem((2, STEP, LOCAL_COLS), F32),
            vmem((2, 256, RANK), F32),
            vmem((2, STEP, LOCAL_COLS), BF16),
            pltpu.SemaphoreType.DMA((2, 5)),
        ],
        compiler_params=pltpu.CompilerParams(vmem_limit_bytes=32 * 2**20),
        name="outputs",
    )(*results)


def solution(mesh):
    placed = (P("fsdp", "tp"), P("fsdp", "tp"), P("tp", None))
    return jax.shard_map(
        body,
        mesh=mesh,
        in_specs=placed,
        out_specs=(P("fsdp", "tp"), P("tp", None), P("fsdp", "tp")),
        check_vma=False,
    )
```
